32 devices in a mesh: dp: 4 (over y, x), expert: 8 (over z, core).
Axes of the slice: x: 2, y: 2, z: 4, core: 2. Of those that a mesh axis runs over, the one named last changes fastest.
Arguments:
- inputs: bfloat16 [32768, 768], P(('dp', 'expert')), may hold values from -6 to 6
- cotangent: bfloat16 [32768, 768], P(('dp', 'expert')), may hold values from -6 to 6
- document_ids: int32 [32, 1024], P(('dp', 'expert')), may hold values from 0 to 3, never falling along the last dimension, each value on 1 to 512 neighbouring positions
- domain_counts: int32 [8], replicated, may hold values from 1 to 8, 32 in all
- domain_weight: float32 [8], replicated, may hold values from 0.5 to 2
- token_order: int32 [32, 1024], P(('dp', 'expert')), may hold values from 0 to 1023, as said below
- expert_counts: int32 [32, 8], P(('dp', 'expert')), may hold values from 0 to 256, as said below
- dense_weights: float32 [4, 768, 768], P(None, ('dp', 'expert')), may hold values from -2.5 to 2.5
- vector_params: float32 [10, 768], P(None, ('dp', 'expert')), may hold values from -1 to 4
- expert_weights: float32 [8, 2, 768, 3072], P('expert', None, None, 'dp'), may hold values from -0.5 to 0.5
- dense_first: float32 [4, 768, 768], P(None, ('dp', 'expert')), may hold values from -0.00024414062 to 0.00024414062
- dense_second: float32 [4, 768, 768], P(None, ('dp', 'expert')), may hold values from 2.4927888e-11 to 9.971155e-11
- dense_average: float32 [4, 768, 768], P(None, ('dp', 'expert')), may hold values from -0.21875 to 0.21875
- vector_first: float32 [10, 768], P(None, ('dp', 'expert')), may hold values from -0.00024414062 to 0.00024414062
- vector_second: float32 [10, 768], P(None, ('dp', 'expert')), may hold values from 2.4927888e-11 to 9.971155e-11
- vector_average: float32 [10, 768], P(None, ('dp', 'expert')), may hold values from 0.5 to 1.5
- expert_first: float32 [8, 2, 768, 3072], P('expert', None, None, 'dp'), may hold values from -3.8146973e-05 to 3.8146973e-05
- expert_second: float32 [8, 2, 768, 3072], P('expert', None, None, 'dp'), may hold values from 4.998293e-13 to 1.9993172e-12
- expert_average: float32 [8, 2, 768, 3072], P('expert', None, None, 'dp'), may hold values from -0.21875 to 0.21875
Outputs:
- block_output: float32 [32768, 768], P(('dp', 'expert'))
- input_grad: float32 [32768, 768], P(('dp', 'expert'))
- dense_updated: float32 [4, 768, 768], P(None, ('dp', 'expert'))
- dense_first_new: float32 [4, 768, 768], P(None, ('dp', 'expert'))
- dense_second_new: float32 [4, 768, 768], P(None, ('dp', 'expert'))
- dense_average_new: float32 [4, 768, 768], P(None, ('dp', 'expert'))
- vector_updated: float32 [10, 768], P(None, ('dp', 'expert'))
- vector_first_new: float32 [10, 768], P(None, ('dp', 'expert'))
- vector_second_new: float32 [10, 768], P(None, ('dp', 'expert'))
- vector_average_new: float32 [10, 768], P(None, ('dp', 'expert'))
- expert_updated: float32 [8, 2, 768, 3072], P('expert', None, None, 'dp')
- expert_first_new: float32 [8, 2, 768, 3072], P('expert', None, None, 'dp')
- expert_second_new: float32 [8, 2, 768, 3072], P('expert', None, None, 'dp')
- expert_average_new: float32 [8, 2, 768, 3072], P('expert', None, None, 'dp')
- grad_norm: float32 [], replicated
The draws below stay inside these ranges and needn't reach their ends.
Inputs may be any that keep to these rules, and one draw needn't show every extreme that they name: `token_order`: each row is a permutation of 0 to 1023. `expert_counts`: each row sums to 1024; no entry exceeds 256, every row has an entry equal to 256, and in every draw one expert takes 256 tokens from every row.
All inputs are finite; a program needn't handle non-finite values.
Results may differ from the reference program's by a relative error of at most 0.014.
The reference program's roundings to bfloat16 on the way count: a program that leaves them out, or rounds other values in their place, can miss the bound.
Values may be sent and summed in bfloat16 or wider, within the bound.
A program may use at most 320 MiB of HBM per device.

```python
import math
from functools import partial
import jax
import jax.numpy as jnp
import numpy as np
from jax import lax

D = 768
HEADS = 12
HEAD_DIM = 64
FF = 3072
EXPERTS = 8
LEN = 1024
QBLK = 512
DOCS = 4
NDOM = 8
STEP = 10
GROUPS = 32
TOK_DEV = 1024
SEQS = 32
TOKENS = 32768
CAP = 256
NPARAMS = 40115712


def draw_token_order(key, part):
    key = jax.random.fold_in(key, 11)
    shard_keys = jax.random.split(key, GROUPS)

    def shuffle(shard_key):
        return jax.random.permutation(shard_key, TOK_DEV)
    return jax.vmap(shuffle)(shard_keys).astype(jnp.int32)


def draw_expert_counts(key, part):
    key = jax.random.fold_in(key, 7)
    prefer_key, noise_key, star_key = jax.random.split(key, 3)
    prefer = jax.random.randint(prefer_key, (EXPERTS,), 0, 2 * EXPERTS)
    noise = jax.random.randint(noise_key, (GROUPS, EXPERTS), 0, 2 * EXPERTS)
    star = jax.random.randint(star_key, (), 0, EXPERTS)
    lifted = (jnp.arange(EXPERTS) == star).astype(jnp.int32) * (8 * EXPERTS)
    score = (prefer[None, :] + noise + lifted[None, :]) * EXPERTS + jnp.arange(EXPERTS)[None, :]
    ranks = jnp.argsort(jnp.argsort(score, axis=1), axis=1)
    lower_half = jnp.arange(EXPERTS // 2) * CAP // EXPERTS
    ladder = jnp.sort(jnp.concatenate([lower_half, CAP - lower_half]))
    return ladder[ranks].astype(jnp.int32)


def draw_dense_weights(key, part):
    key = jax.random.fold_in(key, 13)
    base = jax.random.truncated_normal(key, -3.0, 3.0, (4, D, D), jnp.float32)
    scales = jnp.array([0.6, 0.6, 1.0, 8.0], jnp.float32) * D ** (-0.5)
    return base * scales[:, None, None]


def draw_vector_params(key, part):
    key = jax.random.fold_in(key, 17)
    gain_key, centroid_key = jax.random.split(key)
    ramp = 1.0 + 2.0 * jnp.arange(D).astype(jnp.float32) / (D - 1)
    gains = ramp[None, :] * jax.random.uniform(gain_key, (2, D), jnp.float32, 0.8, 1.2)
    centroids = jax.random.truncated_normal(centroid_key, -3.0, 3.0, (EXPERTS, D), jnp.float32) * (0.336 * D ** (-0.5))
    return jnp.concatenate([gains, centroids], axis=0)


def draw_expert_weights(key, part):
    key = jax.random.fold_in(key, 19)
    base = jax.random.truncated_normal(key, -3.0, 3.0, (EXPERTS, 2, D, FF), jnp.float32)
    scales = jnp.array([D ** (-0.5), FF ** (-0.5)], jnp.float32)
    return base * scales[None, :, None, None]


def level_of(rng, shape, shards, smallest, largest):
    def one(dim, blocks):
        heights = jax.random.uniform(jax.random.fold_in(jax.random.fold_in(rng, 6), dim), (blocks,), jnp.float32, smallest / len(shards), largest / len(shards))
        return jnp.repeat(jnp.exp(heights), shape[dim] // blocks).reshape((-1,) + (1,) * (len(shape) - dim - 1))

    gain = one(*shards[0])
    for cut in shards[1:]:
        gain = gain * one(*cut)
    return gain


def length_profile(number_of, total, reach, slope):
    loads = [(1 << 20) // math.isqrt(grade ** slope) + 1 for grade in range(2, number_of + 1)]
    spare, counts = total - reach - (number_of - 1), [1] * (number_of - 1)
    while spare > 0:
        free = [i for i in range(number_of - 1) if counts[i] < reach]
        pool, budget = sum([loads[i] for i in free]), spare
        for i in free:
            addition = min(reach - counts[i], max(1, budget * loads[i] // pool), spare)
            counts[i] = counts[i] + addition
            spare = spare - addition
    return np.array([reach] + counts)


def uneven(stream_key, count, total, limit, lean):
    if count == 2:
        one = jax.random.randint(stream_key, (), max(1, total - limit), min(limit, total - 1) + 1)
        return jnp.stack([one, total - one])
    sizes = jnp.asarray(length_profile(count, total, limit, lean), jnp.int32)
    couples = (count - 1) // 2
    donor, sink = sizes[1:1 + 2 * couples:2], sizes[2:2 + 2 * couples:2]
    room = jnp.minimum(donor - 1, limit - sink)
    passed = jax.random.randint(jax.random.fold_in(stream_key, 1), (couples,), 0, 1 << 20) % (room + 1)
    sizes = sizes.at[1:1 + 2 * couples:2].set(donor - passed).at[2:2 + 2 * couples:2].set(sink + passed)
    return sizes[jax.random.permutation(jax.random.fold_in(stream_key, 2), count)]


def centred(own_key, dims, width, reach, pieces=(), held_as=jnp.bfloat16):
    values = jax.random.normal(own_key, dims, jnp.float32) * width
    if len(pieces) > 0:
        values = level_of(own_key, dims, pieces, -0.22, 0.18) * values
    return jnp.clip(values, min=-reach, max=reach).astype(held_as)


def setup_inputs(seed: int = 0) -> dict:
    arg_keys = jax.random.split(jax.random.key(seed), 20)
    inputs = centred(arg_keys[0], (TOKENS, D), 1.0, 6.0, ((0, 32),))
    cotangent = centred(arg_keys[1], (TOKENS, D), 1.0, 6.0, ((0, 32),))
    document_ids = jax.vmap(lambda own: jnp.searchsorted(jnp.cumsum(uneven(own, DOCS, LEN, LEN // 2, 1)), jnp.arange(LEN), side="right"))(jax.random.split(arg_keys[2], SEQS)).reshape((SEQS, LEN)).astype(jnp.int32)
    domain_counts = uneven(arg_keys[3], NDOM, SEQS, SEQS // 4, 2).astype(jnp.int32)
    domain_weight = jnp.clip(jax.random.uniform(arg_keys[4], (NDOM,), jnp.float32, 0.5, 2.0), 0.5, 2.0)
    token_order = draw_token_order(jax.random.fold_in(arg_keys[19], 71), 0)
    expert_counts = draw_expert_counts(jax.random.fold_in(arg_keys[19], 71), 0)
    dense_weights = draw_dense_weights(jax.random.fold_in(arg_keys[19], 71), 0)
    vector_params = draw_vector_params(jax.random.fold_in(arg_keys[19], 71), 0)
    expert_weights = draw_expert_weights(jax.random.fold_in(arg_keys[19], 71), 0)
    dense_first = centred(arg_keys[10], (4, D, D), (0.11 * NPARAMS ** -0.5), 0.00024414062, ((1, 32),), jnp.float32)
    dense_second = jnp.clip(jnp.exp(math.log(9.971155151555777e-11) - 1.3862944 * jax.random.uniform(arg_keys[11], (4, D, D), jnp.float32) ** level_of(arg_keys[11], (4, D, D), ((1, 32),), -0.2, 0.2)), 2.4927887878889443e-11, 9.971155151555777e-11)
    dense_average = centred(arg_keys[12], (4, D, D), D ** -0.5, 0.21875, ((1, 32),), jnp.float32)
    vector_first = centred(arg_keys[13], (2 + EXPERTS, D), (0.11 * NPARAMS ** -0.5), 0.00024414062, ((1, 32),), jnp.float32)
    vector_second = jnp.clip(jnp.exp(math.log(9.971155151555777e-11) - 1.3862944 * jax.random.uniform(arg_keys[14], (2 + EXPERTS, D), jnp.float32) ** level_of(arg_keys[14], (2 + EXPERTS, D), ((1, 32),), -0.2, 0.2)), 2.4927887878889443e-11, 9.971155151555777e-11)
    vector_average = jnp.clip(1.0 + 0.1 * jax.random.normal(arg_keys[15], (2 + EXPERTS, D), jnp.float32), 0.5, 1.5)
    expert_first = centred(arg_keys[16], (EXPERTS, 2, D, FF), (0.11 * (424 * EXPERTS * D * D) ** -0.5), 3.814697265625e-05, ((0, 8), (3, 4)), jnp.float32)
    expert_second = jnp.clip(jnp.exp(math.log(1.999317161480163e-12) - 1.3862944 * jax.random.uniform(arg_keys[17], (EXPERTS, 2, D, FF), jnp.float32) ** level_of(arg_keys[17], (EXPERTS, 2, D, FF), ((0, 8), (3, 4)), -0.2, 0.2)), 4.998292903700408e-13, 1.999317161480163e-12)
    expert_average = centred(arg_keys[18], (EXPERTS, 2, D, FF), D ** -0.5, 0.21875, ((0, 8), (3, 4)), jnp.float32)
    return {"inputs": inputs, "cotangent": cotangent, "document_ids": document_ids, "domain_counts": domain_counts, "domain_weight": domain_weight, "token_order": token_order, "expert_counts": expert_counts, "dense_weights": dense_weights, "vector_params": vector_params, "expert_weights": expert_weights, "dense_first": dense_first, "dense_second": dense_second, "dense_average": dense_average, "vector_first": vector_first, "vector_second": vector_second, "vector_average": vector_average, "expert_first": expert_first, "expert_second": expert_second, "expert_average": expert_average}


norm_eps = 1e-05
masked_score = -1e+30
beta_first = 0.9
beta_second = 0.999
adam_eps = 1e-08
dense_rate = 0.1
vector_rate = 0.5
expert_rate = 0.02
weight_decay = 0.1
ema_keep = 0.9
clip_norm = 1.0

@jax.custom_vjp
def low(v):
    return lax.optimization_barrier(v.astype(jnp.bfloat16)).astype(jnp.float32)

@jax.custom_vjp
def low_back(v):
    return v

def low_keep(v):
    return (low(v), None)

def low_pass(kept, grad):
    return (grad,)

def back_keep(v):
    return (v, None)

def back_low(kept, grad):
    return (low(grad),)
low.defvjp(low_keep, low_pass)
low_back.defvjp(back_keep, back_low)

def low_both(values_in):
    return low(low_back(values_in))

def matmul(first_arg, second_arg):
    return jnp.dot(first_arg, second_arg, precision=lax.Precision.HIGHEST, preferred_element_type=jnp.float32)

def layer_norm(values_in, gain_row):
    center = values_in - lax.optimization_barrier(jnp.mean(values_in, axis=-1, keepdims=True))
    spread = lax.optimization_barrier(jnp.mean(center * center, axis=-1, keepdims=True))
    return center * lax.rsqrt(spread + norm_eps) * gain_row

def attend_block(query_block, key_seq, value_seq, docs_seq, block_first):
    score_scale = HEAD_DIM ** (-0.5)
    scores = jnp.einsum('qhd,khd->hqk', query_block, key_seq, precision=lax.Precision.HIGHEST) * score_scale
    scores = low_back(scores)
    query_pos = block_first + jnp.arange(QBLK)
    key_pos = jnp.arange(LEN)
    query_docs = docs_seq[block_first:block_first + QBLK]
    allowed = (key_pos[None, :] <= query_pos[:, None]) & (docs_seq[None, :] == query_docs[:, None])
    scores = jnp.where(allowed[None], scores, masked_score)
    score_top = lax.optimization_barrier(jnp.max(scores, axis=-1, keepdims=True))
    weights = jnp.exp(scores - score_top)
    probabilities = weights / lax.optimization_barrier(jnp.sum(weights, axis=-1, keepdims=True))
    return jnp.einsum('hqk,khd->qhd', low(probabilities), value_seq, precision=lax.Precision.HIGHEST)

def attend_sequence(packed):
    queries, keys_seq, values_seq, docs_seq = packed
    outputs = []
    for block in range(LEN // QBLK):
        block_fn = jax.checkpoint(partial(attend_block, block_first=block * QBLK))
        outputs.append(block_fn(queries[block * QBLK:(block + 1) * QBLK], keys_seq, values_seq, docs_seq))
    return jnp.concatenate(outputs, axis=0)

def expert_rows(packed):
    weights_pair, rows_in, keep_rows = packed
    expert_pre = low_back(matmul(rows_in, weights_pair[0]))
    active = low_both(jax.nn.gelu(expert_pre))
    return low_both(matmul(active, weights_pair[1].T)) * keep_rows[:, None]

def routing(token_order, expert_counts):
    count_ends = jnp.cumsum(expert_counts, axis=1)
    count_starts = count_ends - expert_counts
    slots = jnp.arange(CAP)
    keep = (slots[None, None, :] < expert_counts[:, :, None]).astype(jnp.float32)
    position = jnp.minimum(count_starts[:, :, None] + slots[None, None, :], TOK_DEV - 1).astype(jnp.int32)
    local_rows = jnp.take_along_axis(token_order, position.reshape(GROUPS, EXPERTS * CAP), axis=1)
    whole_rows = local_rows.reshape(GROUPS, EXPERTS, CAP) + (jnp.arange(GROUPS) * TOK_DEV)[:, None, None]
    gather_index = jnp.transpose(whole_rows, (1, 0, 2)).reshape(EXPERTS, GROUPS * CAP).astype(jnp.int32)
    keep = jnp.transpose(keep, (1, 0, 2)).reshape(EXPERTS, GROUPS * CAP)
    sorted_expert = lax.optimization_barrier(jnp.sum((jnp.arange(TOK_DEV)[None, :, None] >= count_ends[:, None, :]).astype(jnp.int32), axis=2))
    shard_rows = jnp.broadcast_to(jnp.arange(GROUPS)[:, None], (GROUPS, TOK_DEV)).astype(jnp.int32)
    token_expert = jnp.zeros((GROUPS, TOK_DEV), jnp.int32).at[shard_rows, token_order].set(sorted_expert.astype(jnp.int32))
    return (gather_index, keep, token_expert.reshape(TOKENS))

def block_forward(inputs_float, dense, vectors, experts, document_ids, gather_index, keep, token_expert):
    dense_low = low(dense)
    vector_low = low(vectors)
    expert_low = low(experts)
    normed_one = low(layer_norm(inputs_float, vector_low[0]))
    shape = (SEQS, LEN, HEADS, HEAD_DIM)
    queries = low_both(matmul(normed_one, dense_low[0])).reshape(shape)
    keys_all = low_both(matmul(normed_one, dense_low[1])).reshape(shape)
    values_all = low_both(matmul(normed_one, dense_low[2])).reshape(shape)
    attn_mixed = lax.map(attend_sequence, (queries, keys_all, values_all, document_ids))
    attn_mixed = low_both(attn_mixed.reshape(TOKENS, D))
    hidden_state = inputs_float + low_back(matmul(attn_mixed, dense_low[3]))
    normed_two = layer_norm(hidden_state, vector_low[1])
    logits = matmul(normed_two, vector_low[2:].T)
    expert_pick = (token_expert[:, None] == jnp.arange(EXPERTS)[None, :]).astype(jnp.float32)
    gate_value = jax.nn.sigmoid(lax.optimization_barrier(jnp.sum(logits * expert_pick, axis=1)))
    sent_rows = low_both(normed_two)
    rows_all = sent_rows[gather_index] * keep[:, :, None]
    returned = lax.map(jax.checkpoint(expert_rows), (expert_low, rows_all, keep))
    combined = jnp.zeros((TOKENS, D), jnp.float32).at[gather_index.reshape(-1)].add(returned.reshape(-1, D))
    return hidden_state + gate_value[:, None] * combined

def adam_update(weight, gradient, first_moment, second_moment, average, factor, rate):
    clipped = gradient * factor
    first_new = beta_first * first_moment + (1.0 - beta_first) * clipped
    second_new = beta_second * second_moment + (1.0 - beta_second) * clipped * clipped
    first_hat = first_new / (1.0 - beta_first ** STEP)
    second_hat = second_new / (1.0 - beta_second ** STEP)
    updated = weight - rate * (first_hat / (jnp.sqrt(second_hat) + adam_eps) + weight_decay * weight)
    average_new = ema_keep * average + (1.0 - ema_keep) * updated
    return (updated, first_new, second_new, average_new)

def reference(inputs, cotangent, document_ids, domain_counts, domain_weight, token_order, expert_counts, dense_weights, vector_params, expert_weights, dense_first, dense_second, dense_average, vector_first, vector_second, vector_average, expert_first, expert_second, expert_average):
    gather_index, keep, token_expert = routing(token_order, expert_counts)
    sequence = jnp.arange(SEQS)
    bounds = jnp.cumsum(domain_counts)
    domain = lax.optimization_barrier(jnp.sum((sequence[:, None] >= bounds[None, :]).astype(jnp.int32), axis=1))
    seq_scale = domain_weight[domain] * SEQS / (NDOM * domain_counts[domain].astype(jnp.float32))
    token_scale = jnp.repeat(seq_scale, LEN)

    def forward(inputs_float, dense, vectors, experts):
        return block_forward(inputs_float, dense, vectors, experts, document_ids, gather_index, keep, token_expert)
    block_output, pullback = jax.vjp(forward, inputs.astype(jnp.float32), dense_weights, vector_params, expert_weights)
    input_grad, dense_grad, vector_grad, expert_grad = pullback(cotangent.astype(jnp.float32) * token_scale[:, None])
    squares = jnp.sum(dense_grad * dense_grad) + jnp.sum(vector_grad * vector_grad) + jnp.sum(expert_grad * expert_grad)
    grad_norm = jnp.sqrt(squares)
    factor = jnp.minimum(1.0, clip_norm / (grad_norm + 1e-06))
    dense_new = adam_update(dense_weights, dense_grad, dense_first, dense_second, dense_average, factor, dense_rate)
    vector_new = adam_update(vector_params, vector_grad, vector_first, vector_second, vector_average, factor, vector_rate)
    expert_new = adam_update(expert_weights, expert_grad, expert_first, expert_second, expert_average, factor, expert_rate)
    return (block_output, input_grad, dense_new[0], dense_new[1], dense_new[2], dense_new[3], vector_new[0], vector_new[1], vector_new[2], vector_new[3], expert_new[0], expert_new[1], expert_new[2], expert_new[3], grad_norm)
```

```python
from functools import partial

import jax
import jax.numpy as jnp
from jax import lax
from jax.experimental import pallas as pl
from jax.experimental.pallas import tpu as pltpu
from jax.sharding import PartitionSpec as P

HEADS = 12
HEAD_DIM = 64
LEN = 1024
WINDOW = 512
NDOM = 8
STEP = 10


norm_eps = 1e-05
masked_score = -1e30
beta_first = 0.9
beta_second = 0.999
adam_eps = 1e-08
dense_rate = 0.1
vector_rate = 0.5
expert_rate = 0.02
weight_decay = 0.1
ema_keep = 0.9
clip_norm = 1.0


def layer_norm(values_in, gain_row):
    center = values_in - jnp.mean(values_in, axis=-1, keepdims=True)
    spread = jnp.mean(center * center, axis=-1, keepdims=True)
    return center * lax.rsqrt(spread + norm_eps) * gain_row


NT = (((1,), (1,)), ((), ()))
TN = (((0,), (0,)), ((), ()))


def fwd_kernel(QB, q_ref,k_ref,v_ref,dcol_ref,drow_ref,o_ref,lse_ref,bias_ref):
    reach = WINDOW//QB
    low_lane = lax.broadcasted_iota(jnp.int32,(QB,128),1) < HEAD_DIM
    @pl.when(pl.program_id(0)==0)
    def _():
        for i in range(LEN//QB):
            first=max(0,i-reach)*QB; W=(i+1)*QB-first
            qp=i*QB+lax.broadcasted_iota(jnp.int32,(QB,W),0)
            kp=first+lax.broadcasted_iota(jnp.int32,(QB,W),1)
            ok=(kp<=qp)&(dcol_ref[i*QB:(i+1)*QB,:]==drow_ref[:,first:first+W])
            bias_ref[i*QB:(i+1)*QB,:W]=jnp.where(ok,0.0,masked_score)
    for i in range(LEN//QB):
        rows=slice(i*QB,(i+1)*QB)
        first=max(0,i-reach)*QB; W=(i+1)*QB-first
        q=q_ref[0,rows,:]*jnp.bfloat16(HEAD_DIM**-0.5)
        zero=jnp.zeros_like(q)
        qs=jnp.concatenate([jnp.where(low_lane,q,zero),jnp.where(low_lane,zero,q)],axis=0)
        s=lax.dot_general(qs,k_ref[0,first:first+W,:],NT,preferred_element_type=jnp.float32)
        s=(s.reshape(2,QB,W)+bias_ref[rows,:W][None]).reshape(2*QB,W)
        top=jnp.max(s,axis=1,keepdims=True)
        e=jnp.exp(s-top)
        total=jnp.sum(e,axis=1,keepdims=True)
        p=(e*(1.0/total)).astype(jnp.bfloat16)
        o=jnp.dot(p,v_ref[0,first:first+W,:],preferred_element_type=jnp.float32)
        o_ref[rows,:]=jnp.where(low_lane,o[:QB],o[QB:]).astype(jnp.bfloat16)
        lse=top+jnp.log(total)
        lse_ref[0,rows,:]=jnp.where(low_lane,lse[:QB],lse[QB:])

def attend_forward(projected, documents, QB=256):
    T=projected.shape[1]; D=projected.shape[2]
    dcol=documents.reshape(T,1); drow=documents.reshape(1,T)
    def sp(c): return pl.BlockSpec((1,T,128),lambda h,c=c:(c,0,h))
    return pl.pallas_call(partial(fwd_kernel,QB),grid=(D//128,),
        in_specs=[sp(0),sp(1),sp(2),pl.BlockSpec((T,1),lambda h:(0,0)),pl.BlockSpec((1,T),lambda h:(0,0))],
        out_specs=[pl.BlockSpec((T,128),lambda h:(0,h)),pl.BlockSpec((1,T,128),lambda h:(h,0,0))],
        out_shape=[jax.ShapeDtypeStruct((T,D),jnp.bfloat16),jax.ShapeDtypeStruct((D//128,T,128),jnp.float32)],
        scratch_shapes=[pltpu.VMEM((T,min(T,WINDOW+QB)),jnp.float32)],
        compiler_params=pltpu.CompilerParams(vmem_limit_bytes=48*2**20),
    )(projected,projected,projected,dcol,drow)

def bwd_kernel(QB,q_ref,k_ref,v_ref,lse_ref,g_ref,dcol_ref,drow_ref,out_ref,bias_ref,dk_ref,dv_ref):
    reach=WINDOW//QB
    low_lane = lax.broadcasted_iota(jnp.int32,(QB,128),1) < HEAD_DIM
    @pl.when(pl.program_id(0)==0)
    def _():
        for i in range(LEN//QB):
            first=max(0,i-reach)*QB; W=(i+1)*QB-first
            kp=first+lax.broadcasted_iota(jnp.int32,(W,QB),0)
            qp=i*QB+lax.broadcasted_iota(jnp.int32,(W,QB),1)
            ok=(kp<=qp)&(dcol_ref[first:first+W,:]==drow_ref[:,i*QB:(i+1)*QB])
            bias_ref[:W,i*QB:(i+1)*QB]=jnp.where(ok,0.0,masked_score)
    dk_ref[...]=jnp.zeros_like(dk_ref)
    dv_ref[...]=jnp.zeros_like(dv_ref)
    for i in range(LEN//QB):
        rows=slice(i*QB,(i+1)*QB)
        first=max(0,i-reach)*QB; W=(i+1)*QB-first
        keys=slice(first,first+W)
        q=q_ref[0,rows,:]*jnp.bfloat16(HEAD_DIM**-0.5)
        zero=jnp.zeros_like(q)
        qs=jnp.concatenate([jnp.where(low_lane,q,zero),jnp.where(low_lane,zero,q)],axis=0)
        g=g_ref[rows,:]
        gs=jnp.concatenate([jnp.where(low_lane,g,zero),jnp.where(low_lane,zero,g)],axis=0)
        k=k_ref[0,keys,:]
        st=lax.dot_general(k,qs,NT,preferred_element_type=jnp.float32)
        bias=bias_ref[:W,rows]
        lse=jnp.transpose(lse_ref[0,rows,:])
        lse=jnp.concatenate([lse[0:1,:],lse[64:65,:]],axis=1)
        p=jnp.exp(st+jnp.concatenate([bias,bias],axis=1)-lse)
        dp=lax.dot_general(v_ref[0,keys,:],gs,NT,preferred_element_type=jnp.float32)
        inner=jnp.sum(p*dp,axis=0,keepdims=True)
        ds=(p*(dp-inner)).astype(jnp.bfloat16)
        dk_ref[keys,:]+=jnp.dot(ds,qs,preferred_element_type=jnp.float32)
        dv_ref[keys,:]+=jnp.dot(p.astype(jnp.bfloat16),gs,preferred_element_type=jnp.float32)
        dq=lax.dot_general(ds,k,TN,preferred_element_type=jnp.float32)
        out_ref[0,rows,:]=(jnp.where(low_lane,dq[:QB],dq[QB:])*HEAD_DIM**-0.5).astype(jnp.bfloat16)
    out_ref[1,:,:]=dk_ref[...].astype(jnp.bfloat16)
    out_ref[2,:,:]=dv_ref[...].astype(jnp.bfloat16)

def attend_backward(projected, documents, lse, grad_mixed, QB=256):
    T=projected.shape[1]; D=projected.shape[2]
    dcol=documents.reshape(T,1); drow=documents.reshape(1,T)
    def sp(c): return pl.BlockSpec((1,T,128),lambda h,c=c:(c,0,h))
    return pl.pallas_call(partial(bwd_kernel,QB),grid=(D//128,),
        in_specs=[sp(0),sp(1),sp(2),pl.BlockSpec((1,T,128),lambda h:(h,0,0)),pl.BlockSpec((T,128),lambda h:(0,h)),pl.BlockSpec((T,1),lambda h:(0,0)),pl.BlockSpec((1,T),lambda h:(0,0))],
        out_specs=pl.BlockSpec((3,T,128),lambda h:(0,0,h)),
        out_shape=jax.ShapeDtypeStruct((3,T,D),jnp.bfloat16),
        scratch_shapes=[pltpu.VMEM((min(T,WINDOW+QB),T),jnp.float32),pltpu.VMEM((T,128),jnp.float32),pltpu.VMEM((T,128),jnp.float32)],
        compiler_params=pltpu.CompilerParams(vmem_limit_bytes=48*2**20),
    )(projected,projected,projected,lse,grad_mixed,dcol,drow)


def adam_update(weight, gradient, first_moment, second_moment, average, factor, rate):
    clipped = gradient * factor
    first_new = beta_first * first_moment + (1.0 - beta_first) * clipped
    second_new = beta_second * second_moment + (1.0 - beta_second) * clipped * clipped
    first_hat = first_new / (1.0 - beta_first**STEP)
    second_hat = second_new / (1.0 - beta_second**STEP)
    updated = weight - rate * (
        first_hat / (jnp.sqrt(second_hat) + adam_eps) + weight_decay * weight
    )
    average_new = ema_keep * average + (1.0 - ema_keep) * updated
    return (updated, first_new, second_new, average_new)


def shards(
    inputs,
    cotangent,
    document_ids,
    domain_counts,
    domain_weight,
    token_order,
    expert_counts,
    dense_weights,
    vector_params,
    expert_weights,
    dense_first,
    dense_second,
    dense_average,
    vector_first,
    vector_second,
    vector_average,
    expert_first,
    expert_second,
    expert_average,
):
    tokens, model_width = inputs.shape
    experts_total = expert_counts.shape[1]
    capacity = 2 * tokens // experts_total
    owners = lax.axis_size("expert")
    local_experts = experts_total // owners
    groups = lax.axis_size(("dp", "expert"))
    sequences = tokens // LEN
    dense_low, vector_low = (
        lax.all_gather(dense_weights.astype(jnp.bfloat16), ("dp", "expert"), axis=1, tiled=True),
        lax.all_gather(vector_params.astype(jnp.bfloat16), ("dp", "expert"), axis=1, tiled=True),
    )
    seq_index = lax.axis_index(("dp", "expert")) * sequences + jnp.arange(sequences)
    bounds = jnp.cumsum(domain_counts)
    domain = jnp.sum((seq_index[:, None] >= bounds[None, :]).astype(jnp.int32), axis=1)
    seq_pick = (domain[:, None] == jnp.arange(NDOM)[None, :]).astype(jnp.float32)
    seq_weight = jnp.sum(seq_pick * domain_weight[None, :], axis=1)
    seq_count = jnp.sum(seq_pick * domain_counts[None, :].astype(jnp.float32), axis=1)
    seq_scale = seq_weight * (sequences * groups) / (NDOM * seq_count)
    token_scale = jnp.repeat(seq_scale, LEN)
    row_counts = expert_counts[0]
    row_order = token_order[0]
    count_ends = jnp.cumsum(row_counts)
    count_starts = count_ends - row_counts
    sorted_pos = jnp.arange(tokens)
    sorted_expert = jnp.sum((sorted_pos[:, None] >= count_ends[None, :]).astype(jnp.int32), axis=1)
    sorted_pick = sorted_expert[:, None] == jnp.arange(experts_total)[None, :]
    sorted_start = jnp.sum(jnp.where(sorted_pick, count_starts[None, :], 0), axis=1)
    sorted_slot = sorted_expert * capacity + sorted_pos - sorted_start
    at_token = row_order[:, None] == jnp.arange(tokens)[None, :]
    token_slot = jnp.sum(jnp.where(at_token, sorted_slot[:, None], 0), axis=0)
    token_expert = token_slot // capacity
    expert_pick = (token_expert[:, None] == jnp.arange(experts_total)[None, :]).astype(jnp.float32)
    slot_pick = token_slot[:, None] == jnp.arange(experts_total * capacity)[None, :]
    slot_pick = slot_pick.astype(jnp.bfloat16)

    def to_slots(rows):
        placed = jnp.dot(slot_pick.T, rows, preferred_element_type=jnp.float32)
        return placed.astype(jnp.bfloat16).reshape(experts_total, capacity, model_width)

    def from_slots(rows):
        return jnp.dot(
            slot_pick, rows.reshape(-1, model_width), preferred_element_type=jnp.float32
        )

    inputs_float = inputs.astype(jnp.float32)
    normed_one, norm_one_back = jax.vjp(layer_norm, inputs_float, vector_low[0].astype(jnp.float32))
    normed_low = normed_one.astype(jnp.bfloat16)
    projected = jnp.einsum(
        "td,cde->cte", normed_low, dense_low[:3], preferred_element_type=jnp.float32
    ).astype(jnp.bfloat16)
    documents = document_ids.reshape(-1)
    mixed_low, totals = attend_forward(projected, documents)
    hidden_state = inputs_float + jnp.dot(
        mixed_low, dense_low[3], preferred_element_type=jnp.float32
    )
    normed_two, norm_two_back = jax.vjp(layer_norm, hidden_state, vector_low[1].astype(jnp.float32))
    centroids = vector_low[2:].astype(jnp.float32)
    logits = jnp.dot(normed_two, centroids.T, precision=lax.Precision.HIGHEST)
    gate_value = jax.nn.sigmoid(jnp.sum(logits * expert_pick, axis=1))
    sent_rows = normed_two.astype(jnp.bfloat16)
    send_rows = to_slots(sent_rows)
    received = lax.all_to_all(send_rows, "expert", split_axis=0, concat_axis=0, tiled=True)
    rows_in = received.reshape(owners, local_experts, capacity, model_width)
    own_low = expert_weights.astype(jnp.bfloat16)
    expert_low = lax.all_gather(own_low, "dp", axis=3, tiled=True)
    expert_pre = jnp.einsum(
        "jkcd,kdf->jkcf", rows_in, expert_low[:, 0], preferred_element_type=jnp.float32
    )
    active, gelu_back = jax.vjp(jax.nn.gelu, expert_pre)
    active_low = active.astype(jnp.bfloat16)
    produced = jnp.einsum(
        "jkcf,kdf->jkcd", active_low, expert_low[:, 1], preferred_element_type=jnp.float32
    )
    produced_low = produced.astype(jnp.bfloat16)
    returned = lax.all_to_all(
        produced_low.reshape(experts_total, capacity, model_width),
        "expert",
        split_axis=0,
        concat_axis=0,
        tiled=True,
    )
    returned_rows = from_slots(returned)
    block_output = hidden_state + gate_value[:, None] * returned_rows
    grad_out = cotangent.astype(jnp.float32) * token_scale[:, None]
    grad_returned = (gate_value[:, None] * grad_out).astype(jnp.bfloat16)
    grad_chosen = jnp.sum(grad_out * returned_rows, axis=1) * gate_value * (1.0 - gate_value)
    grad_rows = to_slots(grad_returned)
    grad_received = lax.all_to_all(grad_rows, "expert", split_axis=0, concat_axis=0, tiled=True)
    grad_in = grad_received.reshape(owners, local_experts, capacity, model_width)
    grad_active = jnp.einsum(
        "jkcd,kdf->jkcf", grad_in, expert_low[:, 1], preferred_element_type=jnp.float32
    ).astype(jnp.bfloat16)
    grad_pre = gelu_back(grad_active.astype(jnp.float32))[0].astype(jnp.bfloat16)
    grad_sent = jnp.einsum(
        "jkcf,kdf->jkcd", grad_pre, expert_low[:, 0], preferred_element_type=jnp.float32
    )
    grad_sent_low = grad_sent.astype(jnp.bfloat16)
    grad_back = lax.all_to_all(
        grad_sent_low.reshape(experts_total, capacity, model_width),
        "expert",
        split_axis=0,
        concat_axis=0,
        tiled=True,
    )
    grad_sent_rows = from_slots(grad_back)
    grad_up = jnp.einsum("jkcd,jkcf->kdf", rows_in, grad_pre, preferred_element_type=jnp.float32)
    grad_down = jnp.einsum(
        "jkcd,jkcf->kdf", grad_in, active_low, preferred_element_type=jnp.float32
    )
    expert_grad = lax.psum_scatter(
        jnp.stack([grad_up, grad_down], axis=1).astype(jnp.bfloat16),
        "dp",
        scatter_dimension=3,
        tiled=True,
    ).astype(jnp.float32)
    chosen_grad = grad_chosen[:, None] * expert_pick
    grad_normed_two = grad_sent_rows + jnp.dot(
        chosen_grad, centroids, precision=lax.Precision.HIGHEST
    )
    grad_centroids = jnp.dot(chosen_grad.T, normed_two, precision=lax.Precision.HIGHEST)
    grad_hidden_norm, grad_gain_two = norm_two_back(grad_normed_two)
    grad_hidden = grad_out + grad_hidden_norm
    grad_attn = grad_hidden.astype(jnp.bfloat16)
    grad_out_proj = jnp.dot(mixed_low.T, grad_attn, preferred_element_type=jnp.float32)
    grad_mixed = jnp.dot(grad_attn, dense_low[3].T, preferred_element_type=jnp.float32).astype(
        jnp.bfloat16
    )
    grad_proj = attend_backward(projected, documents, totals, grad_mixed)
    grad_in_proj = jnp.einsum(
        "td,cte->cde", normed_low, grad_proj, preferred_element_type=jnp.float32
    )
    grad_normed_one = jnp.einsum(
        "cte,cde->td", grad_proj, dense_low[:3], preferred_element_type=jnp.float32
    )
    grad_input_norm, grad_gain_one = norm_one_back(grad_normed_one)
    input_grad = grad_hidden + grad_input_norm
    dense_grad = jnp.concatenate([grad_in_proj, grad_out_proj[None]], axis=0)
    vector_grad = jnp.concatenate(
        [grad_gain_one[None], grad_gain_two[None], grad_centroids], axis=0
    )
    dense_grad, vector_grad = (
        lax.psum_scatter(dense_grad, ("dp", "expert"), scatter_dimension=1, tiled=True),
        lax.psum_scatter(vector_grad, ("dp", "expert"), scatter_dimension=1, tiled=True),
    )
    squares = (
        jnp.sum(dense_grad * dense_grad)
        + jnp.sum(vector_grad * vector_grad)
        + jnp.sum(expert_grad * expert_grad)
    )
    grad_norm = jnp.sqrt(lax.psum(squares, ("dp", "expert")))
    factor = jnp.minimum(1.0, clip_norm / (grad_norm + 1e-06))
    dense_new = adam_update(
        dense_weights, dense_grad, dense_first, dense_second, dense_average, factor, dense_rate
    )
    vector_new = adam_update(
        vector_params, vector_grad, vector_first, vector_second, vector_average, factor, vector_rate
    )
    expert_new = adam_update(
        expert_weights,
        expert_grad,
        expert_first,
        expert_second,
        expert_average,
        factor,
        expert_rate,
    )
    return (
        block_output,
        input_grad,
        dense_new[0],
        dense_new[1],
        dense_new[2],
        dense_new[3],
        vector_new[0],
        vector_new[1],
        vector_new[2],
        vector_new[3],
        expert_new[0],
        expert_new[1],
        expert_new[2],
        expert_new[3],
        grad_norm,
    )


def solution(mesh):
    placed = (
        P(("dp", "expert"), None),
        P(("dp", "expert"), None),
        P(("dp", "expert"), None),
        P(),
        P(),
        P(("dp", "expert"), None),
        P(("dp", "expert"), None),
        P(None, ("dp", "expert"), None),
        P(None, ("dp", "expert")),
        P("expert", None, None, "dp"),
        P(None, ("dp", "expert"), None),
        P(None, ("dp", "expert"), None),
        P(None, ("dp", "expert"), None),
        P(None, ("dp", "expert")),
        P(None, ("dp", "expert")),
        P(None, ("dp", "expert")),
        P("expert", None, None, "dp"),
        P("expert", None, None, "dp"),
        P("expert", None, None, "dp"),
    )
    return jax.shard_map(
        shards,
        mesh=mesh,
        in_specs=placed,
        out_specs=(
            P(("dp", "expert"), None),
            P(("dp", "expert"), None),
            P(None, ("dp", "expert"), None),
            P(None, ("dp", "expert"), None),
            P(None, ("dp", "expert"), None),
            P(None, ("dp", "expert"), None),
            P(None, ("dp", "expert")),
            P(None, ("dp", "expert")),
            P(None, ("dp", "expert")),
            P(None, ("dp", "expert")),
            P("expert", None, None, "dp"),
            P("expert", None, None, "dp"),
            P("expert", None, None, "dp"),
            P("expert", None, None, "dp"),
            P(),
        ),
        check_vma=False,
    )
```

```python
from functools import partial

import jax
import jax.numpy as jnp
from jax import lax
from jax.experimental import pallas as pl
from jax.experimental.pallas import tpu as pltpu
from jax.sharding import PartitionSpec as P

HEADS = 12
HEAD_DIM = 64
LEN = 1024
WINDOW = 512
NDOM = 8
STEP = 10


norm_eps = 1e-05
masked_score = -1e30
beta_first = 0.9
beta_second = 0.999
adam_eps = 1e-08
dense_rate = 0.1
vector_rate = 0.5
expert_rate = 0.02
weight_decay = 0.1
ema_keep = 0.9
clip_norm = 1.0


def layer_norm(values_in, gain_row):
    center = values_in - jnp.mean(values_in, axis=-1, keepdims=True)
    spread = jnp.mean(center * center, axis=-1, keepdims=True)
    return center * lax.rsqrt(spread + norm_eps) * gain_row


NT = (((1,), (1,)), ((), ()))
TN = (((0,), (0,)), ((), ()))


def fwd_kernel(QB, q_ref,k_ref,v_ref,dcol_ref,drow_ref,o_ref,lse_ref,bias_ref):
    reach = WINDOW//QB
    low_lane = lax.broadcasted_iota(jnp.int32,(QB,128),1) < HEAD_DIM
    @pl.when(pl.program_id(0)==0)
    def _():
        for i in range(LEN//QB):
            first=max(0,i-reach)*QB; W=(i+1)*QB-first
            qp=i*QB+lax.broadcasted_iota(jnp.int32,(QB,W),0)
            kp=first+lax.broadcasted_iota(jnp.int32,(QB,W),1)
            ok=(kp<=qp)&(dcol_ref[i*QB:(i+1)*QB,:]==drow_ref[:,first:first+W])
            bias_ref[i*QB:(i+1)*QB,:W]=jnp.where(ok,0.0,masked_score)
    for i in range(LEN//QB):
        rows=slice(i*QB,(i+1)*QB)
        first=max(0,i-reach)*QB; W=(i+1)*QB-first
        q=q_ref[0,rows,:]*jnp.bfloat16(HEAD_DIM**-0.5)
        zero=jnp.zeros_like(q)
        qs=jnp.concatenate([jnp.where(low_lane,q,zero),jnp.where(low_lane,zero,q)],axis=0)
        s=lax.dot_general(qs,k_ref[0,first:first+W,:],NT,preferred_element_type=jnp.float32)
        s=(s.reshape(2,QB,W)+bias_ref[rows,:W][None]).reshape(2*QB,W)
        top=jnp.max(s,axis=1,keepdims=True)
        e=jnp.exp(s-top)
        total=jnp.sum(e,axis=1,keepdims=True)
        p=(e*(1.0/total)).astype(jnp.bfloat16)
        o=jnp.dot(p,v_ref[0,first:first+W,:],preferred_element_type=jnp.float32)
        o_ref[rows,:]=jnp.where(low_lane,o[:QB],o[QB:]).astype(jnp.bfloat16)
        lse=top+jnp.log(total)
        lse_ref[0,rows,:]=jnp.where(low_lane,lse[:QB],lse[QB:])

def attend_forward(projected, documents, QB=256):
    T=projected.shape[1]; D=projected.shape[2]
    dcol=documents.reshape(T,1); drow=documents.reshape(1,T)
    def sp(c): return pl.BlockSpec((1,T,128),lambda h,c=c:(c,0,h))
    return pl.pallas_call(partial(fwd_kernel,QB),grid=(D//128,),
        in_specs=[sp(0),sp(1),sp(2),pl.BlockSpec((T,1),lambda h:(0,0)),pl.BlockSpec((1,T),lambda h:(0,0))],
        out_specs=[pl.BlockSpec((T,128),lambda h:(0,h)),pl.BlockSpec((1,T,128),lambda h:(h,0,0))],
        out_shape=[jax.ShapeDtypeStruct((T,D),jnp.bfloat16),jax.ShapeDtypeStruct((D//128,T,128),jnp.float32)],
        scratch_shapes=[pltpu.VMEM((T,min(T,WINDOW+QB)),jnp.float32)],
        compiler_params=pltpu.CompilerParams(vmem_limit_bytes=48*2**20),
    )(projected,projected,projected,dcol,drow)

def bwd_kernel(QB,q_ref,k_ref,v_ref,lse_ref,g_ref,dcol_ref,drow_ref,out_ref,bias_ref,dk_ref,dv_ref):
    reach=WINDOW//QB
    low_lane = lax.broadcasted_iota(jnp.int32,(QB,128),1) < HEAD_DIM
    @pl.when(pl.program_id(0)==0)
    def _():
        for i in range(LEN//QB):
            first=max(0,i-reach)*QB; W=(i+1)*QB-first
            kp=first+lax.broadcasted_iota(jnp.int32,(W,QB),0)
            qp=i*QB+lax.broadcasted_iota(jnp.int32,(W,QB),1)
            ok=(kp<=qp)&(dcol_ref[first:first+W,:]==drow_ref[:,i*QB:(i+1)*QB])
            bias_ref[:W,i*QB:(i+1)*QB]=jnp.where(ok,0.0,masked_score)
    dk_ref[...]=jnp.zeros_like(dk_ref)
    dv_ref[...]=jnp.zeros_like(dv_ref)
    for i in range(LEN//QB):
        rows=slice(i*QB,(i+1)*QB)
        first=max(0,i-reach)*QB; W=(i+1)*QB-first
        keys=slice(first,first+W)
        q=q_ref[0,rows,:]*jnp.bfloat16(HEAD_DIM**-0.5)
        zero=jnp.zeros_like(q)
        qs=jnp.concatenate([jnp.where(low_lane,q,zero),jnp.where(low_lane,zero,q)],axis=0)
        g=g_ref[rows,:]
        gs=jnp.concatenate([jnp.where(low_lane,g,zero),jnp.where(low_lane,zero,g)],axis=0)
        k=k_ref[0,keys,:]
        st=lax.dot_general(k,qs,NT,preferred_element_type=jnp.float32)
        bias=bias_ref[:W,rows]
        lse=jnp.transpose(lse_ref[0,rows,:])
        lse=jnp.concatenate([lse[0:1,:],lse[64:65,:]],axis=1)
        p=jnp.exp(st+jnp.concatenate([bias,bias],axis=1)-lse)
        dp=lax.dot_general(v_ref[0,keys,:],gs,NT,preferred_element_type=jnp.float32)
        inner=jnp.sum(p*dp,axis=0,keepdims=True)
        ds=(p*(dp-inner)).astype(jnp.bfloat16)
        dk_ref[keys,:]+=jnp.dot(ds,qs,preferred_element_type=jnp.float32)
        dv_ref[keys,:]+=jnp.dot(p.astype(jnp.bfloat16),gs,preferred_element_type=jnp.float32)
        dq=lax.dot_general(ds,k,TN,preferred_element_type=jnp.float32)
        out_ref[0,rows,:]=(jnp.where(low_lane,dq[:QB],dq[QB:])*HEAD_DIM**-0.5).astype(jnp.bfloat16)
    out_ref[1,:,:]=dk_ref[...].astype(jnp.bfloat16)
    out_ref[2,:,:]=dv_ref[...].astype(jnp.bfloat16)

def attend_backward(projected, documents, lse, grad_mixed, QB=256):
    T=projected.shape[1]; D=projected.shape[2]
    dcol=documents.reshape(T,1); drow=documents.reshape(1,T)
    def sp(c): return pl.BlockSpec((1,T,128),lambda h,c=c:(c,0,h))
    return pl.pallas_call(partial(bwd_kernel,QB),grid=(D//128,),
        in_specs=[sp(0),sp(1),sp(2),pl.BlockSpec((1,T,128),lambda h:(h,0,0)),pl.BlockSpec((T,128),lambda h:(0,h)),pl.BlockSpec((T,1),lambda h:(0,0)),pl.BlockSpec((1,T),lambda h:(0,0))],
        out_specs=pl.BlockSpec((3,T,128),lambda h:(0,0,h)),
        out_shape=jax.ShapeDtypeStruct((3,T,D),jnp.bfloat16),
        scratch_shapes=[pltpu.VMEM((min(T,WINDOW+QB),T),jnp.float32),pltpu.VMEM((T,128),jnp.float32),pltpu.VMEM((T,128),jnp.float32)],
        compiler_params=pltpu.CompilerParams(vmem_limit_bytes=48*2**20),
    )(projected,projected,projected,lse,grad_mixed,dcol,drow)


MESH=pl.DeviceIdType.MESH
TILE=256

def flip(a,b,n):
    out=0
    bit=1
    while bit<n:
        out=out+bit*((a//bit+b//bit)%2)
        bit*=2
    return out

def gelu_pair(x):
    c=0.7978845608028654
    sq=x*x
    t=jnp.tanh(c*(x+0.044715*(x*sq)))
    half=0.5*(1.0+t)
    return x*half, half+x*(0.5*(1.0-t*t))*(c+(3*0.044715*c)*sq)

def moe_kernel(n,cap,send_ref,gate_ref,cot_ref,scale_ref,w_ref,
               back_ref,chosen_ref,ret_ref,gw_ref,
               recv,gates,cot,w,gw,ret_s,gs_s,ch_s,g_s,racc,sacc,
               send_sem,recv_sem,gate_send,gate_recv,back_send,back_recv,ch_send,ch_recv,w_sem,loc_sem,ret_sem):
    per=TILE//cap
    chunks=w_ref.shape[0]
    me=lax.axis_index("expert")
    barrier=pltpu.get_barrier_semaphore()
    def greet(o,_):
        pl.semaphore_signal(barrier,inc=1,device_id={"expert":flip(me,o,n)},device_id_type=MESH)
        return 0
    lax.fori_loop(1,n,greet,0)
    pl.semaphore_wait(barrier,n-1)

    def row_copy(peer):
        return pltpu.make_async_remote_copy(src_ref=send_ref.at[peer],dst_ref=recv.at[me],
            send_sem=send_sem.at[peer],recv_sem=recv_sem.at[me],device_id={"expert":peer},device_id_type=MESH)
    def gate_copy(peer):
        return pltpu.make_async_remote_copy(src_ref=gate_ref.at[peer],dst_ref=gates.at[me],
            send_sem=gate_send.at[peer],recv_sem=gate_recv.at[me],device_id={"expert":peer},device_id_type=MESH)
    def row_in(src):
        return pltpu.make_async_remote_copy(src_ref=send_ref.at[src],dst_ref=recv.at[src],
            send_sem=send_sem.at[src],recv_sem=recv_sem.at[src],device_id={"expert":src},device_id_type=MESH)
    def gate_in(src):
        return pltpu.make_async_remote_copy(src_ref=gate_ref.at[src],dst_ref=gates.at[src],
            send_sem=gate_send.at[src],recv_sem=gate_recv.at[src],device_id={"expert":src},device_id_type=MESH)
    def back_copy(src):
        return pltpu.make_async_remote_copy(src_ref=gs_s.at[src],dst_ref=back_ref.at[me],
            send_sem=back_send.at[src],recv_sem=back_recv.at[me],device_id={"expert":src},device_id_type=MESH)
    def ch_copy(src):
        return pltpu.make_async_remote_copy(src_ref=ch_s.at[src],dst_ref=chosen_ref.at[me],
            send_sem=ch_send.at[src],recv_sem=ch_recv.at[me],device_id={"expert":src},device_id_type=MESH)
    def back_in(src):
        return pltpu.make_async_remote_copy(src_ref=gs_s.at[src],dst_ref=back_ref.at[src],
            send_sem=back_send.at[src],recv_sem=back_recv.at[src],device_id={"expert":src},device_id_type=MESH)
    def ch_in(src):
        return pltpu.make_async_remote_copy(src_ref=ch_s.at[src],dst_ref=chosen_ref.at[src],
            send_sem=ch_send.at[src],recv_sem=ch_recv.at[src],device_id={"expert":src},device_id_type=MESH)

    def push(i,_):
        peer=flip(me,n-1-i,n)
        gate_copy(peer).start()
        row_copy(peer).start()
        return 0
    lax.fori_loop(0,n-1,push,0)
    own=[pltpu.make_async_copy(send_ref.at[me],recv.at[me],loc_sem.at[0]),
         pltpu.make_async_copy(gate_ref.at[me],gates.at[me],loc_sem.at[1]),
         pltpu.make_async_copy(cot_ref,cot,loc_sem.at[2]),
         pltpu.make_async_copy(w_ref,w,w_sem)]
    for c in own: c.start()
    def wipe(c,_):
        gw[c]=jnp.zeros(gw.shape[1:],jnp.float32)
        return 0
    lax.fori_loop(0,chunks,wipe,0)
    for c in own: c.wait()

    def tile(t,_):
        block=flip(me//per,t,n//per)
        for j in range(per):
            src=block*per+j
            @pl.when(src!=me)
            def _():
                gate_in(src).wait_recv()
                row_in(src).wait_recv()
        at=pl.ds(pl.multiple_of(block*per,per),per)
        rows=pl.ds(pl.multiple_of(block*TILE,TILE),TILE)
        gate=jnp.transpose(jnp.sum(gates[at],axis=0))[:,0:1]
        grad_out=cot[rows,:].astype(jnp.float32)*scale_ref[rows,:]
        g_s[...]=(gate*grad_out).astype(jnp.bfloat16)
        racc[...]=jnp.zeros_like(racc)
        sacc[...]=jnp.zeros_like(sacc)
        def chunk(c,_):
            x=recv[at].reshape(TILE,recv.shape[2])
            g=g_s[...]
            act,slope=gelu_pair(jnp.dot(x,w[c,0],preferred_element_type=jnp.float32))
            a=act.astype(jnp.bfloat16)
            ga=jnp.dot(g,w[c,1],preferred_element_type=jnp.float32).astype(jnp.bfloat16)
            gp=(ga.astype(jnp.float32)*slope).astype(jnp.bfloat16)
            racc[...]+=lax.dot_general(a,w[c,1],NT,preferred_element_type=jnp.float32)
            sacc[...]+=lax.dot_general(gp,w[c,0],NT,preferred_element_type=jnp.float32)
            gw[c,0]+=lax.dot_general(x,gp,TN,preferred_element_type=jnp.float32)
            gw[c,1]+=lax.dot_general(g,a,TN,preferred_element_type=jnp.float32)
            return 0
        lax.fori_loop(0,chunks,chunk,0)
        ret=racc[...].astype(jnp.bfloat16)
        grad_out=cot[rows,:].astype(jnp.float32)*scale_ref[rows,:]
        chosen=jnp.sum(grad_out*ret.astype(jnp.float32),axis=1,keepdims=True)*gate*(1.0-gate)
        chosen=jnp.transpose(jnp.broadcast_to(chosen,(TILE,128)))[0:8,:]
        gs_s[at]=sacc[...].astype(jnp.bfloat16).reshape(per,cap,recv.shape[2])
        ret_s[at]=ret.reshape(per,cap,recv.shape[2])
        for j in range(per):
            src=block*per+j
            ch_s[src]=chosen
            @pl.when(src!=me)
            def _():
                ch_copy(src).start()
                back_copy(src).start()
            @pl.when(src==me)
            def _():
                pltpu.make_async_copy(ch_s.at[me],chosen_ref.at[me],loc_sem.at[0]).start()
                pltpu.make_async_copy(gs_s.at[me],back_ref.at[me],loc_sem.at[1]).start()
        pltpu.make_async_copy(ret_s.at[at],ret_ref.at[at],ret_sem.at[t]).start()
        return 0
    lax.fori_loop(0,n//per,tile,0)
    def pack(c,_):
        w[c]=gw[c].astype(jnp.bfloat16)
        return 0
    lax.fori_loop(0,chunks,pack,0)
    out=pltpu.make_async_copy(w,gw_ref,w_sem)
    out.start()
    pltpu.make_async_copy(ch_s.at[me],chosen_ref.at[me],loc_sem.at[0]).wait()
    pltpu.make_async_copy(gs_s.at[me],back_ref.at[me],loc_sem.at[1]).wait()
    def settle(o,_):
        peer=flip(me,o,n)
        gate_copy(peer).wait_send()
        row_copy(peer).wait_send()
        ch_copy(peer).wait_send()
        back_copy(peer).wait_send()
        ch_in(peer).wait_recv()
        back_in(peer).wait_recv()
        return 0
    lax.fori_loop(1,n,settle,0)
    def stored(t,_):
        block=flip(me//per,t,n//per)
        at=pl.ds(pl.multiple_of(block*per,per),per)
        pltpu.make_async_copy(ret_s.at[at],ret_ref.at[at],ret_sem.at[t]).wait()
        return 0
    lax.fori_loop(0,n//per,stored,0)
    out.wait()

def moe(send_rows,gate_slots,cot,scale,weights,collective_id=1):
    n,cap,D=send_rows.shape
    chunks,_,_,FC=weights.shape
    any_=pl.BlockSpec(memory_space=pl.ANY)
    bf=jnp.bfloat16; f32=jnp.float32
    dma=pltpu.SemaphoreType.DMA
    flops=6*2*n*cap*D*chunks*FC
    return pl.pallas_call(partial(moe_kernel,n,cap),
        out_shape=[jax.ShapeDtypeStruct((n,cap,D),bf),jax.ShapeDtypeStruct((n,8,TILE),f32),
                   jax.ShapeDtypeStruct((n,cap,D),bf),jax.ShapeDtypeStruct(weights.shape,bf)],
        in_specs=[any_,any_,any_,pl.BlockSpec(memory_space=pltpu.VMEM),any_],
        out_specs=[any_]*4,
        scratch_shapes=[pltpu.VMEM((n,cap,D),bf),pltpu.VMEM((n,8,TILE),f32),pltpu.VMEM((n*cap,D),bf),
            pltpu.VMEM(weights.shape,bf),pltpu.VMEM(weights.shape,f32),pltpu.VMEM((n,cap,D),bf),pltpu.VMEM((n,cap,D),bf),
            pltpu.VMEM((n,8,TILE),f32),pltpu.VMEM((TILE,D),bf),pltpu.VMEM((TILE,D),f32),pltpu.VMEM((TILE,D),f32)]
            +[dma((n,))]*8+[dma(()),dma((3,)),dma((n*cap//TILE,))],
        compiler_params=pltpu.CompilerParams(vmem_limit_bytes=62*2**20,collective_id=collective_id,has_side_effects=True),
        cost_estimate=pl.CostEstimate(flops=flops,bytes_accessed=40*2**20,transcendentals=0),
    )(send_rows,gate_slots,cot,scale,weights)


def adam_update(weight, gradient, first_moment, second_moment, average, factor, rate):
    clipped = gradient * factor
    first_new = beta_first * first_moment + (1.0 - beta_first) * clipped
    second_new = beta_second * second_moment + (1.0 - beta_second) * clipped * clipped
    first_hat = first_new / (1.0 - beta_first**STEP)
    second_hat = second_new / (1.0 - beta_second**STEP)
    updated = weight - rate * (
        first_hat / (jnp.sqrt(second_hat) + adam_eps) + weight_decay * weight
    )
    average_new = ema_keep * average + (1.0 - ema_keep) * updated
    return (updated, first_new, second_new, average_new)


def shards(
    inputs,
    cotangent,
    document_ids,
    domain_counts,
    domain_weight,
    token_order,
    expert_counts,
    dense_weights,
    vector_params,
    expert_weights,
    dense_first,
    dense_second,
    dense_average,
    vector_first,
    vector_second,
    vector_average,
    expert_first,
    expert_second,
    expert_average,
):
    tokens, model_width = inputs.shape
    experts_total = expert_counts.shape[1]
    capacity = 2 * tokens // experts_total
    owners = lax.axis_size("expert")
    groups = lax.axis_size(("dp", "expert"))
    sequences = tokens // LEN
    dense_low, vector_low = (
        lax.all_gather(dense_weights.astype(jnp.bfloat16), ("dp", "expert"), axis=1, tiled=True),
        lax.all_gather(vector_params.astype(jnp.bfloat16), ("dp", "expert"), axis=1, tiled=True),
    )
    me = lax.axis_index("expert")
    seq_index = lax.axis_index("dp") * owners + jnp.arange(owners)
    bounds = jnp.cumsum(domain_counts)
    domain = jnp.sum((seq_index[:, None] >= bounds[None, :]).astype(jnp.int32), axis=1)
    seq_pick = (domain[:, None] == jnp.arange(NDOM)[None, :]).astype(jnp.float32)
    seq_weight = jnp.sum(seq_pick * domain_weight[None, :], axis=1)
    seq_count = jnp.sum(seq_pick * domain_counts[None, :].astype(jnp.float32), axis=1)
    seq_scale = seq_weight * (sequences * groups) / (NDOM * seq_count)
    slot_scale = jnp.repeat(seq_scale, capacity)[:, None]
    token_scale = jnp.broadcast_to(seq_scale[me], (tokens,))
    row_counts = expert_counts[0]
    row_order = token_order[0]
    count_ends = jnp.cumsum(row_counts)
    count_starts = count_ends - row_counts
    sorted_pos = jnp.arange(tokens)
    sorted_expert = jnp.sum((sorted_pos[:, None] >= count_ends[None, :]).astype(jnp.int32), axis=1)
    sorted_pick = sorted_expert[:, None] == jnp.arange(experts_total)[None, :]
    sorted_start = jnp.sum(jnp.where(sorted_pick, count_starts[None, :], 0), axis=1)
    sorted_slot = sorted_expert * capacity + sorted_pos - sorted_start
    at_token = row_order[:, None] == jnp.arange(tokens)[None, :]
    token_slot = jnp.sum(jnp.where(at_token, sorted_slot[:, None], 0), axis=0)
    token_expert = token_slot // capacity
    expert_pick = (token_expert[:, None] == jnp.arange(experts_total)[None, :]).astype(jnp.float32)
    slot_match = token_slot[:, None] == jnp.arange(experts_total * capacity)[None, :]
    slot_pick = slot_match.astype(jnp.bfloat16)

    def to_slots(rows):
        placed = jnp.dot(slot_pick.T, rows, preferred_element_type=jnp.float32)
        return placed.astype(jnp.bfloat16).reshape(experts_total, capacity, model_width)

    def from_slots(rows):
        return jnp.dot(
            slot_pick, rows.reshape(-1, model_width), preferred_element_type=jnp.float32
        )

    cot_received = lax.all_to_all(
        to_slots(cotangent), "expert", split_axis=0, concat_axis=0, tiled=True
    ).reshape(-1, model_width)
    own_low = expert_weights[0].astype(jnp.bfloat16)
    expert_low = lax.all_gather(own_low, "dp", axis=0)
    inputs_float = inputs.astype(jnp.float32)
    normed_one, norm_one_back = jax.vjp(layer_norm, inputs_float, vector_low[0].astype(jnp.float32))
    normed_low = normed_one.astype(jnp.bfloat16)
    projected = jnp.einsum(
        "td,cde->cte", normed_low, dense_low[:3], preferred_element_type=jnp.float32
    ).astype(jnp.bfloat16)
    documents = document_ids.reshape(-1)
    mixed_low, totals = attend_forward(projected, documents)
    hidden_state = inputs_float + jnp.dot(
        mixed_low, dense_low[3], preferred_element_type=jnp.float32
    )
    normed_two, norm_two_back = jax.vjp(layer_norm, hidden_state, vector_low[1].astype(jnp.float32))
    centroids = vector_low[2:].astype(jnp.float32)
    logits = jnp.dot(normed_two, centroids.T, precision=lax.Precision.HIGHEST)
    gate_value = jax.nn.sigmoid(jnp.sum(logits * expert_pick, axis=1))
    sent_rows = normed_two.astype(jnp.bfloat16)
    send_rows = to_slots(sent_rows)
    per = TILE // capacity
    gate_slots = jnp.sum(
        jnp.where(slot_match, gate_value[:, None], 0.0), axis=0
    ).reshape(experts_total, 1, 1, capacity)
    lane_part = (jnp.arange(per) == me % per).astype(jnp.float32)
    gate_tiles = jnp.broadcast_to(
        gate_slots * lane_part[None, None, :, None], (experts_total, 8, per, capacity)
    ).reshape(experts_total, 8, TILE)
    grad_back, chosen_tiles, produced_low, grad_expert = moe(
        send_rows, gate_tiles, cot_received, slot_scale, expert_low
    )
    expert_grad = lax.psum_scatter(grad_expert, "dp", scatter_dimension=0).astype(jnp.float32)[None]
    returned = lax.all_to_all(produced_low, "expert", split_axis=0, concat_axis=0, tiled=True)
    returned_rows = from_slots(returned)
    block_output = hidden_state + gate_value[:, None] * returned_rows
    grad_out = cotangent.astype(jnp.float32) * token_scale[:, None]
    grad_sent_rows = from_slots(grad_back)
    chosen_slots = lax.dynamic_slice_in_dim(
        chosen_tiles[:, 0, :], me % per * capacity, capacity, axis=1
    )
    grad_chosen = jnp.sum(jnp.where(slot_match, chosen_slots.reshape(1, -1), 0.0), axis=1)
    chosen_grad = grad_chosen[:, None] * expert_pick
    grad_normed_two = grad_sent_rows + jnp.dot(
        chosen_grad, centroids, precision=lax.Precision.HIGHEST
    )
    grad_centroids = jnp.dot(chosen_grad.T, normed_two, precision=lax.Precision.HIGHEST)
    grad_hidden_norm, grad_gain_two = norm_two_back(grad_normed_two)
    grad_hidden = grad_out + grad_hidden_norm
    grad_attn = grad_hidden.astype(jnp.bfloat16)
    grad_out_proj = jnp.dot(mixed_low.T, grad_attn, preferred_element_type=jnp.float32)
    grad_mixed = jnp.dot(grad_attn, dense_low[3].T, preferred_element_type=jnp.float32).astype(
        jnp.bfloat16
    )
    grad_proj = attend_backward(projected, documents, totals, grad_mixed)
    grad_in_proj = jnp.einsum(
        "td,cte->cde", normed_low, grad_proj, preferred_element_type=jnp.float32
    )
    grad_normed_one = jnp.einsum(
        "cte,cde->td", grad_proj, dense_low[:3], preferred_element_type=jnp.float32
    )
    grad_input_norm, grad_gain_one = norm_one_back(grad_normed_one)
    input_grad = grad_hidden + grad_input_norm
    dense_grad = jnp.concatenate([grad_in_proj, grad_out_proj[None]], axis=0)
    vector_grad = jnp.concatenate(
        [grad_gain_one[None], grad_gain_two[None], grad_centroids], axis=0
    )
    dense_grad, vector_grad = (
        lax.psum_scatter(dense_grad, ("dp", "expert"), scatter_dimension=1, tiled=True),
        lax.psum_scatter(vector_grad, ("dp", "expert"), scatter_dimension=1, tiled=True),
    )
    squares = (
        jnp.sum(dense_grad * dense_grad)
        + jnp.sum(vector_grad * vector_grad)
        + jnp.sum(expert_grad * expert_grad)
    )
    grad_norm = jnp.sqrt(lax.psum(squares, ("dp", "expert")))
    factor = jnp.minimum(1.0, clip_norm / (grad_norm + 1e-06))
    dense_new = adam_update(
        dense_weights, dense_grad, dense_first, dense_second, dense_average, factor, dense_rate
    )
    vector_new = adam_update(
        vector_params, vector_grad, vector_first, vector_second, vector_average, factor, vector_rate
    )
    expert_new = adam_update(
        expert_weights,
        expert_grad,
        expert_first,
        expert_second,
        expert_average,
        factor,
        expert_rate,
    )
    return (
        block_output,
        input_grad,
        dense_new[0],
        dense_new[1],
        dense_new[2],
        dense_new[3],
        vector_new[0],
        vector_new[1],
        vector_new[2],
        vector_new[3],
        expert_new[0],
        expert_new[1],
        expert_new[2],
        expert_new[3],
        grad_norm,
    )


def solution(mesh):
    placed = (
        P(("dp", "expert"), None),
        P(("dp", "expert"), None),
        P(("dp", "expert"), None),
        P(),
        P(),
        P(("dp", "expert"), None),
        P(("dp", "expert"), None),
        P(None, ("dp", "expert"), None),
        P(None, ("dp", "expert")),
        P("expert", None, None, "dp"),
        P(None, ("dp", "expert"), None),
        P(None, ("dp", "expert"), None),
        P(None, ("dp", "expert"), None),
        P(None, ("dp", "expert")),
        P(None, ("dp", "expert")),
        P(None, ("dp", "expert")),
        P("expert", None, None, "dp"),
        P("expert", None, None, "dp"),
        P("expert", None, None, "dp"),
    )
    return jax.shard_map(
        shards,
        mesh=mesh,
        in_specs=placed,
        out_specs=(
            P(("dp", "expert"), None),
            P(("dp", "expert"), None),
            P(None, ("dp", "expert"), None),
            P(None, ("dp", "expert"), None),
            P(None, ("dp", "expert"), None),
            P(None, ("dp", "expert"), None),
            P(None, ("dp", "expert")),
            P(None, ("dp", "expert")),
            P(None, ("dp", "expert")),
            P(None, ("dp", "expert")),
            P("expert", None, None, "dp"),
            P("expert", None, None, "dp"),
            P("expert", None, None, "dp"),
            P("expert", None, None, "dp"),
            P(),
        ),
        check_vma=False,
    )
```

```python
from functools import partial

import jax
import jax.numpy as jnp
from jax import lax
from jax.experimental import pallas as pl
from jax.experimental.pallas import tpu as pltpu
from jax.sharding import PartitionSpec as P

HEADS = 12
HEAD_DIM = 64
LEN = 1024
WINDOW = 512
NDOM = 8
STEP = 10


norm_eps = 1e-05
masked_score = -1e30
beta_first = 0.9
beta_second = 0.999
adam_eps = 1e-08
dense_rate = 0.1
vector_rate = 0.5
expert_rate = 0.02
weight_decay = 0.1
ema_keep = 0.9
clip_norm = 1.0


def layer_norm(values_in, gain_row):
    center = values_in - jnp.mean(values_in, axis=-1, keepdims=True)
    spread = jnp.mean(center * center, axis=-1, keepdims=True)
    return center * lax.rsqrt(spread + norm_eps) * gain_row


NT = (((1,), (1,)), ((), ()))
TN = (((0,), (0,)), ((), ()))


def fwd_kernel(QB, q_ref,k_ref,v_ref,dcol_ref,drow_ref,o_ref,lse_ref,bias_ref):
    reach = WINDOW//QB
    low_lane = lax.broadcasted_iota(jnp.int32,(QB,128),1) < HEAD_DIM
    @pl.when(pl.program_id(0)==0)
    def _():
        for i in range(LEN//QB):
            first=max(0,i-reach)*QB; W=(i+1)*QB-first
            qp=i*QB+lax.broadcasted_iota(jnp.int32,(QB,W),0)
            kp=first+lax.broadcasted_iota(jnp.int32,(QB,W),1)
            ok=(kp<=qp)&(dcol_ref[i*QB:(i+1)*QB,:]==drow_ref[:,first:first+W])
            bias_ref[i*QB:(i+1)*QB,:W]=jnp.where(ok,0.0,masked_score)
    for i in range(LEN//QB):
        rows=slice(i*QB,(i+1)*QB)
        first=max(0,i-reach)*QB; W=(i+1)*QB-first
        q=q_ref[0,rows,:]*jnp.bfloat16(HEAD_DIM**-0.5)
        zero=jnp.zeros_like(q)
        qs=jnp.concatenate([jnp.where(low_lane,q,zero),jnp.where(low_lane,zero,q)],axis=0)
        s=lax.dot_general(qs,k_ref[0,first:first+W,:],NT,preferred_element_type=jnp.float32)
        s=(s.reshape(2,QB,W)+bias_ref[rows,:W][None]).reshape(2*QB,W)
        top=jnp.max(s,axis=1,keepdims=True)
        e=jnp.exp(s-top)
        total=jnp.sum(e,axis=1,keepdims=True)
        p=(e*(1.0/total)).astype(jnp.bfloat16)
        o=jnp.dot(p,v_ref[0,first:first+W,:],preferred_element_type=jnp.float32)
        o_ref[rows,:]=jnp.where(low_lane,o[:QB],o[QB:]).astype(jnp.bfloat16)
        lse=top+jnp.log(total)
        lse_ref[0,rows,:]=jnp.where(low_lane,lse[:QB],lse[QB:])

def attend_forward(projected, documents, QB=256):
    T=projected.shape[1]; D=projected.shape[2]
    dcol=documents.reshape(T,1); drow=documents.reshape(1,T)
    def sp(c): return pl.BlockSpec((1,T,128),lambda h,c=c:(c,0,h))
    return pl.pallas_call(partial(fwd_kernel,QB),grid=(D//128,),
        in_specs=[sp(0),sp(1),sp(2),pl.BlockSpec((T,1),lambda h:(0,0)),pl.BlockSpec((1,T),lambda h:(0,0))],
        out_specs=[pl.BlockSpec((T,128),lambda h:(0,h)),pl.BlockSpec((1,T,128),lambda h:(h,0,0))],
        out_shape=[jax.ShapeDtypeStruct((T,D),jnp.bfloat16),jax.ShapeDtypeStruct((D//128,T,128),jnp.float32)],
        scratch_shapes=[pltpu.VMEM((T,min(T,WINDOW+QB)),jnp.float32)],
        compiler_params=pltpu.CompilerParams(vmem_limit_bytes=48*2**20),
    )(projected,projected,projected,dcol,drow)

def bwd_kernel(QB,q_ref,k_ref,v_ref,lse_ref,g_ref,dcol_ref,drow_ref,out_ref,bias_ref,dk_ref,dv_ref):
    reach=WINDOW//QB
    low_lane = lax.broadcasted_iota(jnp.int32,(QB,128),1) < HEAD_DIM
    @pl.when(pl.program_id(0)==0)
    def _():
        for i in range(LEN//QB):
            first=max(0,i-reach)*QB; W=(i+1)*QB-first
            kp=first+lax.broadcasted_iota(jnp.int32,(W,QB),0)
            qp=i*QB+lax.broadcasted_iota(jnp.int32,(W,QB),1)
            ok=(kp<=qp)&(dcol_ref[first:first+W,:]==drow_ref[:,i*QB:(i+1)*QB])
            bias_ref[:W,i*QB:(i+1)*QB]=jnp.where(ok,0.0,masked_score)
    dk_ref[...]=jnp.zeros_like(dk_ref)
    dv_ref[...]=jnp.zeros_like(dv_ref)
    for i in range(LEN//QB):
        rows=slice(i*QB,(i+1)*QB)
        first=max(0,i-reach)*QB; W=(i+1)*QB-first
        keys=slice(first,first+W)
        q=q_ref[0,rows,:]*jnp.bfloat16(HEAD_DIM**-0.5)
        zero=jnp.zeros_like(q)
        qs=jnp.concatenate([jnp.where(low_lane,q,zero),jnp.where(low_lane,zero,q)],axis=0)
        g=g_ref[rows,:]
        gs=jnp.concatenate([jnp.where(low_lane,g,zero),jnp.where(low_lane,zero,g)],axis=0)
        k=k_ref[0,keys,:]
        st=lax.dot_general(k,qs,NT,preferred_element_type=jnp.float32)
        bias=bias_ref[:W,rows]
        lse=jnp.transpose(lse_ref[0,rows,:])
        lse=jnp.concatenate([lse[0:1,:],lse[64:65,:]],axis=1)
        p=jnp.exp(st+jnp.concatenate([bias,bias],axis=1)-lse)
        dp=lax.dot_general(v_ref[0,keys,:],gs,NT,preferred_element_type=jnp.float32)
        inner=jnp.sum(p*dp,axis=0,keepdims=True)
        ds=(p*(dp-inner)).astype(jnp.bfloat16)
        dk_ref[keys,:]+=jnp.dot(ds,qs,preferred_element_type=jnp.float32)
        dv_ref[keys,:]+=jnp.dot(p.astype(jnp.bfloat16),gs,preferred_element_type=jnp.float32)
        dq=lax.dot_general(ds,k,TN,preferred_element_type=jnp.float32)
        out_ref[0,rows,:]=(jnp.where(low_lane,dq[:QB],dq[QB:])*HEAD_DIM**-0.5).astype(jnp.bfloat16)
    out_ref[1,:,:]=dk_ref[...].astype(jnp.bfloat16)
    out_ref[2,:,:]=dv_ref[...].astype(jnp.bfloat16)

def attend_backward(projected, documents, lse, grad_mixed, QB=256):
    T=projected.shape[1]; D=projected.shape[2]
    dcol=documents.reshape(T,1); drow=documents.reshape(1,T)
    def sp(c): return pl.BlockSpec((1,T,128),lambda h,c=c:(c,0,h))
    return pl.pallas_call(partial(bwd_kernel,QB),grid=(D//128,),
        in_specs=[sp(0),sp(1),sp(2),pl.BlockSpec((1,T,128),lambda h:(h,0,0)),pl.BlockSpec((T,128),lambda h:(0,h)),pl.BlockSpec((T,1),lambda h:(0,0)),pl.BlockSpec((1,T),lambda h:(0,0))],
        out_specs=pl.BlockSpec((3,T,128),lambda h:(0,0,h)),
        out_shape=jax.ShapeDtypeStruct((3,T,D),jnp.bfloat16),
        scratch_shapes=[pltpu.VMEM((min(T,WINDOW+QB),T),jnp.float32),pltpu.VMEM((T,128),jnp.float32),pltpu.VMEM((T,128),jnp.float32)],
        compiler_params=pltpu.CompilerParams(vmem_limit_bytes=48*2**20),
    )(projected,projected,projected,lse,grad_mixed,dcol,drow)


MESH=pl.DeviceIdType.MESH
TILE=256

def flip(a,b,n):
    out=0
    bit=1
    while bit<n:
        out=out+bit*((a//bit+b//bit)%2)
        bit*=2
    return out

def gelu_pair(x):
    c=0.7978845608028654
    sq=x*x
    t=jnp.tanh(c*(x+0.044715*(x*sq)))
    half=0.5*(1.0+t)
    return x*half, half+x*(0.5*(1.0-t*t))*(c+(3*0.044715*c)*sq)

def moe_kernel(n,cap,send_ref,gate_ref,cot_ref,scale_ref,w_ref,
               back_ref,chosen_ref,ret_ref,gw_ref,
               recv,gates,cot,w,gw,ret_s,gs_s,ch_s,g_s,racc,sacc,
               send_sem,recv_sem,gate_send,gate_recv,back_send,back_recv,ch_send,ch_recv,w_sem,loc_sem,ret_sem):
    per=TILE//cap
    chunks=w_ref.shape[0]
    me=lax.axis_index("expert")
    barrier=pltpu.get_barrier_semaphore()
    def greet(o,_):
        pl.semaphore_signal(barrier,inc=1,device_id={"expert":flip(me,o,n)},device_id_type=MESH)
        return 0
    lax.fori_loop(1,n,greet,0)
    pl.semaphore_wait(barrier,n-1)

    def row_copy(peer):
        return pltpu.make_async_remote_copy(src_ref=send_ref.at[peer],dst_ref=recv.at[me],
            send_sem=send_sem.at[peer],recv_sem=recv_sem.at[me],device_id={"expert":peer},device_id_type=MESH)
    def gate_copy(peer):
        return pltpu.make_async_remote_copy(src_ref=gate_ref.at[peer],dst_ref=gates.at[me],
            send_sem=gate_send.at[peer],recv_sem=gate_recv.at[me],device_id={"expert":peer},device_id_type=MESH)
    def row_in(src):
        return pltpu.make_async_remote_copy(src_ref=send_ref.at[src],dst_ref=recv.at[src],
            send_sem=send_sem.at[src],recv_sem=recv_sem.at[src],device_id={"expert":src},device_id_type=MESH)
    def gate_in(src):
        return pltpu.make_async_remote_copy(src_ref=gate_ref.at[src],dst_ref=gates.at[src],
            send_sem=gate_send.at[src],recv_sem=gate_recv.at[src],device_id={"expert":src},device_id_type=MESH)
    def back_copy(src):
        return pltpu.make_async_remote_copy(src_ref=gs_s.at[src],dst_ref=back_ref.at[me],
            send_sem=back_send.at[src],recv_sem=back_recv.at[me],device_id={"expert":src},device_id_type=MESH)
    def ch_copy(src):
        return pltpu.make_async_remote_copy(src_ref=ch_s.at[src],dst_ref=chosen_ref.at[me],
            send_sem=ch_send.at[src],recv_sem=ch_recv.at[me],device_id={"expert":src},device_id_type=MESH)
    def back_in(src):
        return pltpu.make_async_remote_copy(src_ref=gs_s.at[src],dst_ref=back_ref.at[src],
            send_sem=back_send.at[src],recv_sem=back_recv.at[src],device_id={"expert":src},device_id_type=MESH)
    def ch_in(src):
        return pltpu.make_async_remote_copy(src_ref=ch_s.at[src],dst_ref=chosen_ref.at[src],
            send_sem=ch_send.at[src],recv_sem=ch_recv.at[src],device_id={"expert":src},device_id_type=MESH)

    def push(i,_):
        peer=flip(me,n-1-i,n)
        gate_copy(peer).start()
        row_copy(peer).start()
        return 0
    lax.fori_loop(0,n-1,push,0)
    own=[pltpu.make_async_copy(send_ref.at[me],recv.at[me],loc_sem.at[0]),
         pltpu.make_async_copy(gate_ref.at[me],gates.at[me],loc_sem.at[1]),
         pltpu.make_async_copy(cot_ref,cot,loc_sem.at[2]),
         pltpu.make_async_copy(w_ref,w,w_sem)]
    for c in own: c.start()
    def wipe(c,_):
        gw[c]=jnp.zeros(gw.shape[1:],jnp.float32)
        return 0
    lax.fori_loop(0,chunks,wipe,0)
    for c in own: c.wait()

    def tile(t,_):
        block=flip(me//per,t,n//per)
        for j in range(per):
            src=block*per+j
            @pl.when(src!=me)
            def _():
                gate_in(src).wait_recv()
                row_in(src).wait_recv()
        at=pl.ds(pl.multiple_of(block*per,per),per)
        rows=pl.ds(pl.multiple_of(block*TILE,TILE),TILE)
        gate=jnp.transpose(jnp.sum(gates[at],axis=0))[:,0:1]
        grad_out=cot[rows,:].astype(jnp.float32)*scale_ref[rows,:]
        g_s[...]=(gate*grad_out).astype(jnp.bfloat16)
        racc[...]=jnp.zeros_like(racc)
        sacc[...]=jnp.zeros_like(sacc)
        def chunk(c,_):
            x=recv[at].reshape(TILE,recv.shape[2])
            g=g_s[...]
            act,slope=gelu_pair(jnp.dot(x,w[c,0],preferred_element_type=jnp.float32))
            a=act.astype(jnp.bfloat16)
            ga=jnp.dot(g,w[c,1],preferred_element_type=jnp.float32).astype(jnp.bfloat16)
            gp=(ga.astype(jnp.float32)*slope).astype(jnp.bfloat16)
            racc[...]+=lax.dot_general(a,w[c,1],NT,preferred_element_type=jnp.float32)
            sacc[...]+=lax.dot_general(gp,w[c,0],NT,preferred_element_type=jnp.float32)
            gw[c,0]+=lax.dot_general(x,gp,TN,preferred_element_type=jnp.float32)
            gw[c,1]+=lax.dot_general(g,a,TN,preferred_element_type=jnp.float32)
            return 0
        lax.fori_loop(0,chunks,chunk,0)
        ret=racc[...].astype(jnp.bfloat16)
        grad_out=cot[rows,:].astype(jnp.float32)*scale_ref[rows,:]
        chosen=jnp.sum(grad_out*ret.astype(jnp.float32),axis=1,keepdims=True)*gate*(1.0-gate)
        chosen=jnp.transpose(jnp.broadcast_to(chosen,(TILE,128)))[0:8,:]
        gs_s[at]=sacc[...].astype(jnp.bfloat16).reshape(per,cap,recv.shape[2])
        ret_s[at]=ret.reshape(per,cap,recv.shape[2])
        for j in range(per):
            src=block*per+j
            ch_s[src]=chosen
            @pl.when(src!=me)
            def _():
                ch_copy(src).start()
                back_copy(src).start()
            @pl.when(src==me)
            def _():
                pltpu.make_async_copy(ch_s.at[me],chosen_ref.at[me],loc_sem.at[0]).start()
                pltpu.make_async_copy(gs_s.at[me],back_ref.at[me],loc_sem.at[1]).start()
        pltpu.make_async_copy(ret_s.at[at],ret_ref.at[at],ret_sem.at[t]).start()
        return 0
    lax.fori_loop(0,n//per,tile,0)
    def pack(c,_):
        w[c]=gw[c].astype(jnp.bfloat16)
        return 0
    lax.fori_loop(0,chunks,pack,0)
    out=pltpu.make_async_copy(w,gw_ref,w_sem)
    out.start()
    pltpu.make_async_copy(ch_s.at[me],chosen_ref.at[me],loc_sem.at[0]).wait()
    pltpu.make_async_copy(gs_s.at[me],back_ref.at[me],loc_sem.at[1]).wait()
    def settle(o,_):
        peer=flip(me,o,n)
        gate_copy(peer).wait_send()
        row_copy(peer).wait_send()
        ch_copy(peer).wait_send()
        back_copy(peer).wait_send()
        ch_in(peer).wait_recv()
        back_in(peer).wait_recv()
        return 0
    lax.fori_loop(1,n,settle,0)
    def stored(t,_):
        block=flip(me//per,t,n//per)
        at=pl.ds(pl.multiple_of(block*per,per),per)
        pltpu.make_async_copy(ret_s.at[at],ret_ref.at[at],ret_sem.at[t]).wait()
        return 0
    lax.fori_loop(0,n//per,stored,0)
    out.wait()

def moe(send_rows,gate_slots,cot,scale,weights,collective_id=1):
    n,cap,D=send_rows.shape
    chunks,_,_,FC=weights.shape
    any_=pl.BlockSpec(memory_space=pl.ANY)
    bf=jnp.bfloat16; f32=jnp.float32
    dma=pltpu.SemaphoreType.DMA
    flops=6*2*n*cap*D*chunks*FC
    return pl.pallas_call(partial(moe_kernel,n,cap),
        out_shape=[jax.ShapeDtypeStruct((n,cap,D),bf),jax.ShapeDtypeStruct((n,8,TILE),f32),
                   jax.ShapeDtypeStruct((n,cap,D),bf),jax.ShapeDtypeStruct(weights.shape,bf)],
        in_specs=[any_,any_,any_,pl.BlockSpec(memory_space=pltpu.VMEM),any_],
        out_specs=[any_]*4,
        scratch_shapes=[pltpu.VMEM((n,cap,D),bf),pltpu.VMEM((n,8,TILE),f32),pltpu.VMEM((n*cap,D),bf),
            pltpu.VMEM(weights.shape,bf),pltpu.VMEM(weights.shape,f32),pltpu.VMEM((n,cap,D),bf),pltpu.VMEM((n,cap,D),bf),
            pltpu.VMEM((n,8,TILE),f32),pltpu.VMEM((TILE,D),bf),pltpu.VMEM((TILE,D),f32),pltpu.VMEM((TILE,D),f32)]
            +[dma((n,))]*8+[dma(()),dma((3,)),dma((n*cap//TILE,))],
        compiler_params=pltpu.CompilerParams(vmem_limit_bytes=62*2**20,collective_id=collective_id,has_side_effects=True),
        cost_estimate=pl.CostEstimate(flops=flops,bytes_accessed=40*2**20,transcendentals=0),
    )(send_rows,gate_slots,cot,scale,weights)


def near(dps,pairs):
    d=lax.axis_index("dp"); me=lax.axis_index("expert")
    core=me%2; pair=me//2
    partner={"expert":me+1-2*core}
    over=[((d+k)%dps,{"dp":(d+k)%dps}) for k in range(1,dps)]
    along=[((pair+k)%pairs,{"expert":2*((pair+k)%pairs)+core}) for k in range(1,pairs)]
    return d,pair,core,partner,over,along

def greet_all(devices):
    barrier=pltpu.get_barrier_semaphore()
    for dev in devices:
        pl.semaphore_signal(barrier,inc=1,device_id=dev,device_id_type=MESH)
    pl.semaphore_wait(barrier,len(devices))

def remote(src,dst,send,recv,dev):
    return pltpu.make_async_remote_copy(src_ref=src,dst_ref=dst,send_sem=send,recv_sem=recv,device_id=dev,device_id_type=MESH)

def gather_kernel(dps,pairs,w_ref,v_ref,out_ref,vout_ref,both,blk,vboth,vblk,
                  s1,r1,loc,zs,zr,vzs,vzr,ds_,dr,vds,vdr,ps,pr):
    r=w_ref.shape[1]; R=2*r
    d,pair,core,partner,over,along=near(dps,pairs)
    greet_all([partner]+[x[1] for x in over]+[x[1] for x in along])
    mine=pl.ds(pl.multiple_of(core*r,8),r)
    lanes=pl.ds(pl.multiple_of(core*128,128),128)
    half=pl.ds(core*2,2); rest=pl.ds(2-core*2,2)
    def rows(dd,q): return pl.ds(pl.multiple_of((dd*pairs+q)*R,16),R)
    c1=[remote(w_ref,both.at[:,mine,:],s1.at[0],r1.at[0],partner),
        remote(v_ref,vboth.at[:,lanes],s1.at[1],r1.at[1],partner)]
    for c in c1: c.start()
    both[:,mine,:]=w_ref[...]
    vboth[:,lanes]=v_ref[...]
    for c in c1: c.wait()
    blk[...]=both[...].astype(jnp.bfloat16)
    vblk[...]=vboth[...].astype(jnp.bfloat16)
    own=[pltpu.make_async_copy(blk,out_ref.at[:,rows(d,pair),:],loc.at[0]),
         pltpu.make_async_copy(vblk,vout_ref.at[d,pair],loc.at[1])]
    for c in own: c.start()
    zc=[]; dc=[]; pc=[]; vc=[]
    for q,dev in along:
        zc.append(remote(blk.at[half],out_ref.at[half,rows(d,pair),:],zs.at[q],zr.at[pair],dev)); zc[-1].start()
        vc.append(remote(vblk,vout_ref.at[d,pair],vzs.at[q],vzr.at[pair],dev)); vc[-1].start()
    for dd,dev in over:
        c=remote(blk.at[half],out_ref.at[half,rows(d,pair),:],ds_.at[dd,pair],dr.at[d,pair],dev); c.start(); dc.append(c)
    for q,dev in along:
        here=out_ref.at[half,rows(d,q),:]
        remote(here,here,zs.at[q],zr.at[q],dev).wait_recv()
        for dd,dev2 in over:
            c=remote(here,here,ds_.at[dd,q],dr.at[d,q],dev2); c.start(); dc.append(c)
        c=remote(here,here,ps.at[d,q],pr.at[d,q],partner); c.start(); pc.append(c)
    for q,dev in along:
        remote(vblk,vout_ref.at[d,q],vzs.at[q],vzr.at[q],dev).wait_recv()
    own[1].wait()
    for dd,dev in over:
        c=remote(vout_ref.at[d],vout_ref.at[d],vds.at[dd],vdr.at[d],dev); c.start(); vc.append(c)
    for q in [pair]+[x[0] for x in along]:
        for dd,dev in over:
            here=out_ref.at[half,rows(dd,q),:]
            remote(here,here,ds_.at[dd,q],dr.at[dd,q],dev).wait_recv()
            c=remote(here,here,ps.at[dd,q],pr.at[dd,q],partner); c.start(); pc.append(c)
    for q in [pair]+[x[0] for x in along]:
        for dd in [d]+[x[0] for x in over]:
            if q is pair and dd is d: continue
            there=out_ref.at[rest,rows(dd,q),:]
            remote(there,there,ps.at[dd,q],pr.at[dd,q],partner).wait_recv()
    for dd,dev in over:
        remote(vout_ref.at[dd],vout_ref.at[dd],vds.at[dd],vdr.at[dd],dev).wait_recv()
    for c in zc+dc+pc+vc: c.wait_send()
    own[0].wait()

def gather_dense(weights,vectors,dps,n,collective_id=2):
    pairs=n//2
    m,r,D=weights.shape
    V=jnp.zeros((16,128),jnp.float32).at[:vectors.shape[0],:r].set(vectors)
    dma=pltpu.SemaphoreType.DMA
    f32=jnp.float32; bf=jnp.bfloat16
    out,vout=pl.pallas_call(partial(gather_kernel,dps,pairs),
        out_shape=[jax.ShapeDtypeStruct((m,r*n*dps,D),bf),jax.ShapeDtypeStruct((dps,pairs,16,256),bf)],
        in_specs=[pl.BlockSpec(memory_space=pltpu.VMEM)]*2,
        out_specs=[pl.BlockSpec(memory_space=pl.ANY)]*2,
        scratch_shapes=[pltpu.VMEM((m,2*r,D),f32),pltpu.VMEM((m,2*r,D),bf),pltpu.VMEM((16,256),f32),pltpu.VMEM((16,256),bf),
            dma((2,)),dma((2,)),dma((2,)),dma((pairs,)),dma((pairs,)),dma((pairs,)),dma((pairs,)),
            dma((dps,pairs)),dma((dps,pairs)),dma((dps,)),dma((dps,)),dma((dps,pairs)),dma((dps,pairs))],
        compiler_params=pltpu.CompilerParams(vmem_limit_bytes=16*2**20,collective_id=collective_id,has_side_effects=True),
        cost_estimate=pl.CostEstimate(flops=0,bytes_accessed=100*2**20,transcendentals=0),
    )(weights,V)
    k=vectors.shape[0]
    vec=vout[:,:,:k].reshape(dps,pairs,k,2,128)[...,:r]
    vec=jnp.transpose(vec,(2,0,1,3,4)).reshape(k,r*n*dps)
    return out,vec

def scatter_kernel(dps,pairs,x_ref,mixed_ref,ga_ref,gp_ref,v_ref,out_ref,vout_ref,
                   left,right,got,own,total,in2,t32,tb,in3,u,in4,v1,v2,v3,
                   ls,s1,r1,s2,r2,s3,r3,s4,r4,vs1,vr1,vs2,vr2,vs3,vr3):
    d,pair,core,partner,over,along=near(dps,pairs)
    rows=out_ref.shape[1]; R=2*rows; D=out_ref.shape[2]
    loads=[pltpu.make_async_copy(x_ref,left.at[0],ls.at[0]),pltpu.make_async_copy(mixed_ref,left.at[1],ls.at[1]),
           pltpu.make_async_copy(gp_ref,right.at[pl.ds(0,3)],ls.at[2]),pltpu.make_async_copy(ga_ref,right.at[3],ls.at[3])]
    for c in loads: c.start()
    greet_all([partner]+[x[1] for x in over]+[x[1] for x in along])
    vc=[remote(v_ref,v1,vs1,vr1,partner)]
    vc[0].start()
    for c in loads: c.wait()
    def product(m):
        return lax.dot_general(left[m//3],right[m],TN,preferred_element_type=jnp.float32)
    sends=[]
    for i in range(2):
        total[i]=product(2-2*core+i).astype(jnp.bfloat16)
        c=remote(total.at[i],got.at[i],s1.at[i],r1.at[i],partner); c.start(); sends.append(c)
    for i in range(2):
        own[i]=product(2*core+i)
    remote(v_ref,v1,vs1,vr1,partner).wait_recv()
    v2[d]=v_ref[...]+v1[...]
    for dd,dev in over:
        c=remote(v2.at[d],v2.at[d],vs2.at[dd],vr2.at[d],dev); c.start(); vc.append(c)
    for i in range(2):
        sends[i].wait_send()
        remote(total.at[i],got.at[i],s1.at[i],r1.at[i],partner).wait_recv()
        total[i]=(own[i]+got[i].astype(jnp.float32)).astype(jnp.bfloat16)
    c2=[]
    order=along+[(pair,None)]
    def piece(dd,q): return pl.ds(pl.multiple_of((dd*pairs+q)*R,16),R)
    for q,_ in order:
        for dd,dev in over:
            c=remote(total.at[:,piece(dd,q),:],in2.at[d,q],s2.at[dd,q],r2.at[d,q],dev); c.start(); c2.append(c)
    for dd,dev in over:
        remote(v2.at[dd],v2.at[dd],vs2.at[dd],vr2.at[dd],dev).wait_recv()
    v3[pair]=sum(v2[k] for k in range(dps))
    for q,dev in along:
        c=remote(v3.at[pair],v3.at[pair],vs3.at[q],vr3.at[pair],dev); c.start(); vc.append(c)
    c3=[]
    for q,zdev in order:
        acc=total[:,piece(d,q),:].astype(jnp.float32)
        for dd,dev in over:
            remote(in2.at[dd,q],in2.at[dd,q],s2.at[dd,q],r2.at[dd,q],dev).wait_recv()
            acc=acc+in2[dd,q].astype(jnp.float32)
        if zdev is None:
            u[...]=acc
        else:
            tb[q]=acc.astype(jnp.bfloat16)
            c=remote(tb.at[q],in3.at[pair],s3.at[q],r3.at[pair],zdev); c.start(); c3.append(c)
    acc=u[...]
    for q,dev in along:
        remote(in3.at[q],in3.at[q],s3.at[q],r3.at[q],dev).wait_recv()
        acc=acc+in3[q].astype(jnp.float32)
    u[...]=acc
    theirs=pl.ds(pl.multiple_of((1-core)*rows,8),rows); mine=pl.ds(pl.multiple_of(core*rows,8),rows)
    c4=remote(u.at[:,theirs,:],in4,s4,r4,partner); c4.start()
    for q,dev in along:
        remote(v3.at[q],v3.at[q],vs3.at[q],vr3.at[q],dev).wait_recv()
    vout_ref[...]=sum(v3[k] for k in range(pairs))
    out_ref[pl.ds(2*core,2)]=u[:,mine,:]
    c4.wait_recv()
    out_ref[pl.ds(2-2*core,2)]=in4[...]
    for c in c2+c3+vc+[c4]: c.wait_send()

def scatter_dense(x,mixed,ga,gp,vec,dps,n,collective_id=3):
    pairs=n//2
    T,D=x.shape; rows=D//(dps*n); R=2*rows
    dma=pltpu.SemaphoreType.DMA
    f32=jnp.float32; bf=jnp.bfloat16
    any_=pl.BlockSpec(memory_space=pl.ANY); vm=pl.BlockSpec(memory_space=pltpu.VMEM)
    k=vec.shape[0]
    V=jnp.zeros((16,D),f32).at[:k].set(vec)
    out,vout=pl.pallas_call(partial(scatter_kernel,dps,pairs),
        out_shape=[jax.ShapeDtypeStruct((4,rows,D),f32),jax.ShapeDtypeStruct((16,D),f32)],
        in_specs=[any_]*4+[vm],out_specs=[vm]*2,
        scratch_shapes=[pltpu.VMEM((2,T,D),bf),pltpu.VMEM((4,T,D),bf),pltpu.VMEM((2,D,D),bf),pltpu.VMEM((2,D,D),f32),pltpu.VMEM((2,D,D),bf),
            pltpu.VMEM((dps,pairs,2,R,D),bf),pltpu.VMEM((8,128),f32),pltpu.VMEM((pairs,2,R,D),bf),pltpu.VMEM((pairs,2,R,D),bf),
            pltpu.VMEM((2,R,D),f32),pltpu.VMEM((2,rows,D),f32),pltpu.VMEM((16,D),f32),pltpu.VMEM((dps,16,D),f32),pltpu.VMEM((pairs,16,D),f32),
            dma((4,)),dma((2,)),dma((2,)),dma((dps,pairs)),dma((dps,pairs)),dma((pairs,)),dma((pairs,)),dma(()),dma(()),
            dma(()),dma(()),dma((dps,)),dma((dps,)),dma((pairs,)),dma((pairs,))],
        compiler_params=pltpu.CompilerParams(vmem_limit_bytes=48*2**20,collective_id=collective_id,has_side_effects=True),
        cost_estimate=pl.CostEstimate(flops=8*T*D*D,bytes_accessed=100*2**20,transcendentals=0),
    )(x,mixed,ga,gp,V)
    dev=lax.axis_index("dp")*n+lax.axis_index("expert")
    return out,lax.dynamic_slice_in_dim(vout[:k],dev*rows,rows,axis=1)

def norm_kernel(dps,pairs,d_ref,v_ref,e_ref,out_ref,a,b,c,s1,r1,s2,r2,s3,r3):
    d,pair,core,partner,over,along=near(dps,pairs)
    greet_all([partner]+[x[1] for x in over]+[x[1] for x in along])
    def squares(ref):
        x=ref[...].astype(jnp.float32)
        return jnp.sum(x*x)
    part=squares(d_ref)+squares(v_ref)
    for i in range(e_ref.shape[0]):
        part=part+squares(e_ref.at[i])
    a[core]=jnp.full((8,128),part,jnp.float32)
    cs=[remote(a.at[core],a.at[core],s1,r1.at[core],partner)]
    cs[0].start()
    remote(a.at[1-core],a.at[1-core],s1,r1.at[1-core],partner).wait_recv()
    b[d]=a[0]+a[1]
    for dd,dev in over:
        x=remote(b.at[d],b.at[d],s2.at[dd],r2.at[d],dev); x.start(); cs.append(x)
    for dd,dev in over:
        remote(b.at[dd],b.at[dd],s2.at[dd],r2.at[dd],dev).wait_recv()
    c[pair]=sum(b[k] for k in range(dps))
    for q,dev in along:
        x=remote(c.at[pair],c.at[pair],s3.at[q],r3.at[pair],dev); x.start(); cs.append(x)
    for q,dev in along:
        remote(c.at[q],c.at[q],s3.at[q],r3.at[q],dev).wait_recv()
    out_ref[...]=sum(c[k] for k in range(pairs))
    for x in cs: x.wait_send()

def norm_squares(dense,vec,expert,dps,n,collective_id=4):
    pairs=n//2
    dma=pltpu.SemaphoreType.DMA; f32=jnp.float32
    vm=pl.BlockSpec(memory_space=pltpu.VMEM)
    out=pl.pallas_call(partial(norm_kernel,dps,pairs),
        out_shape=jax.ShapeDtypeStruct((8,128),f32),in_specs=[vm]*3,out_specs=vm,
        scratch_shapes=[pltpu.VMEM((2,8,128),f32),pltpu.VMEM((dps,8,128),f32),pltpu.VMEM((pairs,8,128),f32),
            dma(()),dma((2,)),dma((dps,)),dma((dps,)),dma((pairs,)),dma((pairs,))],
        compiler_params=pltpu.CompilerParams(vmem_limit_bytes=16*2**20,collective_id=collective_id,has_side_effects=True),
    )(dense,vec,expert)
    return out[0,0]


def adam_update(weight, gradient, first_moment, second_moment, average, factor, rate):
    clipped = gradient * factor
    first_new = beta_first * first_moment + (1.0 - beta_first) * clipped
    second_new = beta_second * second_moment + (1.0 - beta_second) * clipped * clipped
    first_hat = first_new / (1.0 - beta_first**STEP)
    second_hat = second_new / (1.0 - beta_second**STEP)
    updated = weight - rate * (
        first_hat / (jnp.sqrt(second_hat) + adam_eps) + weight_decay * weight
    )
    average_new = ema_keep * average + (1.0 - ema_keep) * updated
    return (updated, first_new, second_new, average_new)


def shards(
    inputs,
    cotangent,
    document_ids,
    domain_counts,
    domain_weight,
    token_order,
    expert_counts,
    dense_weights,
    vector_params,
    expert_weights,
    dense_first,
    dense_second,
    dense_average,
    vector_first,
    vector_second,
    vector_average,
    expert_first,
    expert_second,
    expert_average,
):
    tokens, model_width = inputs.shape
    experts_total = expert_counts.shape[1]
    capacity = 2 * tokens // experts_total
    owners = lax.axis_size("expert")
    groups = lax.axis_size(("dp", "expert"))
    sequences = tokens // LEN
    splits = lax.axis_size("dp")
    own_rows = dense_weights.shape[1]
    if own_rows % 8 == 0:
        dense_low, vector_low = gather_dense(dense_weights, vector_params, splits, owners)
    else:
        dense_low, vector_low = (
            lax.all_gather(dense_weights.astype(jnp.bfloat16), ("dp", "expert"), axis=1, tiled=True),
            lax.all_gather(vector_params.astype(jnp.bfloat16), ("dp", "expert"), axis=1, tiled=True),
        )
    me = lax.axis_index("expert")
    seq_index = lax.axis_index("dp") * owners + jnp.arange(owners)
    bounds = jnp.cumsum(domain_counts)
    domain = jnp.sum((seq_index[:, None] >= bounds[None, :]).astype(jnp.int32), axis=1)
    seq_pick = (domain[:, None] == jnp.arange(NDOM)[None, :]).astype(jnp.float32)
    seq_weight = jnp.sum(seq_pick * domain_weight[None, :], axis=1)
    seq_count = jnp.sum(seq_pick * domain_counts[None, :].astype(jnp.float32), axis=1)
    seq_scale = seq_weight * (sequences * groups) / (NDOM * seq_count)
    slot_scale = jnp.repeat(seq_scale, capacity)[:, None]
    token_scale = jnp.broadcast_to(seq_scale[me], (tokens,))
    row_counts = expert_counts[0]
    row_order = token_order[0]
    count_ends = jnp.cumsum(row_counts)
    count_starts = count_ends - row_counts
    sorted_pos = jnp.arange(tokens)
    sorted_expert = jnp.sum((sorted_pos[:, None] >= count_ends[None, :]).astype(jnp.int32), axis=1)
    sorted_pick = sorted_expert[:, None] == jnp.arange(experts_total)[None, :]
    sorted_start = jnp.sum(jnp.where(sorted_pick, count_starts[None, :], 0), axis=1)
    sorted_slot = sorted_expert * capacity + sorted_pos - sorted_start
    at_token = row_order[:, None] == jnp.arange(tokens)[None, :]
    token_slot = jnp.sum(jnp.where(at_token, sorted_slot[:, None], 0), axis=0)
    token_expert = token_slot // capacity
    expert_pick = (token_expert[:, None] == jnp.arange(experts_total)[None, :]).astype(jnp.float32)
    slot_match = token_slot[:, None] == jnp.arange(experts_total * capacity)[None, :]
    slot_pick = slot_match.astype(jnp.bfloat16)

    def to_slots(rows):
        placed = jnp.dot(slot_pick.T, rows, preferred_element_type=jnp.float32)
        return placed.astype(jnp.bfloat16).reshape(experts_total, capacity, model_width)

    def from_slots(rows):
        return jnp.dot(
            slot_pick, rows.reshape(-1, model_width), preferred_element_type=jnp.float32
        )

    cot_received = lax.all_to_all(
        to_slots(cotangent), "expert", split_axis=0, concat_axis=0, tiled=True
    ).reshape(-1, model_width)
    own_low = expert_weights[0].astype(jnp.bfloat16)
    expert_low = lax.all_gather(own_low, "dp", axis=0)
    inputs_float = inputs.astype(jnp.float32)
    normed_one, norm_one_back = jax.vjp(layer_norm, inputs_float, vector_low[0].astype(jnp.float32))
    normed_low = normed_one.astype(jnp.bfloat16)
    projected = jnp.einsum(
        "td,cde->cte", normed_low, dense_low[:3], preferred_element_type=jnp.float32
    ).astype(jnp.bfloat16)
    documents = document_ids.reshape(-1)
    mixed_low, totals = attend_forward(projected, documents)
    hidden_state = inputs_float + jnp.dot(
        mixed_low, dense_low[3], preferred_element_type=jnp.float32
    )
    normed_two, norm_two_back = jax.vjp(layer_norm, hidden_state, vector_low[1].astype(jnp.float32))
    centroids = vector_low[2:].astype(jnp.float32)
    logits = jnp.dot(normed_two, centroids.T, precision=lax.Precision.HIGHEST)
    gate_value = jax.nn.sigmoid(jnp.sum(logits * expert_pick, axis=1))
    sent_rows = normed_two.astype(jnp.bfloat16)
    send_rows = to_slots(sent_rows)
    per = TILE // capacity
    gate_slots = jnp.sum(
        jnp.where(slot_match, gate_value[:, None], 0.0), axis=0
    ).reshape(experts_total, 1, 1, capacity)
    lane_part = (jnp.arange(per) == me % per).astype(jnp.float32)
    gate_tiles = jnp.broadcast_to(
        gate_slots * lane_part[None, None, :, None], (experts_total, 8, per, capacity)
    ).reshape(experts_total, 8, TILE)
    grad_back, chosen_tiles, produced_low, grad_expert = moe(
        send_rows, gate_tiles, cot_received, slot_scale, expert_low
    )
    expert_low_grad = lax.psum_scatter(grad_expert, "dp", scatter_dimension=0)
    expert_grad = expert_low_grad.astype(jnp.float32)[None]
    returned = lax.all_to_all(produced_low, "expert", split_axis=0, concat_axis=0, tiled=True)
    returned_rows = from_slots(returned)
    block_output = hidden_state + gate_value[:, None] * returned_rows
    grad_out = cotangent.astype(jnp.float32) * token_scale[:, None]
    grad_sent_rows = from_slots(grad_back)
    chosen_slots = lax.dynamic_slice_in_dim(
        chosen_tiles[:, 0, :], me % per * capacity, capacity, axis=1
    )
    grad_chosen = jnp.sum(jnp.where(slot_match, chosen_slots.reshape(1, -1), 0.0), axis=1)
    chosen_grad = grad_chosen[:, None] * expert_pick
    grad_normed_two = grad_sent_rows + jnp.dot(
        chosen_grad, centroids, precision=lax.Precision.HIGHEST
    )
    grad_centroids = jnp.dot(chosen_grad.T, normed_two, precision=lax.Precision.HIGHEST)
    grad_hidden_norm, grad_gain_two = norm_two_back(grad_normed_two)
    grad_hidden = grad_out + grad_hidden_norm
    grad_attn = grad_hidden.astype(jnp.bfloat16)
    grad_mixed = jnp.dot(grad_attn, dense_low[3].T, preferred_element_type=jnp.float32).astype(
        jnp.bfloat16
    )
    grad_proj = attend_backward(projected, documents, totals, grad_mixed)
    grad_normed_one = jnp.einsum(
        "cte,cde->td", grad_proj, dense_low[:3], preferred_element_type=jnp.float32
    )
    grad_input_norm, grad_gain_one = norm_one_back(grad_normed_one)
    input_grad = grad_hidden + grad_input_norm
    vector_grad = jnp.concatenate(
        [grad_gain_one[None], grad_gain_two[None], grad_centroids], axis=0
    )
    if own_rows % 8 == 0:
        dense_grad, vector_grad = scatter_dense(
            normed_low, mixed_low, grad_attn, grad_proj, vector_grad, splits, owners
        )
    else:
        grad_in_proj = jnp.einsum(
            "td,cte->cde", normed_low, grad_proj, preferred_element_type=jnp.float32
        )
        grad_out_proj = jnp.dot(mixed_low.T, grad_attn, preferred_element_type=jnp.float32)
        dense_grad, vector_grad = (
            lax.psum_scatter(
                jnp.concatenate([grad_in_proj, grad_out_proj[None]], axis=0),
                ("dp", "expert"),
                scatter_dimension=1,
                tiled=True,
            ),
            lax.psum_scatter(vector_grad, ("dp", "expert"), scatter_dimension=1, tiled=True),
        )
    squares = norm_squares(dense_grad, vector_grad, expert_low_grad, splits, owners)
    grad_norm = jnp.sqrt(squares)
    factor = jnp.minimum(1.0, clip_norm / (grad_norm + 1e-06))
    dense_new = adam_update(
        dense_weights, dense_grad, dense_first, dense_second, dense_average, factor, dense_rate
    )
    vector_new = adam_update(
        vector_params, vector_grad, vector_first, vector_second, vector_average, factor, vector_rate
    )
    expert_new = adam_update(
        expert_weights,
        expert_grad,
        expert_first,
        expert_second,
        expert_average,
        factor,
        expert_rate,
    )
    return (
        block_output,
        input_grad,
        dense_new[0],
        dense_new[1],
        dense_new[2],
        dense_new[3],
        vector_new[0],
        vector_new[1],
        vector_new[2],
        vector_new[3],
        expert_new[0],
        expert_new[1],
        expert_new[2],
        expert_new[3],
        grad_norm,
    )


def solution(mesh):
    placed = (
        P(("dp", "expert"), None),
        P(("dp", "expert"), None),
        P(("dp", "expert"), None),
        P(),
        P(),
        P(("dp", "expert"), None),
        P(("dp", "expert"), None),
        P(None, ("dp", "expert"), None),
        P(None, ("dp", "expert")),
        P("expert", None, None, "dp"),
        P(None, ("dp", "expert"), None),
        P(None, ("dp", "expert"), None),
        P(None, ("dp", "expert"), None),
        P(None, ("dp", "expert")),
        P(None, ("dp", "expert")),
        P(None, ("dp", "expert")),
        P("expert", None, None, "dp"),
        P("expert", None, None, "dp"),
        P("expert", None, None, "dp"),
    )
    return jax.shard_map(
        shards,
        mesh=mesh,
        in_specs=placed,
        out_specs=(
            P(("dp", "expert"), None),
            P(("dp", "expert"), None),
            P(None, ("dp", "expert"), None),
            P(None, ("dp", "expert"), None),
            P(None, ("dp", "expert"), None),
            P(None, ("dp", "expert"), None),
            P(None, ("dp", "expert")),
            P(None, ("dp", "expert")),
            P(None, ("dp", "expert")),
            P(None, ("dp", "expert")),
            P("expert", None, None, "dp"),
            P("expert", None, None, "dp"),
            P("expert", None, None, "dp"),
            P("expert", None, None, "dp"),
            P(),
        ),
        check_vma=False,
    )
```

```python
from functools import partial

import jax
import jax.numpy as jnp
from jax import lax
from jax.experimental import pallas as pl
from jax.experimental.pallas import tpu as pltpu
from jax.sharding import PartitionSpec as P

HEADS = 12
HEAD_DIM = 64
LEN = 1024
WINDOW = 512
NDOM = 8
STEP = 10


norm_eps = 1e-05
masked_score = -1e30
beta_first = 0.9
beta_second = 0.999
adam_eps = 1e-08
dense_rate = 0.1
vector_rate = 0.5
expert_rate = 0.02
weight_decay = 0.1
ema_keep = 0.9
clip_norm = 1.0


def layer_norm(values_in, gain_row):
    center = values_in - jnp.mean(values_in, axis=-1, keepdims=True)
    spread = jnp.mean(center * center, axis=-1, keepdims=True)
    return center * lax.rsqrt(spread + norm_eps) * gain_row


NT = (((1,), (1,)), ((), ()))
TN = (((0,), (0,)), ((), ()))


def fwd_kernel(QB, q_ref,k_ref,v_ref,dcol_ref,drow_ref,o_ref,lse_ref,bias_ref):
    reach = WINDOW//QB
    low_lane = lax.broadcasted_iota(jnp.int32,(QB,128),1) < HEAD_DIM
    @pl.when(pl.program_id(0)==0)
    def _():
        for i in range(LEN//QB):
            first=max(0,i-reach)*QB; W=(i+1)*QB-first
            qp=i*QB+lax.broadcasted_iota(jnp.int32,(QB,W),0)
            kp=first+lax.broadcasted_iota(jnp.int32,(QB,W),1)
            ok=(kp<=qp)&(dcol_ref[i*QB:(i+1)*QB,:]==drow_ref[:,first:first+W])
            bias_ref[i*QB:(i+1)*QB,:W]=jnp.where(ok,0.0,masked_score)
    for i in range(LEN//QB):
        rows=slice(i*QB,(i+1)*QB)
        first=max(0,i-reach)*QB; W=(i+1)*QB-first
        q=q_ref[0,rows,:]*jnp.bfloat16(HEAD_DIM**-0.5)
        zero=jnp.zeros_like(q)
        qs=jnp.concatenate([jnp.where(low_lane,q,zero),jnp.where(low_lane,zero,q)],axis=0)
        s=lax.dot_general(qs,k_ref[0,first:first+W,:],NT,preferred_element_type=jnp.float32)
        s=(s.reshape(2,QB,W)+bias_ref[rows,:W][None]).reshape(2*QB,W)
        top=jnp.max(s,axis=1,keepdims=True)
        e=jnp.exp(s-top)
        total=jnp.sum(e,axis=1,keepdims=True)
        p=(e*(1.0/total)).astype(jnp.bfloat16)
        o=jnp.dot(p,v_ref[0,first:first+W,:],preferred_element_type=jnp.float32)
        o_ref[rows,:]=jnp.where(low_lane,o[:QB],o[QB:]).astype(jnp.bfloat16)
        lse=top+jnp.log(total)
        lse_ref[0,rows,:]=jnp.where(low_lane,lse[:QB],lse[QB:])

def attend_forward(projected, documents, QB=256):
    T=projected.shape[1]; D=projected.shape[2]
    dcol=documents.reshape(T,1); drow=documents.reshape(1,T)
    def sp(c): return pl.BlockSpec((1,T,128),lambda h,c=c:(c,0,h))
    return pl.pallas_call(partial(fwd_kernel,QB),grid=(D//128,),
        in_specs=[sp(0),sp(1),sp(2),pl.BlockSpec((T,1),lambda h:(0,0)),pl.BlockSpec((1,T),lambda h:(0,0))],
        out_specs=[pl.BlockSpec((T,128),lambda h:(0,h)),pl.BlockSpec((1,T,128),lambda h:(h,0,0))],
        out_shape=[jax.ShapeDtypeStruct((T,D),jnp.bfloat16),jax.ShapeDtypeStruct((D//128,T,128),jnp.float32)],
        scratch_shapes=[pltpu.VMEM((T,min(T,WINDOW+QB)),jnp.float32)],
        compiler_params=pltpu.CompilerParams(vmem_limit_bytes=48*2**20),
    )(projected,projected,projected,dcol,drow)

QB = 256


def transposed_bias(bias_ref, dcol_ref, drow_ref, QB):
    reach = WINDOW // QB
    for i in range(LEN // QB):
        first = max(0, i - reach) * QB
        W = (i + 1) * QB - first
        kp = first + lax.broadcasted_iota(jnp.int32, (W, QB), 0)
        qp = i * QB + lax.broadcasted_iota(jnp.int32, (W, QB), 1)
        ok = (kp <= qp) & (dcol_ref[first : first + W, :] == drow_ref[:, i * QB : (i + 1) * QB])
        bias_ref[:W, i * QB : (i + 1) * QB] = jnp.where(ok, 0.0, masked_score)


def head_pair_backward(QB, q_ref, k_ref, v_ref, lse_ref, g_ref, bias_ref, dk_ref, dv_ref, put_dq):
    reach = WINDOW // QB
    low_lane = lax.broadcasted_iota(jnp.int32, (QB, 128), 1) < HEAD_DIM
    dk_ref[...] = jnp.zeros_like(dk_ref)
    dv_ref[...] = jnp.zeros_like(dv_ref)
    for i in range(LEN // QB):
        rows = slice(i * QB, (i + 1) * QB)
        first = max(0, i - reach) * QB
        W = (i + 1) * QB - first
        keys = slice(first, first + W)
        q = q_ref[0, rows, :] * jnp.bfloat16(HEAD_DIM**-0.5)
        zero = jnp.zeros_like(q)
        qs = jnp.concatenate([jnp.where(low_lane, q, zero), jnp.where(low_lane, zero, q)], axis=0)
        g = g_ref[rows, :]
        gs = jnp.concatenate([jnp.where(low_lane, g, zero), jnp.where(low_lane, zero, g)], axis=0)
        k = k_ref[0, keys, :]
        st = lax.dot_general(k, qs, NT, preferred_element_type=jnp.float32)
        bias = bias_ref[:W, rows]
        lse = jnp.transpose(lse_ref[0, rows, :])
        lse = jnp.concatenate([lse[0:1, :], lse[64:65, :]], axis=1)
        p = jnp.exp(st + jnp.concatenate([bias, bias], axis=1) - lse)
        dp = lax.dot_general(v_ref[0, keys, :], gs, NT, preferred_element_type=jnp.float32)
        inner = jnp.sum(p * dp, axis=0, keepdims=True)
        ds = (p * (dp - inner)).astype(jnp.bfloat16)
        dk_ref[keys, :] += jnp.dot(ds, qs, preferred_element_type=jnp.float32)
        dv_ref[keys, :] += jnp.dot(p.astype(jnp.bfloat16), gs, preferred_element_type=jnp.float32)
        dq = lax.dot_general(ds, k, TN, preferred_element_type=jnp.float32)
        put_dq(rows, (jnp.where(low_lane, dq[:QB], dq[QB:]) * HEAD_DIM**-0.5).astype(jnp.bfloat16))


def bwd_kernel(QB, q_ref, k_ref, v_ref, lse_ref, g_ref, dcol_ref, drow_ref, out_ref, bias_ref, dk_ref, dv_ref):
    @pl.when(pl.program_id(0) == 0)
    def _():
        transposed_bias(bias_ref, dcol_ref, drow_ref, QB)

    def put_dq(rows, value):
        out_ref[0, rows, :] = value

    head_pair_backward(QB, q_ref, k_ref, v_ref, lse_ref, g_ref, bias_ref, dk_ref, dv_ref, put_dq)
    out_ref[1, :, :] = dk_ref[...].astype(jnp.bfloat16)
    out_ref[2, :, :] = dv_ref[...].astype(jnp.bfloat16)


def attend_backward(projected, documents, lse, grad_mixed, QB=256):
    T=projected.shape[1]; D=projected.shape[2]
    dcol=documents.reshape(T,1); drow=documents.reshape(1,T)
    def sp(c): return pl.BlockSpec((1,T,128),lambda h,c=c:(c,0,h))
    return pl.pallas_call(partial(bwd_kernel,QB),grid=(D//128,),
        in_specs=[sp(0),sp(1),sp(2),pl.BlockSpec((1,T,128),lambda h:(h,0,0)),pl.BlockSpec((T,128),lambda h:(0,h)),pl.BlockSpec((T,1),lambda h:(0,0)),pl.BlockSpec((1,T),lambda h:(0,0))],
        out_specs=pl.BlockSpec((3,T,128),lambda h:(0,0,h)),
        out_shape=jax.ShapeDtypeStruct((3,T,D),jnp.bfloat16),
        scratch_shapes=[pltpu.VMEM((min(T,WINDOW+QB),T),jnp.float32),pltpu.VMEM((T,128),jnp.float32),pltpu.VMEM((T,128),jnp.float32)],
        compiler_params=pltpu.CompilerParams(vmem_limit_bytes=48*2**20),
    )(projected,projected,projected,lse,grad_mixed,dcol,drow)


MESH=pl.DeviceIdType.MESH
TILE=512

def flip(a,b,n):
    out=0
    bit=1
    while bit<n:
        out=out+bit*((a//bit+b//bit)%2)
        bit*=2
    return out

def gelu_pair(x):
    c=0.7978845608028654
    sq=x*x
    t=jnp.tanh(c*(x+0.044715*(x*sq)))
    half=0.5*(1.0+t)
    return x*half, half+x*(0.5*(1.0-t*t))*(c+(3*0.044715*c)*sq)

def moe_kernel(n,cap,send_ref,gate_ref,cot_ref,scale_ref,w_ref,
               back_ref,late_ref,chosen_ref,ret_ref,gw_ref,
               recv,gates,cot,w,gw,ret_s,gs_s,ch_s,g_s,racc,sacc,
               send_sem,recv_sem,gate_send,gate_recv,back_send,back_recv,ch_send,ch_recv,w_sem,loc_sem,ret_sem):
    per=TILE//cap
    tiles=n//per
    chunks=w_ref.shape[0]
    me=lax.axis_index("expert")
    barrier=pltpu.get_barrier_semaphore()
    def greet(o,_):
        pl.semaphore_signal(barrier,inc=1,device_id={"expert":flip(me,o,n)},device_id_type=MESH)
        return 0
    lax.fori_loop(1,n,greet,0)
    pl.semaphore_wait(barrier,n-1)

    def copies(src,dst,send,recv_,peer,there):
        return pltpu.make_async_remote_copy(src_ref=src,dst_ref=dst,send_sem=send.at[peer],recv_sem=recv_.at[there],
            device_id={"expert":peer},device_id_type=MESH)
    def row_copy(peer): return copies(send_ref.at[peer],recv.at[me],send_sem,recv_sem,peer,me)
    def gate_copy(peer): return copies(gate_ref.at[peer],gates.at[me],gate_send,gate_recv,peer,me)
    def row_in(src): return copies(send_ref.at[src],recv.at[src],send_sem,recv_sem,src,src)
    def gate_in(src): return copies(gate_ref.at[src],gates.at[src],gate_send,gate_recv,src,src)
    def back_copy(src): return copies(gs_s.at[src],back_ref.at[flip(src,me,n)],back_send,back_recv,src,me)
    def ch_copy(src): return copies(ch_s.at[src],chosen_ref.at[flip(src,me,n)],ch_send,ch_recv,src,me)
    def back_in(src): return copies(gs_s.at[src],back_ref.at[flip(src,me,n)],back_send,back_recv,src,src)
    def ch_in(src): return copies(ch_s.at[src],chosen_ref.at[flip(src,me,n)],ch_send,ch_recv,src,src)

    def push(o,_):
        gate_copy(flip(me,o,n)).start()
        row_copy(flip(me,o,n)).start()
        return 0
    last=(tiles-1)*per
    lax.fori_loop(0,last-1,lambda i,c: push(last-1-i,c),0)
    own=[pltpu.make_async_copy(send_ref.at[me],recv.at[me],loc_sem.at[0]),
         pltpu.make_async_copy(gate_ref.at[me],gates.at[me],loc_sem.at[1]),
         pltpu.make_async_copy(cot_ref,cot,loc_sem.at[2]),
         pltpu.make_async_copy(w_ref,w,w_sem)]
    for c in own: c.start()
    def wipe(c,_):
        gw[c]=jnp.zeros(gw.shape[1:],jnp.float32)
        return 0
    lax.fori_loop(0,chunks,wipe,0)
    for c in own: c.wait()
    own_back=pltpu.make_async_copy(gs_s.at[me],back_ref.at[0],loc_sem.at[1])
    own_ch=pltpu.make_async_copy(ch_s.at[me],chosen_ref.at[0],loc_sem.at[0])

    def tile(t,_):
        @pl.when(t==1)
        def _():
            lax.fori_loop(last,n,push,0)
        block=flip(me//per,t,tiles)
        def arrive(j,_):
            src=block*per+j
            @pl.when(src!=me)
            def _():
                gate_in(src).wait_recv()
                row_in(src).wait_recv()
            return 0
        lax.fori_loop(0,per,arrive,0)
        at=pl.ds(pl.multiple_of(block*per,per),per)
        rows=pl.ds(pl.multiple_of(block*TILE,TILE),TILE)
        gate=jnp.transpose(jnp.sum(gates[at],axis=0))[:,0:1]
        grad_out=cot[rows,:].astype(jnp.float32)*scale_ref[rows,:]
        g_s[...]=(gate*grad_out).astype(jnp.bfloat16)
        racc[...]=jnp.zeros_like(racc)
        sacc[...]=jnp.zeros_like(sacc)
        def chunk(c,_):
            x=recv[at].reshape(TILE,recv.shape[2])
            g=g_s[...]
            act,slope=gelu_pair(jnp.dot(x,w[c,0],preferred_element_type=jnp.float32))
            a=act.astype(jnp.bfloat16)
            ga=jnp.dot(g,w[c,1],preferred_element_type=jnp.float32).astype(jnp.bfloat16)
            gp=(ga.astype(jnp.float32)*slope).astype(jnp.bfloat16)
            racc[...]+=lax.dot_general(a,w[c,1],NT,preferred_element_type=jnp.float32)
            sacc[...]+=lax.dot_general(gp,w[c,0],NT,preferred_element_type=jnp.float32)
            gw[c,0]+=lax.dot_general(x,gp,TN,preferred_element_type=jnp.float32)
            gw[c,1]+=lax.dot_general(g,a,TN,preferred_element_type=jnp.float32)
            return 0
        lax.fori_loop(0,chunks,chunk,0)
        gs_s[at]=sacc[...].astype(jnp.bfloat16).reshape(per,cap,recv.shape[2])
        def give(j,_):
            src=block*per+j
            @pl.when(src!=me)
            def _():
                back_copy(src).start()
            @pl.when(src==me)
            def _():
                own_back.start()
            return 0
        @pl.when(t<tiles-1)
        def _():
            lax.fori_loop(0,per,give,0)
        @pl.when(t==tiles-1)
        def _():
            pltpu.make_async_copy(gs_s.at[at],late_ref,loc_sem.at[2]).start()
        ret=racc[...].astype(jnp.bfloat16)
        ret_s[at]=ret.reshape(per,cap,recv.shape[2])
        pltpu.make_async_copy(ret_s.at[at],ret_ref.at[at],ret_sem.at[t]).start()
        grad_out=cot[rows,:].astype(jnp.float32)*scale_ref[rows,:]
        chosen=jnp.sum(grad_out*ret.astype(jnp.float32),axis=1,keepdims=True)*gate*(1.0-gate)
        chosen=jnp.transpose(jnp.broadcast_to(chosen,(TILE,128)))[0:8,:]
        def tell(j,_):
            src=block*per+j
            ch_s[src]=chosen
            @pl.when(src!=me)
            def _():
                ch_copy(src).start()
            @pl.when(src==me)
            def _():
                own_ch.start()
            return 0
        lax.fori_loop(0,per,tell,0)
        return 0
    lax.fori_loop(0,tiles,tile,0)
    def pack(c,_):
        w[c]=gw[c].astype(jnp.bfloat16)
        pltpu.make_async_copy(w.at[c],gw_ref.at[c],w_sem).start()
        return 0
    lax.fori_loop(0,chunks,pack,0)
    own_ch.wait()
    own_back.wait()
    block=flip(me//per,tiles-1,tiles)
    at=pl.ds(pl.multiple_of(block*per,per),per)
    pltpu.make_async_copy(gs_s.at[at],late_ref,loc_sem.at[2]).wait()
    def settle(o,_):
        peer=flip(me,o,n)
        gate_copy(peer).wait_send()
        row_copy(peer).wait_send()
        ch_copy(peer).wait_send()
        ch_in(peer).wait_recv()
        @pl.when(o<last)
        def _():
            back_copy(peer).wait_send()
            back_in(peer).wait_recv()
        return 0
    lax.fori_loop(1,n,settle,0)
    def stored(t,_):
        block=flip(me//per,t,tiles)
        at=pl.ds(pl.multiple_of(block*per,per),per)
        pltpu.make_async_copy(ret_s.at[at],ret_ref.at[at],ret_sem.at[t]).wait()
        return 0
    lax.fori_loop(0,tiles,stored,0)
    pltpu.make_async_copy(w,gw_ref,w_sem).wait()

def late_kernel(n,gs_ref,out_ref,send_sem,recv_sem):
    per=gs_ref.shape[0]
    tiles=n//per
    me=lax.axis_index("expert")
    block=flip(me//per,tiles-1,tiles)
    barrier=pltpu.get_barrier_semaphore()
    def greet(j,_):
        pl.semaphore_signal(barrier,inc=1,device_id={"expert":block*per+j},device_id_type=MESH)
        return 0
    lax.fori_loop(0,per,greet,0)
    pl.semaphore_wait(barrier,per)
    def copy(j):
        k=flip(j,me%per,per)
        return pltpu.make_async_remote_copy(src_ref=gs_ref.at[j],dst_ref=out_ref.at[k],send_sem=send_sem.at[k],recv_sem=recv_sem.at[k],
            device_id={"expert":block*per+j},device_id_type=MESH)
    def go(j,_):
        copy(j).start()
        return 0
    lax.fori_loop(0,per,go,0)
    def end(j,_):
        copy(j).wait()
        return 0
    lax.fori_loop(0,per,end,0)

def moe(send_rows,gate_slots,cot,scale,weights):
    n,cap,D=send_rows.shape
    chunks,_,_,FC=weights.shape
    per=TILE//cap
    any_=pl.BlockSpec(memory_space=pl.ANY)
    bf=jnp.bfloat16; f32=jnp.float32
    dma=pltpu.SemaphoreType.DMA
    flops=6*2*n*cap*D*chunks*FC
    back,late,chosen,ret,gw=pl.pallas_call(partial(moe_kernel,n,cap),
        out_shape=[jax.ShapeDtypeStruct((n-per,cap,D),bf),jax.ShapeDtypeStruct((per,cap,D),bf),jax.ShapeDtypeStruct((n,8,TILE),f32),
                   jax.ShapeDtypeStruct((n,cap,D),bf),jax.ShapeDtypeStruct(weights.shape,bf)],
        in_specs=[any_,any_,any_,pl.BlockSpec(memory_space=pltpu.VMEM),any_],
        out_specs=[any_]*5,
        scratch_shapes=[pltpu.VMEM((n,cap,D),bf),pltpu.VMEM((n,8,TILE),f32),pltpu.VMEM((n*cap,D),bf),
            pltpu.VMEM(weights.shape,bf),pltpu.VMEM(weights.shape,f32),pltpu.VMEM((n,cap,D),bf),pltpu.VMEM((n,cap,D),bf),
            pltpu.VMEM((n,8,TILE),f32),pltpu.VMEM((TILE,D),bf),pltpu.VMEM((TILE,D),f32),pltpu.VMEM((TILE,D),f32)]
            +[dma((n,))]*8+[dma(()),dma((3,)),dma((n//per,))],
        compiler_params=pltpu.CompilerParams(vmem_limit_bytes=62*2**20,collective_id=1,has_side_effects=True),
        cost_estimate=pl.CostEstimate(flops=flops,bytes_accessed=40*2**20,transcendentals=0),
    )(send_rows,gate_slots,cot,scale,weights)
    late=pl.pallas_call(partial(late_kernel,n),
        out_shape=jax.ShapeDtypeStruct((per,cap,D),bf),in_specs=[any_],out_specs=any_,
        scratch_shapes=[dma((per,)),dma((per,))],
        compiler_params=pltpu.CompilerParams(collective_id=5,has_side_effects=True),
        cost_estimate=pl.CostEstimate(flops=0,bytes_accessed=100*2**20,transcendentals=0),
    )(late)
    return back,late,chosen,ret,gw


def near(dps,pairs):
    d=lax.axis_index("dp"); me=lax.axis_index("expert")
    core=me%2; pair=me//2
    partner={"expert":me+1-2*core}
    over=[((d+k)%dps,{"dp":(d+k)%dps}) for k in range(1,dps)]
    along=[((pair+k)%pairs,{"expert":2*((pair+k)%pairs)+core}) for k in range(1,pairs)]
    return d,pair,core,partner,over,along

def greet_all(devices):
    barrier=pltpu.get_barrier_semaphore()
    for dev in devices:
        pl.semaphore_signal(barrier,inc=1,device_id=dev,device_id_type=MESH)
    pl.semaphore_wait(barrier,len(devices))

def remote(src,dst,send,recv,dev):
    return pltpu.make_async_remote_copy(src_ref=src,dst_ref=dst,send_sem=send,recv_sem=recv,device_id=dev,device_id_type=MESH)

def gather_kernel(dps,pairs,w_ref,v_ref,out_ref,vout_ref,both,blk,vboth,vblk,
                  s1,r1,loc,us,ur,ls,lr,vzs,vzr,ds_,dr,vds,vdr,ps,pr):
    r=w_ref.shape[1]; R=2*r
    d,pair,core,partner,over,along=near(dps,pairs)
    greet_all([partner]+[x[1] for x in over]+[x[1] for x in along])
    mine=pl.ds(pl.multiple_of(core*r,8),r)
    lanes=pl.ds(pl.multiple_of(core*128,128),128)
    half=pl.ds(core*2,2); rest=pl.ds(2-core*2,2)
    def rows(dd,q): return pl.ds(pl.multiple_of((dd*pairs+q)*R,16),R)
    c1=[remote(w_ref,both.at[:,mine,:],s1.at[0],r1.at[0],partner),
        remote(v_ref,vboth.at[:,lanes],s1.at[1],r1.at[1],partner)]
    for c in c1: c.start()
    both[:,mine,:]=w_ref[...]
    vboth[:,lanes]=v_ref[...]
    for c in c1: c.wait()
    blk[...]=both[...].astype(jnp.bfloat16)
    vblk[...]=vboth[...].astype(jnp.bfloat16)
    own=[pltpu.make_async_copy(blk,out_ref.at[:,rows(d,pair),:],loc.at[0]),
         pltpu.make_async_copy(vblk,vout_ref.at[d,pair],loc.at[1])]
    for c in own: c.start()
    above={"expert":2*lax.rem(pair+1,pairs)+core}; below={"expert":2*lax.rem(pair+pairs-1,pairs)+core}
    has_above=pair<pairs-1; has_below=pair>0
    def up(dd,q,src=None):
        here=out_ref.at[half,rows(dd,q),:]
        return remote(here if src is None else src,here,us.at[dd,q],ur.at[dd,q],above)
    def down(dd,q,src=None):
        here=out_ref.at[half,rows(dd,q),:]
        return remote(here if src is None else src,here,ls.at[dd,q],lr.at[dd,q],below)
    def hand(dd,q):
        here=out_ref.at[half,rows(dd,q),:]
        return remote(here,here,ps.at[dd,q],pr.at[dd,q],partner)
    def over_copy(dd,dev):
        here=out_ref.at[half,rows(d,pair),:]
        return remote(blk.at[half],here,ds_.at[dd],dr.at[d],dev)
    def over_in(dd,dev):
        here=out_ref.at[half,rows(dd,pair),:]
        return remote(here,here,ds_.at[dd],dr.at[dd],dev)
    def v_over(dd,dev): return remote(vblk,vout_ref.at[d,pair],vds.at[dd],vdr.at[d],dev)
    def v_along(q,dev): return remote(vout_ref.at[:,pair],vout_ref.at[:,pair],vzs.at[q],vzr.at[pair],dev)
    for dd,dev in over:
        over_copy(dd,dev).start()
        v_over(dd,dev).start()
    mine_out=blk.at[half]
    @pl.when(has_above)
    def _(): up(d,pair,mine_out).start()
    @pl.when(has_below)
    def _(): down(d,pair,mine_out).start()
    for dd,dev in over:
        over_in(dd,dev).wait_recv()
        @pl.when(has_above)
        def _(): up(dd,pair).start()
        @pl.when(has_below)
        def _(): down(dd,pair).start()
        hand(dd,pair).start()
    for dd,dev in over:
        remote(vblk,vout_ref.at[dd,pair],vds.at[dd],vdr.at[dd],dev).wait_recv()
    own[1].wait()
    for q,dev in along: v_along(q,dev).start()
    groups=[d]+[x[0] for x in over]
    for k in range(1,pairs):
        for dd in groups:
            @pl.when(pair>=k)
            def _():
                up(dd,pair-k).wait_recv()
                @pl.when(has_above)
                def _(): up(dd,pair-k).start()
                hand(dd,pair-k).start()
            @pl.when(pair+k<pairs)
            def _():
                down(dd,pair+k).wait_recv()
                @pl.when(has_below)
                def _(): down(dd,pair+k).start()
                hand(dd,pair+k).start()
    for q,dev in along:
        remote(vout_ref.at[:,q],vout_ref.at[:,q],vzs.at[q],vzr.at[q],dev).wait_recv()
    def from_partner(dd,q):
        there=out_ref.at[rest,rows(dd,q),:]
        remote(there,there,ps.at[dd,q],pr.at[dd,q],partner).wait_recv()
    for dd,dev in over: from_partner(dd,pair)
    for q,_ in along:
        for dd in groups: from_partner(dd,q)
    for dd,dev in over:
        over_copy(dd,dev).wait_send(); v_over(dd,dev).wait_send(); hand(dd,pair).wait_send()
    for q,dev in along:
        v_along(q,dev).wait_send()
        for dd in groups: hand(dd,q).wait_send()
    for dd in groups:
        for k in range(pairs):
            @pl.when((pair>=k)&has_above)
            def _(): up(dd,pair-k).wait_send()
            @pl.when((pair+k<pairs)&has_below)
            def _(): down(dd,pair+k).wait_send()
    own[0].wait()

def gather_dense(weights,vectors,dps,n,collective_id=2):
    pairs=n//2
    m,r,D=weights.shape
    V=jnp.zeros((16,128),jnp.float32).at[:vectors.shape[0],:r].set(vectors)
    dma=pltpu.SemaphoreType.DMA
    f32=jnp.float32; bf=jnp.bfloat16
    out,vout=pl.pallas_call(partial(gather_kernel,dps,pairs),
        out_shape=[jax.ShapeDtypeStruct((m,r*n*dps,D),bf),jax.ShapeDtypeStruct((dps,pairs,16,256),bf)],
        in_specs=[pl.BlockSpec(memory_space=pltpu.VMEM)]*2,
        out_specs=[pl.BlockSpec(memory_space=pl.ANY)]*2,
        scratch_shapes=[pltpu.VMEM((m,2*r,D),f32),pltpu.VMEM((m,2*r,D),bf),pltpu.VMEM((16,256),f32),pltpu.VMEM((16,256),bf),
            dma((2,)),dma((2,)),dma((2,)),dma((dps,pairs)),dma((dps,pairs)),dma((dps,pairs)),dma((dps,pairs)),dma((pairs,)),dma((pairs,)),
            dma((dps,)),dma((dps,)),dma((dps,)),dma((dps,)),dma((dps,pairs)),dma((dps,pairs))],
        compiler_params=pltpu.CompilerParams(vmem_limit_bytes=16*2**20,collective_id=collective_id,has_side_effects=True),
        cost_estimate=pl.CostEstimate(flops=0,bytes_accessed=100*2**20,transcendentals=0),
    )(weights,V)
    k=vectors.shape[0]
    vec=vout[:,:,:k].reshape(dps,pairs,k,2,128)[...,:r]
    vec=jnp.transpose(vec,(2,0,1,3,4)).reshape(k,r*n*dps)
    return out,vec

def tail_kernel(dps, pairs, cap, q_ref, k_ref, v_ref, lse_ref, g_ref, dcol_ref, drow_ref, gain_ref,
                x_ref, mixed_ref, ga_ref, prod_ref, w_ref, gh_ref, in_ref,
                out_ref, gain_out, returned_ref, dx_ref,
                bias_ref, dk_ref, dv_ref, left, right, got, own, total, in2, tb, in3, u, in4, w, gh, xin,
                ls, s1, r1, s2, r2, s3, r3, s4, r4, rs, rr, own_sem, dx_sem):
    h = pl.program_id(0)
    n = 2 * pairs
    me = lax.axis_index("expert")
    d, pair, core, partner, over, along = near(dps, pairs)
    rows = out_ref.shape[1]
    R = 2 * rows
    T, D = x_ref.shape
    loads = [
        pltpu.make_async_copy(x_ref, left.at[0], ls.at[0]),
        pltpu.make_async_copy(mixed_ref, left.at[1], ls.at[1]),
        pltpu.make_async_copy(ga_ref, right.at[3], ls.at[2]),
        pltpu.make_async_copy(w_ref.at[pl.ds(0, 3)], w, ls.at[3]),
        pltpu.make_async_copy(gh_ref, gh, ls.at[4]),
        pltpu.make_async_copy(in_ref, xin, ls.at[5]),
    ]

    def product(m):
        return lax.dot_general(left[m // 3], right[m], TN, preferred_element_type=jnp.float32)

    def ret_copy(peer):
        return remote(prod_ref.at[peer], returned_ref.at[me], rs.at[peer], rr.at[me], {"expert": peer})

    def ret_in(peer):
        return remote(prod_ref.at[peer], returned_ref.at[peer], rs.at[peer], rr.at[peer], {"expert": peer})

    own_ret = pltpu.make_async_copy(prod_ref.at[me], returned_ref.at[me], own_sem)

    def to_partner(i):
        return remote(total.at[i], got.at[i], s1.at[i], r1.at[i], partner)

    @pl.when(h == 0)
    def _():
        for c in loads:
            c.start()
        barrier = pltpu.get_barrier_semaphore()

        def greet(o, _):
            pl.semaphore_signal(barrier, inc=1, device_id={"expert": flip(me, o, n)}, device_id_type=MESH)
            return 0

        lax.fori_loop(1, n, greet, 0)
        for _, dev in over:
            pl.semaphore_signal(barrier, inc=1, device_id=dev, device_id_type=MESH)
        pl.semaphore_wait(barrier, n - 1 + dps - 1)

        def send(i, _):
            ret_copy(flip(me, n - 1 - i, n)).start()
            return 0

        lax.fori_loop(0, n - 1, send, 0)
        own_ret.start()
        transposed_bias(bias_ref, dcol_ref, drow_ref, QB)
        for c in loads[:3]:
            c.wait()
        out = product(3)

        @pl.when(core == 0)
        def _():
            total[1] = out.astype(jnp.bfloat16)
            to_partner(1).start()

        @pl.when(core == 1)
        def _():
            own[1] = out

    lanes = pl.ds(pl.multiple_of(h * 128, 128), 128)
    dq_at = lambda r, value: right.__setitem__((0, r, lanes), value)
    head_pair_backward(QB, q_ref, k_ref, v_ref, lse_ref, g_ref, bias_ref, dk_ref, dv_ref, dq_at)
    right[1, :, lanes] = dk_ref[...].astype(jnp.bfloat16)
    right[2, :, lanes] = dv_ref[...].astype(jnp.bfloat16)

    @pl.when(h == pl.num_programs(0) - 1)
    def _():
        @pl.when(core == 0)
        def _():
            total[0] = product(2).astype(jnp.bfloat16)
            to_partner(0).start()
            own[0] = product(0)
            own[1] = product(1)

        @pl.when(core == 1)
        def _():
            total[0] = product(0).astype(jnp.bfloat16)
            to_partner(0).start()
            total[1] = product(1).astype(jnp.bfloat16)
            to_partner(1).start()
            own[0] = product(2)

        for i in range(2):
            to_partner(i).wait_send()
            to_partner(i).wait_recv()
            total[i] = (own[i] + got[i].astype(jnp.float32)).astype(jnp.bfloat16)

        order = along + [(pair, None)]

        def piece(dd, q):
            return pl.ds(pl.multiple_of((dd * pairs + q) * R, 16), R)

        c2 = []
        for q, _ in order:
            for dd, dev in over:
                c = remote(total.at[:, piece(dd, q), :], in2.at[d, q], s2.at[dd, q], r2.at[d, q], dev)
                c.start()
                c2.append(c)
        for c in loads[3:]:
            c.wait()
        gain = gain_ref[...]
        gain_sum = jnp.zeros((8, D), jnp.float32)
        for b in range(T // 256):
            at = pl.ds(b * 256, 256)
            gn = sum(
                lax.dot_general(right[c, at, :], w[c], NT, preferred_element_type=jnp.float32)
                for c in range(3)
            )
            x = xin[at, :].astype(jnp.float32)
            center = x - jnp.mean(x, axis=-1, keepdims=True)
            scale = lax.rsqrt(jnp.mean(center * center, axis=-1, keepdims=True) + norm_eps)
            unit = center * scale
            gain_sum = gain_sum + jnp.sum((gn * unit).reshape(32, 8, D), axis=0)
            gu = gn * gain
            gx = scale * (
                gu
                - jnp.mean(gu, axis=-1, keepdims=True)
                - unit * jnp.mean(gu * unit, axis=-1, keepdims=True)
            )
            gh[at, :] = gh[at, :] + gx
        gain_out[...] = gain_sum
        dx = pltpu.make_async_copy(gh, dx_ref, dx_sem)
        dx.start()
        c3 = []
        for q, zdev in order:
            acc = total[:, piece(d, q), :].astype(jnp.float32)
            for dd, dev in over:
                remote(in2.at[dd, q], in2.at[dd, q], s2.at[dd, q], r2.at[dd, q], dev).wait_recv()
                acc = acc + in2[dd, q].astype(jnp.float32)
            if zdev is None:
                u[...] = acc
            else:
                tb[q] = acc.astype(jnp.bfloat16)
                c = remote(tb.at[q], in3.at[pair], s3.at[q], r3.at[pair], zdev)
                c.start()
                c3.append(c)
        acc = u[...]
        for q, dev in along:
            remote(in3.at[q], in3.at[q], s3.at[q], r3.at[q], dev).wait_recv()
            acc = acc + in3[q].astype(jnp.float32)
        u[...] = acc
        theirs = pl.ds(pl.multiple_of((1 - core) * rows, 8), rows)
        mine = pl.ds(pl.multiple_of(core * rows, 8), rows)
        c4 = remote(u.at[:, theirs, :], in4, s4, r4, partner)
        c4.start()
        out_ref[pl.ds(2 * core, 2)] = u[:, mine, :]
        c4.wait_recv()
        out_ref[pl.ds(2 - 2 * core, 2)] = in4[...]
        for c in c2 + c3 + [c4]:
            c.wait_send()

        def settle(o, _):
            peer = flip(me, o, n)
            ret_copy(peer).wait_send()
            ret_in(peer).wait_recv()
            return 0

        lax.fori_loop(1, n, settle, 0)
        own_ret.wait()
        dx.wait()


def tail(projected, lse, grad_mixed, documents, gain, normed, mixed, grad_attn, produced, dense_low,
         grad_hidden, inputs, dps, n):
    pairs = n // 2
    _, T, D = projected.shape
    rows = D // (dps * n)
    R = 2 * rows
    cap = produced.shape[1]
    f32, bf = jnp.float32, jnp.bfloat16
    dma = pltpu.SemaphoreType.DMA
    any_ = pl.BlockSpec(memory_space=pl.ANY)

    def sp(c):
        return pl.BlockSpec((1, T, 128), lambda h, c=c: (c, 0, h))

    fixed = lambda shape: pl.BlockSpec(shape, lambda h: (0,) * len(shape))
    return pl.pallas_call(
        partial(tail_kernel, dps, pairs, cap),
        grid=(D // 128,),
        out_shape=[
            jax.ShapeDtypeStruct((4, rows, D), f32),
            jax.ShapeDtypeStruct((8, D), f32),
            jax.ShapeDtypeStruct(produced.shape, bf),
            jax.ShapeDtypeStruct((T, D), f32),
        ],
        in_specs=[sp(0), sp(1), sp(2), pl.BlockSpec((1, T, 128), lambda h: (h, 0, 0)),
                  pl.BlockSpec((T, 128), lambda h: (0, h)), fixed((T, 1)), fixed((1, T)), fixed((1, D))]
        + [any_] * 7,
        out_specs=[fixed((4, rows, D)), fixed((8, D)), any_, any_],
        scratch_shapes=[
            pltpu.VMEM((min(T, WINDOW + QB), T), f32),
            pltpu.VMEM((T, 128), f32),
            pltpu.VMEM((T, 128), f32),
            pltpu.VMEM((2, T, D), bf),
            pltpu.VMEM((4, T, D), bf),
            pltpu.VMEM((2, D, D), bf),
            pltpu.VMEM((2, D, D), f32),
            pltpu.VMEM((2, D, D), bf),
            pltpu.VMEM((dps, pairs, 2, R, D), bf),
            pltpu.VMEM((pairs, 2, R, D), bf),
            pltpu.VMEM((pairs, 2, R, D), bf),
            pltpu.VMEM((2, R, D), f32),
            pltpu.VMEM((2, rows, D), f32),
            pltpu.VMEM((3, D, D), bf),
            pltpu.VMEM((T, D), f32),
            pltpu.VMEM((T, D), bf),
            dma((6,)), dma((2,)), dma((2,)), dma((dps, pairs)), dma((dps, pairs)), dma((pairs,)), dma((pairs,)),
            dma(()), dma(()), dma((n,)), dma((n,)), dma(()), dma(()),
        ],
        compiler_params=pltpu.CompilerParams(
            vmem_limit_bytes=56 * 2**20, collective_id=3, has_side_effects=True
        ),
        cost_estimate=pl.CostEstimate(flops=30 * T * D * D, bytes_accessed=100 * 2**20, transcendentals=0),
    )(projected, projected, projected, lse, grad_mixed, documents.reshape(T, 1), documents.reshape(1, T), gain,
      normed, mixed, grad_attn, produced, dense_low, grad_hidden, inputs)


def norm_kernel(dps, pairs, d_ref, v_ref, e_ref, out_ref, a, b, c, s1, r1, s2, r2, s3, r3):
    d, pair, core, partner, over, along = near(dps, pairs)
    greet_all([partner] + [x[1] for x in over] + [x[1] for x in along])

    def squares(ref):
        x = ref[...].astype(jnp.float32)
        return jnp.sum(x * x)

    part = squares(d_ref)
    for i in range(e_ref.shape[0]):
        part = part + squares(e_ref.at[i])
    last = lax.broadcasted_iota(jnp.int32, v_ref.shape, 0) == v_ref.shape[0] - 1
    a[core] = jnp.where(last, part, v_ref[...])
    cs = [remote(a.at[core], a.at[core], s1, r1.at[core], partner)]
    cs[0].start()
    remote(a.at[1 - core], a.at[1 - core], s1, r1.at[1 - core], partner).wait_recv()
    b[d] = a[0] + a[1]
    for dd, dev in over:
        x = remote(b.at[d], b.at[d], s2.at[dd], r2.at[d], dev)
        x.start()
        cs.append(x)
    for dd, dev in over:
        remote(b.at[dd], b.at[dd], s2.at[dd], r2.at[dd], dev).wait_recv()
    c[pair] = sum(b[k] for k in range(dps))
    for q, dev in along:
        x = remote(c.at[pair], c.at[pair], s3.at[q], r3.at[pair], dev)
        x.start()
        cs.append(x)
    for q, dev in along:
        remote(c.at[q], c.at[q], s3.at[q], r3.at[q], dev).wait_recv()
    out_ref[...] = sum(c[k] for k in range(pairs))
    for x in cs:
        x.wait_send()


def norm_squares(dense, vec, expert, dps, n):
    pairs = n // 2
    k, D = vec.shape
    R = (k // 8 + 1) * 8
    dma = pltpu.SemaphoreType.DMA
    vm = pl.BlockSpec(memory_space=pltpu.VMEM)
    out = pl.pallas_call(
        partial(norm_kernel, dps, pairs),
        out_shape=jax.ShapeDtypeStruct((R, D), jnp.float32),
        in_specs=[vm] * 3,
        out_specs=vm,
        scratch_shapes=[
            pltpu.VMEM((2, R, D), jnp.float32),
            pltpu.VMEM((dps, R, D), jnp.float32),
            pltpu.VMEM((pairs, R, D), jnp.float32),
            dma(()), dma((2,)), dma((dps,)), dma((dps,)), dma((pairs,)), dma((pairs,)),
        ],
        compiler_params=pltpu.CompilerParams(
            vmem_limit_bytes=24 * 2**20, collective_id=4, has_side_effects=True
        ),
    )(dense, jnp.pad(vec, ((0, R - k), (0, 0))), expert)
    total = out[:k]
    dev = lax.axis_index("dp") * n + lax.axis_index("expert")
    width = D // (dps * n)
    return lax.dynamic_slice_in_dim(total, dev * width, width, axis=1), out[R - 1, 0] + jnp.sum(total * total)


def adam_update(weight, gradient, first_moment, second_moment, average, factor, rate):
    clipped = gradient * factor
    first_new = beta_first * first_moment + (1.0 - beta_first) * clipped
    second_new = beta_second * second_moment + (1.0 - beta_second) * clipped * clipped
    first_hat = first_new / (1.0 - beta_first**STEP)
    second_hat = second_new / (1.0 - beta_second**STEP)
    updated = weight - rate * (
        first_hat / (jnp.sqrt(second_hat) + adam_eps) + weight_decay * weight
    )
    average_new = ema_keep * average + (1.0 - ema_keep) * updated
    return (updated, first_new, second_new, average_new)


def shards(
    inputs,
    cotangent,
    document_ids,
    domain_counts,
    domain_weight,
    token_order,
    expert_counts,
    dense_weights,
    vector_params,
    expert_weights,
    dense_first,
    dense_second,
    dense_average,
    vector_first,
    vector_second,
    vector_average,
    expert_first,
    expert_second,
    expert_average,
):
    tokens, model_width = inputs.shape
    experts_total = expert_counts.shape[1]
    capacity = 2 * tokens // experts_total
    owners = lax.axis_size("expert")
    groups = lax.axis_size(("dp", "expert"))
    sequences = tokens // LEN
    splits = lax.axis_size("dp")
    own_rows = dense_weights.shape[1]
    if own_rows % 8 == 0:
        dense_low, vector_low = gather_dense(dense_weights, vector_params, splits, owners)
    else:
        dense_low, vector_low = (
            lax.all_gather(dense_weights.astype(jnp.bfloat16), ("dp", "expert"), axis=1, tiled=True),
            lax.all_gather(vector_params.astype(jnp.bfloat16), ("dp", "expert"), axis=1, tiled=True),
        )
    me = lax.axis_index("expert")
    seq_index = lax.axis_index("dp") * owners + jnp.arange(owners)
    bounds = jnp.cumsum(domain_counts)
    domain = jnp.sum((seq_index[:, None] >= bounds[None, :]).astype(jnp.int32), axis=1)
    seq_pick = (domain[:, None] == jnp.arange(NDOM)[None, :]).astype(jnp.float32)
    seq_weight = jnp.sum(seq_pick * domain_weight[None, :], axis=1)
    seq_count = jnp.sum(seq_pick * domain_counts[None, :].astype(jnp.float32), axis=1)
    seq_scale = seq_weight * (sequences * groups) / (NDOM * seq_count)
    slot_scale = jnp.repeat(seq_scale, capacity)[:, None]
    token_scale = jnp.broadcast_to(seq_scale[me], (tokens,))
    row_counts = expert_counts[0]
    row_order = token_order[0]
    count_ends = jnp.cumsum(row_counts)
    count_starts = count_ends - row_counts
    sorted_pos = jnp.arange(tokens)
    sorted_expert = jnp.sum((sorted_pos[:, None] >= count_ends[None, :]).astype(jnp.int32), axis=1)
    sorted_pick = sorted_expert[:, None] == jnp.arange(experts_total)[None, :]
    sorted_start = jnp.sum(jnp.where(sorted_pick, count_starts[None, :], 0), axis=1)
    sorted_slot = sorted_expert * capacity + sorted_pos - sorted_start
    at_token = row_order[:, None] == jnp.arange(tokens)[None, :]
    token_slot = jnp.sum(jnp.where(at_token, sorted_slot[:, None], 0), axis=0)
    token_expert = token_slot // capacity
    expert_pick = (token_expert[:, None] == jnp.arange(experts_total)[None, :]).astype(jnp.float32)
    slot_match = token_slot[:, None] == jnp.arange(experts_total * capacity)[None, :]
    slot_pick = slot_match.astype(jnp.bfloat16)

    def to_slots(rows):
        placed = jnp.dot(slot_pick.T, rows, preferred_element_type=jnp.float32)
        return placed.astype(jnp.bfloat16).reshape(experts_total, capacity, model_width)

    def from_slots(rows):
        return jnp.dot(
            slot_pick, rows.reshape(-1, model_width), preferred_element_type=jnp.float32
        )

    later_cot, dense_low = lax.optimization_barrier((cotangent, dense_low))
    cot_received = lax.all_to_all(
        to_slots(later_cot), "expert", split_axis=0, concat_axis=0, tiled=True
    ).reshape(-1, model_width)
    own_low = expert_weights[0].astype(jnp.bfloat16)
    expert_low = lax.all_gather(own_low, "dp", axis=0)
    inputs_float = inputs.astype(jnp.float32)
    normed_one, norm_one_back = jax.vjp(layer_norm, inputs_float, vector_low[0].astype(jnp.float32))
    normed_low = normed_one.astype(jnp.bfloat16)
    projected = jnp.einsum(
        "td,cde->cte", normed_low, dense_low[:3], preferred_element_type=jnp.float32
    ).astype(jnp.bfloat16)
    documents = document_ids.reshape(-1)
    mixed_low, totals = attend_forward(projected, documents)
    hidden_state = inputs_float + jnp.dot(
        mixed_low, dense_low[3], preferred_element_type=jnp.float32
    )
    normed_two, norm_two_back = jax.vjp(layer_norm, hidden_state, vector_low[1].astype(jnp.float32))
    centroids = vector_low[2:].astype(jnp.float32)
    logits = jnp.dot(normed_two, centroids.T, precision=lax.Precision.HIGHEST)
    gate_value = jax.nn.sigmoid(jnp.sum(logits * expert_pick, axis=1))
    sent_rows = normed_two.astype(jnp.bfloat16)
    send_rows = to_slots(sent_rows)
    per = TILE // capacity
    gate_slots = jnp.sum(
        jnp.where(slot_match, gate_value[:, None], 0.0), axis=0
    ).reshape(experts_total, 1, 1, capacity)
    lane_part = (jnp.arange(per) == me % per).astype(jnp.float32)
    gate_tiles = jnp.broadcast_to(
        gate_slots * lane_part[None, None, :, None], (experts_total, 8, per, capacity)
    ).reshape(experts_total, 8, TILE)
    back_rows, late_rows, chosen_tiles, produced_low, grad_expert = moe(
        send_rows, gate_tiles, cot_received, slot_scale, expert_low
    )
    expert_low_grad = lax.psum_scatter(grad_expert, "dp", scatter_dimension=0)
    expert_grad = expert_low_grad.astype(jnp.float32)[None]
    grad_out = cotangent.astype(jnp.float32) * token_scale[:, None]
    back_slot = (token_slot // capacity ^ me) * capacity + token_slot % capacity
    back_match = back_slot[:, None] == jnp.arange(experts_total * capacity)[None, :]
    back_pick = back_match.astype(jnp.bfloat16)
    early = back_rows.shape[0] * capacity
    grad_sent_rows = jnp.dot(
        back_pick[:, :early], back_rows.reshape(-1, model_width), preferred_element_type=jnp.float32
    ) + jnp.dot(
        back_pick[:, early:], late_rows.reshape(-1, model_width), preferred_element_type=jnp.float32
    )
    chosen_slots = lax.dynamic_slice_in_dim(
        chosen_tiles[:, 0, :], me % per * capacity, capacity, axis=1
    )
    grad_chosen = jnp.sum(jnp.where(back_match, chosen_slots.reshape(1, -1), 0.0), axis=1)
    chosen_grad = grad_chosen[:, None] * expert_pick
    grad_normed_two = grad_sent_rows + jnp.dot(
        chosen_grad, centroids, precision=lax.Precision.HIGHEST
    )
    grad_centroids = jnp.dot(chosen_grad.T, normed_two, precision=lax.Precision.HIGHEST)
    grad_hidden_norm, grad_gain_two = norm_two_back(grad_normed_two)
    grad_hidden = grad_out + grad_hidden_norm
    grad_attn = grad_hidden.astype(jnp.bfloat16)
    grad_mixed = jnp.dot(grad_attn, dense_low[3].T, preferred_element_type=jnp.float32).astype(
        jnp.bfloat16
    )
    if own_rows % 8 == 0:
        dense_grad, gain_tiles, returned, input_grad = tail(
            projected, totals, grad_mixed, documents, vector_low[0:1].astype(jnp.float32), normed_low,
            mixed_low, grad_attn, produced_low, dense_low, grad_hidden, inputs, splits, owners
        )
        grad_gain_one = jnp.sum(gain_tiles, axis=0)
    else:
        returned = lax.all_to_all(produced_low, "expert", split_axis=0, concat_axis=0, tiled=True)
        grad_proj = attend_backward(projected, documents, totals, grad_mixed)
        grad_normed_one = jnp.einsum(
            "cte,cde->td", grad_proj, dense_low[:3], preferred_element_type=jnp.float32
        )
        grad_input_norm, grad_gain_one = norm_one_back(grad_normed_one)
        input_grad = grad_hidden + grad_input_norm
        grad_in_proj = jnp.einsum(
            "td,cte->cde", normed_low, grad_proj, preferred_element_type=jnp.float32
        )
        grad_out_proj = jnp.dot(mixed_low.T, grad_attn, preferred_element_type=jnp.float32)
        dense_grad = lax.psum_scatter(
            jnp.concatenate([grad_in_proj, grad_out_proj[None]], axis=0),
            ("dp", "expert"),
            scatter_dimension=1,
            tiled=True,
        )
    returned_rows = from_slots(returned)
    block_output = hidden_state + gate_value[:, None] * returned_rows
    vector_grad = jnp.concatenate(
        [grad_gain_one[None], grad_gain_two[None], grad_centroids], axis=0
    )
    vector_grad, squares = norm_squares(dense_grad, vector_grad, expert_low_grad, splits, owners)
    grad_norm = jnp.sqrt(squares)
    factor = jnp.minimum(1.0, clip_norm / (grad_norm + 1e-06))
    dense_new = adam_update(
        dense_weights, dense_grad, dense_first, dense_second, dense_average, factor, dense_rate
    )
    vector_new = adam_update(
        vector_params, vector_grad, vector_first, vector_second, vector_average, factor, vector_rate
    )
    expert_new = adam_update(
        expert_weights,
        expert_grad,
        expert_first,
        expert_second,
        expert_average,
        factor,
        expert_rate,
    )
    return (
        block_output,
        input_grad,
        dense_new[0],
        dense_new[1],
        dense_new[2],
        dense_new[3],
        vector_new[0],
        vector_new[1],
        vector_new[2],
        vector_new[3],
        expert_new[0],
        expert_new[1],
        expert_new[2],
        expert_new[3],
        grad_norm,
    )


def solution(mesh):
    placed = (
        P(("dp", "expert"), None),
        P(("dp", "expert"), None),
        P(("dp", "expert"), None),
        P(),
        P(),
        P(("dp", "expert"), None),
        P(("dp", "expert"), None),
        P(None, ("dp", "expert"), None),
        P(None, ("dp", "expert")),
        P("expert", None, None, "dp"),
        P(None, ("dp", "expert"), None),
        P(None, ("dp", "expert"), None),
        P(None, ("dp", "expert"), None),
        P(None, ("dp", "expert")),
        P(None, ("dp", "expert")),
        P(None, ("dp", "expert")),
        P("expert", None, None, "dp"),
        P("expert", None, None, "dp"),
        P("expert", None, None, "dp"),
    )
    return jax.shard_map(
        shards,
        mesh=mesh,
        in_specs=placed,
        out_specs=(
            P(("dp", "expert"), None),
            P(("dp", "expert"), None),
            P(None, ("dp", "expert"), None),
            P(None, ("dp", "expert"), None),
            P(None, ("dp", "expert"), None),
            P(None, ("dp", "expert"), None),
            P(None, ("dp", "expert")),
            P(None, ("dp", "expert")),
            P(None, ("dp", "expert")),
            P(None, ("dp", "expert")),
            P("expert", None, None, "dp"),
            P("expert", None, None, "dp"),
            P("expert", None, None, "dp"),
            P("expert", None, None, "dp"),
            P(),
        ),
        check_vma=False,
    )
```

```python
from functools import partial

import jax
import jax.numpy as jnp
from jax import lax
from jax.experimental import pallas as pl
from jax.experimental.pallas import tpu as pltpu
from jax.sharding import PartitionSpec as P

HEADS = 12
HEAD_DIM = 64
LEN = 1024
WINDOW = 512
NDOM = 8
STEP = 10


norm_eps = 1e-05
masked_score = -1e30
beta_first = 0.9
beta_second = 0.999
adam_eps = 1e-08
dense_rate = 0.1
vector_rate = 0.5
expert_rate = 0.02
weight_decay = 0.1
ema_keep = 0.9
clip_norm = 1.0


def layer_norm(values_in, gain_row):
    center = values_in - jnp.mean(values_in, axis=-1, keepdims=True)
    spread = jnp.mean(center * center, axis=-1, keepdims=True)
    return center * lax.rsqrt(spread + norm_eps) * gain_row


NT = (((1,), (1,)), ((), ()))
TN = (((0,), (0,)), ((), ()))


def fwd_kernel(QB, q_ref,k_ref,v_ref,dcol_ref,drow_ref,o_ref,lse_ref,bias_ref):
    reach = WINDOW//QB
    low_lane = lax.broadcasted_iota(jnp.int32,(QB,128),1) < HEAD_DIM
    @pl.when(pl.program_id(0)==0)
    def _():
        for i in range(LEN//QB):
            first=max(0,i-reach)*QB; W=(i+1)*QB-first
            qp=i*QB+lax.broadcasted_iota(jnp.int32,(QB,W),0)
            kp=first+lax.broadcasted_iota(jnp.int32,(QB,W),1)
            ok=(kp<=qp)&(dcol_ref[i*QB:(i+1)*QB,:]==drow_ref[:,first:first+W])
            bias_ref[i*QB:(i+1)*QB,:W]=jnp.where(ok,0.0,masked_score)
    for i in range(LEN//QB):
        rows=slice(i*QB,(i+1)*QB)
        first=max(0,i-reach)*QB; W=(i+1)*QB-first
        q=q_ref[0,rows,:]*jnp.bfloat16(HEAD_DIM**-0.5)
        zero=jnp.zeros_like(q)
        qs=jnp.concatenate([jnp.where(low_lane,q,zero),jnp.where(low_lane,zero,q)],axis=0)
        s=lax.dot_general(qs,k_ref[0,first:first+W,:],NT,preferred_element_type=jnp.float32)
        s=(s.reshape(2,QB,W)+bias_ref[rows,:W][None]).reshape(2*QB,W)
        top=jnp.max(s,axis=1,keepdims=True)
        e=jnp.exp(s-top)
        total=jnp.sum(e,axis=1,keepdims=True)
        p=(e*(1.0/total)).astype(jnp.bfloat16)
        o=jnp.dot(p,v_ref[0,first:first+W,:],preferred_element_type=jnp.float32)
        o_ref[rows,:]=jnp.where(low_lane,o[:QB],o[QB:]).astype(jnp.bfloat16)
        lse=top+jnp.log(total)
        lse_ref[0,rows,:]=jnp.where(low_lane,lse[:QB],lse[QB:])

def attend_forward(projected, documents, QB=256):
    T=projected.shape[1]; D=projected.shape[2]
    dcol=documents.reshape(T,1); drow=documents.reshape(1,T)
    def sp(c): return pl.BlockSpec((1,T,128),lambda h,c=c:(c,0,h))
    return pl.pallas_call(partial(fwd_kernel,QB),grid=(D//128,),
        in_specs=[sp(0),sp(1),sp(2),pl.BlockSpec((T,1),lambda h:(0,0)),pl.BlockSpec((1,T),lambda h:(0,0))],
        out_specs=[pl.BlockSpec((T,128),lambda h:(0,h)),pl.BlockSpec((1,T,128),lambda h:(h,0,0))],
        out_shape=[jax.ShapeDtypeStruct((T,D),jnp.bfloat16),jax.ShapeDtypeStruct((D//128,T,128),jnp.float32)],
        scratch_shapes=[pltpu.VMEM((T,min(T,WINDOW+QB)),jnp.float32)],
        compiler_params=pltpu.CompilerParams(vmem_limit_bytes=48*2**20),
    )(projected,projected,projected,dcol,drow)

QB = 256


def transposed_bias(bias_ref, dcol_ref, drow_ref, QB):
    reach = WINDOW // QB
    for i in range(LEN // QB):
        first = max(0, i - reach) * QB
        W = (i + 1) * QB - first
        kp = first + lax.broadcasted_iota(jnp.int32, (W, QB), 0)
        qp = i * QB + lax.broadcasted_iota(jnp.int32, (W, QB), 1)
        ok = (kp <= qp) & (dcol_ref[first : first + W, :] == drow_ref[:, i * QB : (i + 1) * QB])
        bias_ref[:W, i * QB : (i + 1) * QB] = jnp.where(ok, 0.0, masked_score)


def head_pair_backward(QB, q_ref, k_ref, v_ref, lse_ref, g_ref, bias_ref, dk_ref, dv_ref, put_dq):
    reach = WINDOW // QB
    low_lane = lax.broadcasted_iota(jnp.int32, (QB, 128), 1) < HEAD_DIM
    dk_ref[...] = jnp.zeros_like(dk_ref)
    dv_ref[...] = jnp.zeros_like(dv_ref)
    for i in range(LEN // QB):
        rows = slice(i * QB, (i + 1) * QB)
        first = max(0, i - reach) * QB
        W = (i + 1) * QB - first
        keys = slice(first, first + W)
        q = q_ref[0, rows, :] * jnp.bfloat16(HEAD_DIM**-0.5)
        zero = jnp.zeros_like(q)
        qs = jnp.concatenate([jnp.where(low_lane, q, zero), jnp.where(low_lane, zero, q)], axis=0)
        g = g_ref[rows, :]
        gs = jnp.concatenate([jnp.where(low_lane, g, zero), jnp.where(low_lane, zero, g)], axis=0)
        k = k_ref[0, keys, :]
        st = lax.dot_general(k, qs, NT, preferred_element_type=jnp.float32)
        bias = bias_ref[:W, rows]
        lse = jnp.transpose(lse_ref[0, rows, :])
        lse = jnp.concatenate([lse[0:1, :], lse[64:65, :]], axis=1)
        p = jnp.exp(st + jnp.concatenate([bias, bias], axis=1) - lse)
        dp = lax.dot_general(v_ref[0, keys, :], gs, NT, preferred_element_type=jnp.float32)
        inner = jnp.sum(p * dp, axis=0, keepdims=True)
        ds = (p * (dp - inner)).astype(jnp.bfloat16)
        dk_ref[keys, :] += jnp.dot(ds, qs, preferred_element_type=jnp.float32)
        dv_ref[keys, :] += jnp.dot(p.astype(jnp.bfloat16), gs, preferred_element_type=jnp.float32)
        dq = lax.dot_general(ds, k, TN, preferred_element_type=jnp.float32)
        put_dq(rows, (jnp.where(low_lane, dq[:QB], dq[QB:]) * HEAD_DIM**-0.5).astype(jnp.bfloat16))


def bwd_kernel(QB, q_ref, k_ref, v_ref, lse_ref, g_ref, dcol_ref, drow_ref, out_ref, bias_ref, dk_ref, dv_ref):
    @pl.when(pl.program_id(0) == 0)
    def _():
        transposed_bias(bias_ref, dcol_ref, drow_ref, QB)

    def put_dq(rows, value):
        out_ref[0, rows, :] = value

    head_pair_backward(QB, q_ref, k_ref, v_ref, lse_ref, g_ref, bias_ref, dk_ref, dv_ref, put_dq)
    out_ref[1, :, :] = dk_ref[...].astype(jnp.bfloat16)
    out_ref[2, :, :] = dv_ref[...].astype(jnp.bfloat16)


def attend_backward(projected, documents, lse, grad_mixed, QB=256):
    T=projected.shape[1]; D=projected.shape[2]
    dcol=documents.reshape(T,1); drow=documents.reshape(1,T)
    def sp(c): return pl.BlockSpec((1,T,128),lambda h,c=c:(c,0,h))
    return pl.pallas_call(partial(bwd_kernel,QB),grid=(D//128,),
        in_specs=[sp(0),sp(1),sp(2),pl.BlockSpec((1,T,128),lambda h:(h,0,0)),pl.BlockSpec((T,128),lambda h:(0,h)),pl.BlockSpec((T,1),lambda h:(0,0)),pl.BlockSpec((1,T),lambda h:(0,0))],
        out_specs=pl.BlockSpec((3,T,128),lambda h:(0,0,h)),
        out_shape=jax.ShapeDtypeStruct((3,T,D),jnp.bfloat16),
        scratch_shapes=[pltpu.VMEM((min(T,WINDOW+QB),T),jnp.float32),pltpu.VMEM((T,128),jnp.float32),pltpu.VMEM((T,128),jnp.float32)],
        compiler_params=pltpu.CompilerParams(vmem_limit_bytes=48*2**20),
    )(projected,projected,projected,lse,grad_mixed,dcol,drow)


MESH=pl.DeviceIdType.MESH
TILE=512

def flip(a,b,n):
    out=0
    bit=1
    while bit<n:
        out=out+bit*((a//bit+b//bit)%2)
        bit*=2
    return out

def gelu_pair(x):
    c=0.7978845608028654
    sq=x*x
    t=jnp.tanh(c*(x+0.044715*(x*sq)))
    half=0.5*(1.0+t)
    return x*half, half+x*(0.5*(1.0-t*t))*(c+(3*0.044715*c)*sq)

def moe_kernel(n,cap,square,send_ref,gate_ref,cot_ref,scale_ref,w_ref,
               back_ref,late_ref,chosen_ref,ret_ref,gw_ref,
               recv,gates,cot,w,gw,ret_s,gs_s,ch_s,g_s,racc,sacc,
               send_sem,recv_sem,gate_send,gate_recv,back_send,back_recv,ch_send,ch_recv,on_send,on_recv,w_sem,loc_sem,ret_sem):
    per=TILE//cap
    tiles=n//per
    chunks=w_ref.shape[0]
    me=lax.axis_index("expert")
    barrier=pltpu.get_barrier_semaphore()
    def greet(o,_):
        pl.semaphore_signal(barrier,inc=1,device_id={"expert":flip(me,o,n)},device_id_type=MESH)
        return 0
    lax.fori_loop(1,n,greet,0)
    d=lax.axis_index("dp")
    sides=[flip(d,1,chunks),flip(d,2,chunks)] if square else []
    for side in sides:
        pl.semaphore_signal(barrier,inc=1,device_id={"dp":side},device_id_type=MESH)
    pl.semaphore_wait(barrier,n-1+len(sides))
    def on_copy(k):
        return pltpu.make_async_remote_copy(src_ref=w_ref.at[sides[k],k],dst_ref=w.at[sides[k],k],
            send_sem=on_send.at[k],recv_sem=on_recv.at[k],device_id={"dp":sides[1-k]},device_id_type=MESH)
    def on_in(k):
        across=flip(d,3,chunks)
        return pltpu.make_async_remote_copy(src_ref=w_ref.at[sides[k],k],dst_ref=w.at[across,k],
            send_sem=on_send.at[k],recv_sem=on_recv.at[k],device_id={"dp":sides[1-k]},device_id_type=MESH)
    for k in range(len(sides)): on_copy(k).start()

    def copies(src,dst,send,recv_,peer,there):
        return pltpu.make_async_remote_copy(src_ref=src,dst_ref=dst,send_sem=send.at[peer],recv_sem=recv_.at[there],
            device_id={"expert":peer},device_id_type=MESH)
    def row_copy(peer): return copies(send_ref.at[peer],recv.at[me],send_sem,recv_sem,peer,me)
    def gate_copy(peer): return copies(gate_ref.at[peer],gates.at[me],gate_send,gate_recv,peer,me)
    def row_in(src): return copies(send_ref.at[src],recv.at[src],send_sem,recv_sem,src,src)
    def gate_in(src): return copies(gate_ref.at[src],gates.at[src],gate_send,gate_recv,src,src)
    def back_copy(src): return copies(gs_s.at[src],back_ref.at[flip(src,me,n)],back_send,back_recv,src,me)
    def ch_copy(src): return copies(ch_s.at[src],chosen_ref.at[flip(src,me,n)],ch_send,ch_recv,src,me)
    def back_in(src): return copies(gs_s.at[src],back_ref.at[flip(src,me,n)],back_send,back_recv,src,src)
    def ch_in(src): return copies(ch_s.at[src],chosen_ref.at[flip(src,me,n)],ch_send,ch_recv,src,src)

    def push(o,_):
        gate_copy(flip(me,o,n)).start()
        row_copy(flip(me,o,n)).start()
        return 0
    last=(tiles-1)*per
    lax.fori_loop(0,last-1,lambda i,c: push(last-1-i,c),0)
    own=[pltpu.make_async_copy(send_ref.at[me],recv.at[me],loc_sem.at[0]),
         pltpu.make_async_copy(gate_ref.at[me],gates.at[me],loc_sem.at[1]),
         pltpu.make_async_copy(cot_ref,cot,loc_sem.at[2]),
        ]+[pltpu.make_async_copy(w_ref.at[c],w.at[c],w_sem.at[i]) for i,c in enumerate(([d]+sides) if square else range(chunks))]
    for c in own: c.start()
    def wipe(c,_):
        gw[c]=jnp.zeros(gw.shape[1:],jnp.float32)
        return 0
    lax.fori_loop(0,chunks,wipe,0)
    for c in own: c.wait()
    own_back=pltpu.make_async_copy(gs_s.at[me],back_ref.at[0],loc_sem.at[1])
    own_ch=pltpu.make_async_copy(ch_s.at[me],chosen_ref.at[0],loc_sem.at[0])

    def tile(t,_):
        @pl.when(t==1)
        def _():
            lax.fori_loop(last,n,push,0)
        block=flip(me//per,t,tiles)
        def arrive(j,_):
            src=block*per+j
            @pl.when(src!=me)
            def _():
                gate_in(src).wait_recv()
                row_in(src).wait_recv()
            return 0
        lax.fori_loop(0,per,arrive,0)
        at=pl.ds(pl.multiple_of(block*per,per),per)
        rows=pl.ds(pl.multiple_of(block*TILE,TILE),TILE)
        gate=jnp.transpose(jnp.sum(gates[at],axis=0))[:,0:1]
        scale=jnp.concatenate([jnp.broadcast_to(scale_ref[pl.ds(block*per+j,1),0:1],(cap,1)) for j in range(per)],axis=0)
        grad_out=cot[rows,:].astype(jnp.float32)*scale
        g_s[...]=(gate*grad_out).astype(jnp.bfloat16)
        racc[...]=jnp.zeros_like(racc)
        sacc[...]=jnp.zeros_like(sacc)
        def chunk(i,_):
            c=flip(d,i,chunks)
            if square:
                @pl.when((t==0)&(i==chunks-1))
                def _():
                    for k in range(2): on_in(k).wait_recv()
            x=recv[at].reshape(TILE,recv.shape[2])
            g=g_s[...]
            act,slope=gelu_pair(jnp.dot(x,w[c,0],preferred_element_type=jnp.float32))
            a=act.astype(jnp.bfloat16)
            ga=jnp.dot(g,w[c,1],preferred_element_type=jnp.float32).astype(jnp.bfloat16)
            gp=(ga.astype(jnp.float32)*slope).astype(jnp.bfloat16)
            racc[...]+=lax.dot_general(a,w[c,1],NT,preferred_element_type=jnp.float32)
            sacc[...]+=lax.dot_general(gp,w[c,0],NT,preferred_element_type=jnp.float32)
            gw[c,0]+=lax.dot_general(x,gp,TN,preferred_element_type=jnp.float32)
            gw[c,1]+=lax.dot_general(g,a,TN,preferred_element_type=jnp.float32)
            return 0
        lax.fori_loop(0,chunks,chunk,0)
        gs_s[at]=sacc[...].astype(jnp.bfloat16).reshape(per,cap,recv.shape[2])
        def give(j,_):
            src=block*per+j
            @pl.when(src!=me)
            def _():
                back_copy(src).start()
            @pl.when(src==me)
            def _():
                own_back.start()
            return 0
        @pl.when(t<tiles-1)
        def _():
            lax.fori_loop(0,per,give,0)
        @pl.when(t==tiles-1)
        def _():
            pltpu.make_async_copy(gs_s.at[at],late_ref,loc_sem.at[2]).start()
        ret=racc[...].astype(jnp.bfloat16)
        ret_s[at]=ret.reshape(per,cap,recv.shape[2])
        pltpu.make_async_copy(ret_s.at[at],ret_ref.at[at],ret_sem.at[t]).start()
        grad_out=cot[rows,:].astype(jnp.float32)*scale
        chosen=jnp.sum(grad_out*ret.astype(jnp.float32),axis=1,keepdims=True)*gate*(1.0-gate)
        chosen=jnp.transpose(jnp.broadcast_to(chosen,(TILE,128)))[0:8,:]
        def tell(j,_):
            src=block*per+j
            ch_s[src]=chosen
            @pl.when(src!=me)
            def _():
                ch_copy(src).start()
            @pl.when(src==me)
            def _():
                own_ch.start()
            return 0
        lax.fori_loop(0,per,tell,0)
        return 0
    lax.fori_loop(0,tiles,tile,0)
    def pack(c,_):
        w[c]=gw[c].astype(jnp.bfloat16)
        pltpu.make_async_copy(w.at[c],gw_ref.at[c],w_sem.at[c]).start()
        return 0
    lax.fori_loop(0,chunks,pack,0)
    own_ch.wait()
    own_back.wait()
    block=flip(me//per,tiles-1,tiles)
    at=pl.ds(pl.multiple_of(block*per,per),per)
    pltpu.make_async_copy(gs_s.at[at],late_ref,loc_sem.at[2]).wait()
    def settle(o,_):
        peer=flip(me,o,n)
        gate_copy(peer).wait_send()
        row_copy(peer).wait_send()
        ch_copy(peer).wait_send()
        ch_in(peer).wait_recv()
        @pl.when(o<last)
        def _():
            back_copy(peer).wait_send()
            back_in(peer).wait_recv()
        return 0
    lax.fori_loop(1,n,settle,0)
    def stored(t,_):
        block=flip(me//per,t,tiles)
        at=pl.ds(pl.multiple_of(block*per,per),per)
        pltpu.make_async_copy(ret_s.at[at],ret_ref.at[at],ret_sem.at[t]).wait()
        return 0
    lax.fori_loop(0,tiles,stored,0)
    for c in range(chunks): pltpu.make_async_copy(w.at[c],gw_ref.at[c],w_sem.at[c]).wait()
    for k in range(len(sides)): on_copy(k).wait_send()

def late_kernel(n,gs_ref,out_ref,send_sem,recv_sem):
    per=gs_ref.shape[0]
    tiles=n//per
    me=lax.axis_index("expert")
    block=flip(me//per,tiles-1,tiles)
    barrier=pltpu.get_barrier_semaphore()
    def greet(j,_):
        pl.semaphore_signal(barrier,inc=1,device_id={"expert":block*per+j},device_id_type=MESH)
        return 0
    lax.fori_loop(0,per,greet,0)
    pl.semaphore_wait(barrier,per)
    def copy(j):
        k=flip(j,me%per,per)
        return pltpu.make_async_remote_copy(src_ref=gs_ref.at[j],dst_ref=out_ref.at[k],send_sem=send_sem.at[k],recv_sem=recv_sem.at[k],
            device_id={"expert":block*per+j},device_id_type=MESH)
    def go(j,_):
        copy(j).start()
        return 0
    lax.fori_loop(0,per,go,0)
    def end(j,_):
        copy(j).wait()
        return 0
    lax.fori_loop(0,per,end,0)

def moe(send_rows,gate_slots,cot,scale,weights,square):
    n,cap,D=send_rows.shape
    chunks,_,_,FC=weights.shape
    per=TILE//cap
    any_=pl.BlockSpec(memory_space=pl.ANY)
    bf=jnp.bfloat16; f32=jnp.float32
    dma=pltpu.SemaphoreType.DMA
    flops=6*2*n*cap*D*chunks*FC
    back,late,chosen,ret,gw=pl.pallas_call(partial(moe_kernel,n,cap,square),
        out_shape=[jax.ShapeDtypeStruct((n-per,cap,D),bf),jax.ShapeDtypeStruct((per,cap,D),bf),jax.ShapeDtypeStruct((n,8,TILE),f32),
                   jax.ShapeDtypeStruct((n,cap,D),bf),jax.ShapeDtypeStruct(weights.shape,bf)],
        in_specs=[any_,any_,any_,pl.BlockSpec(memory_space=pltpu.VMEM),any_],
        out_specs=[any_]*5,
        scratch_shapes=[pltpu.VMEM((n,cap,D),bf),pltpu.VMEM((n,8,TILE),f32),pltpu.VMEM((n*cap,D),bf),
            pltpu.VMEM(weights.shape,bf),pltpu.VMEM(weights.shape,f32),pltpu.VMEM((n,cap,D),bf),pltpu.VMEM((n,cap,D),bf),
            pltpu.VMEM((n,8,TILE),f32),pltpu.VMEM((TILE,D),bf),pltpu.VMEM((TILE,D),f32),pltpu.VMEM((TILE,D),f32)]
            +[dma((n,))]*8+[dma((2,)),dma((2,)),dma((chunks,)),dma((3,)),dma((n//per,))],
        compiler_params=pltpu.CompilerParams(vmem_limit_bytes=62*2**20,collective_id=1,has_side_effects=True),
        cost_estimate=pl.CostEstimate(flops=flops,bytes_accessed=40*2**20,transcendentals=0),
    )(send_rows,gate_slots,cot,scale,weights)
    return back,late,chosen,ret,gw

def send_late(late,n):
    per,cap,D=late.shape
    any_=pl.BlockSpec(memory_space=pl.ANY)
    bf=jnp.bfloat16
    dma=pltpu.SemaphoreType.DMA
    return pl.pallas_call(partial(late_kernel,n),
        out_shape=jax.ShapeDtypeStruct((per,cap,D),bf),in_specs=[any_],out_specs=any_,
        scratch_shapes=[dma((per,)),dma((per,))],
        compiler_params=pltpu.CompilerParams(collective_id=5,has_side_effects=True),
        cost_estimate=pl.CostEstimate(flops=0,bytes_accessed=100*2**20,transcendentals=0),
    )(late)


def near(dps,pairs):
    d=lax.axis_index("dp"); me=lax.axis_index("expert")
    core=me%2; pair=me//2
    partner={"expert":me+1-2*core}
    over=[((d+k)%dps,{"dp":(d+k)%dps}) for k in range(1,dps)]
    along=[((pair+k)%pairs,{"expert":2*((pair+k)%pairs)+core}) for k in range(1,pairs)]
    return d,pair,core,partner,over,along

def greet_all(devices):
    barrier=pltpu.get_barrier_semaphore()
    for dev in devices:
        pl.semaphore_signal(barrier,inc=1,device_id=dev,device_id_type=MESH)
    pl.semaphore_wait(barrier,len(devices))

def remote(src,dst,send,recv,dev):
    return pltpu.make_async_remote_copy(src_ref=src,dst_ref=dst,send_sem=send,recv_sem=recv,device_id=dev,device_id_type=MESH)

def upright(row):
    return jnp.transpose(row.astype(jnp.float32))[:, 0:1].astype(jnp.int32)


def head_kernel(dps, pairs, n, cap, w_ref, v_ref, x_ref, cot_ref, order_ref, counts_ref, drow_ref, ew_ref,
                w_out, vec_out, slot_out, cot_out, proj_out, normed_out, mixed_out, lse_out, hidden_out,
                gate_out, send_out, tile_out, ew_out,
                ew32, ew, both, blk, vboth, vblk, w, vall, slots, unit, normed, proj, mixed, lse, bias, sent, cots, sends,
                tiles, s1, r1, loc, zs, zr, vzs, vzr, ds_, dr, vds, vdr, ps, pr, cs, cr, ewl, xs, xr, ys, yr, out_sem, send_sem):
    r = w_ref.shape[1]
    R = 2 * r
    T, D = x_ref.shape
    d, pair, core, partner, over, along = near(dps, pairs)
    me = lax.axis_index("expert")
    bf, f32 = jnp.bfloat16, jnp.float32
    ew_load = pltpu.make_async_copy(ew_ref.at[0], ew32, ewl.at[0])
    ew_load.start()
    barrier = pltpu.get_barrier_semaphore()

    def greet(o, _):
        pl.semaphore_signal(barrier, inc=1, device_id={"expert": flip(me, o, n)}, device_id_type=MESH)
        return 0

    lax.fori_loop(1, n, greet, 0)
    for _, dev in over:
        pl.semaphore_signal(barrier, inc=1, device_id=dev, device_id_type=MESH)
    pl.semaphore_wait(barrier, n - 1 + dps - 1)

    side_x, side_y = flip(d, 1, dps), flip(d, 2, dps)
    to_x, to_y = {"dp": side_x}, {"dp": side_y}

    def x_copy(src, slot, m):
        return remote(src, ew_out.at[slot, m], xs.at[slot, m], xr.at[slot, m], to_x)

    def y_copy(src, slot, m):
        return remote(src, ew_out.at[slot, m], ys.at[slot, m], yr.at[slot, m], to_y)

    mine = pl.ds(pl.multiple_of(core * r, 8), r)
    half = pl.ds(core * 2, 2)
    rest = pl.ds(2 - core * 2, 2)

    def rows(dd, q):
        return pl.ds(pl.multiple_of((dd * pairs + q) * R, 16), R)

    c1 = [
        remote(w_ref, both.at[:, mine, :], s1.at[0], r1.at[0], partner),
        remote(v_ref, vboth.at[core], s1.at[1], r1.at[1], partner),
    ]
    for c in c1:
        c.start()
    both[:, mine, :] = w_ref[...]
    vboth[core] = v_ref[...]
    for c in c1:
        c.wait()
    blk[...] = both[...].astype(bf)
    vblk[...] = (vboth[0] + vboth[1]).astype(bf)
    w[:, rows(d, pair), :] = blk[...]
    vall[d, pair] = vblk[...]
    def along_copy(q, dev):
        return remote(blk.at[half], w.at[half, rows(d, pair), :], zs.at[q], zr.at[pair], dev)

    def over_copy(dd, q, dev):
        here = w.at[half, rows(d, q), :]
        return remote(here, here, ds_.at[dd, q], dr.at[d, q], dev)

    def hand(dd, q):
        here = w.at[half, rows(dd, q), :]
        return remote(here, here, ps.at[dd, q], pr.at[dd, q], partner)

    def v_along(q, dev):
        return remote(vblk, vall.at[d, pair], vzs.at[q], vzr.at[pair], dev)

    def v_over(dd, dev):
        return remote(vall.at[d], vall.at[d], vds.at[dd], vdr.at[d], dev)

    for q, dev in along:
        along_copy(q, dev).start()
        v_along(q, dev).start()
    for dd, dev in over:
        over_copy(dd, pair, dev).start()

    tokens_across = lax.broadcasted_iota(jnp.int32, (T, T), 1)
    position = lax.broadcasted_iota(jnp.int32, (8, T), 1)
    sorted_slot, end = position, 0
    for e in range(n):
        count = counts_ref[0, e]
        end = end + count
        sorted_slot = sorted_slot + jnp.where(position >= end, cap - count, 0)
    slot_col = upright(sorted_slot)
    order_col = upright(jnp.broadcast_to(order_ref[...], (8, T)))
    slots[...] = jnp.broadcast_to(
        jnp.sum(jnp.where(order_col == tokens_across, slot_col, 0), axis=0, keepdims=True), (8, T)
    )
    doc_col = upright(jnp.broadcast_to(drow_ref[...], (8, T)))

    def pick(p):
        here = lax.broadcasted_iota(jnp.int32, (cap, T), 0) + p * cap
        return here == slots[0:1, :]

    def cot_copy(p):
        return remote(cots.at[p], cot_out.at[me], cs.at[p], cr.at[me], {"expert": p})

    def cot_in(p):
        return remote(cots.at[p], cot_out.at[p], cs.at[p], cr.at[p], {"expert": p})

    def place(i, _):
        p = flip(me, n - 1 - i, n)
        cots[p] = jnp.dot(pick(p).astype(bf), cot_ref[...], preferred_element_type=f32).astype(bf)

        return 0

    groups = [d] + [x[0] for x in over]
    lax.fori_loop(0, n // 2, place, 0)
    for q, dev in along:
        here = w.at[half, rows(d, q), :]
        remote(here, here, zs.at[q], zr.at[q], dev).wait_recv()
        for dd, dev2 in over:
            over_copy(dd, q, dev2).start()
        hand(d, q).start()
    for q, dev in along:
        remote(vblk, vall.at[d, q], vzs.at[q], vzr.at[q], dev).wait_recv()
    for dd, dev in over:
        v_over(dd, dev).start()
    ew_load.wait()
    for m in range(2):
        ew[m] = ew32[m].astype(bf)
    own_ew = pltpu.make_async_copy(ew, ew_out.at[d], ewl.at[0])
    own_ew.start()
    for m in range(2):
        x_copy(ew.at[m], d, m).start()
        y_copy(ew.at[1 - m], d, 1 - m).start()
    lax.fori_loop(n // 2, n, place, 0)

    def give(i, _):
        cot_copy(flip(me, n - 1 - i, n)).start()
        return 0

    lax.fori_loop(0, n - 1, give, 0)
    own_cot = pltpu.make_async_copy(cots.at[me], cot_out.at[me], loc.at[0])
    own_cot.start()

    def unit_rows(b):
        at = pl.ds(b * 256, 256)
        x = x_ref[at, :].astype(f32)
        center = x - jnp.mean(x, axis=-1, keepdims=True)
        unit[at, :] = center * lax.rsqrt(jnp.mean(center * center, axis=-1, keepdims=True) + norm_eps)

    for b in range(T // 256):
        unit_rows(b)
    for i in range(LEN // QB):
        first = max(0, i - WINDOW // QB) * QB
        W = (i + 1) * QB - first
        qp = i * QB + lax.broadcasted_iota(jnp.int32, (QB, W), 0)
        kp = first + lax.broadcasted_iota(jnp.int32, (QB, W), 1)
        ok = (kp <= qp) & (doc_col[i * QB : (i + 1) * QB, :] == drow_ref[:, first : first + W])
        bias[i * QB : (i + 1) * QB, :W] = jnp.where(ok, 0.0, masked_score)
    for q in [pair] + [x[0] for x in along]:
        for dd, dev in over:
            here = w.at[half, rows(dd, q), :]
            remote(here, here, ds_.at[dd, q], dr.at[dd, q], dev).wait_recv()
            hand(dd, q).start()
    for dd, dev in over:
        remote(vall.at[dd], vall.at[dd], vds.at[dd], vdr.at[dd], dev).wait_recv()
    vec = jnp.zeros(vec_out.shape, f32)
    for dd in range(dps):
        for q in range(pairs):
            vec = vec + vall[dd, q].astype(f32)
    vec_out[...] = vec
    slot_out[...] = slots[...]
    normed[...] = (unit[...] * vec_out[0:1, :]).astype(bf)

    def from_partner(dd, q):
        there = w.at[rest, rows(dd, q), :]
        remote(there, there, ps.at[dd, q], pr.at[dd, q], partner).wait_recv()

    for dd, dev in over:
        from_partner(dd, pair)
    for q, _ in along:
        for dd in groups:
            from_partner(dd, q)

    outs = [
        pltpu.make_async_copy(w, w_out, out_sem.at[0]),
        pltpu.make_async_copy(normed, normed_out, out_sem.at[1]),
    ]
    for c in outs:
        c.start()

    def project(i, _):
        c = i // 2
        at = pl.ds(pl.multiple_of(i % 2 * (T // 2), T // 2), T // 2)
        proj[c, at, :] = jnp.dot(normed[at, :], w[c], preferred_element_type=f32).astype(bf)
        return 0

    lax.fori_loop(0, 6, project, 0)
    outs.append(pltpu.make_async_copy(proj, proj_out, out_sem.at[2]))
    outs[-1].start()
    low_lane = lax.broadcasted_iota(jnp.int32, (QB, 128), 1) < HEAD_DIM

    def attend(h, _):
        lanes = pl.ds(pl.multiple_of(h * 128, 128), 128)
        for i in range(LEN // QB):
            here = slice(i * QB, (i + 1) * QB)
            first = max(0, i - WINDOW // QB) * QB
            W = (i + 1) * QB - first
            keys = slice(first, first + W)
            q = proj[0, here, lanes] * jnp.bfloat16(HEAD_DIM**-0.5)
            zero = jnp.zeros_like(q)
            qs = jnp.concatenate([jnp.where(low_lane, q, zero), jnp.where(low_lane, zero, q)], axis=0)
            s = lax.dot_general(qs, proj[1, keys, lanes], NT, preferred_element_type=f32)
            s = (s.reshape(2, QB, W) + bias[here, :W][None]).reshape(2 * QB, W)
            top = jnp.max(s, axis=1, keepdims=True)
            e = jnp.exp(s - top)
            total = jnp.sum(e, axis=1, keepdims=True)
            p = (e * (1.0 / total)).astype(bf)
            o = jnp.dot(p, proj[2, keys, lanes], preferred_element_type=f32)
            mixed[here, lanes] = jnp.where(low_lane, o[:QB], o[QB:]).astype(bf)
            ends = top + jnp.log(total)
            lse[h, here, :] = jnp.where(low_lane, ends[:QB], ends[QB:])
        return 0

    lax.fori_loop(0, D // 128, attend, 0)
    outs += [
        pltpu.make_async_copy(mixed, mixed_out, out_sem.at[3]),
        pltpu.make_async_copy(lse, lse_out, out_sem.at[4]),
    ]
    outs[-2].start()
    outs[-1].start()
    E = vec_out.shape[0] - 2
    hidden = unit

    def finish(b, _):
        at = pl.ds(pl.multiple_of(b * 256, 256), 256)
        state = x_ref[at, :].astype(f32) + jnp.dot(mixed[at, :], w[3], preferred_element_type=f32)
        hidden[at, :] = state
        center = state - jnp.mean(state, axis=-1, keepdims=True)
        spread = jnp.mean(center * center, axis=-1, keepdims=True)
        two = center * lax.rsqrt(spread + norm_eps) * vec_out[1:2, :]
        sent[at, :] = two.astype(bf)
        which = lax.broadcasted_iota(jnp.int32, (vec_out.shape[0], 256), 0) - 2
        chosen = (which == slots[0:1, at] // cap).astype(bf)
        rows_c = lax.dot_general(chosen, vec_out[...].astype(bf), TN, preferred_element_type=f32)
        logit = jnp.sum(two * rows_c, axis=1, keepdims=True)
        gate = 1.0 / (1.0 + jnp.exp(-logit))
        gate_out[:, at] = jnp.transpose(jnp.broadcast_to(gate, (256, 128)))[0:8, :]
        return 0

    lax.fori_loop(0, T // 256, finish, 0)
    outs.append(pltpu.make_async_copy(hidden, hidden_out, out_sem.at[5]))
    outs[-1].start()
    tiles[...] = jnp.zeros(tiles.shape, f32)
    part = pl.ds(pl.multiple_of(me % (TILE // cap) * cap, 128), cap)

    def fill(p, _):
        chosen = pick(p)
        sends[p] = jnp.dot(chosen.astype(bf), sent[...], preferred_element_type=f32).astype(bf)
        tiles[p, :, part] = lax.dot_general(
            gate_out[...], chosen.astype(f32), NT, precision=lax.Precision.HIGHEST, preferred_element_type=f32
        )
        pltpu.make_async_copy(sends.at[p], send_out.at[p], send_sem).start()
        return 0

    lax.fori_loop(0, n, fill, 0)
    outs.append(pltpu.make_async_copy(tiles, tile_out, out_sem.at[6]))
    outs[-1].start()
    for q, dev in along:
        along_copy(q, dev).wait_send()
        v_along(q, dev).wait_send()
        hand(d, q).wait_send()
    for dd, dev in over:
        v_over(dd, dev).wait_send()
        for q in [pair] + [x[0] for x in along]:
            over_copy(dd, q, dev).wait_send()
            hand(dd, q).wait_send()

    def settle(o, _):
        p = flip(me, o, n)
        cot_copy(p).wait_send()
        cot_in(p).wait_recv()
        return 0

    lax.fori_loop(1, n, settle, 0)
    pltpu.make_async_copy(cots.at[me], cot_out.at[me], loc.at[0]).wait()
    own_ew.wait()
    for m in range(2):
        x_copy(ew.at[m], d, m).wait_send()
        y_copy(ew.at[m], d, m).wait_send()
        x_copy(ew.at[m], side_x, m).wait_recv()
        y_copy(ew.at[m], side_y, m).wait_recv()
    for c in outs:
        c.wait()
    pltpu.make_async_copy(sends, send_out, send_sem).wait()


def head(weights, vectors, inputs, cotangent, token_order, counts, documents, expert_weights, dps, n, cap):
    pairs = n // 2
    m, r, D = weights.shape
    T = inputs.shape[0]
    k = vectors.shape[0]
    f32, bf = jnp.float32, jnp.bfloat16
    dma = pltpu.SemaphoreType.DMA
    any_ = pl.BlockSpec(memory_space=pl.ANY)
    vm = pl.BlockSpec(memory_space=pltpu.VMEM)
    dev = lax.axis_index("dp") * n + lax.axis_index("expert")
    K = (k + 15) // 16 * 16
    placed = lax.dynamic_update_slice(jnp.zeros((K, D), f32), vectors, (0, dev * r))
    shape = jax.ShapeDtypeStruct
    grid = lambda: dma((dps, pairs))
    return pl.pallas_call(
        partial(head_kernel, dps, pairs, n, cap),
        out_shape=[
            shape((m, D, D), bf), shape((K, D), f32), shape((8, T), jnp.int32), shape((n, cap, D), bf),
            shape((3, T, D), bf), shape((T, D), bf), shape((T, D), bf), shape((D // 128, T, 128), f32),
            shape((T, D), f32), shape((8, T), f32), shape((n, cap, D), bf), shape((n, 8, TILE), f32),
            shape((dps,) + expert_weights.shape[1:], bf),
        ],
        in_specs=[vm] * 5 + [pl.BlockSpec(memory_space=pltpu.SMEM), vm, any_],
        out_specs=[any_, vm, vm, any_, any_, any_, any_, any_, any_, vm, any_, any_, any_],
        scratch_shapes=[
            pltpu.VMEM(expert_weights.shape[1:], f32), pltpu.VMEM(expert_weights.shape[1:], bf),
            pltpu.VMEM((m, 2 * r, D), f32), pltpu.VMEM((m, 2 * r, D), bf), pltpu.VMEM((2, K, D), f32),
            pltpu.VMEM((K, D), bf), pltpu.VMEM((m, D, D), bf), pltpu.VMEM((dps, pairs, K, D), bf),
            pltpu.VMEM((8, T), jnp.int32), pltpu.VMEM((T, D), f32), pltpu.VMEM((T, D), bf),
            pltpu.VMEM((3, T, D), bf), pltpu.VMEM((T, D), bf), pltpu.VMEM((D // 128, T, 128), f32),
            pltpu.VMEM((T, min(T, WINDOW + QB)), f32), pltpu.VMEM((T, D), bf), pltpu.VMEM((n, cap, D), bf),
            pltpu.VMEM((n, cap, D), bf), pltpu.VMEM((n, 8, TILE), f32),
            dma((2,)), dma((2,)), dma((1,)), dma((pairs,)), dma((pairs,)), dma((pairs,)), dma((pairs,)),
            grid(), grid(), dma((dps,)), dma((dps,)), grid(), grid(), dma((n,)), dma((n,)),
            dma((1,)), dma((dps, 2)), dma((dps, 2)), dma((dps, 2)), dma((dps, 2)), dma((7,)), dma(()),
        ],
        compiler_params=pltpu.CompilerParams(
            vmem_limit_bytes=60 * 2**20, collective_id=2, has_side_effects=True
        ),
        cost_estimate=pl.CostEstimate(flops=20 * T * D * D, bytes_accessed=200 * 2**20, transcendentals=0),
    )(weights, placed, inputs, cotangent, token_order, counts, documents, expert_weights)


def tail_kernel(dps, pairs, cap, q_ref, k_ref, v_ref, lse_ref, drow_ref, vec_ref, slot_ref, gate_ref,
                scale_ref, chosen_ref, x_ref, mixed_ref, prod_ref, w_ref, in_ref, late_ref, back_ref, cot_ref,
                hidden_ref,
                out_ref, vec_out, dx_ref, block_ref,
                bias_ref, dk_ref, dv_ref, left, right, got, own, total, in2, tb, in3, u, in4, w, gh, xin,
                ret, hid, back, cot, g_ref, chs, dcol_ref,
                ls, s1, r1, s2, r2, s3, r3, s4, r4, rs, rr, bs, br, own_sem, dx_sem, block_sem):
    h = pl.program_id(0)
    n = 2 * pairs
    per = late_ref.shape[0]
    early = (n - per) * cap
    me = lax.axis_index("expert")
    d, pair, core, partner, over, along = near(dps, pairs)
    rows = out_ref.shape[1]
    R = 2 * rows
    T, D = x_ref.shape
    bf, f32 = jnp.bfloat16, jnp.float32
    B = 256
    loads = [
        pltpu.make_async_copy(back_ref, back.at[pl.ds(0, n - per)], ls.at[0]),
        pltpu.make_async_copy(hidden_ref, hid, ls.at[1]),
        pltpu.make_async_copy(cot_ref, cot, ls.at[2]),
        pltpu.make_async_copy(w_ref, w, ls.at[3]),
        pltpu.make_async_copy(mixed_ref, left.at[1], ls.at[4]),
        pltpu.make_async_copy(x_ref, left.at[0], ls.at[5]),
        pltpu.make_async_copy(in_ref, xin, ls.at[6]),
    ]

    def product(m):
        return lax.dot_general(left[m // 3], right[m], TN, preferred_element_type=f32)

    def ret_copy(peer):
        return remote(prod_ref.at[peer], ret.at[me], rs.at[peer], rr.at[me], {"expert": peer})

    def ret_in(peer):
        return remote(prod_ref.at[peer], ret.at[peer], rs.at[peer], rr.at[peer], {"expert": peer})

    own_ret = pltpu.make_async_copy(prod_ref.at[me], ret.at[me], own_sem)
    last = flip(me // per, n // per - 1, n // per) * per

    def late_copy(j):
        k = flip(j, me % per, per)
        return remote(late_ref.at[j], back.at[n - per + k], bs.at[k], br.at[k], {"expert": last + j})

    def to_partner(i):
        return remote(total.at[i], got.at[i], s1.at[i], r1.at[i], partner)

    def column(row):
        return jnp.transpose(row)[:, 0:1]

    def normal(x):
        center = x - jnp.mean(x, axis=-1, keepdims=True)
        scale = lax.rsqrt(jnp.mean(center * center, axis=-1, keepdims=True) + norm_eps)
        return center * scale, scale

    def normal_back(grad, unit, scale, gain):
        gu = grad * gain
        return scale * (
            gu - jnp.mean(gu, axis=-1, keepdims=True) - unit * jnp.mean(gu * unit, axis=-1, keepdims=True)
        )

    def offset_slots(at):
        slot = slot_ref[:, at]
        return flip(slot // cap, me, n) * cap + slot % cap

    def match(slot_rows, first, count):
        here = column(slot_rows.astype(f32))
        return here == (first + lax.broadcasted_iota(jnp.int32, (B, count), 1)).astype(f32)

    @pl.when(h == 0)
    def _():
        for c in loads:
            c.start()
        barrier = pltpu.get_barrier_semaphore()

        def greet(o, _):
            pl.semaphore_signal(barrier, inc=1, device_id={"expert": flip(me, o, n)}, device_id_type=MESH)
            return 0

        lax.fori_loop(1, n, greet, 0)
        for _, dev in over:
            pl.semaphore_signal(barrier, inc=1, device_id=dev, device_id_type=MESH)
        pl.semaphore_wait(barrier, n - 1 + dps - 1)
        for j in range(per):
            late_copy(j).start()

        def send(i, _):
            ret_copy(flip(me, n - 1 - i, n)).start()
            return 0

        lax.fori_loop(0, n - 1, send, 0)
        own_ret.start()
        dcol_ref[...] = upright(jnp.broadcast_to(drow_ref[...], (8, T)))
        transposed_bias(bias_ref, dcol_ref, drow_ref, QB)
        part = pl.ds(pl.multiple_of(me % per * cap, 128), cap)
        for o in range(n):
            chs[:, o * cap : (o + 1) * cap] = chosen_ref[o, :, part]
        loads[0].wait()

        def first_rows(b, _):
            at = pl.ds(pl.multiple_of(b * B, B), B)
            pick = match(offset_slots(at), 0, early).astype(bf)
            gh[at, :] = jnp.dot(pick, back[pl.ds(0, n - per)].reshape(early, D), preferred_element_type=f32)
            return 0

        lax.fori_loop(0, T // B, first_rows, 0)
        vec_out[...] = jnp.zeros(vec_out.shape, f32)
        for c in loads[1:4]:
            c.wait()
        for j in range(per):
            late_copy(j).wait_recv()

        def second(b, _):
            at = pl.ds(pl.multiple_of(b * B, B), B)
            slot_rows = offset_slots(at)
            all_slots = match(slot_rows, 0, n * cap)
            chosen = jnp.sum(jnp.where(all_slots, chs[0:1, :], 0.0), axis=1, keepdims=True)
            pick = match(slot_rows, early, per * cap).astype(bf)
            sent = gh[at, :] + jnp.dot(
                pick, back[pl.ds(n - per, per)].reshape(per * cap, D), preferred_element_type=f32
            )
            which = lax.broadcasted_iota(jnp.int32, (vec_ref.shape[0], B), 0) - 2
            expert = which == slot_ref[0:1, at] // cap
            centroid = lax.dot_general(
                expert.astype(bf), vec_ref[...].astype(bf), TN, preferred_element_type=f32
            )
            grad = sent + chosen * centroid
            unit, scale = normal(hid[at, :])
            gain = vec_ref[1:2, :]
            chosen_row = jnp.transpose(jnp.broadcast_to(chosen, (B, 128)))[0:1, :]
            vec_out[...] += jnp.dot(
                jnp.where(expert, chosen_row, 0.0), unit * gain,
                precision=lax.Precision.HIGHEST, preferred_element_type=f32,
            )
            vec_out[1:2, :] += jnp.sum(grad * unit, axis=0, keepdims=True)
            total_grad = cot[at, :].astype(f32) * scale_ref[0:1, 0:1] + normal_back(grad, unit, scale, gain)
            gh[at, :] = total_grad
            low = total_grad.astype(bf)
            right[3, at, :] = low
            g_ref[at, :] = lax.dot_general(low, w[3], NT, preferred_element_type=f32).astype(bf)
            return 0

        lax.fori_loop(0, T // B, second, 0)
        loads[4].wait()
        out = product(3)

        @pl.when(core == 0)
        def _():
            total[1] = out.astype(bf)
            to_partner(1).start()

        @pl.when(core == 1)
        def _():
            own[1] = out

    lanes = pl.ds(pl.multiple_of(h * 128, 128), 128)

    def put_dq(r, value):
        right[0, r, lanes] = value

    head_pair_backward(
        QB, q_ref, k_ref, v_ref, lse_ref, g_ref.at[:, lanes], bias_ref, dk_ref, dv_ref, put_dq
    )
    right[1, :, lanes] = dk_ref[...].astype(bf)
    right[2, :, lanes] = dv_ref[...].astype(bf)

    @pl.when(h == pl.num_programs(0) - 1)
    def _():
        loads[5].wait()

        @pl.when(core == 0)
        def _():
            total[0] = product(2).astype(bf)
            to_partner(0).start()
            own[0] = product(0)
            own[1] = product(1)

        @pl.when(core == 1)
        def _():
            total[0] = product(0).astype(bf)
            to_partner(0).start()
            total[1] = product(1).astype(bf)
            to_partner(1).start()
            own[0] = product(2)

        for i in range(2):
            to_partner(i).wait_send()
            to_partner(i).wait_recv()
            total[i] = (own[i] + got[i].astype(f32)).astype(bf)

        order = along + [(pair, None)]

        def piece(dd, q):
            return pl.ds(pl.multiple_of((dd * pairs + q) * R, 16), R)

        c2 = []
        for q, _ in order:
            for dd, dev in over:
                c = remote(total.at[:, piece(dd, q), :], in2.at[d, q], s2.at[dd, q], r2.at[d, q], dev)
                c.start()
                c2.append(c)
        loads[6].wait()

        def norm_one(b, _):
            at = pl.ds(pl.multiple_of(b * B, B), B)
            gn = sum(
                lax.dot_general(right[c, at, :], w[c], NT, preferred_element_type=f32) for c in range(3)
            )
            unit, scale = normal(xin[at, :].astype(f32))
            vec_out[0:1, :] += jnp.sum(gn * unit, axis=0, keepdims=True)
            gh[at, :] += normal_back(gn, unit, scale, vec_ref[0:1, :])
            return 0

        lax.fori_loop(0, T // B, norm_one, 0)
        dx = pltpu.make_async_copy(gh, dx_ref, dx_sem)
        dx.start()
        c3 = []
        for q, zdev in order:
            acc = total[:, piece(d, q), :].astype(f32)
            for dd, dev in over:
                remote(in2.at[dd, q], in2.at[dd, q], s2.at[dd, q], r2.at[dd, q], dev).wait_recv()
                acc = acc + in2[dd, q].astype(f32)
            if zdev is None:
                u[...] = acc
            else:
                tb[q] = acc.astype(bf)
                c = remote(tb.at[q], in3.at[pair], s3.at[q], r3.at[pair], zdev)
                c.start()
                c3.append(c)

        def settle(o, _):
            peer = flip(me, o, n)
            ret_copy(peer).wait_send()
            ret_in(peer).wait_recv()
            return 0

        lax.fori_loop(1, n, settle, 0)
        own_ret.wait()

        def add_rows(b, _):
            at = pl.ds(pl.multiple_of(b * B, B), B)
            pick = match(slot_ref[:, at], 0, n * cap).astype(bf)
            got_rows = jnp.dot(pick, ret[...].reshape(n * cap, D), preferred_element_type=f32)
            hid[at, :] += column(gate_ref[:, at]) * got_rows
            return 0

        lax.fori_loop(0, T // B, add_rows, 0)
        block = pltpu.make_async_copy(hid, block_ref, block_sem)
        block.start()
        acc = u[...]
        for q, dev in along:
            remote(in3.at[q], in3.at[q], s3.at[q], r3.at[q], dev).wait_recv()
            acc = acc + in3[q].astype(f32)
        u[...] = acc
        theirs = pl.ds(pl.multiple_of((1 - core) * rows, 8), rows)
        mine = pl.ds(pl.multiple_of(core * rows, 8), rows)
        c4 = remote(u.at[:, theirs, :], in4, s4, r4, partner)
        c4.start()
        out_ref[pl.ds(2 * core, 2)] = u[:, mine, :]
        c4.wait_recv()
        out_ref[pl.ds(2 - 2 * core, 2)] = in4[...]
        for c in c2 + c3 + [c4]:
            c.wait_send()
        for j in range(per):
            late_copy(j).wait_send()
        dx.wait()
        block.wait()


def tail(projected, lse, documents, vec, slot_rows, gate_rows, scale, chosen, normed, mixed, produced, dense_low,
         inputs, late, back, cotangent, hidden, dps, n):
    pairs = n // 2
    _, T, D = projected.shape
    rows = D // (dps * n)
    R = 2 * rows
    cap = produced.shape[1]
    per = late.shape[0]
    f32, bf = jnp.float32, jnp.bfloat16
    dma = pltpu.SemaphoreType.DMA
    any_ = pl.BlockSpec(memory_space=pl.ANY)

    def sp(c):
        return pl.BlockSpec((1, T, 128), lambda h, c=c: (c, 0, h))

    def fixed(shape):
        return pl.BlockSpec(shape, lambda h: (0,) * len(shape))

    return pl.pallas_call(
        partial(tail_kernel, dps, pairs, cap),
        grid=(D // 128,),
        out_shape=[
            jax.ShapeDtypeStruct((4, rows, D), f32),
            jax.ShapeDtypeStruct(vec.shape, f32),
            jax.ShapeDtypeStruct((T, D), f32),
            jax.ShapeDtypeStruct((T, D), f32),
        ],
        in_specs=[sp(0), sp(1), sp(2), pl.BlockSpec((1, T, 128), lambda h: (h, 0, 0)),
                  fixed((1, T)), fixed(vec.shape), fixed((8, T)), fixed((8, T)), fixed((8, 128)),
                  fixed(chosen.shape)]
        + [any_] * 9,
        out_specs=[fixed((4, rows, D)), fixed(vec.shape), any_, any_],
        scratch_shapes=[
            pltpu.VMEM((min(T, WINDOW + QB), T), f32),
            pltpu.VMEM((T, 128), f32),
            pltpu.VMEM((T, 128), f32),
            pltpu.VMEM((2, T, D), bf),
            pltpu.VMEM((4, T, D), bf),
            pltpu.VMEM((2, D, D), bf),
            pltpu.VMEM((2, D, D), f32),
            pltpu.VMEM((2, D, D), bf),
            pltpu.VMEM((dps, pairs, 2, R, D), bf),
            pltpu.VMEM((pairs, 2, R, D), bf),
            pltpu.VMEM((pairs, 2, R, D), bf),
            pltpu.VMEM((2, R, D), f32),
            pltpu.VMEM((2, rows, D), f32),
            pltpu.VMEM((4, D, D), bf),
            pltpu.VMEM((T, D), f32),
            pltpu.VMEM((T, D), bf),
            pltpu.VMEM((n, cap, D), bf),
            pltpu.VMEM((T, D), f32),
            pltpu.VMEM((n, cap, D), bf),
            pltpu.VMEM((T, D), bf),
            pltpu.VMEM((T, D), bf),
            pltpu.VMEM((8, n * cap), f32),
            pltpu.VMEM((T, 1), jnp.int32),
            dma((7,)), dma((2,)), dma((2,)), dma((dps, pairs)), dma((dps, pairs)), dma((pairs,)), dma((pairs,)),
            dma(()), dma(()), dma((n,)), dma((n,)), dma((per,)), dma((per,)), dma(()), dma(()), dma(()),
        ],
        compiler_params=pltpu.CompilerParams(
            vmem_limit_bytes=62 * 2**20, collective_id=3, has_side_effects=True
        ),
        cost_estimate=pl.CostEstimate(flops=40 * T * D * D, bytes_accessed=200 * 2**20, transcendentals=0),
    )(projected, projected, projected, lse, documents, vec, slot_rows,
      gate_rows, scale, chosen, normed, mixed, produced, dense_low, inputs, late, back, cotangent, hidden)


def norm_kernel(dps, pairs, d_ref, v_ref, e_ref, out_ref, a, b, c, s1, r1, s2, r2, s3, r3):
    d, pair, core, partner, over, along = near(dps, pairs)
    greet_all([partner] + [x[1] for x in over] + [x[1] for x in along])

    def squares(ref):
        x = ref[...].astype(jnp.float32)
        return jnp.sum(x * x)

    part = squares(d_ref)
    for i in range(e_ref.shape[0]):
        part = part + squares(e_ref.at[i])
    last = lax.broadcasted_iota(jnp.int32, v_ref.shape, 0) == v_ref.shape[0] - 1
    a[core] = jnp.where(last, part, v_ref[...])
    cs = [remote(a.at[core], a.at[core], s1, r1.at[core], partner)]
    cs[0].start()
    remote(a.at[1 - core], a.at[1 - core], s1, r1.at[1 - core], partner).wait_recv()
    b[d] = a[0] + a[1]
    for dd, dev in over:
        x = remote(b.at[d], b.at[d], s2.at[dd], r2.at[d], dev)
        x.start()
        cs.append(x)
    for dd, dev in over:
        remote(b.at[dd], b.at[dd], s2.at[dd], r2.at[dd], dev).wait_recv()
    c[pair] = sum(b[k] for k in range(dps))
    for q, dev in along:
        x = remote(c.at[pair], c.at[pair], s3.at[q], r3.at[pair], dev)
        x.start()
        cs.append(x)
    for q, dev in along:
        remote(c.at[q], c.at[q], s3.at[q], r3.at[q], dev).wait_recv()
    out_ref[...] = sum(c[k] for k in range(pairs))
    for x in cs:
        x.wait_send()


def norm_squares(dense, vec, expert, dps, n):
    pairs = n // 2
    k, D = vec.shape
    R = (k // 8 + 1) * 8
    dma = pltpu.SemaphoreType.DMA
    vm = pl.BlockSpec(memory_space=pltpu.VMEM)
    out = pl.pallas_call(
        partial(norm_kernel, dps, pairs),
        out_shape=jax.ShapeDtypeStruct((R, D), jnp.float32),
        in_specs=[vm] * 3,
        out_specs=vm,
        scratch_shapes=[
            pltpu.VMEM((2, R, D), jnp.float32),
            pltpu.VMEM((dps, R, D), jnp.float32),
            pltpu.VMEM((pairs, R, D), jnp.float32),
            dma(()), dma((2,)), dma((dps,)), dma((dps,)), dma((pairs,)), dma((pairs,)),
        ],
        compiler_params=pltpu.CompilerParams(
            vmem_limit_bytes=24 * 2**20, collective_id=4, has_side_effects=True
        ),
    )(dense, jnp.pad(vec, ((0, R - k), (0, 0))), expert)
    total = out[:k]
    dev = lax.axis_index("dp") * n + lax.axis_index("expert")
    width = D // (dps * n)
    return lax.dynamic_slice_in_dim(total, dev * width, width, axis=1), out[R - 1, 0] + jnp.sum(total * total)


def adam_update(weight, gradient, first_moment, second_moment, average, factor, rate):
    clipped = gradient * factor
    first_new = beta_first * first_moment + (1.0 - beta_first) * clipped
    second_new = beta_second * second_moment + (1.0 - beta_second) * clipped * clipped
    first_hat = first_new / (1.0 - beta_first**STEP)
    second_hat = second_new / (1.0 - beta_second**STEP)
    updated = weight - rate * (
        first_hat / (jnp.sqrt(second_hat) + adam_eps) + weight_decay * weight
    )
    average_new = ema_keep * average + (1.0 - ema_keep) * updated
    return (updated, first_new, second_new, average_new)


def inverse_order(row_order, sorted_slot):
    at_token = row_order[:, None] == jnp.arange(row_order.shape[0])[None, :]
    return jnp.sum(jnp.where(at_token, sorted_slot[:, None], 0), axis=0)


def shards(
    inputs,
    cotangent,
    document_ids,
    domain_counts,
    domain_weight,
    token_order,
    expert_counts,
    dense_weights,
    vector_params,
    expert_weights,
    dense_first,
    dense_second,
    dense_average,
    vector_first,
    vector_second,
    vector_average,
    expert_first,
    expert_second,
    expert_average,
):
    tokens, model_width = inputs.shape
    experts_total = expert_counts.shape[1]
    capacity = 2 * tokens // experts_total
    owners = lax.axis_size("expert")
    groups = lax.axis_size(("dp", "expert"))
    sequences = tokens // LEN
    splits = lax.axis_size("dp")
    own_rows = dense_weights.shape[1]
    me = lax.axis_index("expert")
    seq_index = lax.axis_index("dp") * owners + jnp.arange(owners)
    domains = jnp.arange(NDOM)
    bounds = jnp.sum(jnp.where(domains[None, :] <= domains[:, None], domain_counts[None, :], 0), axis=1)
    domain = jnp.sum((seq_index[:, None] >= bounds[None, :]).astype(jnp.int32), axis=1)
    seq_pick = (domain[:, None] == jnp.arange(NDOM)[None, :]).astype(jnp.float32)
    seq_weight = jnp.sum(seq_pick * domain_weight[None, :], axis=1)
    seq_count = jnp.sum(seq_pick * domain_counts[None, :].astype(jnp.float32), axis=1)
    seq_scale = seq_weight * (sequences * groups) / (NDOM * seq_count)
    source_scale = jnp.broadcast_to(seq_scale[:, None], (owners, 128))
    documents = document_ids.reshape(-1)
    inputs_float = inputs.astype(jnp.float32)
    per = TILE // capacity
    fused = own_rows % 8 == 0 and capacity % 128 == 0 and splits == 4
    if fused:
        (dense_low, vec_rows, slot_rows, cot_received, projected, normed_low, mixed_low, totals,
         hidden_state, gate_rows, send_rows, gate_tiles, expert_low) = head(
            dense_weights, vector_params, inputs, cotangent, token_order, expert_counts, document_ids,
            expert_weights, splits, owners, capacity
        )
    else:
        row_counts = expert_counts[0]
        row_order = token_order[0]
        count_ends = jnp.cumsum(row_counts)
        count_starts = count_ends - row_counts
        sorted_pos = jnp.arange(tokens)
        sorted_expert = jnp.sum((sorted_pos[:, None] >= count_ends[None, :]).astype(jnp.int32), axis=1)
        sorted_pick = sorted_expert[:, None] == jnp.arange(experts_total)[None, :]
        sorted_start = jnp.sum(jnp.where(sorted_pick, count_starts[None, :], 0), axis=1)
        sorted_slot = sorted_expert * capacity + sorted_pos - sorted_start
        token_slot = inverse_order(row_order, sorted_slot)
        own_low = expert_weights[0].astype(jnp.bfloat16)
        expert_low = lax.all_gather(own_low, "dp", axis=0)
        dense_low, vector_low = (
            lax.all_gather(dense_weights.astype(jnp.bfloat16), ("dp", "expert"), axis=1, tiled=True),
            lax.all_gather(vector_params.astype(jnp.bfloat16), ("dp", "expert"), axis=1, tiled=True),
        )
        vector_low = vector_low.astype(jnp.float32)
        token_expert = token_slot // capacity
        expert_pick = (token_expert[:, None] == jnp.arange(experts_total)[None, :]).astype(jnp.float32)
        slot_match = token_slot[:, None] == jnp.arange(experts_total * capacity)[None, :]
        slot_pick = slot_match.astype(jnp.bfloat16)

        def to_slots(rows):
            placed = jnp.dot(slot_pick.T, rows, preferred_element_type=jnp.float32)
            return placed.astype(jnp.bfloat16).reshape(experts_total, capacity, model_width)

        def from_slots(rows):
            return jnp.dot(
                slot_pick, rows.reshape(-1, model_width), preferred_element_type=jnp.float32
            )

        cot_received = lax.all_to_all(
            to_slots(cotangent), "expert", split_axis=0, concat_axis=0, tiled=True
        )
        normed_one, norm_one_back = jax.vjp(layer_norm, inputs_float, vector_low[0])
        normed_low = normed_one.astype(jnp.bfloat16)
        projected = jnp.einsum(
            "td,cde->cte", normed_low, dense_low[:3], preferred_element_type=jnp.float32
        ).astype(jnp.bfloat16)
        mixed_low, totals = attend_forward(projected, documents)
        hidden_state = inputs_float + jnp.dot(
            mixed_low, dense_low[3], preferred_element_type=jnp.float32
        )
        normed_two, norm_two_back = jax.vjp(layer_norm, hidden_state, vector_low[1])
        centroids = vector_low[2:]
        logits = jnp.dot(normed_two, centroids.T, precision=lax.Precision.HIGHEST)
        gate_value = jax.nn.sigmoid(jnp.sum(logits * expert_pick, axis=1))
        send_rows = to_slots(normed_two.astype(jnp.bfloat16))
        gate_slots = jnp.sum(
            jnp.where(slot_match, gate_value[:, None], 0.0), axis=0
        ).reshape(experts_total, 1, 1, capacity)
        lane_part = (jnp.arange(per) == me % per).astype(jnp.float32)
        gate_tiles = jnp.broadcast_to(
            gate_slots * lane_part[None, None, :, None], (experts_total, 8, per, capacity)
        ).reshape(experts_total, 8, TILE)
    back_rows, late_rows, chosen_tiles, produced_low, grad_expert = moe(
        send_rows, gate_tiles, cot_received.reshape(-1, model_width), source_scale, expert_low, fused
    )
    expert_low_grad = lax.psum_scatter(grad_expert, "dp", scatter_dimension=0)
    expert_grad = expert_low_grad.astype(jnp.float32)[None]
    if fused:
        dense_grad, vector_grad, input_grad, block_output = tail(
            projected, totals, document_ids, vec_rows, slot_rows, gate_rows,
            jnp.broadcast_to(seq_scale[me], (8, 128)), chosen_tiles, normed_low, mixed_low, produced_low,
            dense_low, inputs, late_rows, back_rows, cotangent, hidden_state, splits, owners
        )
        vector_grad = vector_grad[: vector_params.shape[0]]
    else:
        late_rows = send_late(late_rows, owners)
        grad_out = cotangent.astype(jnp.float32) * seq_scale[me]
        back_slot = (token_slot // capacity ^ me) * capacity + token_slot % capacity
        back_match = back_slot[:, None] == jnp.arange(experts_total * capacity)[None, :]
        back_pick = back_match.astype(jnp.bfloat16)
        early = back_rows.shape[0] * capacity
        grad_sent_rows = jnp.dot(
            back_pick[:, :early], back_rows.reshape(-1, model_width), preferred_element_type=jnp.float32
        ) + jnp.dot(
            back_pick[:, early:], late_rows.reshape(-1, model_width), preferred_element_type=jnp.float32
        )
        chosen_slots = lax.dynamic_slice_in_dim(
            chosen_tiles[:, 0, :], me % per * capacity, capacity, axis=1
        )
        grad_chosen = jnp.sum(jnp.where(back_match, chosen_slots.reshape(1, -1), 0.0), axis=1)
        chosen_grad = grad_chosen[:, None] * expert_pick
        grad_normed_two = grad_sent_rows + jnp.dot(
            chosen_grad, centroids, precision=lax.Precision.HIGHEST
        )
        grad_centroids = jnp.dot(chosen_grad.T, normed_two, precision=lax.Precision.HIGHEST)
        grad_hidden_norm, grad_gain_two = norm_two_back(grad_normed_two)
        grad_hidden = grad_out + grad_hidden_norm
        grad_attn = grad_hidden.astype(jnp.bfloat16)
        grad_mixed = jnp.dot(grad_attn, dense_low[3].T, preferred_element_type=jnp.float32).astype(
            jnp.bfloat16
        )
        returned = lax.all_to_all(produced_low, "expert", split_axis=0, concat_axis=0, tiled=True)
        grad_proj = attend_backward(projected, documents, totals, grad_mixed)
        grad_normed_one = jnp.einsum(
            "cte,cde->td", grad_proj, dense_low[:3], preferred_element_type=jnp.float32
        )
        grad_input_norm, grad_gain_one = norm_one_back(grad_normed_one)
        input_grad = grad_hidden + grad_input_norm
        grad_in_proj = jnp.einsum(
            "td,cte->cde", normed_low, grad_proj, preferred_element_type=jnp.float32
        )
        grad_out_proj = jnp.dot(mixed_low.T, grad_attn, preferred_element_type=jnp.float32)
        dense_grad = lax.psum_scatter(
            jnp.concatenate([grad_in_proj, grad_out_proj[None]], axis=0),
            ("dp", "expert"),
            scatter_dimension=1,
            tiled=True,
        )
        returned_rows = from_slots(returned)
        block_output = hidden_state + gate_value[:, None] * returned_rows
        vector_grad = jnp.concatenate(
            [grad_gain_one[None], grad_gain_two[None], grad_centroids], axis=0
        )
    vector_grad, squares = norm_squares(dense_grad, vector_grad, expert_low_grad, splits, owners)
    grad_norm = jnp.sqrt(squares)
    factor = jnp.minimum(1.0, clip_norm / (grad_norm + 1e-06))
    dense_new = adam_update(
        dense_weights, dense_grad, dense_first, dense_second, dense_average, factor, dense_rate
    )
    vector_new = adam_update(
        vector_params, vector_grad, vector_first, vector_second, vector_average, factor, vector_rate
    )
    expert_new = adam_update(
        expert_weights,
        expert_grad,
        expert_first,
        expert_second,
        expert_average,
        factor,
        expert_rate,
    )
    return (
        block_output,
        input_grad,
        dense_new[0],
        dense_new[1],
        dense_new[2],
        dense_new[3],
        vector_new[0],
        vector_new[1],
        vector_new[2],
        vector_new[3],
        expert_new[0],
        expert_new[1],
        expert_new[2],
        expert_new[3],
        grad_norm,
    )


def solution(mesh):
    placed = (
        P(("dp", "expert"), None),
        P(("dp", "expert"), None),
        P(("dp", "expert"), None),
        P(),
        P(),
        P(("dp", "expert"), None),
        P(("dp", "expert"), None),
        P(None, ("dp", "expert"), None),
        P(None, ("dp", "expert")),
        P("expert", None, None, "dp"),
        P(None, ("dp", "expert"), None),
        P(None, ("dp", "expert"), None),
        P(None, ("dp", "expert"), None),
        P(None, ("dp", "expert")),
        P(None, ("dp", "expert")),
        P(None, ("dp", "expert")),
        P("expert", None, None, "dp"),
        P("expert", None, None, "dp"),
        P("expert", None, None, "dp"),
    )
    return jax.shard_map(
        shards,
        mesh=mesh,
        in_specs=placed,
        out_specs=(
            P(("dp", "expert"), None),
            P(("dp", "expert"), None),
            P(None, ("dp", "expert"), None),
            P(None, ("dp", "expert"), None),
            P(None, ("dp", "expert"), None),
            P(None, ("dp", "expert"), None),
            P(None, ("dp", "expert")),
            P(None, ("dp", "expert")),
            P(None, ("dp", "expert")),
            P(None, ("dp", "expert")),
            P("expert", None, None, "dp"),
            P("expert", None, None, "dp"),
            P("expert", None, None, "dp"),
            P("expert", None, None, "dp"),
            P(),
        ),
        check_vma=False,
    )
```

```python
from functools import partial

import jax
import jax.numpy as jnp
from jax import lax
from jax.experimental import pallas as pl
from jax.experimental.pallas import tpu as pltpu
from jax.sharding import PartitionSpec as P

HEADS = 12
HEAD_DIM = 64
LEN = 1024
WINDOW = 512
NDOM = 8
STEP = 10


norm_eps = 1e-05
masked_score = -1e30
beta_first = 0.9
beta_second = 0.999
adam_eps = 1e-08
dense_rate = 0.1
vector_rate = 0.5
expert_rate = 0.02
weight_decay = 0.1
ema_keep = 0.9
clip_norm = 1.0


def layer_norm(values_in, gain_row):
    center = values_in - jnp.mean(values_in, axis=-1, keepdims=True)
    spread = jnp.mean(center * center, axis=-1, keepdims=True)
    return center * lax.rsqrt(spread + norm_eps) * gain_row


NT = (((1,), (1,)), ((), ()))
TN = (((0,), (0,)), ((), ()))


def fwd_kernel(QB, q_ref,k_ref,v_ref,dcol_ref,drow_ref,o_ref,lse_ref,bias_ref):
    reach = WINDOW//QB
    low_lane = lax.broadcasted_iota(jnp.int32,(QB,128),1) < HEAD_DIM
    @pl.when(pl.program_id(0)==0)
    def _():
        for i in range(LEN//QB):
            first=max(0,i-reach)*QB; W=(i+1)*QB-first
            qp=i*QB+lax.broadcasted_iota(jnp.int32,(QB,W),0)
            kp=first+lax.broadcasted_iota(jnp.int32,(QB,W),1)
            ok=(kp<=qp)&(dcol_ref[i*QB:(i+1)*QB,:]==drow_ref[:,first:first+W])
            bias_ref[i*QB:(i+1)*QB,:W]=jnp.where(ok,0.0,masked_score)
    for i in range(LEN//QB):
        rows=slice(i*QB,(i+1)*QB)
        first=max(0,i-reach)*QB; W=(i+1)*QB-first
        q=q_ref[0,rows,:]*jnp.bfloat16(HEAD_DIM**-0.5)
        zero=jnp.zeros_like(q)
        qs=jnp.concatenate([jnp.where(low_lane,q,zero),jnp.where(low_lane,zero,q)],axis=0)
        s=lax.dot_general(qs,k_ref[0,first:first+W,:],NT,preferred_element_type=jnp.float32)
        s=(s.reshape(2,QB,W)+bias_ref[rows,:W][None]).reshape(2*QB,W)
        top=jnp.max(s,axis=1,keepdims=True)
        e=jnp.exp(s-top)
        total=jnp.sum(e,axis=1,keepdims=True)
        p=(e*(1.0/total)).astype(jnp.bfloat16)
        o=jnp.dot(p,v_ref[0,first:first+W,:],preferred_element_type=jnp.float32)
        o_ref[rows,:]=jnp.where(low_lane,o[:QB],o[QB:]).astype(jnp.bfloat16)
        lse=top+jnp.log(total)
        lse_ref[0,rows,:]=jnp.where(low_lane,lse[:QB],lse[QB:])

def attend_forward(projected, documents, QB=256):
    T=projected.shape[1]; D=projected.shape[2]
    dcol=documents.reshape(T,1); drow=documents.reshape(1,T)
    def sp(c): return pl.BlockSpec((1,T,128),lambda h,c=c:(c,0,h))
    return pl.pallas_call(partial(fwd_kernel,QB),grid=(D//128,),
        in_specs=[sp(0),sp(1),sp(2),pl.BlockSpec((T,1),lambda h:(0,0)),pl.BlockSpec((1,T),lambda h:(0,0))],
        out_specs=[pl.BlockSpec((T,128),lambda h:(0,h)),pl.BlockSpec((1,T,128),lambda h:(h,0,0))],
        out_shape=[jax.ShapeDtypeStruct((T,D),jnp.bfloat16),jax.ShapeDtypeStruct((D//128,T,128),jnp.float32)],
        scratch_shapes=[pltpu.VMEM((T,min(T,WINDOW+QB)),jnp.float32)],
        compiler_params=pltpu.CompilerParams(vmem_limit_bytes=48*2**20),
    )(projected,projected,projected,dcol,drow)

QB = 256


def transposed_bias(bias_ref, dcol_ref, drow_ref, QB):
    reach = WINDOW // QB
    for i in range(LEN // QB):
        first = max(0, i - reach) * QB
        W = (i + 1) * QB - first
        kp = first + lax.broadcasted_iota(jnp.int32, (W, QB), 0)
        qp = i * QB + lax.broadcasted_iota(jnp.int32, (W, QB), 1)
        ok = (kp <= qp) & (dcol_ref[first : first + W, :] == drow_ref[:, i * QB : (i + 1) * QB])
        bias_ref[:W, i * QB : (i + 1) * QB] = jnp.where(ok, 0.0, masked_score)


def head_pair_backward(QB, q_ref, k_ref, v_ref, lse_ref, g_ref, bias_ref, dk_ref, dv_ref, put_dq):
    reach = WINDOW // QB
    low_lane = lax.broadcasted_iota(jnp.int32, (QB, 128), 1) < HEAD_DIM
    dk_ref[...] = jnp.zeros_like(dk_ref)
    dv_ref[...] = jnp.zeros_like(dv_ref)
    for i in range(LEN // QB):
        rows = slice(i * QB, (i + 1) * QB)
        first = max(0, i - reach) * QB
        W = (i + 1) * QB - first
        keys = slice(first, first + W)
        q = q_ref[0, rows, :] * jnp.bfloat16(HEAD_DIM**-0.5)
        zero = jnp.zeros_like(q)
        qs = jnp.concatenate([jnp.where(low_lane, q, zero), jnp.where(low_lane, zero, q)], axis=0)
        g = g_ref[rows, :]
        gs = jnp.concatenate([jnp.where(low_lane, g, zero), jnp.where(low_lane, zero, g)], axis=0)
        k = k_ref[0, keys, :]
        st = lax.dot_general(k, qs, NT, preferred_element_type=jnp.float32)
        bias = bias_ref[:W, rows]
        lse = jnp.transpose(lse_ref[0, rows, :])
        lse = jnp.concatenate([lse[0:1, :], lse[64:65, :]], axis=1)
        p = jnp.exp(st + jnp.concatenate([bias, bias], axis=1) - lse)
        dp = lax.dot_general(v_ref[0, keys, :], gs, NT, preferred_element_type=jnp.float32)
        inner = jnp.sum(p * dp, axis=0, keepdims=True)
        ds = (p * (dp - inner)).astype(jnp.bfloat16)
        dk_ref[keys, :] += jnp.dot(ds, qs, preferred_element_type=jnp.float32)
        dv_ref[keys, :] += jnp.dot(p.astype(jnp.bfloat16), gs, preferred_element_type=jnp.float32)
        dq = lax.dot_general(ds, k, TN, preferred_element_type=jnp.float32)
        put_dq(rows, (jnp.where(low_lane, dq[:QB], dq[QB:]) * HEAD_DIM**-0.5).astype(jnp.bfloat16))


def bwd_kernel(QB, q_ref, k_ref, v_ref, lse_ref, g_ref, dcol_ref, drow_ref, out_ref, bias_ref, dk_ref, dv_ref):
    @pl.when(pl.program_id(0) == 0)
    def _():
        transposed_bias(bias_ref, dcol_ref, drow_ref, QB)

    def put_dq(rows, value):
        out_ref[0, rows, :] = value

    head_pair_backward(QB, q_ref, k_ref, v_ref, lse_ref, g_ref, bias_ref, dk_ref, dv_ref, put_dq)
    out_ref[1, :, :] = dk_ref[...].astype(jnp.bfloat16)
    out_ref[2, :, :] = dv_ref[...].astype(jnp.bfloat16)


def attend_backward(projected, documents, lse, grad_mixed, QB=256):
    T=projected.shape[1]; D=projected.shape[2]
    dcol=documents.reshape(T,1); drow=documents.reshape(1,T)
    def sp(c): return pl.BlockSpec((1,T,128),lambda h,c=c:(c,0,h))
    return pl.pallas_call(partial(bwd_kernel,QB),grid=(D//128,),
        in_specs=[sp(0),sp(1),sp(2),pl.BlockSpec((1,T,128),lambda h:(h,0,0)),pl.BlockSpec((T,128),lambda h:(0,h)),pl.BlockSpec((T,1),lambda h:(0,0)),pl.BlockSpec((1,T),lambda h:(0,0))],
        out_specs=pl.BlockSpec((3,T,128),lambda h:(0,0,h)),
        out_shape=jax.ShapeDtypeStruct((3,T,D),jnp.bfloat16),
        scratch_shapes=[pltpu.VMEM((min(T,WINDOW+QB),T),jnp.float32),pltpu.VMEM((T,128),jnp.float32),pltpu.VMEM((T,128),jnp.float32)],
        compiler_params=pltpu.CompilerParams(vmem_limit_bytes=48*2**20),
    )(projected,projected,projected,lse,grad_mixed,dcol,drow)


MESH=pl.DeviceIdType.MESH
TILE=512

def flip(a,b,n):
    out=0
    bit=1
    while bit<n:
        out=out+bit*((a//bit+b//bit)%2)
        bit*=2
    return out

def gelu_pair(x):
    c=0.7978845608028654
    sq=x*x
    t=jnp.tanh(c*(x+0.044715*(x*sq)))
    half=0.5*(1.0+t)
    return x*half, half+x*(0.5*(1.0-t*t))*(c+(3*0.044715*c)*sq)

def moe_kernel(n,cap,square,send_ref,gate_ref,cot_ref,scale_ref,w_ref,
               back_ref,late_ref,chosen_ref,ret_ref,gw_ref,
               recv,gates,cot,w,gw,ret_s,gs_s,ch_s,g_s,racc,sacc,
               send_sem,recv_sem,gate_send,gate_recv,back_send,back_recv,ch_send,ch_recv,on_send,on_recv,w_sem,loc_sem,ret_sem,late_sem):
    per=TILE//cap
    tiles=n//per
    chunks=w_ref.shape[0]
    me=lax.axis_index("expert")
    barrier=pltpu.get_barrier_semaphore()
    def greet(o,_):
        pl.semaphore_signal(barrier,inc=1,device_id={"expert":flip(me,o,n)},device_id_type=MESH)
        return 0
    lax.fori_loop(1,n,greet,0)
    d=lax.axis_index("dp")
    sides=[flip(d,1,chunks),flip(d,2,chunks)] if square else []
    for side in sides:
        pl.semaphore_signal(barrier,inc=1,device_id={"dp":side},device_id_type=MESH)
    pl.semaphore_wait(barrier,n-1+len(sides))
    def on_copy(k):
        return pltpu.make_async_remote_copy(src_ref=w_ref.at[sides[k],k],dst_ref=w.at[sides[k],k],
            send_sem=on_send.at[k],recv_sem=on_recv.at[k],device_id={"dp":sides[1-k]},device_id_type=MESH)
    def on_in(k):
        across=flip(d,3,chunks)
        return pltpu.make_async_remote_copy(src_ref=w_ref.at[sides[k],k],dst_ref=w.at[across,k],
            send_sem=on_send.at[k],recv_sem=on_recv.at[k],device_id={"dp":sides[1-k]},device_id_type=MESH)
    for k in range(len(sides)): on_copy(k).start()

    def copies(src,dst,send,recv_,peer,there):
        return pltpu.make_async_remote_copy(src_ref=src,dst_ref=dst,send_sem=send.at[peer],recv_sem=recv_.at[there],
            device_id={"expert":peer},device_id_type=MESH)
    def row_copy(peer): return copies(send_ref.at[peer],recv.at[me],send_sem,recv_sem,peer,me)
    def gate_copy(peer): return copies(gate_ref.at[peer],gates.at[me],gate_send,gate_recv,peer,me)
    def row_in(src): return copies(send_ref.at[src],recv.at[src],send_sem,recv_sem,src,src)
    def gate_in(src): return copies(gate_ref.at[src],gates.at[src],gate_send,gate_recv,src,src)
    def back_copy(src): return copies(gs_s.at[src],back_ref.at[flip(src,me,n)],back_send,back_recv,src,me)
    def ch_copy(src): return copies(ch_s.at[src],chosen_ref.at[flip(src,me,n)],ch_send,ch_recv,src,me)
    def back_in(src): return copies(gs_s.at[src],back_ref.at[flip(src,me,n)],back_send,back_recv,src,src)
    def ch_in(src): return copies(ch_s.at[src],chosen_ref.at[flip(src,me,n)],ch_send,ch_recv,src,src)

    def push(o,_):
        gate_copy(flip(me,o,n)).start()
        row_copy(flip(me,o,n)).start()
        return 0
    last=(tiles-1)*per
    kept=n-late_ref.shape[0]
    lax.fori_loop(0,last-1,lambda i,c: push(last-1-i,c),0)
    own=[pltpu.make_async_copy(send_ref.at[me],recv.at[me],loc_sem.at[0]),
         pltpu.make_async_copy(gate_ref.at[me],gates.at[me],loc_sem.at[1]),
         pltpu.make_async_copy(cot_ref,cot,loc_sem.at[2]),
        ]+[pltpu.make_async_copy(w_ref.at[c],w.at[c],w_sem.at[i]) for i,c in enumerate(([d]+sides) if square else range(chunks))]
    for c in own: c.start()
    def wipe(c,_):
        gw[c]=jnp.zeros(gw.shape[1:],jnp.float32)
        return 0
    lax.fori_loop(0,chunks,wipe,0)
    for c in own: c.wait()
    own_back=pltpu.make_async_copy(gs_s.at[me],back_ref.at[0],loc_sem.at[1])
    own_ch=pltpu.make_async_copy(ch_s.at[me],chosen_ref.at[0],loc_sem.at[0])
    def keep(o): return pltpu.make_async_copy(gs_s.at[flip(me,o,n)],late_ref.at[o-kept],late_sem.at[o-kept])

    def tile(t,_):
        @pl.when(t==1)
        def _():
            lax.fori_loop(last,n,push,0)
        block=flip(me//per,t,tiles)
        def arrive(j,_):
            src=block*per+j
            @pl.when(src!=me)
            def _():
                gate_in(src).wait_recv()
                row_in(src).wait_recv()
            return 0
        lax.fori_loop(0,per,arrive,0)
        at=pl.ds(pl.multiple_of(block*per,per),per)
        rows=pl.ds(pl.multiple_of(block*TILE,TILE),TILE)
        gate=jnp.transpose(jnp.sum(gates[at],axis=0))[:,0:1]
        scale=jnp.concatenate([jnp.broadcast_to(scale_ref[pl.ds(block*per+j,1),0:1],(cap,1)) for j in range(per)],axis=0)
        grad_out=cot[rows,:].astype(jnp.float32)*scale
        g_s[...]=(gate*grad_out).astype(jnp.bfloat16)
        racc[...]=jnp.zeros_like(racc)
        sacc[...]=jnp.zeros_like(sacc)
        def chunk(i,_):
            c=flip(d,i,chunks)
            if square:
                @pl.when((t==0)&(i==chunks-1))
                def _():
                    for k in range(2): on_in(k).wait_recv()
            x=recv[at].reshape(TILE,recv.shape[2])
            g=g_s[...]
            act,slope=gelu_pair(jnp.dot(x,w[c,0],preferred_element_type=jnp.float32))
            a=act.astype(jnp.bfloat16)
            ga=jnp.dot(g,w[c,1],preferred_element_type=jnp.float32).astype(jnp.bfloat16)
            gp=(ga.astype(jnp.float32)*slope).astype(jnp.bfloat16)
            racc[...]+=lax.dot_general(a,w[c,1],NT,preferred_element_type=jnp.float32)
            sacc[...]+=lax.dot_general(gp,w[c,0],NT,preferred_element_type=jnp.float32)
            gw[c,0]+=lax.dot_general(x,gp,TN,preferred_element_type=jnp.float32)
            gw[c,1]+=lax.dot_general(g,a,TN,preferred_element_type=jnp.float32)
            @pl.when(t==tiles-1)
            def _():
                w[c]=gw[c].astype(jnp.bfloat16)
                pltpu.make_async_copy(w.at[c],gw_ref.at[c],w_sem.at[c]).start()
            return 0
        lax.fori_loop(0,chunks,chunk,0)
        gs_s[at]=sacc[...].astype(jnp.bfloat16).reshape(per,cap,recv.shape[2])
        def give(j,_):
            src=block*per+j
            o=flip(src,me,n)
            @pl.when((src!=me)&(o<kept))
            def _():
                back_copy(src).start()
            @pl.when(src==me)
            def _():
                own_back.start()
            @pl.when(o>=kept)
            def _():
                keep(o).start()
            return 0
        lax.fori_loop(0,per,give,0)
        ret=racc[...].astype(jnp.bfloat16)
        ret_s[at]=ret.reshape(per,cap,recv.shape[2])
        pltpu.make_async_copy(ret_s.at[at],ret_ref.at[at],ret_sem.at[t]).start()
        grad_out=cot[rows,:].astype(jnp.float32)*scale
        chosen=jnp.sum(grad_out*ret.astype(jnp.float32),axis=1,keepdims=True)*gate*(1.0-gate)
        chosen=jnp.transpose(jnp.broadcast_to(chosen,(TILE,128)))[0:8,:]
        def tell(j,_):
            src=block*per+j
            ch_s[src]=chosen
            @pl.when(src!=me)
            def _():
                ch_copy(src).start()
            @pl.when(src==me)
            def _():
                own_ch.start()
            return 0
        lax.fori_loop(0,per,tell,0)
        return 0
    lax.fori_loop(0,tiles,tile,0)
    own_ch.wait()
    own_back.wait()
    def settle(o,_):
        peer=flip(me,o,n)
        gate_copy(peer).wait_send()
        row_copy(peer).wait_send()
        ch_copy(peer).wait_send()
        ch_in(peer).wait_recv()
        @pl.when(o<kept)
        def _():
            back_copy(peer).wait_send()
            back_in(peer).wait_recv()
        @pl.when(o>=kept)
        def _():
            keep(o).wait()
        return 0
    lax.fori_loop(1,n,settle,0)
    def stored(t,_):
        block=flip(me//per,t,tiles)
        at=pl.ds(pl.multiple_of(block*per,per),per)
        pltpu.make_async_copy(ret_s.at[at],ret_ref.at[at],ret_sem.at[t]).wait()
        return 0
    lax.fori_loop(0,tiles,stored,0)
    for c in range(chunks): pltpu.make_async_copy(w.at[c],gw_ref.at[c],w_sem.at[c]).wait()
    for k in range(len(sides)): on_copy(k).wait_send()

def late_kernel(n,gs_ref,out_ref,send_sem,recv_sem):
    count=gs_ref.shape[0]
    me=lax.axis_index("expert")
    barrier=pltpu.get_barrier_semaphore()
    def greet(k,_):
        pl.semaphore_signal(barrier,inc=1,device_id={"expert":flip(me,n-count+k,n)},device_id_type=MESH)
        return 0
    lax.fori_loop(0,count,greet,0)
    pl.semaphore_wait(barrier,count)
    def copy(k):
        return pltpu.make_async_remote_copy(src_ref=gs_ref.at[k],dst_ref=out_ref.at[k],send_sem=send_sem.at[k],recv_sem=recv_sem.at[k],
            device_id={"expert":flip(me,n-count+k,n)},device_id_type=MESH)
    def go(k,_):
        copy(k).start()
        return 0
    lax.fori_loop(0,count,go,0)
    def end(k,_):
        copy(k).wait()
        return 0
    lax.fori_loop(0,count,end,0)

def moe(send_rows,gate_slots,cot,scale,weights,square):
    n,cap,D=send_rows.shape
    chunks,_,_,FC=weights.shape
    per=TILE//cap
    any_=pl.BlockSpec(memory_space=pl.ANY)
    bf=jnp.bfloat16; f32=jnp.float32
    dma=pltpu.SemaphoreType.DMA
    flops=6*2*n*cap*D*chunks*FC
    back,late,chosen,ret,gw=pl.pallas_call(partial(moe_kernel,n,cap,square),
        out_shape=[jax.ShapeDtypeStruct((n-per//2,cap,D),bf),jax.ShapeDtypeStruct((per//2,cap,D),bf),jax.ShapeDtypeStruct((n,8,TILE),f32),
                   jax.ShapeDtypeStruct((n,cap,D),bf),jax.ShapeDtypeStruct(weights.shape,bf)],
        in_specs=[any_,any_,any_,pl.BlockSpec(memory_space=pltpu.VMEM),any_],
        out_specs=[any_]*5,
        scratch_shapes=[pltpu.VMEM((n,cap,D),bf),pltpu.VMEM((n,8,TILE),f32),pltpu.VMEM((n*cap,D),bf),
            pltpu.VMEM(weights.shape,bf),pltpu.VMEM(weights.shape,f32),pltpu.VMEM((n,cap,D),bf),pltpu.VMEM((n,cap,D),bf),
            pltpu.VMEM((n,8,TILE),f32),pltpu.VMEM((TILE,D),bf),pltpu.VMEM((TILE,D),f32),pltpu.VMEM((TILE,D),f32)]
            +[dma((n,))]*8+[dma((2,)),dma((2,)),dma((chunks,)),dma((3,)),dma((n//per,)),dma((per//2,))],
        compiler_params=pltpu.CompilerParams(vmem_limit_bytes=62*2**20,collective_id=1,has_side_effects=True),
        cost_estimate=pl.CostEstimate(flops=flops,bytes_accessed=40*2**20,transcendentals=0),
    )(send_rows,gate_slots,cot,scale,weights)
    return back,late,chosen,ret,gw

def send_late(late,n):
    per,cap,D=late.shape
    any_=pl.BlockSpec(memory_space=pl.ANY)
    bf=jnp.bfloat16
    dma=pltpu.SemaphoreType.DMA
    return pl.pallas_call(partial(late_kernel,n),
        out_shape=jax.ShapeDtypeStruct((per,cap,D),bf),in_specs=[any_],out_specs=any_,
        scratch_shapes=[dma((per,)),dma((per,))],
        compiler_params=pltpu.CompilerParams(collective_id=5,has_side_effects=True),
        cost_estimate=pl.CostEstimate(flops=0,bytes_accessed=100*2**20,transcendentals=0),
    )(late)


def near(dps,pairs):
    d=lax.axis_index("dp"); me=lax.axis_index("expert")
    core=me%2; pair=me//2
    partner={"expert":me+1-2*core}
    over=[((d+k)%dps,{"dp":(d+k)%dps}) for k in range(1,dps)]
    along=[((pair+k)%pairs,{"expert":2*((pair+k)%pairs)+core}) for k in range(1,pairs)]
    return d,pair,core,partner,over,along

def greet_all(devices):
    barrier=pltpu.get_barrier_semaphore()
    for dev in devices:
        pl.semaphore_signal(barrier,inc=1,device_id=dev,device_id_type=MESH)
    pl.semaphore_wait(barrier,len(devices))

def remote(src,dst,send,recv,dev):
    return pltpu.make_async_remote_copy(src_ref=src,dst_ref=dst,send_sem=send,recv_sem=recv,device_id=dev,device_id_type=MESH)

def upright(row):
    return jnp.transpose(row.astype(jnp.float32))[:, 0:1].astype(jnp.int32)


def head_kernel(dps, pairs, n, cap, w_ref, v_ref, x_ref, cot_ref, order_ref, counts_ref, drow_ref, ew_ref,
                w_out, vec_out, slot_out, cot_out, proj_out, normed_out, mixed_out, lse_out, hidden_out,
                gate_out, send_out, tile_out, ew_out,
                ew32, ew, both, blk, vboth, vblk, w, vall, slots, unit, normed, proj, mixed, lse, bias, sent, cots, sends,
                tiles, s1, r1, loc, zs, zr, vzs, vzr, ds_, dr, vds, vdr, ps, pr, cs, cr, ewl, xs, xr, ys, yr, out_sem, send_sem):
    r = w_ref.shape[1]
    R = 2 * r
    T, D = x_ref.shape
    d, pair, core, partner, over, along = near(dps, pairs)
    me = lax.axis_index("expert")
    bf, f32 = jnp.bfloat16, jnp.float32
    ew_load = pltpu.make_async_copy(ew_ref.at[0], ew32, ewl.at[0])
    ew_load.start()
    barrier = pltpu.get_barrier_semaphore()

    def greet(o, _):
        pl.semaphore_signal(barrier, inc=1, device_id={"expert": flip(me, o, n)}, device_id_type=MESH)
        return 0

    lax.fori_loop(1, n, greet, 0)
    for _, dev in over:
        pl.semaphore_signal(barrier, inc=1, device_id=dev, device_id_type=MESH)
    pl.semaphore_wait(barrier, n - 1 + dps - 1)

    side_x, side_y = flip(d, 1, dps), flip(d, 2, dps)
    to_x, to_y = {"dp": side_x}, {"dp": side_y}

    def x_copy(src, slot, m):
        return remote(src, ew_out.at[slot, m], xs.at[slot, m], xr.at[slot, m], to_x)

    def y_copy(src, slot, m):
        return remote(src, ew_out.at[slot, m], ys.at[slot, m], yr.at[slot, m], to_y)

    mine = pl.ds(pl.multiple_of(core * r, 8), r)
    half = pl.ds(core * 2, 2)
    rest = pl.ds(2 - core * 2, 2)

    def rows(dd, q):
        return pl.ds(pl.multiple_of((dd * pairs + q) * R, 16), R)

    c1 = [
        remote(w_ref, both.at[:, mine, :], s1.at[0], r1.at[0], partner),
        remote(v_ref, vboth.at[core], s1.at[1], r1.at[1], partner),
    ]
    for c in c1:
        c.start()
    both[:, mine, :] = w_ref[...]
    vboth[core] = v_ref[...]
    for c in c1:
        c.wait()
    blk[...] = both[...].astype(bf)
    vblk[...] = (vboth[0] + vboth[1]).astype(bf)
    w[:, rows(d, pair), :] = blk[...]
    vall[d, pair] = vblk[...]
    def along_copy(q, dev):
        return remote(blk.at[half], w.at[half, rows(d, pair), :], zs.at[q], zr.at[pair], dev)

    def over_copy(dd, q, dev):
        here = w.at[half, rows(d, q), :]
        return remote(here, here, ds_.at[dd, q], dr.at[d, q], dev)

    def hand(dd, q):
        here = w.at[half, rows(dd, q), :]
        return remote(here, here, ps.at[dd, q], pr.at[dd, q], partner)

    def v_along(q, dev):
        return remote(vblk, vall.at[d, pair], vzs.at[q], vzr.at[pair], dev)

    def v_over(dd, dev):
        return remote(vall.at[d], vall.at[d], vds.at[dd], vdr.at[d], dev)

    for q, dev in along:
        along_copy(q, dev).start()
        v_along(q, dev).start()
    for dd, dev in over:
        over_copy(dd, pair, dev).start()

    tokens_across = lax.broadcasted_iota(jnp.int32, (T, T), 1)
    position = lax.broadcasted_iota(jnp.int32, (8, T), 1)
    sorted_slot, end = position, 0
    for e in range(n):
        count = counts_ref[0, e]
        end = end + count
        sorted_slot = sorted_slot + jnp.where(position >= end, cap - count, 0)
    slot_col = upright(sorted_slot)
    order_col = upright(jnp.broadcast_to(order_ref[...], (8, T)))
    slots[...] = jnp.broadcast_to(
        jnp.sum(jnp.where(order_col == tokens_across, slot_col, 0), axis=0, keepdims=True), (8, T)
    )
    doc_col = upright(jnp.broadcast_to(drow_ref[...], (8, T)))

    def pick(p):
        here = lax.broadcasted_iota(jnp.int32, (cap, T), 0) + p * cap
        return here == slots[0:1, :]

    def cot_copy(p):
        return remote(cots.at[p], cot_out.at[me], cs.at[p], cr.at[me], {"expert": p})

    def cot_in(p):
        return remote(cots.at[p], cot_out.at[p], cs.at[p], cr.at[p], {"expert": p})

    def place(i, _):
        p = flip(me, n - 1 - i, n)
        cots[p] = jnp.dot(pick(p).astype(bf), cot_ref[...], preferred_element_type=f32).astype(bf)

        return 0

    groups = [d] + [x[0] for x in over]
    lax.fori_loop(0, n // 2, place, 0)
    for q, dev in along:
        here = w.at[half, rows(d, q), :]
        remote(here, here, zs.at[q], zr.at[q], dev).wait_recv()
        for dd, dev2 in over:
            over_copy(dd, q, dev2).start()
        hand(d, q).start()
    for q, dev in along:
        remote(vblk, vall.at[d, q], vzs.at[q], vzr.at[q], dev).wait_recv()
    for dd, dev in over:
        v_over(dd, dev).start()
    ew_load.wait()
    for m in range(2):
        ew[m] = ew32[m].astype(bf)
    own_ew = pltpu.make_async_copy(ew, ew_out.at[d], ewl.at[0])
    own_ew.start()
    for m in range(2):
        x_copy(ew.at[m], d, m).start()
        y_copy(ew.at[1 - m], d, 1 - m).start()
    lax.fori_loop(n // 2, n, place, 0)

    def give(i, _):
        cot_copy(flip(me, n - 1 - i, n)).start()
        return 0

    lax.fori_loop(0, n - 1, give, 0)
    own_cot = pltpu.make_async_copy(cots.at[me], cot_out.at[me], loc.at[0])
    own_cot.start()

    def unit_rows(b):
        at = pl.ds(b * 256, 256)
        x = x_ref[at, :].astype(f32)
        center = x - jnp.mean(x, axis=-1, keepdims=True)
        unit[at, :] = center * lax.rsqrt(jnp.mean(center * center, axis=-1, keepdims=True) + norm_eps)

    for b in range(T // 256):
        unit_rows(b)
    for i in range(LEN // QB):
        first = max(0, i - WINDOW // QB) * QB
        W = (i + 1) * QB - first
        qp = i * QB + lax.broadcasted_iota(jnp.int32, (QB, W), 0)
        kp = first + lax.broadcasted_iota(jnp.int32, (QB, W), 1)
        ok = (kp <= qp) & (doc_col[i * QB : (i + 1) * QB, :] == drow_ref[:, first : first + W])
        bias[i * QB : (i + 1) * QB, :W] = jnp.where(ok, 0.0, masked_score)
    for q in [pair] + [x[0] for x in along]:
        for dd, dev in over:
            here = w.at[half, rows(dd, q), :]
            remote(here, here, ds_.at[dd, q], dr.at[dd, q], dev).wait_recv()
            hand(dd, q).start()
    for dd, dev in over:
        remote(vall.at[dd], vall.at[dd], vds.at[dd], vdr.at[dd], dev).wait_recv()
    vec = jnp.zeros(vec_out.shape, f32)
    for dd in range(dps):
        for q in range(pairs):
            vec = vec + vall[dd, q].astype(f32)
    vec_out[...] = vec
    slot_out[...] = slots[...]
    normed[...] = (unit[...] * vec_out[0:1, :]).astype(bf)

    def from_partner(dd, q):
        there = w.at[rest, rows(dd, q), :]
        remote(there, there, ps.at[dd, q], pr.at[dd, q], partner).wait_recv()

    for dd, dev in over:
        from_partner(dd, pair)
    for q, _ in along:
        for dd in groups:
            from_partner(dd, q)

    outs = [
        pltpu.make_async_copy(w, w_out, out_sem.at[0]),
        pltpu.make_async_copy(normed, normed_out, out_sem.at[1]),
    ]
    for c in outs:
        c.start()

    def project(i, _):
        c = i // 2
        at = pl.ds(pl.multiple_of(i % 2 * (T // 2), T // 2), T // 2)
        proj[c, at, :] = jnp.dot(normed[at, :], w[c], preferred_element_type=f32).astype(bf)
        return 0

    lax.fori_loop(0, 6, project, 0)
    outs.append(pltpu.make_async_copy(proj, proj_out, out_sem.at[2]))
    outs[-1].start()
    low_lane = lax.broadcasted_iota(jnp.int32, (QB, 128), 1) < HEAD_DIM

    def attend(h, _):
        lanes = pl.ds(pl.multiple_of(h * 128, 128), 128)
        for i in range(LEN // QB):
            here = slice(i * QB, (i + 1) * QB)
            first = max(0, i - WINDOW // QB) * QB
            W = (i + 1) * QB - first
            keys = slice(first, first + W)
            q = proj[0, here, lanes] * jnp.bfloat16(HEAD_DIM**-0.5)
            zero = jnp.zeros_like(q)
            qs = jnp.concatenate([jnp.where(low_lane, q, zero), jnp.where(low_lane, zero, q)], axis=0)
            s = lax.dot_general(qs, proj[1, keys, lanes], NT, preferred_element_type=f32)
            s = (s.reshape(2, QB, W) + bias[here, :W][None]).reshape(2 * QB, W)
            top = jnp.max(s, axis=1, keepdims=True)
            e = jnp.exp(s - top)
            total = jnp.sum(e, axis=1, keepdims=True)
            p = (e * (1.0 / total)).astype(bf)
            o = jnp.dot(p, proj[2, keys, lanes], preferred_element_type=f32)
            mixed[here, lanes] = jnp.where(low_lane, o[:QB], o[QB:]).astype(bf)
            ends = top + jnp.log(total)
            lse[h, here, :] = jnp.where(low_lane, ends[:QB], ends[QB:])
        return 0

    lax.fori_loop(0, D // 128, attend, 0)
    outs += [
        pltpu.make_async_copy(mixed, mixed_out, out_sem.at[3]),
        pltpu.make_async_copy(lse, lse_out, out_sem.at[4]),
    ]
    outs[-2].start()
    outs[-1].start()
    E = vec_out.shape[0] - 2
    hidden = unit

    def finish(b, _):
        at = pl.ds(pl.multiple_of(b * 256, 256), 256)
        state = x_ref[at, :].astype(f32) + jnp.dot(mixed[at, :], w[3], preferred_element_type=f32)
        hidden[at, :] = state
        center = state - jnp.mean(state, axis=-1, keepdims=True)
        spread = jnp.mean(center * center, axis=-1, keepdims=True)
        two = center * lax.rsqrt(spread + norm_eps) * vec_out[1:2, :]
        sent[at, :] = two.astype(bf)
        which = lax.broadcasted_iota(jnp.int32, (vec_out.shape[0], 256), 0) - 2
        chosen = (which == slots[0:1, at] // cap).astype(bf)
        rows_c = lax.dot_general(chosen, vec_out[...].astype(bf), TN, preferred_element_type=f32)
        logit = jnp.sum(two * rows_c, axis=1, keepdims=True)
        gate = 1.0 / (1.0 + jnp.exp(-logit))
        gate_out[:, at] = jnp.transpose(jnp.broadcast_to(gate, (256, 128)))[0:8, :]
        return 0

    lax.fori_loop(0, T // 256, finish, 0)
    outs.append(pltpu.make_async_copy(hidden, hidden_out, out_sem.at[5]))
    outs[-1].start()
    tiles[...] = jnp.zeros(tiles.shape, f32)
    part = pl.ds(pl.multiple_of(me % (TILE // cap) * cap, 128), cap)

    def fill(p, _):
        chosen = pick(p)
        sends[p] = jnp.dot(chosen.astype(bf), sent[...], preferred_element_type=f32).astype(bf)
        tiles[p, :, part] = lax.dot_general(
            gate_out[...], chosen.astype(f32), NT, precision=lax.Precision.HIGHEST, preferred_element_type=f32
        )
        pltpu.make_async_copy(sends.at[p], send_out.at[p], send_sem).start()
        return 0

    lax.fori_loop(0, n, fill, 0)
    outs.append(pltpu.make_async_copy(tiles, tile_out, out_sem.at[6]))
    outs[-1].start()
    for q, dev in along:
        along_copy(q, dev).wait_send()
        v_along(q, dev).wait_send()
        hand(d, q).wait_send()
    for dd, dev in over:
        v_over(dd, dev).wait_send()
        for q in [pair] + [x[0] for x in along]:
            over_copy(dd, q, dev).wait_send()
            hand(dd, q).wait_send()

    def settle(o, _):
        p = flip(me, o, n)
        cot_copy(p).wait_send()
        cot_in(p).wait_recv()
        return 0

    lax.fori_loop(1, n, settle, 0)
    pltpu.make_async_copy(cots.at[me], cot_out.at[me], loc.at[0]).wait()
    own_ew.wait()
    for m in range(2):
        x_copy(ew.at[m], d, m).wait_send()
        y_copy(ew.at[m], d, m).wait_send()
        x_copy(ew.at[m], side_x, m).wait_recv()
        y_copy(ew.at[m], side_y, m).wait_recv()
    for c in outs:
        c.wait()
    pltpu.make_async_copy(sends, send_out, send_sem).wait()


def head(weights, vectors, inputs, cotangent, token_order, counts, documents, expert_weights, dps, n, cap):
    pairs = n // 2
    m, r, D = weights.shape
    T = inputs.shape[0]
    k = vectors.shape[0]
    f32, bf = jnp.float32, jnp.bfloat16
    dma = pltpu.SemaphoreType.DMA
    any_ = pl.BlockSpec(memory_space=pl.ANY)
    vm = pl.BlockSpec(memory_space=pltpu.VMEM)
    dev = lax.axis_index("dp") * n + lax.axis_index("expert")
    K = (k + 15) // 16 * 16
    placed = lax.dynamic_update_slice(jnp.zeros((K, D), f32), vectors, (0, dev * r))
    shape = jax.ShapeDtypeStruct
    grid = lambda: dma((dps, pairs))
    return pl.pallas_call(
        partial(head_kernel, dps, pairs, n, cap),
        out_shape=[
            shape((m, D, D), bf), shape((K, D), f32), shape((8, T), jnp.int32), shape((n, cap, D), bf),
            shape((3, T, D), bf), shape((T, D), bf), shape((T, D), bf), shape((D // 128, T, 128), f32),
            shape((T, D), f32), shape((8, T), f32), shape((n, cap, D), bf), shape((n, 8, TILE), f32),
            shape((dps,) + expert_weights.shape[1:], bf),
        ],
        in_specs=[vm] * 5 + [pl.BlockSpec(memory_space=pltpu.SMEM), vm, any_],
        out_specs=[any_, vm, vm, any_, any_, any_, any_, any_, any_, vm, any_, any_, any_],
        scratch_shapes=[
            pltpu.VMEM(expert_weights.shape[1:], f32), pltpu.VMEM(expert_weights.shape[1:], bf),
            pltpu.VMEM((m, 2 * r, D), f32), pltpu.VMEM((m, 2 * r, D), bf), pltpu.VMEM((2, K, D), f32),
            pltpu.VMEM((K, D), bf), pltpu.VMEM((m, D, D), bf), pltpu.VMEM((dps, pairs, K, D), bf),
            pltpu.VMEM((8, T), jnp.int32), pltpu.VMEM((T, D), f32), pltpu.VMEM((T, D), bf),
            pltpu.VMEM((3, T, D), bf), pltpu.VMEM((T, D), bf), pltpu.VMEM((D // 128, T, 128), f32),
            pltpu.VMEM((T, min(T, WINDOW + QB)), f32), pltpu.VMEM((T, D), bf), pltpu.VMEM((n, cap, D), bf),
            pltpu.VMEM((n, cap, D), bf), pltpu.VMEM((n, 8, TILE), f32),
            dma((2,)), dma((2,)), dma((1,)), dma((pairs,)), dma((pairs,)), dma((pairs,)), dma((pairs,)),
            grid(), grid(), dma((dps,)), dma((dps,)), grid(), grid(), dma((n,)), dma((n,)),
            dma((1,)), dma((dps, 2)), dma((dps, 2)), dma((dps, 2)), dma((dps, 2)), dma((7,)), dma(()),
        ],
        compiler_params=pltpu.CompilerParams(
            vmem_limit_bytes=60 * 2**20, collective_id=2, has_side_effects=True
        ),
        cost_estimate=pl.CostEstimate(flops=20 * T * D * D, bytes_accessed=200 * 2**20, transcendentals=0),
    )(weights, placed, inputs, cotangent, token_order, counts, documents, expert_weights)


def tail_kernel(dps, pairs, cap, q_ref, k_ref, v_ref, lse_ref, drow_ref, vec_ref, slot_ref, gate_ref,
                scale_ref, chosen_ref, x_ref, mixed_ref, prod_ref, w_ref, in_ref, late_ref, back_ref, cot_ref,
                hidden_ref,
                out_ref, vec_out, dx_ref, block_ref,
                bias_ref, dk_ref, dv_ref, left, right, got, own, total, in2, tb, in3, u, in4, w, gh, xin,
                ret, hid, back, cot, g_ref, chs, dcol_ref,
                ls, s1, r1, s2, r2, s3, r3, s4, r4, rs, rr, bs, br, own_sem, dx_sem, block_sem):
    h = pl.program_id(0)
    n = 2 * pairs
    count = late_ref.shape[0]
    kept = n - count
    early = kept * cap
    per = TILE // cap
    me = lax.axis_index("expert")
    d, pair, core, partner, over, along = near(dps, pairs)
    rows = out_ref.shape[1]
    R = 2 * rows
    T, D = x_ref.shape
    bf, f32 = jnp.bfloat16, jnp.float32
    B = 256
    loads = [
        pltpu.make_async_copy(back_ref, back.at[pl.ds(0, kept)], ls.at[0]),
        pltpu.make_async_copy(hidden_ref, hid, ls.at[1]),
        pltpu.make_async_copy(cot_ref, cot, ls.at[2]),
        pltpu.make_async_copy(w_ref, w, ls.at[3]),
        pltpu.make_async_copy(mixed_ref, left.at[1], ls.at[4]),
        pltpu.make_async_copy(x_ref, left.at[0], ls.at[5]),
        pltpu.make_async_copy(in_ref, xin, ls.at[6]),
    ]

    def product(m):
        return lax.dot_general(left[m // 3], right[m], TN, preferred_element_type=f32)

    def ret_copy(peer):
        return remote(prod_ref.at[peer], ret.at[me], rs.at[peer], rr.at[me], {"expert": peer})

    def ret_in(peer):
        return remote(prod_ref.at[peer], ret.at[peer], rs.at[peer], rr.at[peer], {"expert": peer})

    own_ret = pltpu.make_async_copy(prod_ref.at[me], ret.at[me], own_sem)

    def late_copy(k):
        return remote(late_ref.at[k], back.at[kept + k], bs.at[k], br.at[k], {"expert": flip(me, kept + k, n)})

    def to_partner(i):
        return remote(total.at[i], got.at[i], s1.at[i], r1.at[i], partner)

    def column(row):
        return jnp.transpose(row)[:, 0:1]

    def normal(x):
        center = x - jnp.mean(x, axis=-1, keepdims=True)
        scale = lax.rsqrt(jnp.mean(center * center, axis=-1, keepdims=True) + norm_eps)
        return center * scale, scale

    def normal_back(grad, unit, scale, gain):
        gu = grad * gain
        return scale * (
            gu - jnp.mean(gu, axis=-1, keepdims=True) - unit * jnp.mean(gu * unit, axis=-1, keepdims=True)
        )

    def offset_slots(at):
        slot = slot_ref[:, at]
        return flip(slot // cap, me, n) * cap + slot % cap

    def match(slot_rows, first, count):
        here = column(slot_rows.astype(f32))
        return here == (first + lax.broadcasted_iota(jnp.int32, (B, count), 1)).astype(f32)

    @pl.when(h == 0)
    def _():
        for c in loads:
            c.start()
        barrier = pltpu.get_barrier_semaphore()

        def greet(o, _):
            pl.semaphore_signal(barrier, inc=1, device_id={"expert": flip(me, o, n)}, device_id_type=MESH)
            return 0

        lax.fori_loop(1, n, greet, 0)
        for _, dev in over:
            pl.semaphore_signal(barrier, inc=1, device_id=dev, device_id_type=MESH)
        pl.semaphore_wait(barrier, n - 1 + dps - 1)
        for j in range(count):
            late_copy(j).start()

        def send(i, _):
            ret_copy(flip(me, 1 + i, n)).start()
            return 0

        lax.fori_loop(0, n // 2 - 1, send, 0)
        own_ret.start()
        dcol_ref[...] = upright(jnp.broadcast_to(drow_ref[...], (8, T)))
        transposed_bias(bias_ref, dcol_ref, drow_ref, QB)
        part = pl.ds(pl.multiple_of(me % per * cap, 128), cap)
        for o in range(n):
            chs[:, o * cap : (o + 1) * cap] = chosen_ref[o, :, part]
        loads[0].wait()

        def first_rows(b, _):
            at = pl.ds(pl.multiple_of(b * B, B), B)
            pick = match(offset_slots(at), 0, early).astype(bf)
            gh[at, :] = jnp.dot(pick, back[pl.ds(0, kept)].reshape(early, D), preferred_element_type=f32)
            return 0

        lax.fori_loop(0, T // B, first_rows, 0)
        vec_out[...] = jnp.zeros(vec_out.shape, f32)
        for c in loads[1:4]:
            c.wait()
        for j in range(count):
            late_copy(j).wait_recv()
        lax.fori_loop(n // 2 - 1, n - 1, send, 0)

        def second(b, _):
            at = pl.ds(pl.multiple_of(b * B, B), B)
            slot_rows = offset_slots(at)
            all_slots = match(slot_rows, 0, n * cap)
            chosen = jnp.sum(jnp.where(all_slots, chs[0:1, :], 0.0), axis=1, keepdims=True)
            pick = match(slot_rows, early, count * cap).astype(bf)
            sent = gh[at, :] + jnp.dot(
                pick, back[pl.ds(kept, count)].reshape(count * cap, D), preferred_element_type=f32
            )
            which = lax.broadcasted_iota(jnp.int32, (vec_ref.shape[0], B), 0) - 2
            expert = which == slot_ref[0:1, at] // cap
            centroid = lax.dot_general(
                expert.astype(bf), vec_ref[...].astype(bf), TN, preferred_element_type=f32
            )
            grad = sent + chosen * centroid
            unit, scale = normal(hid[at, :])
            gain = vec_ref[1:2, :]
            chosen_row = jnp.transpose(jnp.broadcast_to(chosen, (B, 128)))[0:1, :]
            vec_out[...] += jnp.dot(
                jnp.where(expert, chosen_row, 0.0), unit * gain,
                precision=lax.Precision.HIGHEST, preferred_element_type=f32,
            )
            vec_out[1:2, :] += jnp.sum(grad * unit, axis=0, keepdims=True)
            total_grad = cot[at, :].astype(f32) * scale_ref[0:1, 0:1] + normal_back(grad, unit, scale, gain)
            gh[at, :] = total_grad
            low = total_grad.astype(bf)
            right[3, at, :] = low
            g_ref[at, :] = lax.dot_general(low, w[3], NT, preferred_element_type=f32).astype(bf)
            return 0

        lax.fori_loop(0, T // B, second, 0)
        loads[4].wait()
        out = product(3)

        @pl.when(core == 0)
        def _():
            total[1] = out.astype(bf)
            to_partner(1).start()

        @pl.when(core == 1)
        def _():
            own[1] = out

    lanes = pl.ds(pl.multiple_of(h * 128, 128), 128)

    def put_dq(r, value):
        right[0, r, lanes] = value

    head_pair_backward(
        QB, q_ref, k_ref, v_ref, lse_ref, g_ref.at[:, lanes], bias_ref, dk_ref, dv_ref, put_dq
    )
    right[1, :, lanes] = dk_ref[...].astype(bf)
    right[2, :, lanes] = dv_ref[...].astype(bf)

    @pl.when(h == pl.num_programs(0) - 1)
    def _():
        loads[5].wait()

        @pl.when(core == 0)
        def _():
            total[0] = product(2).astype(bf)
            to_partner(0).start()
            own[0] = product(0)
            own[1] = product(1)

        @pl.when(core == 1)
        def _():
            total[0] = product(0).astype(bf)
            to_partner(0).start()
            total[1] = product(1).astype(bf)
            to_partner(1).start()
            own[0] = product(2)

        for i in range(2):
            to_partner(i).wait_send()
            to_partner(i).wait_recv()
            total[i] = (own[i] + got[i].astype(f32)).astype(bf)

        order = along + [(pair, None)]

        def piece(dd, q):
            return pl.ds(pl.multiple_of((dd * pairs + q) * R, 16), R)

        c2 = []
        for q, _ in order:
            for dd, dev in over:
                c = remote(total.at[:, piece(dd, q), :], in2.at[d, q], s2.at[dd, q], r2.at[d, q], dev)
                c.start()
                c2.append(c)
        loads[6].wait()

        def norm_one(b, _):
            at = pl.ds(pl.multiple_of(b * B, B), B)
            gn = sum(
                lax.dot_general(right[c, at, :], w[c], NT, preferred_element_type=f32) for c in range(3)
            )
            unit, scale = normal(xin[at, :].astype(f32))
            vec_out[0:1, :] += jnp.sum(gn * unit, axis=0, keepdims=True)
            gh[at, :] += normal_back(gn, unit, scale, vec_ref[0:1, :])
            return 0

        lax.fori_loop(0, T // B, norm_one, 0)
        dx = pltpu.make_async_copy(gh, dx_ref, dx_sem)
        dx.start()
        c3 = []
        for q, zdev in order:
            acc = total[:, piece(d, q), :].astype(f32)
            for dd, dev in over:
                remote(in2.at[dd, q], in2.at[dd, q], s2.at[dd, q], r2.at[dd, q], dev).wait_recv()
                acc = acc + in2[dd, q].astype(f32)
            if zdev is None:
                u[...] = acc
            else:
                tb[q] = acc.astype(bf)
                c = remote(tb.at[q], in3.at[pair], s3.at[q], r3.at[pair], zdev)
                c.start()
                c3.append(c)

        def settle(o, _):
            peer = flip(me, o, n)
            ret_copy(peer).wait_send()
            ret_in(peer).wait_recv()
            return 0

        lax.fori_loop(1, n, settle, 0)
        own_ret.wait()

        def add_rows(b, _):
            at = pl.ds(pl.multiple_of(b * B, B), B)
            pick = match(slot_ref[:, at], 0, n * cap).astype(bf)
            got_rows = jnp.dot(pick, ret[...].reshape(n * cap, D), preferred_element_type=f32)
            hid[at, :] += column(gate_ref[:, at]) * got_rows
            return 0

        lax.fori_loop(0, T // B, add_rows, 0)
        block = pltpu.make_async_copy(hid, block_ref, block_sem)
        block.start()
        acc = u[...]
        for q, dev in along:
            remote(in3.at[q], in3.at[q], s3.at[q], r3.at[q], dev).wait_recv()
            acc = acc + in3[q].astype(f32)
        u[...] = acc
        theirs = pl.ds(pl.multiple_of((1 - core) * rows, 8), rows)
        mine = pl.ds(pl.multiple_of(core * rows, 8), rows)
        c4 = remote(u.at[:, theirs, :], in4, s4, r4, partner)
        c4.start()
        out_ref[pl.ds(2 * core, 2)] = u[:, mine, :]
        c4.wait_recv()
        out_ref[pl.ds(2 - 2 * core, 2)] = in4[...]
        for c in c2 + c3 + [c4]:
            c.wait_send()
        for j in range(count):
            late_copy(j).wait_send()
        dx.wait()
        block.wait()


def tail(projected, lse, documents, vec, slot_rows, gate_rows, scale, chosen, normed, mixed, produced, dense_low,
         inputs, late, back, cotangent, hidden, dps, n):
    pairs = n // 2
    _, T, D = projected.shape
    rows = D // (dps * n)
    R = 2 * rows
    cap = produced.shape[1]
    count = late.shape[0]
    f32, bf = jnp.float32, jnp.bfloat16
    dma = pltpu.SemaphoreType.DMA
    any_ = pl.BlockSpec(memory_space=pl.ANY)

    def sp(c):
        return pl.BlockSpec((1, T, 128), lambda h, c=c: (c, 0, h))

    def fixed(shape):
        return pl.BlockSpec(shape, lambda h: (0,) * len(shape))

    return pl.pallas_call(
        partial(tail_kernel, dps, pairs, cap),
        grid=(D // 128,),
        out_shape=[
            jax.ShapeDtypeStruct((4, rows, D), f32),
            jax.ShapeDtypeStruct(vec.shape, f32),
            jax.ShapeDtypeStruct((T, D), f32),
            jax.ShapeDtypeStruct((T, D), f32),
        ],
        in_specs=[sp(0), sp(1), sp(2), pl.BlockSpec((1, T, 128), lambda h: (h, 0, 0)),
                  fixed((1, T)), fixed(vec.shape), fixed((8, T)), fixed((8, T)), fixed((8, 128)),
                  fixed(chosen.shape)]
        + [any_] * 9,
        out_specs=[fixed((4, rows, D)), fixed(vec.shape), any_, any_],
        scratch_shapes=[
            pltpu.VMEM((min(T, WINDOW + QB), T), f32),
            pltpu.VMEM((T, 128), f32),
            pltpu.VMEM((T, 128), f32),
            pltpu.VMEM((2, T, D), bf),
            pltpu.VMEM((4, T, D), bf),
            pltpu.VMEM((2, D, D), bf),
            pltpu.VMEM((2, D, D), f32),
            pltpu.VMEM((2, D, D), bf),
            pltpu.VMEM((dps, pairs, 2, R, D), bf),
            pltpu.VMEM((pairs, 2, R, D), bf),
            pltpu.VMEM((pairs, 2, R, D), bf),
            pltpu.VMEM((2, R, D), f32),
            pltpu.VMEM((2, rows, D), f32),
            pltpu.VMEM((4, D, D), bf),
            pltpu.VMEM((T, D), f32),
            pltpu.VMEM((T, D), bf),
            pltpu.VMEM((n, cap, D), bf),
            pltpu.VMEM((T, D), f32),
            pltpu.VMEM((n, cap, D), bf),
            pltpu.VMEM((T, D), bf),
            pltpu.VMEM((T, D), bf),
            pltpu.VMEM((8, n * cap), f32),
            pltpu.VMEM((T, 1), jnp.int32),
            dma((7,)), dma((2,)), dma((2,)), dma((dps, pairs)), dma((dps, pairs)), dma((pairs,)), dma((pairs,)),
            dma(()), dma(()), dma((n,)), dma((n,)), dma((count,)), dma((count,)), dma(()), dma(()), dma(()),
        ],
        compiler_params=pltpu.CompilerParams(
            vmem_limit_bytes=62 * 2**20, collective_id=3, has_side_effects=True
        ),
        cost_estimate=pl.CostEstimate(flops=40 * T * D * D, bytes_accessed=200 * 2**20, transcendentals=0),
    )(projected, projected, projected, lse, documents, vec, slot_rows,
      gate_rows, scale, chosen, normed, mixed, produced, dense_low, inputs, late, back, cotangent, hidden)


def norm_kernel(dps, pairs, d_ref, v_ref, e_ref, out_ref, a, b, c, s1, r1, s2, r2, s3, r3):
    d, pair, core, partner, over, along = near(dps, pairs)
    devices = [partner] + [x[1] for x in over] + [x[1] for x in along]
    barrier = pltpu.get_barrier_semaphore()
    for dev in devices:
        pl.semaphore_signal(barrier, inc=1, device_id=dev, device_id_type=MESH)

    def squares(ref):
        x = ref[...].astype(jnp.float32)
        return jnp.sum(x * x)

    part = squares(d_ref)
    for i in range(e_ref.shape[0]):
        part = part + squares(e_ref.at[i])
    pl.semaphore_wait(barrier, len(devices))
    last = lax.broadcasted_iota(jnp.int32, v_ref.shape, 0) == v_ref.shape[0] - 1
    a[core] = jnp.where(last, part, v_ref[...])
    cs = [remote(a.at[core], a.at[core], s1, r1.at[core], partner)]
    cs[0].start()
    remote(a.at[1 - core], a.at[1 - core], s1, r1.at[1 - core], partner).wait_recv()
    b[d] = a[0] + a[1]
    for dd, dev in over:
        x = remote(b.at[d], b.at[d], s2.at[dd], r2.at[d], dev)
        x.start()
        cs.append(x)
    for dd, dev in over:
        remote(b.at[dd], b.at[dd], s2.at[dd], r2.at[dd], dev).wait_recv()
    c[pair] = sum(b[k] for k in range(dps))
    for q, dev in along:
        x = remote(c.at[pair], c.at[pair], s3.at[q], r3.at[pair], dev)
        x.start()
        cs.append(x)
    for q, dev in along:
        remote(c.at[q], c.at[q], s3.at[q], r3.at[q], dev).wait_recv()
    out_ref[...] = sum(c[k] for k in range(pairs))
    for x in cs:
        x.wait_send()


def norm_squares(dense, vec, expert, k, dps, n):
    pairs = n // 2
    rows, D = vec.shape
    R = max(rows, (k // 8 + 1) * 8)
    dma = pltpu.SemaphoreType.DMA
    vm = pl.BlockSpec(memory_space=pltpu.VMEM)
    out = pl.pallas_call(
        partial(norm_kernel, dps, pairs),
        out_shape=jax.ShapeDtypeStruct((R, D), jnp.float32),
        in_specs=[vm] * 3,
        out_specs=vm,
        scratch_shapes=[
            pltpu.VMEM((2, R, D), jnp.float32),
            pltpu.VMEM((dps, R, D), jnp.float32),
            pltpu.VMEM((pairs, R, D), jnp.float32),
            dma(()), dma((2,)), dma((dps,)), dma((dps,)), dma((pairs,)), dma((pairs,)),
        ],
        compiler_params=pltpu.CompilerParams(
            vmem_limit_bytes=24 * 2**20, collective_id=4, has_side_effects=True
        ),
    )(dense, jnp.pad(vec, ((0, R - rows), (0, 0))), expert)
    total = out[:k]
    dev = lax.axis_index("dp") * n + lax.axis_index("expert")
    width = D // (dps * n)
    return lax.dynamic_slice_in_dim(total, dev * width, width, axis=1), out[R - 1, 0] + jnp.sum(total * total)


def adam_update(weight, gradient, first_moment, second_moment, average, factor, rate):
    clipped = gradient * factor
    first_new = beta_first * first_moment + (1.0 - beta_first) * clipped
    second_new = beta_second * second_moment + (1.0 - beta_second) * clipped * clipped
    first_hat = first_new / (1.0 - beta_first**STEP)
    second_hat = second_new / (1.0 - beta_second**STEP)
    updated = weight - rate * (
        first_hat / (jnp.sqrt(second_hat) + adam_eps) + weight_decay * weight
    )
    average_new = ema_keep * average + (1.0 - ema_keep) * updated
    return (updated, first_new, second_new, average_new)


def inverse_order(row_order, sorted_slot):
    at_token = row_order[:, None] == jnp.arange(row_order.shape[0])[None, :]
    return jnp.sum(jnp.where(at_token, sorted_slot[:, None], 0), axis=0)


def shards(
    inputs,
    cotangent,
    document_ids,
    domain_counts,
    domain_weight,
    token_order,
    expert_counts,
    dense_weights,
    vector_params,
    expert_weights,
    dense_first,
    dense_second,
    dense_average,
    vector_first,
    vector_second,
    vector_average,
    expert_first,
    expert_second,
    expert_average,
):
    tokens, model_width = inputs.shape
    experts_total = expert_counts.shape[1]
    capacity = 2 * tokens // experts_total
    owners = lax.axis_size("expert")
    groups = lax.axis_size(("dp", "expert"))
    sequences = tokens // LEN
    splits = lax.axis_size("dp")
    own_rows = dense_weights.shape[1]
    me = lax.axis_index("expert")
    seq_index = lax.axis_index("dp") * owners + jnp.arange(owners)
    domains = jnp.arange(NDOM)
    bounds = jnp.sum(jnp.where(domains[None, :] <= domains[:, None], domain_counts[None, :], 0), axis=1)
    domain = jnp.sum((seq_index[:, None] >= bounds[None, :]).astype(jnp.int32), axis=1)
    seq_pick = (domain[:, None] == jnp.arange(NDOM)[None, :]).astype(jnp.float32)
    seq_weight = jnp.sum(seq_pick * domain_weight[None, :], axis=1)
    seq_count = jnp.sum(seq_pick * domain_counts[None, :].astype(jnp.float32), axis=1)
    seq_scale = seq_weight * (sequences * groups) / (NDOM * seq_count)
    source_scale = jnp.broadcast_to(seq_scale[:, None], (owners, 128))
    documents = document_ids.reshape(-1)
    inputs_float = inputs.astype(jnp.float32)
    per = TILE // capacity
    fused = own_rows % 8 == 0 and capacity % 128 == 0 and splits == 4
    if fused:
        (dense_low, vec_rows, slot_rows, cot_received, projected, normed_low, mixed_low, totals,
         hidden_state, gate_rows, send_rows, gate_tiles, expert_low) = head(
            dense_weights, vector_params, inputs, cotangent, token_order, expert_counts, document_ids,
            expert_weights, splits, owners, capacity
        )
    else:
        row_counts = expert_counts[0]
        row_order = token_order[0]
        count_ends = jnp.cumsum(row_counts)
        count_starts = count_ends - row_counts
        sorted_pos = jnp.arange(tokens)
        sorted_expert = jnp.sum((sorted_pos[:, None] >= count_ends[None, :]).astype(jnp.int32), axis=1)
        sorted_pick = sorted_expert[:, None] == jnp.arange(experts_total)[None, :]
        sorted_start = jnp.sum(jnp.where(sorted_pick, count_starts[None, :], 0), axis=1)
        sorted_slot = sorted_expert * capacity + sorted_pos - sorted_start
        token_slot = inverse_order(row_order, sorted_slot)
        own_low = expert_weights[0].astype(jnp.bfloat16)
        expert_low = lax.all_gather(own_low, "dp", axis=0)
        dense_low, vector_low = (
            lax.all_gather(dense_weights.astype(jnp.bfloat16), ("dp", "expert"), axis=1, tiled=True),
            lax.all_gather(vector_params.astype(jnp.bfloat16), ("dp", "expert"), axis=1, tiled=True),
        )
        vector_low = vector_low.astype(jnp.float32)
        token_expert = token_slot // capacity
        expert_pick = (token_expert[:, None] == jnp.arange(experts_total)[None, :]).astype(jnp.float32)
        slot_match = token_slot[:, None] == jnp.arange(experts_total * capacity)[None, :]
        slot_pick = slot_match.astype(jnp.bfloat16)

        def to_slots(rows):
            placed = jnp.dot(slot_pick.T, rows, preferred_element_type=jnp.float32)
            return placed.astype(jnp.bfloat16).reshape(experts_total, capacity, model_width)

        def from_slots(rows):
            return jnp.dot(
                slot_pick, rows.reshape(-1, model_width), preferred_element_type=jnp.float32
            )

        cot_received = lax.all_to_all(
            to_slots(cotangent), "expert", split_axis=0, concat_axis=0, tiled=True
        )
        normed_one, norm_one_back = jax.vjp(layer_norm, inputs_float, vector_low[0])
        normed_low = normed_one.astype(jnp.bfloat16)
        projected = jnp.einsum(
            "td,cde->cte", normed_low, dense_low[:3], preferred_element_type=jnp.float32
        ).astype(jnp.bfloat16)
        mixed_low, totals = attend_forward(projected, documents)
        hidden_state = inputs_float + jnp.dot(
            mixed_low, dense_low[3], preferred_element_type=jnp.float32
        )
        normed_two, norm_two_back = jax.vjp(layer_norm, hidden_state, vector_low[1])
        centroids = vector_low[2:]
        logits = jnp.dot(normed_two, centroids.T, precision=lax.Precision.HIGHEST)
        gate_value = jax.nn.sigmoid(jnp.sum(logits * expert_pick, axis=1))
        send_rows = to_slots(normed_two.astype(jnp.bfloat16))
        gate_slots = jnp.sum(
            jnp.where(slot_match, gate_value[:, None], 0.0), axis=0
        ).reshape(experts_total, 1, 1, capacity)
        lane_part = (jnp.arange(per) == me % per).astype(jnp.float32)
        gate_tiles = jnp.broadcast_to(
            gate_slots * lane_part[None, None, :, None], (experts_total, 8, per, capacity)
        ).reshape(experts_total, 8, TILE)
    back_rows, late_rows, chosen_tiles, produced_low, grad_expert = moe(
        send_rows, gate_tiles, cot_received.reshape(-1, model_width), source_scale, expert_low, fused
    )
    expert_low_grad = lax.psum_scatter(grad_expert, "dp", scatter_dimension=0)
    expert_grad = expert_low_grad.astype(jnp.float32)[None]
    if fused:
        dense_grad, vector_grad, input_grad, block_output = tail(
            projected, totals, document_ids, vec_rows, slot_rows, gate_rows,
            jnp.broadcast_to(seq_scale[me], (8, 128)), chosen_tiles, normed_low, mixed_low, produced_low,
            dense_low, inputs, late_rows, back_rows, cotangent, hidden_state, splits, owners
        )
    else:
        late_rows = send_late(late_rows, owners)
        grad_out = cotangent.astype(jnp.float32) * seq_scale[me]
        back_slot = (token_slot // capacity ^ me) * capacity + token_slot % capacity
        back_match = back_slot[:, None] == jnp.arange(experts_total * capacity)[None, :]
        back_pick = back_match.astype(jnp.bfloat16)
        early = back_rows.shape[0] * capacity
        grad_sent_rows = jnp.dot(
            back_pick[:, :early], back_rows.reshape(-1, model_width), preferred_element_type=jnp.float32
        ) + jnp.dot(
            back_pick[:, early:], late_rows.reshape(-1, model_width), preferred_element_type=jnp.float32
        )
        chosen_slots = lax.dynamic_slice_in_dim(
            chosen_tiles[:, 0, :], me % per * capacity, capacity, axis=1
        )
        grad_chosen = jnp.sum(jnp.where(back_match, chosen_slots.reshape(1, -1), 0.0), axis=1)
        chosen_grad = grad_chosen[:, None] * expert_pick
        grad_normed_two = grad_sent_rows + jnp.dot(
            chosen_grad, centroids, precision=lax.Precision.HIGHEST
        )
        grad_centroids = jnp.dot(chosen_grad.T, normed_two, precision=lax.Precision.HIGHEST)
        grad_hidden_norm, grad_gain_two = norm_two_back(grad_normed_two)
        grad_hidden = grad_out + grad_hidden_norm
        grad_attn = grad_hidden.astype(jnp.bfloat16)
        grad_mixed = jnp.dot(grad_attn, dense_low[3].T, preferred_element_type=jnp.float32).astype(
            jnp.bfloat16
        )
        returned = lax.all_to_all(produced_low, "expert", split_axis=0, concat_axis=0, tiled=True)
        grad_proj = attend_backward(projected, documents, totals, grad_mixed)
        grad_normed_one = jnp.einsum(
            "cte,cde->td", grad_proj, dense_low[:3], preferred_element_type=jnp.float32
        )
        grad_input_norm, grad_gain_one = norm_one_back(grad_normed_one)
        input_grad = grad_hidden + grad_input_norm
        grad_in_proj = jnp.einsum(
            "td,cte->cde", normed_low, grad_proj, preferred_element_type=jnp.float32
        )
        grad_out_proj = jnp.dot(mixed_low.T, grad_attn, preferred_element_type=jnp.float32)
        dense_grad = lax.psum_scatter(
            jnp.concatenate([grad_in_proj, grad_out_proj[None]], axis=0),
            ("dp", "expert"),
            scatter_dimension=1,
            tiled=True,
        )
        returned_rows = from_slots(returned)
        block_output = hidden_state + gate_value[:, None] * returned_rows
        vector_grad = jnp.concatenate(
            [grad_gain_one[None], grad_gain_two[None], grad_centroids], axis=0
        )
    vector_grad, squares = norm_squares(
        dense_grad, vector_grad, expert_low_grad, vector_params.shape[0], splits, owners
    )
    grad_norm = jnp.sqrt(squares)
    factor = jnp.minimum(1.0, clip_norm / (grad_norm + 1e-06))
    dense_new = adam_update(
        dense_weights, dense_grad, dense_first, dense_second, dense_average, factor, dense_rate
    )
    vector_new = adam_update(
        vector_params, vector_grad, vector_first, vector_second, vector_average, factor, vector_rate
    )
    expert_new = adam_update(
        expert_weights,
        expert_grad,
        expert_first,
        expert_second,
        expert_average,
        factor,
        expert_rate,
    )
    return (
        block_output,
        input_grad,
        dense_new[0],
        dense_new[1],
        dense_new[2],
        dense_new[3],
        vector_new[0],
        vector_new[1],
        vector_new[2],
        vector_new[3],
        expert_new[0],
        expert_new[1],
        expert_new[2],
        expert_new[3],
        grad_norm,
    )


def solution(mesh):
    placed = (
        P(("dp", "expert"), None),
        P(("dp", "expert"), None),
        P(("dp", "expert"), None),
        P(),
        P(),
        P(("dp", "expert"), None),
        P(("dp", "expert"), None),
        P(None, ("dp", "expert"), None),
        P(None, ("dp", "expert")),
        P("expert", None, None, "dp"),
        P(None, ("dp", "expert"), None),
        P(None, ("dp", "expert"), None),
        P(None, ("dp", "expert"), None),
        P(None, ("dp", "expert")),
        P(None, ("dp", "expert")),
        P(None, ("dp", "expert")),
        P("expert", None, None, "dp"),
        P("expert", None, None, "dp"),
        P("expert", None, None, "dp"),
    )
    return jax.shard_map(
        shards,
        mesh=mesh,
        in_specs=placed,
        out_specs=(
            P(("dp", "expert"), None),
            P(("dp", "expert"), None),
            P(None, ("dp", "expert"), None),
            P(None, ("dp", "expert"), None),
            P(None, ("dp", "expert"), None),
            P(None, ("dp", "expert"), None),
            P(None, ("dp", "expert")),
            P(None, ("dp", "expert")),
            P(None, ("dp", "expert")),
            P(None, ("dp", "expert")),
            P("expert", None, None, "dp"),
            P("expert", None, None, "dp"),
            P("expert", None, None, "dp"),
            P("expert", None, None, "dp"),
            P(),
        ),
        check_vma=False,
    )
```

```python
from functools import partial

import jax
import jax.numpy as jnp
from jax import lax
from jax.experimental import pallas as pl
from jax.experimental.pallas import tpu as pltpu
from jax.sharding import PartitionSpec as P

HEADS = 12
HEAD_DIM = 64
LEN = 1024
WINDOW = 512
NDOM = 8
STEP = 10


norm_eps = 1e-05
masked_score = -1e30
beta_first = 0.9
beta_second = 0.999
adam_eps = 1e-08
dense_rate = 0.1
vector_rate = 0.5
expert_rate = 0.02
weight_decay = 0.1
ema_keep = 0.9
clip_norm = 1.0


def layer_norm(values_in, gain_row):
    center = values_in - jnp.mean(values_in, axis=-1, keepdims=True)
    spread = jnp.mean(center * center, axis=-1, keepdims=True)
    return center * lax.rsqrt(spread + norm_eps) * gain_row


NT = (((1,), (1,)), ((), ()))
TN = (((0,), (0,)), ((), ()))


def fwd_kernel(QB, q_ref,k_ref,v_ref,dcol_ref,drow_ref,o_ref,lse_ref,bias_ref):
    reach = WINDOW//QB
    low_lane = lax.broadcasted_iota(jnp.int32,(QB,128),1) < HEAD_DIM
    @pl.when(pl.program_id(0)==0)
    def _():
        for i in range(LEN//QB):
            first=max(0,i-reach)*QB; W=(i+1)*QB-first
            qp=i*QB+lax.broadcasted_iota(jnp.int32,(QB,W),0)
            kp=first+lax.broadcasted_iota(jnp.int32,(QB,W),1)
            ok=(kp<=qp)&(dcol_ref[i*QB:(i+1)*QB,:]==drow_ref[:,first:first+W])
            bias_ref[i*QB:(i+1)*QB,:W]=jnp.where(ok,0.0,masked_score)
    for i in range(LEN//QB):
        rows=slice(i*QB,(i+1)*QB)
        first=max(0,i-reach)*QB; W=(i+1)*QB-first
        q=q_ref[0,rows,:]*jnp.bfloat16(HEAD_DIM**-0.5)
        zero=jnp.zeros_like(q)
        qs=jnp.concatenate([jnp.where(low_lane,q,zero),jnp.where(low_lane,zero,q)],axis=0)
        s=lax.dot_general(qs,k_ref[0,first:first+W,:],NT,preferred_element_type=jnp.float32)
        s=(s.reshape(2,QB,W)+bias_ref[rows,:W][None]).reshape(2*QB,W)
        top=jnp.max(s,axis=1,keepdims=True)
        e=jnp.exp(s-top)
        total=jnp.sum(e,axis=1,keepdims=True)
        p=(e*(1.0/total)).astype(jnp.bfloat16)
        o=jnp.dot(p,v_ref[0,first:first+W,:],preferred_element_type=jnp.float32)
        o_ref[rows,:]=jnp.where(low_lane,o[:QB],o[QB:]).astype(jnp.bfloat16)
        lse=top+jnp.log(total)
        lse_ref[0,rows,:]=jnp.where(low_lane,lse[:QB],lse[QB:])

def attend_forward(projected, documents, QB=256):
    T=projected.shape[1]; D=projected.shape[2]
    dcol=documents.reshape(T,1); drow=documents.reshape(1,T)
    def sp(c): return pl.BlockSpec((1,T,128),lambda h,c=c:(c,0,h))
    return pl.pallas_call(partial(fwd_kernel,QB),grid=(D//128,),
        in_specs=[sp(0),sp(1),sp(2),pl.BlockSpec((T,1),lambda h:(0,0)),pl.BlockSpec((1,T),lambda h:(0,0))],
        out_specs=[pl.BlockSpec((T,128),lambda h:(0,h)),pl.BlockSpec((1,T,128),lambda h:(h,0,0))],
        out_shape=[jax.ShapeDtypeStruct((T,D),jnp.bfloat16),jax.ShapeDtypeStruct((D//128,T,128),jnp.float32)],
        scratch_shapes=[pltpu.VMEM((T,min(T,WINDOW+QB)),jnp.float32)],
        compiler_params=pltpu.CompilerParams(vmem_limit_bytes=48*2**20),
    )(projected,projected,projected,dcol,drow)

QB = 256


def transposed_bias(bias_ref, dcol_ref, drow_ref, QB):
    reach = WINDOW // QB
    for i in range(LEN // QB):
        first = max(0, i - reach) * QB
        W = (i + 1) * QB - first
        kp = first + lax.broadcasted_iota(jnp.int32, (W, QB), 0)
        qp = i * QB + lax.broadcasted_iota(jnp.int32, (W, QB), 1)
        ok = (kp <= qp) & (dcol_ref[first : first + W, :] == drow_ref[:, i * QB : (i + 1) * QB])
        bias_ref[:W, i * QB : (i + 1) * QB] = jnp.where(ok, 0.0, masked_score)


def head_pair_backward(QB, q_ref, k_ref, v_ref, lse_ref, g_ref, bias_ref, dk_ref, dv_ref, put_dq):
    reach = WINDOW // QB
    low_lane = lax.broadcasted_iota(jnp.int32, (QB, 128), 1) < HEAD_DIM
    dk_ref[...] = jnp.zeros_like(dk_ref)
    dv_ref[...] = jnp.zeros_like(dv_ref)
    for i in range(LEN // QB):
        rows = slice(i * QB, (i + 1) * QB)
        first = max(0, i - reach) * QB
        W = (i + 1) * QB - first
        keys = slice(first, first + W)
        q = q_ref[0, rows, :] * jnp.bfloat16(HEAD_DIM**-0.5)
        zero = jnp.zeros_like(q)
        qs = jnp.concatenate([jnp.where(low_lane, q, zero), jnp.where(low_lane, zero, q)], axis=0)
        g = g_ref[rows, :]
        gs = jnp.concatenate([jnp.where(low_lane, g, zero), jnp.where(low_lane, zero, g)], axis=0)
        k = k_ref[0, keys, :]
        st = lax.dot_general(k, qs, NT, preferred_element_type=jnp.float32)
        bias = bias_ref[:W, rows]
        lse = jnp.transpose(lse_ref[0, rows, :])
        lse = jnp.concatenate([lse[0:1, :], lse[64:65, :]], axis=1)
        p = jnp.exp(st + jnp.concatenate([bias, bias], axis=1) - lse)
        dp = lax.dot_general(v_ref[0, keys, :], gs, NT, preferred_element_type=jnp.float32)
        inner = jnp.sum(p * dp, axis=0, keepdims=True)
        ds = (p * (dp - inner)).astype(jnp.bfloat16)
        dk_ref[keys, :] += jnp.dot(ds, qs, preferred_element_type=jnp.float32)
        dv_ref[keys, :] += jnp.dot(p.astype(jnp.bfloat16), gs, preferred_element_type=jnp.float32)
        dq = lax.dot_general(ds, k, TN, preferred_element_type=jnp.float32)
        put_dq(rows, (jnp.where(low_lane, dq[:QB], dq[QB:]) * HEAD_DIM**-0.5).astype(jnp.bfloat16))


def bwd_kernel(QB, q_ref, k_ref, v_ref, lse_ref, g_ref, dcol_ref, drow_ref, out_ref, bias_ref, dk_ref, dv_ref):
    @pl.when(pl.program_id(0) == 0)
    def _():
        transposed_bias(bias_ref, dcol_ref, drow_ref, QB)

    def put_dq(rows, value):
        out_ref[0, rows, :] = value

    head_pair_backward(QB, q_ref, k_ref, v_ref, lse_ref, g_ref, bias_ref, dk_ref, dv_ref, put_dq)
    out_ref[1, :, :] = dk_ref[...].astype(jnp.bfloat16)
    out_ref[2, :, :] = dv_ref[...].astype(jnp.bfloat16)


def attend_backward(projected, documents, lse, grad_mixed, QB=256):
    T=projected.shape[1]; D=projected.shape[2]
    dcol=documents.reshape(T,1); drow=documents.reshape(1,T)
    def sp(c): return pl.BlockSpec((1,T,128),lambda h,c=c:(c,0,h))
    return pl.pallas_call(partial(bwd_kernel,QB),grid=(D//128,),
        in_specs=[sp(0),sp(1),sp(2),pl.BlockSpec((1,T,128),lambda h:(h,0,0)),pl.BlockSpec((T,128),lambda h:(0,h)),pl.BlockSpec((T,1),lambda h:(0,0)),pl.BlockSpec((1,T),lambda h:(0,0))],
        out_specs=pl.BlockSpec((3,T,128),lambda h:(0,0,h)),
        out_shape=jax.ShapeDtypeStruct((3,T,D),jnp.bfloat16),
        scratch_shapes=[pltpu.VMEM((min(T,WINDOW+QB),T),jnp.float32),pltpu.VMEM((T,128),jnp.float32),pltpu.VMEM((T,128),jnp.float32)],
        compiler_params=pltpu.CompilerParams(vmem_limit_bytes=48*2**20),
    )(projected,projected,projected,lse,grad_mixed,dcol,drow)


MESH=pl.DeviceIdType.MESH
TILE=512

def flip(a,b,n):
    out=0
    bit=1
    while bit<n:
        out=out+bit*((a//bit+b//bit)%2)
        bit*=2
    return out

def gelu_pair(x):
    c=0.7978845608028654
    sq=x*x
    t=jnp.tanh(c*(x+0.044715*(x*sq)))
    half=0.5*(1.0+t)
    return x*half, half+x*(0.5*(1.0-t*t))*(c+(3*0.044715*c)*sq)

def moe_kernel(n,cap,square,send_ref,gate_ref,cot_ref,scale_ref,w_ref,
               back_ref,late_ref,chosen_ref,ret_ref,gw_ref,
               recv,gates,cot,w,gw,ret_s,gs_s,ch_s,g_s,racc,sacc,
               send_sem,recv_sem,gate_send,gate_recv,back_send,back_recv,ch_send,ch_recv,on_send,on_recv,w_sem,loc_sem,ret_sem,late_sem):
    per=TILE//cap
    tiles=n//per
    chunks=w_ref.shape[0]
    me=lax.axis_index("expert")
    barrier=pltpu.get_barrier_semaphore()
    def greet(o,_):
        pl.semaphore_signal(barrier,inc=1,device_id={"expert":flip(me,o,n)},device_id_type=MESH)
        return 0
    lax.fori_loop(1,n,greet,0)
    d=lax.axis_index("dp")
    sides=[flip(d,1,chunks),flip(d,2,chunks)] if square else []
    for side in sides:
        pl.semaphore_signal(barrier,inc=1,device_id={"dp":side},device_id_type=MESH)
    pl.semaphore_wait(barrier,n-1+len(sides))
    def on_copy(k):
        return pltpu.make_async_remote_copy(src_ref=w_ref.at[sides[k],k],dst_ref=w.at[sides[k],k],
            send_sem=on_send.at[k],recv_sem=on_recv.at[k],device_id={"dp":sides[1-k]},device_id_type=MESH)
    def on_in(k):
        across=flip(d,3,chunks)
        return pltpu.make_async_remote_copy(src_ref=w_ref.at[sides[k],k],dst_ref=w.at[across,k],
            send_sem=on_send.at[k],recv_sem=on_recv.at[k],device_id={"dp":sides[1-k]},device_id_type=MESH)
    for k in range(len(sides)): on_copy(k).start()

    def copies(src,dst,send,recv_,peer,there):
        return pltpu.make_async_remote_copy(src_ref=src,dst_ref=dst,send_sem=send.at[peer],recv_sem=recv_.at[there],
            device_id={"expert":peer},device_id_type=MESH)
    def row_copy(peer): return copies(send_ref.at[peer],recv.at[me],send_sem,recv_sem,peer,me)
    def gate_copy(peer): return copies(gate_ref.at[peer],gates.at[me],gate_send,gate_recv,peer,me)
    def row_in(src): return copies(send_ref.at[src],recv.at[src],send_sem,recv_sem,src,src)
    def gate_in(src): return copies(gate_ref.at[src],gates.at[src],gate_send,gate_recv,src,src)
    def back_copy(src): return copies(gs_s.at[src],back_ref.at[flip(src,me,n)],back_send,back_recv,src,me)
    def ch_copy(src): return copies(ch_s.at[src],chosen_ref.at[flip(src,me,n)],ch_send,ch_recv,src,me)
    def back_in(src): return copies(gs_s.at[src],back_ref.at[flip(src,me,n)],back_send,back_recv,src,src)
    def ch_in(src): return copies(ch_s.at[src],chosen_ref.at[flip(src,me,n)],ch_send,ch_recv,src,src)

    def push(o,_):
        gate_copy(flip(me,o,n)).start()
        row_copy(flip(me,o,n)).start()
        return 0
    last=(tiles-1)*per
    kept=n-late_ref.shape[0]
    lax.fori_loop(0,last-1,lambda i,c: push(last-1-i,c),0)
    own=[pltpu.make_async_copy(send_ref.at[me],recv.at[me],loc_sem.at[0]),
         pltpu.make_async_copy(gate_ref.at[me],gates.at[me],loc_sem.at[1]),
         pltpu.make_async_copy(cot_ref,cot,loc_sem.at[2]),
        ]+[pltpu.make_async_copy(w_ref.at[c],w.at[c],w_sem.at[i]) for i,c in enumerate(([d]+sides) if square else range(chunks))]
    for c in own: c.start()
    def wipe(c,_):
        gw[c]=jnp.zeros(gw.shape[1:],jnp.float32)
        return 0
    lax.fori_loop(0,chunks,wipe,0)
    for c in own: c.wait()
    own_back=pltpu.make_async_copy(gs_s.at[me],back_ref.at[0],loc_sem.at[1])
    own_ch=pltpu.make_async_copy(ch_s.at[me],chosen_ref.at[0],loc_sem.at[0])
    def keep(o): return pltpu.make_async_copy(gs_s.at[flip(me,o,n)],late_ref.at[o-kept],late_sem.at[o-kept])

    def tile(t,_):
        @pl.when(t==1)
        def _():
            lax.fori_loop(last,n,push,0)
        block=flip(me//per,t,tiles)
        def arrive(j,_):
            src=block*per+j
            @pl.when(src!=me)
            def _():
                gate_in(src).wait_recv()
                row_in(src).wait_recv()
            return 0
        lax.fori_loop(0,per,arrive,0)
        at=pl.ds(pl.multiple_of(block*per,per),per)
        rows=pl.ds(pl.multiple_of(block*TILE,TILE),TILE)
        gate=jnp.transpose(jnp.sum(gates[at],axis=0))[:,0:1]
        scale=jnp.concatenate([jnp.broadcast_to(scale_ref[pl.ds(block*per+j,1),0:1],(cap,1)) for j in range(per)],axis=0)
        grad_out=cot[rows,:].astype(jnp.float32)*scale
        g_s[...]=(gate*grad_out).astype(jnp.bfloat16)
        racc[...]=jnp.zeros_like(racc)
        sacc[...]=jnp.zeros_like(sacc)
        def chunk(i,_):
            c=flip(d,i,chunks)
            if square:
                @pl.when((t==0)&(i==chunks-1))
                def _():
                    for k in range(2): on_in(k).wait_recv()
            x=recv[at].reshape(TILE,recv.shape[2])
            g=g_s[...]
            act,slope=gelu_pair(jnp.dot(x,w[c,0],preferred_element_type=jnp.float32))
            a=act.astype(jnp.bfloat16)
            ga=jnp.dot(g,w[c,1],preferred_element_type=jnp.float32).astype(jnp.bfloat16)
            gp=(ga.astype(jnp.float32)*slope).astype(jnp.bfloat16)
            racc[...]+=lax.dot_general(a,w[c,1],NT,preferred_element_type=jnp.float32)
            sacc[...]+=lax.dot_general(gp,w[c,0],NT,preferred_element_type=jnp.float32)
            gw[c,0]+=lax.dot_general(x,gp,TN,preferred_element_type=jnp.float32)
            gw[c,1]+=lax.dot_general(g,a,TN,preferred_element_type=jnp.float32)
            @pl.when(t==tiles-1)
            def _():
                w[c]=gw[c].astype(jnp.bfloat16)
                pltpu.make_async_copy(w.at[c],gw_ref.at[c],w_sem.at[c]).start()
            return 0
        lax.fori_loop(0,chunks,chunk,0)
        gs_s[at]=sacc[...].astype(jnp.bfloat16).reshape(per,cap,recv.shape[2])
        def give(j,_):
            src=block*per+j
            o=flip(src,me,n)
            @pl.when((src!=me)&(o<kept))
            def _():
                back_copy(src).start()
            @pl.when(src==me)
            def _():
                own_back.start()
            @pl.when(o>=kept)
            def _():
                keep(o).start()
            return 0
        lax.fori_loop(0,per,give,0)
        ret=racc[...].astype(jnp.bfloat16)
        ret_s[at]=ret.reshape(per,cap,recv.shape[2])
        pltpu.make_async_copy(ret_s.at[at],ret_ref.at[at],ret_sem.at[t]).start()
        grad_out=cot[rows,:].astype(jnp.float32)*scale
        chosen=jnp.sum(grad_out*ret.astype(jnp.float32),axis=1,keepdims=True)*gate*(1.0-gate)
        chosen=jnp.transpose(jnp.broadcast_to(chosen,(TILE,128)))[0:8,:]
        def tell(j,_):
            src=block*per+j
            ch_s[src]=chosen
            @pl.when(src!=me)
            def _():
                ch_copy(src).start()
            @pl.when(src==me)
            def _():
                own_ch.start()
            return 0
        lax.fori_loop(0,per,tell,0)
        return 0
    lax.fori_loop(0,tiles,tile,0)
    own_ch.wait()
    own_back.wait()
    def settle(o,_):
        peer=flip(me,o,n)
        gate_copy(peer).wait_send()
        row_copy(peer).wait_send()
        ch_copy(peer).wait_send()
        ch_in(peer).wait_recv()
        @pl.when(o<kept)
        def _():
            back_copy(peer).wait_send()
            back_in(peer).wait_recv()
        @pl.when(o>=kept)
        def _():
            keep(o).wait()
        return 0
    lax.fori_loop(1,n,settle,0)
    def stored(t,_):
        block=flip(me//per,t,tiles)
        at=pl.ds(pl.multiple_of(block*per,per),per)
        pltpu.make_async_copy(ret_s.at[at],ret_ref.at[at],ret_sem.at[t]).wait()
        return 0
    lax.fori_loop(0,tiles,stored,0)
    for c in range(chunks): pltpu.make_async_copy(w.at[c],gw_ref.at[c],w_sem.at[c]).wait()
    for k in range(len(sides)): on_copy(k).wait_send()

def late_kernel(n,gs_ref,out_ref,send_sem,recv_sem):
    count=gs_ref.shape[0]
    me=lax.axis_index("expert")
    barrier=pltpu.get_barrier_semaphore()
    def greet(k,_):
        pl.semaphore_signal(barrier,inc=1,device_id={"expert":flip(me,n-count+k,n)},device_id_type=MESH)
        return 0
    lax.fori_loop(0,count,greet,0)
    pl.semaphore_wait(barrier,count)
    def copy(k):
        return pltpu.make_async_remote_copy(src_ref=gs_ref.at[k],dst_ref=out_ref.at[k],send_sem=send_sem.at[k],recv_sem=recv_sem.at[k],
            device_id={"expert":flip(me,n-count+k,n)},device_id_type=MESH)
    def go(k,_):
        copy(k).start()
        return 0
    lax.fori_loop(0,count,go,0)
    def end(k,_):
        copy(k).wait()
        return 0
    lax.fori_loop(0,count,end,0)

def moe(send_rows,gate_slots,cot,scale,weights,square):
    n,cap,D=send_rows.shape
    chunks,_,_,FC=weights.shape
    per=TILE//cap
    any_=pl.BlockSpec(memory_space=pl.ANY)
    bf=jnp.bfloat16; f32=jnp.float32
    dma=pltpu.SemaphoreType.DMA
    flops=6*2*n*cap*D*chunks*FC
    back,late,chosen,ret,gw=pl.pallas_call(partial(moe_kernel,n,cap,square),
        out_shape=[jax.ShapeDtypeStruct((n-per,cap,D),bf),jax.ShapeDtypeStruct((per,cap,D),bf),jax.ShapeDtypeStruct((n,8,TILE),f32),
                   jax.ShapeDtypeStruct((n,cap,D),bf),jax.ShapeDtypeStruct(weights.shape,bf)],
        in_specs=[any_,any_,any_,pl.BlockSpec(memory_space=pltpu.VMEM),any_],
        out_specs=[any_]*5,
        scratch_shapes=[pltpu.VMEM((n,cap,D),bf),pltpu.VMEM((n,8,TILE),f32),pltpu.VMEM((n*cap,D),bf),
            pltpu.VMEM(weights.shape,bf),pltpu.VMEM(weights.shape,f32),pltpu.VMEM((n,cap,D),bf),pltpu.VMEM((n,cap,D),bf),
            pltpu.VMEM((n,8,TILE),f32),pltpu.VMEM((TILE,D),bf),pltpu.VMEM((TILE,D),f32),pltpu.VMEM((TILE,D),f32)]
            +[dma((n,))]*8+[dma((2,)),dma((2,)),dma((chunks,)),dma((3,)),dma((n//per,)),dma((per,))],
        compiler_params=pltpu.CompilerParams(vmem_limit_bytes=62*2**20,collective_id=1,has_side_effects=True),
        cost_estimate=pl.CostEstimate(flops=flops,bytes_accessed=40*2**20,transcendentals=0),
    )(send_rows,gate_slots,cot,scale,weights)
    return back,late,chosen,ret,gw

def send_late(late,n):
    per,cap,D=late.shape
    any_=pl.BlockSpec(memory_space=pl.ANY)
    bf=jnp.bfloat16
    dma=pltpu.SemaphoreType.DMA
    return pl.pallas_call(partial(late_kernel,n),
        out_shape=jax.ShapeDtypeStruct((per,cap,D),bf),in_specs=[any_],out_specs=any_,
        scratch_shapes=[dma((per,)),dma((per,))],
        compiler_params=pltpu.CompilerParams(collective_id=5,has_side_effects=True),
        cost_estimate=pl.CostEstimate(flops=0,bytes_accessed=100*2**20,transcendentals=0),
    )(late)


def near(dps,pairs):
    d=lax.axis_index("dp"); me=lax.axis_index("expert")
    core=me%2; pair=me//2
    partner={"expert":me+1-2*core}
    over=[((d+k)%dps,{"dp":(d+k)%dps}) for k in range(1,dps)]
    along=[((pair+k)%pairs,{"expert":2*((pair+k)%pairs)+core}) for k in range(1,pairs)]
    return d,pair,core,partner,over,along

def greet_all(devices):
    barrier=pltpu.get_barrier_semaphore()
    for dev in devices:
        pl.semaphore_signal(barrier,inc=1,device_id=dev,device_id_type=MESH)
    pl.semaphore_wait(barrier,len(devices))

def remote(src,dst,send,recv,dev):
    return pltpu.make_async_remote_copy(src_ref=src,dst_ref=dst,send_sem=send,recv_sem=recv,device_id=dev,device_id_type=MESH)

def upright(row):
    return jnp.transpose(row.astype(jnp.float32))[:, 0:1].astype(jnp.int32)


def head_kernel(dps, pairs, n, cap, w_ref, v_ref, x_ref, cot_ref, order_ref, counts_ref, drow_ref, ew_ref,
                w_out, vec_out, slot_out, cot_out, proj_out, normed_out, mixed_out, lse_out, hidden_out,
                gate_out, send_out, tile_out, ew_out,
                ew32, ew, both, blk, vboth, vblk, w, vall, slots, unit, normed, proj, mixed, lse, bias, sent, cots, sends,
                tiles, s1, r1, loc, zs, zr, vzs, vzr, ds_, dr, vds, vdr, ps, pr, cs, cr, ewl, xs, xr, ys, yr, out_sem, send_sem):
    r = w_ref.shape[1]
    R = 2 * r
    T, D = x_ref.shape
    d, pair, core, partner, over, along = near(dps, pairs)
    me = lax.axis_index("expert")
    bf, f32 = jnp.bfloat16, jnp.float32
    ew_load = pltpu.make_async_copy(ew_ref.at[0], ew32, ewl.at[0])
    ew_load.start()
    barrier = pltpu.get_barrier_semaphore()

    def greet(o, _):
        pl.semaphore_signal(barrier, inc=1, device_id={"expert": flip(me, o, n)}, device_id_type=MESH)
        return 0

    lax.fori_loop(1, n, greet, 0)
    for _, dev in over:
        pl.semaphore_signal(barrier, inc=1, device_id=dev, device_id_type=MESH)
    pl.semaphore_wait(barrier, n - 1 + dps - 1)

    side_x, side_y = flip(d, 1, dps), flip(d, 2, dps)
    to_x, to_y = {"dp": side_x}, {"dp": side_y}

    def x_copy(src, slot, m):
        return remote(src, ew_out.at[slot, m], xs.at[slot, m], xr.at[slot, m], to_x)

    def y_copy(src, slot, m):
        return remote(src, ew_out.at[slot, m], ys.at[slot, m], yr.at[slot, m], to_y)

    mine = pl.ds(pl.multiple_of(core * r, 8), r)
    half = pl.ds(core * 2, 2)
    rest = pl.ds(2 - core * 2, 2)

    def rows(dd, q):
        return pl.ds(pl.multiple_of((dd * pairs + q) * R, 16), R)

    c1 = [
        remote(w_ref, both.at[:, mine, :], s1.at[0], r1.at[0], partner),
        remote(v_ref, vboth.at[core], s1.at[1], r1.at[1], partner),
    ]
    for c in c1:
        c.start()
    both[:, mine, :] = w_ref[...]
    vboth[core] = v_ref[...]
    for c in c1:
        c.wait()
    blk[...] = both[...].astype(bf)
    vblk[...] = (vboth[0] + vboth[1]).astype(bf)
    w[:, rows(d, pair), :] = blk[...]
    vall[d, pair] = vblk[...]
    def along_copy(q, dev):
        return remote(blk.at[half], w.at[half, rows(d, pair), :], zs.at[q], zr.at[pair], dev)

    def over_copy(dd, q, dev):
        here = w.at[half, rows(d, q), :]
        return remote(here, here, ds_.at[dd, q], dr.at[d, q], dev)

    def hand(dd, q):
        here = w.at[half, rows(dd, q), :]
        return remote(here, here, ps.at[dd, q], pr.at[dd, q], partner)

    def v_along(q, dev):
        return remote(vblk, vall.at[d, pair], vzs.at[q], vzr.at[pair], dev)

    def v_over(dd, dev):
        return remote(vall.at[d], vall.at[d], vds.at[dd], vdr.at[d], dev)

    for q, dev in along:
        along_copy(q, dev).start()
        v_along(q, dev).start()
    for dd, dev in over:
        over_copy(dd, pair, dev).start()

    tokens_across = lax.broadcasted_iota(jnp.int32, (T, T), 1)
    position = lax.broadcasted_iota(jnp.int32, (8, T), 1)
    sorted_slot, end = position, 0
    for e in range(n):
        count = counts_ref[0, e]
        end = end + count
        sorted_slot = sorted_slot + jnp.where(position >= end, cap - count, 0)
    slot_col = upright(sorted_slot)
    order_col = upright(jnp.broadcast_to(order_ref[...], (8, T)))
    slots[...] = jnp.broadcast_to(
        jnp.sum(jnp.where(order_col == tokens_across, slot_col, 0), axis=0, keepdims=True), (8, T)
    )
    doc_col = upright(jnp.broadcast_to(drow_ref[...], (8, T)))

    def pick(p):
        here = lax.broadcasted_iota(jnp.int32, (cap, T), 0) + p * cap
        return here == slots[0:1, :]

    def cot_copy(p):
        return remote(cots.at[p], cot_out.at[me], cs.at[p], cr.at[me], {"expert": p})

    def cot_in(p):
        return remote(cots.at[p], cot_out.at[p], cs.at[p], cr.at[p], {"expert": p})

    def place(i, _):
        p = flip(me, n - 1 - i, n)
        cots[p] = jnp.dot(pick(p).astype(bf), cot_ref[...], preferred_element_type=f32).astype(bf)

        return 0

    groups = [d] + [x[0] for x in over]
    lax.fori_loop(0, n // 2, place, 0)
    for q, dev in along:
        here = w.at[half, rows(d, q), :]
        remote(here, here, zs.at[q], zr.at[q], dev).wait_recv()
        for dd, dev2 in over:
            over_copy(dd, q, dev2).start()
        hand(d, q).start()
    for q, dev in along:
        remote(vblk, vall.at[d, q], vzs.at[q], vzr.at[q], dev).wait_recv()
    for dd, dev in over:
        v_over(dd, dev).start()
    ew_load.wait()
    for m in range(2):
        ew[m] = ew32[m].astype(bf)
    own_ew = pltpu.make_async_copy(ew, ew_out.at[d], ewl.at[0])
    own_ew.start()
    for m in range(2):
        x_copy(ew.at[m], d, m).start()
        y_copy(ew.at[1 - m], d, 1 - m).start()
    lax.fori_loop(n // 2, n, place, 0)

    def give(i, _):
        cot_copy(flip(me, n - 1 - i, n)).start()
        return 0

    lax.fori_loop(0, n - 1, give, 0)
    own_cot = pltpu.make_async_copy(cots.at[me], cot_out.at[me], loc.at[0])
    own_cot.start()

    def unit_rows(b):
        at = pl.ds(b * 256, 256)
        x = x_ref[at, :].astype(f32)
        center = x - jnp.mean(x, axis=-1, keepdims=True)
        unit[at, :] = center * lax.rsqrt(jnp.mean(center * center, axis=-1, keepdims=True) + norm_eps)

    for b in range(T // 256):
        unit_rows(b)
    for i in range(LEN // QB):
        first = max(0, i - WINDOW // QB) * QB
        W = (i + 1) * QB - first
        qp = i * QB + lax.broadcasted_iota(jnp.int32, (QB, W), 0)
        kp = first + lax.broadcasted_iota(jnp.int32, (QB, W), 1)
        ok = (kp <= qp) & (doc_col[i * QB : (i + 1) * QB, :] == drow_ref[:, first : first + W])
        bias[i * QB : (i + 1) * QB, :W] = jnp.where(ok, 0.0, masked_score)
    for q in [pair] + [x[0] for x in along]:
        for dd, dev in over:
            here = w.at[half, rows(dd, q), :]
            remote(here, here, ds_.at[dd, q], dr.at[dd, q], dev).wait_recv()
            hand(dd, q).start()
    for dd, dev in over:
        remote(vall.at[dd], vall.at[dd], vds.at[dd], vdr.at[dd], dev).wait_recv()
    vec = jnp.zeros(vec_out.shape, f32)
    for dd in range(dps):
        for q in range(pairs):
            vec = vec + vall[dd, q].astype(f32)
    vec_out[...] = vec
    slot_out[...] = slots[...]
    normed[...] = (unit[...] * vec_out[0:1, :]).astype(bf)

    def from_partner(dd, q):
        there = w.at[rest, rows(dd, q), :]
        remote(there, there, ps.at[dd, q], pr.at[dd, q], partner).wait_recv()

    for dd, dev in over:
        from_partner(dd, pair)
    for q, _ in along:
        for dd in groups:
            from_partner(dd, q)

    outs = [
        pltpu.make_async_copy(w, w_out, out_sem.at[0]),
        pltpu.make_async_copy(normed, normed_out, out_sem.at[1]),
    ]
    for c in outs:
        c.start()

    def project(i, _):
        c = i // 2
        at = pl.ds(pl.multiple_of(i % 2 * (T // 2), T // 2), T // 2)
        proj[c, at, :] = jnp.dot(normed[at, :], w[c], preferred_element_type=f32).astype(bf)
        return 0

    lax.fori_loop(0, 6, project, 0)
    outs.append(pltpu.make_async_copy(proj, proj_out, out_sem.at[2]))
    outs[-1].start()
    low_lane = lax.broadcasted_iota(jnp.int32, (QB, 128), 1) < HEAD_DIM

    def attend(h, _):
        lanes = pl.ds(pl.multiple_of(h * 128, 128), 128)
        for i in range(LEN // QB):
            here = slice(i * QB, (i + 1) * QB)
            first = max(0, i - WINDOW // QB) * QB
            W = (i + 1) * QB - first
            keys = slice(first, first + W)
            q = proj[0, here, lanes] * jnp.bfloat16(HEAD_DIM**-0.5)
            zero = jnp.zeros_like(q)
            qs = jnp.concatenate([jnp.where(low_lane, q, zero), jnp.where(low_lane, zero, q)], axis=0)
            s = lax.dot_general(qs, proj[1, keys, lanes], NT, preferred_element_type=f32)
            s = (s.reshape(2, QB, W) + bias[here, :W][None]).reshape(2 * QB, W)
            top = jnp.max(s, axis=1, keepdims=True)
            e = jnp.exp(s - top)
            total = jnp.sum(e, axis=1, keepdims=True)
            p = (e * (1.0 / total)).astype(bf)
            o = jnp.dot(p, proj[2, keys, lanes], preferred_element_type=f32)
            mixed[here, lanes] = jnp.where(low_lane, o[:QB], o[QB:]).astype(bf)
            ends = top + jnp.log(total)
            lse[h, here, :] = jnp.where(low_lane, ends[:QB], ends[QB:])
        return 0

    lax.fori_loop(0, D // 128, attend, 0)
    outs += [
        pltpu.make_async_copy(mixed, mixed_out, out_sem.at[3]),
        pltpu.make_async_copy(lse, lse_out, out_sem.at[4]),
    ]
    outs[-2].start()
    outs[-1].start()
    E = vec_out.shape[0] - 2
    hidden = unit

    def finish(b, _):
        at = pl.ds(pl.multiple_of(b * 256, 256), 256)
        state = x_ref[at, :].astype(f32) + jnp.dot(mixed[at, :], w[3], preferred_element_type=f32)
        hidden[at, :] = state
        center = state - jnp.mean(state, axis=-1, keepdims=True)
        spread = jnp.mean(center * center, axis=-1, keepdims=True)
        two = center * lax.rsqrt(spread + norm_eps) * vec_out[1:2, :]
        sent[at, :] = two.astype(bf)
        which = lax.broadcasted_iota(jnp.int32, (vec_out.shape[0], 256), 0) - 2
        chosen = (which == slots[0:1, at] // cap).astype(bf)
        rows_c = lax.dot_general(chosen, vec_out[...].astype(bf), TN, preferred_element_type=f32)
        logit = jnp.sum(two * rows_c, axis=1, keepdims=True)
        gate = 1.0 / (1.0 + jnp.exp(-logit))
        gate_out[:, at] = jnp.transpose(jnp.broadcast_to(gate, (256, 128)))[0:8, :]
        return 0

    lax.fori_loop(0, T // 256, finish, 0)
    outs.append(pltpu.make_async_copy(hidden, hidden_out, out_sem.at[5]))
    outs[-1].start()
    tiles[...] = jnp.zeros(tiles.shape, f32)
    part = pl.ds(pl.multiple_of(me % (TILE // cap) * cap, 128), cap)

    def fill(p, _):
        chosen = pick(p)
        sends[p] = jnp.dot(chosen.astype(bf), sent[...], preferred_element_type=f32).astype(bf)
        tiles[p, :, part] = lax.dot_general(
            gate_out[...], chosen.astype(f32), NT, precision=lax.Precision.HIGHEST, preferred_element_type=f32
        )
        pltpu.make_async_copy(sends.at[p], send_out.at[p], send_sem).start()
        return 0

    lax.fori_loop(0, n, fill, 0)
    outs.append(pltpu.make_async_copy(tiles, tile_out, out_sem.at[6]))
    outs[-1].start()
    for q, dev in along:
        along_copy(q, dev).wait_send()
        v_along(q, dev).wait_send()
        hand(d, q).wait_send()
    for dd, dev in over:
        v_over(dd, dev).wait_send()
        for q in [pair] + [x[0] for x in along]:
            over_copy(dd, q, dev).wait_send()
            hand(dd, q).wait_send()

    def settle(o, _):
        p = flip(me, o, n)
        cot_copy(p).wait_send()
        cot_in(p).wait_recv()
        return 0

    lax.fori_loop(1, n, settle, 0)
    pltpu.make_async_copy(cots.at[me], cot_out.at[me], loc.at[0]).wait()
    own_ew.wait()
    for m in range(2):
        x_copy(ew.at[m], d, m).wait_send()
        y_copy(ew.at[m], d, m).wait_send()
        x_copy(ew.at[m], side_x, m).wait_recv()
        y_copy(ew.at[m], side_y, m).wait_recv()
    for c in outs:
        c.wait()
    pltpu.make_async_copy(sends, send_out, send_sem).wait()


def head(weights, vectors, inputs, cotangent, token_order, counts, documents, expert_weights, dps, n, cap):
    pairs = n // 2
    m, r, D = weights.shape
    T = inputs.shape[0]
    k = vectors.shape[0]
    f32, bf = jnp.float32, jnp.bfloat16
    dma = pltpu.SemaphoreType.DMA
    any_ = pl.BlockSpec(memory_space=pl.ANY)
    vm = pl.BlockSpec(memory_space=pltpu.VMEM)
    dev = lax.axis_index("dp") * n + lax.axis_index("expert")
    K = (k + 15) // 16 * 16
    placed = lax.dynamic_update_slice(jnp.zeros((K, D), f32), vectors, (0, dev * r))
    shape = jax.ShapeDtypeStruct
    grid = lambda: dma((dps, pairs))
    return pl.pallas_call(
        partial(head_kernel, dps, pairs, n, cap),
        out_shape=[
            shape((m, D, D), bf), shape((K, D), f32), shape((8, T), jnp.int32), shape((n, cap, D), bf),
            shape((3, T, D), bf), shape((T, D), bf), shape((T, D), bf), shape((D // 128, T, 128), f32),
            shape((T, D), f32), shape((8, T), f32), shape((n, cap, D), bf), shape((n, 8, TILE), f32),
            shape((dps,) + expert_weights.shape[1:], bf),
        ],
        in_specs=[vm] * 5 + [pl.BlockSpec(memory_space=pltpu.SMEM), vm, any_],
        out_specs=[any_, vm, vm, any_, any_, any_, any_, any_, any_, vm, any_, any_, any_],
        scratch_shapes=[
            pltpu.VMEM(expert_weights.shape[1:], f32), pltpu.VMEM(expert_weights.shape[1:], bf),
            pltpu.VMEM((m, 2 * r, D), f32), pltpu.VMEM((m, 2 * r, D), bf), pltpu.VMEM((2, K, D), f32),
            pltpu.VMEM((K, D), bf), pltpu.VMEM((m, D, D), bf), pltpu.VMEM((dps, pairs, K, D), bf),
            pltpu.VMEM((8, T), jnp.int32), pltpu.VMEM((T, D), f32), pltpu.VMEM((T, D), bf),
            pltpu.VMEM((3, T, D), bf), pltpu.VMEM((T, D), bf), pltpu.VMEM((D // 128, T, 128), f32),
            pltpu.VMEM((T, min(T, WINDOW + QB)), f32), pltpu.VMEM((T, D), bf), pltpu.VMEM((n, cap, D), bf),
            pltpu.VMEM((n, cap, D), bf), pltpu.VMEM((n, 8, TILE), f32),
            dma((2,)), dma((2,)), dma((1,)), dma((pairs,)), dma((pairs,)), dma((pairs,)), dma((pairs,)),
            grid(), grid(), dma((dps,)), dma((dps,)), grid(), grid(), dma((n,)), dma((n,)),
            dma((1,)), dma((dps, 2)), dma((dps, 2)), dma((dps, 2)), dma((dps, 2)), dma((7,)), dma(()),
        ],
        compiler_params=pltpu.CompilerParams(
            vmem_limit_bytes=60 * 2**20, collective_id=2, has_side_effects=True
        ),
        cost_estimate=pl.CostEstimate(flops=20 * T * D * D, bytes_accessed=200 * 2**20, transcendentals=0),
    )(weights, placed, inputs, cotangent, token_order, counts, documents, expert_weights)


def tail_kernel(dps, pairs, cap, q_ref, k_ref, v_ref, lse_ref, drow_ref, vec_ref, slot_ref, gate_ref,
                scale_ref, chosen_ref, x_ref, mixed_ref, prod_ref, w_ref, in_ref, late_ref, back_ref, cot_ref,
                hidden_ref,
                out_ref, vec_out, dx_ref, block_ref,
                bias_ref, dk_ref, dv_ref, left, right, got, own, total, in2, tb, in3, u, in4, w, gh, xin,
                ret, hid, back, cot, g_ref, chs, dcol_ref,
                ls, s1, r1, s2, r2, s3, r3, s4, r4, rs, rr, bs, br, own_sem, dx_sem, block_sem):
    h = pl.program_id(0)
    n = 2 * pairs
    count = late_ref.shape[0]
    kept = n - count
    early = kept * cap
    per = TILE // cap
    me = lax.axis_index("expert")
    d, pair, core, partner, over, along = near(dps, pairs)
    rows = out_ref.shape[1]
    R = 2 * rows
    T, D = x_ref.shape
    bf, f32 = jnp.bfloat16, jnp.float32
    B = 256
    loads = [
        pltpu.make_async_copy(back_ref, back.at[pl.ds(0, kept)], ls.at[0]),
        pltpu.make_async_copy(hidden_ref, hid, ls.at[1]),
        pltpu.make_async_copy(cot_ref, cot, ls.at[2]),
        pltpu.make_async_copy(w_ref, w, ls.at[3]),
        pltpu.make_async_copy(mixed_ref, left.at[1], ls.at[4]),
        pltpu.make_async_copy(x_ref, left.at[0], ls.at[5]),
        pltpu.make_async_copy(in_ref, xin, ls.at[6]),
    ]

    def product(m):
        return lax.dot_general(left[m // 3], right[m], TN, preferred_element_type=f32)

    def ret_copy(peer):
        return remote(prod_ref.at[peer], ret.at[me], rs.at[peer], rr.at[me], {"expert": peer})

    def ret_in(peer):
        return remote(prod_ref.at[peer], ret.at[peer], rs.at[peer], rr.at[peer], {"expert": peer})

    own_ret = pltpu.make_async_copy(prod_ref.at[me], ret.at[me], own_sem)

    def late_copy(k):
        return remote(late_ref.at[k], back.at[kept + k], bs.at[k], br.at[k], {"expert": flip(me, kept + k, n)})

    def to_partner(i):
        return remote(total.at[i], got.at[i], s1.at[i], r1.at[i], partner)

    def column(row):
        return jnp.transpose(row)[:, 0:1]

    def normal(x):
        center = x - jnp.mean(x, axis=-1, keepdims=True)
        scale = lax.rsqrt(jnp.mean(center * center, axis=-1, keepdims=True) + norm_eps)
        return center * scale, scale

    def normal_back(grad, unit, scale, gain):
        gu = grad * gain
        return scale * (
            gu - jnp.mean(gu, axis=-1, keepdims=True) - unit * jnp.mean(gu * unit, axis=-1, keepdims=True)
        )

    def offset_slots(at):
        slot = slot_ref[:, at]
        return flip(slot // cap, me, n) * cap + slot % cap

    def match(slot_rows, first, count):
        here = column(slot_rows.astype(f32))
        return here == (first + lax.broadcasted_iota(jnp.int32, (B, count), 1)).astype(f32)

    @pl.when(h == 0)
    def _():
        for c in loads:
            c.start()
        barrier = pltpu.get_barrier_semaphore()

        def greet(o, _):
            pl.semaphore_signal(barrier, inc=1, device_id={"expert": flip(me, o, n)}, device_id_type=MESH)
            return 0

        lax.fori_loop(1, n, greet, 0)
        for _, dev in over:
            pl.semaphore_signal(barrier, inc=1, device_id=dev, device_id_type=MESH)
        pl.semaphore_wait(barrier, n - 1 + dps - 1)
        for j in range(count):
            late_copy(j).start()

        def send(i, _):
            ret_copy(flip(me, 1 + i, n)).start()
            return 0

        lax.fori_loop(0, n // 2 - 1, send, 0)
        own_ret.start()
        dcol_ref[...] = upright(jnp.broadcast_to(drow_ref[...], (8, T)))
        transposed_bias(bias_ref, dcol_ref, drow_ref, QB)
        part = pl.ds(pl.multiple_of(me % per * cap, 128), cap)
        for o in range(n):
            chs[:, o * cap : (o + 1) * cap] = chosen_ref[o, :, part]
        loads[0].wait()

        def first_rows(b, _):
            at = pl.ds(pl.multiple_of(b * B, B), B)
            pick = match(offset_slots(at), 0, early).astype(bf)
            gh[at, :] = jnp.dot(pick, back[pl.ds(0, kept)].reshape(early, D), preferred_element_type=f32)
            return 0

        lax.fori_loop(0, T // B, first_rows, 0)
        vec_out[...] = jnp.zeros(vec_out.shape, f32)
        for c in loads[1:4]:
            c.wait()
        for j in range(count):
            late_copy(j).wait_recv()
        lax.fori_loop(n // 2 - 1, n - 1, send, 0)

        def second(b, _):
            at = pl.ds(pl.multiple_of(b * B, B), B)
            slot_rows = offset_slots(at)
            all_slots = match(slot_rows, 0, n * cap)
            chosen = jnp.sum(jnp.where(all_slots, chs[0:1, :], 0.0), axis=1, keepdims=True)
            pick = match(slot_rows, early, count * cap).astype(bf)
            sent = gh[at, :] + jnp.dot(
                pick, back[pl.ds(kept, count)].reshape(count * cap, D), preferred_element_type=f32
            )
            which = lax.broadcasted_iota(jnp.int32, (vec_ref.shape[0], B), 0) - 2
            expert = which == slot_ref[0:1, at] // cap
            centroid = lax.dot_general(
                expert.astype(bf), vec_ref[...].astype(bf), TN, preferred_element_type=f32
            )
            grad = sent + chosen * centroid
            unit, scale = normal(hid[at, :])
            gain = vec_ref[1:2, :]
            chosen_row = jnp.transpose(jnp.broadcast_to(chosen, (B, 128)))[0:1, :]
            vec_out[...] += jnp.dot(
                jnp.where(expert, chosen_row, 0.0), unit * gain,
                precision=lax.Precision.HIGHEST, preferred_element_type=f32,
            )
            vec_out[1:2, :] += jnp.sum(grad * unit, axis=0, keepdims=True)
            total_grad = cot[at, :].astype(f32) * scale_ref[0:1, 0:1] + normal_back(grad, unit, scale, gain)
            gh[at, :] = total_grad
            low = total_grad.astype(bf)
            right[3, at, :] = low
            g_ref[at, :] = lax.dot_general(low, w[3], NT, preferred_element_type=f32).astype(bf)
            return 0

        lax.fori_loop(0, T // B, second, 0)
        loads[4].wait()
        out = product(3)

        @pl.when(core == 0)
        def _():
            total[1] = out.astype(bf)
            to_partner(1).start()

        @pl.when(core == 1)
        def _():
            own[1] = out

    lanes = pl.ds(pl.multiple_of(h * 128, 128), 128)

    def put_dq(r, value):
        right[0, r, lanes] = value

    head_pair_backward(
        QB, q_ref, k_ref, v_ref, lse_ref, g_ref.at[:, lanes], bias_ref, dk_ref, dv_ref, put_dq
    )
    right[1, :, lanes] = dk_ref[...].astype(bf)
    right[2, :, lanes] = dv_ref[...].astype(bf)

    @pl.when(h == pl.num_programs(0) - 1)
    def _():
        loads[5].wait()

        @pl.when(core == 0)
        def _():
            total[0] = product(2).astype(bf)
            to_partner(0).start()
            own[0] = product(0)
            own[1] = product(1)

        @pl.when(core == 1)
        def _():
            total[0] = product(0).astype(bf)
            to_partner(0).start()
            total[1] = product(1).astype(bf)
            to_partner(1).start()
            own[0] = product(2)

        for i in range(2):
            to_partner(i).wait_send()
            to_partner(i).wait_recv()
            total[i] = (own[i] + got[i].astype(f32)).astype(bf)

        order = along + [(pair, None)]

        def piece(dd, q):
            return pl.ds(pl.multiple_of((dd * pairs + q) * R, 16), R)

        c2 = []
        for q, _ in order:
            for dd, dev in over:
                c = remote(total.at[:, piece(dd, q), :], in2.at[d, q], s2.at[dd, q], r2.at[d, q], dev)
                c.start()
                c2.append(c)
        loads[6].wait()

        def norm_one(b, _):
            at = pl.ds(pl.multiple_of(b * B, B), B)
            gn = sum(
                lax.dot_general(right[c, at, :], w[c], NT, preferred_element_type=f32) for c in range(3)
            )
            unit, scale = normal(xin[at, :].astype(f32))
            vec_out[0:1, :] += jnp.sum(gn * unit, axis=0, keepdims=True)
            gh[at, :] += normal_back(gn, unit, scale, vec_ref[0:1, :])
            return 0

        lax.fori_loop(0, T // B, norm_one, 0)
        dx = pltpu.make_async_copy(gh, dx_ref, dx_sem)
        dx.start()
        c3 = []
        for q, zdev in order:
            acc = total[:, piece(d, q), :].astype(f32)
            for dd, dev in over:
                remote(in2.at[dd, q], in2.at[dd, q], s2.at[dd, q], r2.at[dd, q], dev).wait_recv()
                acc = acc + in2[dd, q].astype(f32)
            if zdev is None:
                u[...] = acc
            else:
                tb[q] = acc.astype(bf)
                c = remote(tb.at[q], in3.at[pair], s3.at[q], r3.at[pair], zdev)
                c.start()
                c3.append(c)

        def settle(o, _):
            peer = flip(me, o, n)
            ret_copy(peer).wait_send()
            ret_in(peer).wait_recv()
            return 0

        lax.fori_loop(1, n, settle, 0)
        own_ret.wait()

        def add_rows(b, _):
            at = pl.ds(pl.multiple_of(b * B, B), B)
            pick = match(slot_ref[:, at], 0, n * cap).astype(bf)
            got_rows = jnp.dot(pick, ret[...].reshape(n * cap, D), preferred_element_type=f32)
            hid[at, :] += column(gate_ref[:, at]) * got_rows
            return 0

        lax.fori_loop(0, T // B, add_rows, 0)
        block = pltpu.make_async_copy(hid, block_ref, block_sem)
        block.start()
        acc = u[...]
        for q, dev in along:
            remote(in3.at[q], in3.at[q], s3.at[q], r3.at[q], dev).wait_recv()
            acc = acc + in3[q].astype(f32)
        u[...] = acc
        theirs = pl.ds(pl.multiple_of((1 - core) * rows, 8), rows)
        mine = pl.ds(pl.multiple_of(core * rows, 8), rows)
        c4 = remote(u.at[:, theirs, :], in4, s4, r4, partner)
        c4.start()
        out_ref[pl.ds(2 * core, 2)] = u[:, mine, :]
        c4.wait_recv()
        out_ref[pl.ds(2 - 2 * core, 2)] = in4[...]
        for c in c2 + c3 + [c4]:
            c.wait_send()
        for j in range(count):
            late_copy(j).wait_send()
        dx.wait()
        block.wait()


def tail(projected, lse, documents, vec, slot_rows, gate_rows, scale, chosen, normed, mixed, produced, dense_low,
         inputs, late, back, cotangent, hidden, dps, n):
    pairs = n // 2
    _, T, D = projected.shape
    rows = D // (dps * n)
    R = 2 * rows
    cap = produced.shape[1]
    count = late.shape[0]
    f32, bf = jnp.float32, jnp.bfloat16
    dma = pltpu.SemaphoreType.DMA
    any_ = pl.BlockSpec(memory_space=pl.ANY)

    def sp(c):
        return pl.BlockSpec((1, T, 128), lambda h, c=c: (c, 0, h))

    def fixed(shape):
        return pl.BlockSpec(shape, lambda h: (0,) * len(shape))

    return pl.pallas_call(
        partial(tail_kernel, dps, pairs, cap),
        grid=(D // 128,),
        out_shape=[
            jax.ShapeDtypeStruct((4, rows, D), f32),
            jax.ShapeDtypeStruct(vec.shape, f32),
            jax.ShapeDtypeStruct((T, D), f32),
            jax.ShapeDtypeStruct((T, D), f32),
        ],
        in_specs=[sp(0), sp(1), sp(2), pl.BlockSpec((1, T, 128), lambda h: (h, 0, 0)),
                  fixed((1, T)), fixed(vec.shape), fixed((8, T)), fixed((8, T)), fixed((8, 128)),
                  fixed(chosen.shape)]
        + [any_] * 9,
        out_specs=[fixed((4, rows, D)), fixed(vec.shape), any_, any_],
        scratch_shapes=[
            pltpu.VMEM((min(T, WINDOW + QB), T), f32),
            pltpu.VMEM((T, 128), f32),
            pltpu.VMEM((T, 128), f32),
            pltpu.VMEM((2, T, D), bf),
            pltpu.VMEM((4, T, D), bf),
            pltpu.VMEM((2, D, D), bf),
            pltpu.VMEM((2, D, D), f32),
            pltpu.VMEM((2, D, D), bf),
            pltpu.VMEM((dps, pairs, 2, R, D), bf),
            pltpu.VMEM((pairs, 2, R, D), bf),
            pltpu.VMEM((pairs, 2, R, D), bf),
            pltpu.VMEM((2, R, D), f32),
            pltpu.VMEM((2, rows, D), f32),
            pltpu.VMEM((4, D, D), bf),
            pltpu.VMEM((T, D), f32),
            pltpu.VMEM((T, D), bf),
            pltpu.VMEM((n, cap, D), bf),
            pltpu.VMEM((T, D), f32),
            pltpu.VMEM((n, cap, D), bf),
            pltpu.VMEM((T, D), bf),
            pltpu.VMEM((T, D), bf),
            pltpu.VMEM((8, n * cap), f32),
            pltpu.VMEM((T, 1), jnp.int32),
            dma((7,)), dma((2,)), dma((2,)), dma((dps, pairs)), dma((dps, pairs)), dma((pairs,)), dma((pairs,)),
            dma(()), dma(()), dma((n,)), dma((n,)), dma((count,)), dma((count,)), dma(()), dma(()), dma(()),
        ],
        compiler_params=pltpu.CompilerParams(
            vmem_limit_bytes=62 * 2**20, collective_id=3, has_side_effects=True
        ),
        cost_estimate=pl.CostEstimate(flops=40 * T * D * D, bytes_accessed=200 * 2**20, transcendentals=0),
    )(projected, projected, projected, lse, documents, vec, slot_rows,
      gate_rows, scale, chosen, normed, mixed, produced, dense_low, inputs, late, back, cotangent, hidden)


def norm_kernel(dps, pairs, d_ref, v_ref, e_ref, out_ref, a, b, c, s1, r1, s2, r2, s3, r3):
    d, pair, core, partner, over, along = near(dps, pairs)
    devices = [partner] + [x[1] for x in over] + [x[1] for x in along]
    barrier = pltpu.get_barrier_semaphore()
    for dev in devices:
        pl.semaphore_signal(barrier, inc=1, device_id=dev, device_id_type=MESH)

    def squares(ref):
        x = ref[...].astype(jnp.float32)
        return jnp.sum(x * x)

    part = squares(d_ref)
    for i in range(e_ref.shape[0]):
        part = part + squares(e_ref.at[i])
    pl.semaphore_wait(barrier, len(devices))
    last = lax.broadcasted_iota(jnp.int32, v_ref.shape, 0) == v_ref.shape[0] - 1
    a[core] = jnp.where(last, part, v_ref[...])
    cs = [remote(a.at[core], a.at[core], s1, r1.at[core], partner)]
    cs[0].start()
    remote(a.at[1 - core], a.at[1 - core], s1, r1.at[1 - core], partner).wait_recv()
    b[d] = a[0] + a[1]
    for dd, dev in over:
        x = remote(b.at[d], b.at[d], s2.at[dd], r2.at[d], dev)
        x.start()
        cs.append(x)
    for dd, dev in over:
        remote(b.at[dd], b.at[dd], s2.at[dd], r2.at[dd], dev).wait_recv()
    c[pair] = sum(b[k] for k in range(dps))
    for q, dev in along:
        x = remote(c.at[pair], c.at[pair], s3.at[q], r3.at[pair], dev)
        x.start()
        cs.append(x)
    for q, dev in along:
        remote(c.at[q], c.at[q], s3.at[q], r3.at[q], dev).wait_recv()
    out_ref[...] = sum(c[k] for k in range(pairs))
    for x in cs:
        x.wait_send()


def norm_squares(dense, vec, expert, k, dps, n):
    pairs = n // 2
    rows, D = vec.shape
    R = max(rows, (k // 8 + 1) * 8)
    dma = pltpu.SemaphoreType.DMA
    vm = pl.BlockSpec(memory_space=pltpu.VMEM)
    out = pl.pallas_call(
        partial(norm_kernel, dps, pairs),
        out_shape=jax.ShapeDtypeStruct((R, D), jnp.float32),
        in_specs=[vm] * 3,
        out_specs=vm,
        scratch_shapes=[
            pltpu.VMEM((2, R, D), jnp.float32),
            pltpu.VMEM((dps, R, D), jnp.float32),
            pltpu.VMEM((pairs, R, D), jnp.float32),
            dma(()), dma((2,)), dma((dps,)), dma((dps,)), dma((pairs,)), dma((pairs,)),
        ],
        compiler_params=pltpu.CompilerParams(
            vmem_limit_bytes=24 * 2**20, collective_id=4, has_side_effects=True
        ),
    )(dense, jnp.pad(vec, ((0, R - rows), (0, 0))), expert)
    total = out[:k]
    dev = lax.axis_index("dp") * n + lax.axis_index("expert")
    width = D // (dps * n)
    return lax.dynamic_slice_in_dim(total, dev * width, width, axis=1), out[R - 1, 0] + jnp.sum(total * total)


def adam_update(weight, gradient, first_moment, second_moment, average, factor, rate):
    clipped = gradient * factor
    first_new = beta_first * first_moment + (1.0 - beta_first) * clipped
    second_new = beta_second * second_moment + (1.0 - beta_second) * clipped * clipped
    first_hat = first_new / (1.0 - beta_first**STEP)
    second_hat = second_new / (1.0 - beta_second**STEP)
    updated = weight - rate * (
        first_hat / (jnp.sqrt(second_hat) + adam_eps) + weight_decay * weight
    )
    average_new = ema_keep * average + (1.0 - ema_keep) * updated
    return (updated, first_new, second_new, average_new)


def inverse_order(row_order, sorted_slot):
    at_token = row_order[:, None] == jnp.arange(row_order.shape[0])[None, :]
    return jnp.sum(jnp.where(at_token, sorted_slot[:, None], 0), axis=0)


def shards(
    inputs,
    cotangent,
    document_ids,
    domain_counts,
    domain_weight,
    token_order,
    expert_counts,
    dense_weights,
    vector_params,
    expert_weights,
    dense_first,
    dense_second,
    dense_average,
    vector_first,
    vector_second,
    vector_average,
    expert_first,
    expert_second,
    expert_average,
):
    tokens, model_width = inputs.shape
    experts_total = expert_counts.shape[1]
    capacity = 2 * tokens // experts_total
    owners = lax.axis_size("expert")
    groups = lax.axis_size(("dp", "expert"))
    sequences = tokens // LEN
    splits = lax.axis_size("dp")
    own_rows = dense_weights.shape[1]
    me = lax.axis_index("expert")
    seq_index = lax.axis_index("dp") * owners + jnp.arange(owners)
    domains = jnp.arange(NDOM)
    bounds = jnp.sum(jnp.where(domains[None, :] <= domains[:, None], domain_counts[None, :], 0), axis=1)
    domain = jnp.sum((seq_index[:, None] >= bounds[None, :]).astype(jnp.int32), axis=1)
    seq_pick = (domain[:, None] == jnp.arange(NDOM)[None, :]).astype(jnp.float32)
    seq_weight = jnp.sum(seq_pick * domain_weight[None, :], axis=1)
    seq_count = jnp.sum(seq_pick * domain_counts[None, :].astype(jnp.float32), axis=1)
    seq_scale = seq_weight * (sequences * groups) / (NDOM * seq_count)
    source_scale = jnp.broadcast_to(seq_scale[:, None], (owners, 128))
    documents = document_ids.reshape(-1)
    inputs_float = inputs.astype(jnp.float32)
    per = TILE // capacity
    fused = own_rows % 8 == 0 and capacity % 128 == 0 and splits == 4
    if fused:
        (dense_low, vec_rows, slot_rows, cot_received, projected, normed_low, mixed_low, totals,
         hidden_state, gate_rows, send_rows, gate_tiles, expert_low) = head(
            dense_weights, vector_params, inputs, cotangent, token_order, expert_counts, document_ids,
            expert_weights, splits, owners, capacity
        )
    else:
        row_counts = expert_counts[0]
        row_order = token_order[0]
        count_ends = jnp.cumsum(row_counts)
        count_starts = count_ends - row_counts
        sorted_pos = jnp.arange(tokens)
        sorted_expert = jnp.sum((sorted_pos[:, None] >= count_ends[None, :]).astype(jnp.int32), axis=1)
        sorted_pick = sorted_expert[:, None] == jnp.arange(experts_total)[None, :]
        sorted_start = jnp.sum(jnp.where(sorted_pick, count_starts[None, :], 0), axis=1)
        sorted_slot = sorted_expert * capacity + sorted_pos - sorted_start
        token_slot = inverse_order(row_order, sorted_slot)
        own_low = expert_weights[0].astype(jnp.bfloat16)
        expert_low = lax.all_gather(own_low, "dp", axis=0)
        dense_low, vector_low = (
            lax.all_gather(dense_weights.astype(jnp.bfloat16), ("dp", "expert"), axis=1, tiled=True),
            lax.all_gather(vector_params.astype(jnp.bfloat16), ("dp", "expert"), axis=1, tiled=True),
        )
        vector_low = vector_low.astype(jnp.float32)
        token_expert = token_slot // capacity
        expert_pick = (token_expert[:, None] == jnp.arange(experts_total)[None, :]).astype(jnp.float32)
        slot_match = token_slot[:, None] == jnp.arange(experts_total * capacity)[None, :]
        slot_pick = slot_match.astype(jnp.bfloat16)

        def to_slots(rows):
            placed = jnp.dot(slot_pick.T, rows, preferred_element_type=jnp.float32)
            return placed.astype(jnp.bfloat16).reshape(experts_total, capacity, model_width)

        def from_slots(rows):
            return jnp.dot(
                slot_pick, rows.reshape(-1, model_width), preferred_element_type=jnp.float32
            )

        cot_received = lax.all_to_all(
            to_slots(cotangent), "expert", split_axis=0, concat_axis=0, tiled=True
        )
        normed_one, norm_one_back = jax.vjp(layer_norm, inputs_float, vector_low[0])
        normed_low = normed_one.astype(jnp.bfloat16)
        projected = jnp.einsum(
            "td,cde->cte", normed_low, dense_low[:3], preferred_element_type=jnp.float32
        ).astype(jnp.bfloat16)
        mixed_low, totals = attend_forward(projected, documents)
        hidden_state = inputs_float + jnp.dot(
            mixed_low, dense_low[3], preferred_element_type=jnp.float32
        )
        normed_two, norm_two_back = jax.vjp(layer_norm, hidden_state, vector_low[1])
        centroids = vector_low[2:]
        logits = jnp.dot(normed_two, centroids.T, precision=lax.Precision.HIGHEST)
        gate_value = jax.nn.sigmoid(jnp.sum(logits * expert_pick, axis=1))
        send_rows = to_slots(normed_two.astype(jnp.bfloat16))
        gate_slots = jnp.sum(
            jnp.where(slot_match, gate_value[:, None], 0.0), axis=0
        ).reshape(experts_total, 1, 1, capacity)
        lane_part = (jnp.arange(per) == me % per).astype(jnp.float32)
        gate_tiles = jnp.broadcast_to(
            gate_slots * lane_part[None, None, :, None], (experts_total, 8, per, capacity)
        ).reshape(experts_total, 8, TILE)
    back_rows, late_rows, chosen_tiles, produced_low, grad_expert = moe(
        send_rows, gate_tiles, cot_received.reshape(-1, model_width), source_scale, expert_low, fused
    )
    expert_low_grad = lax.psum_scatter(grad_expert, "dp", scatter_dimension=0)
    expert_grad = expert_low_grad.astype(jnp.float32)[None]
    if fused:
        dense_grad, vector_grad, input_grad, block_output = tail(
            projected, totals, document_ids, vec_rows, slot_rows, gate_rows,
            jnp.broadcast_to(seq_scale[me], (8, 128)), chosen_tiles, normed_low, mixed_low, produced_low,
            dense_low, inputs, late_rows, back_rows, cotangent, hidden_state, splits, owners
        )
    else:
        late_rows = send_late(late_rows, owners)
        grad_out = cotangent.astype(jnp.float32) * seq_scale[me]
        back_slot = (token_slot // capacity ^ me) * capacity + token_slot % capacity
        back_match = back_slot[:, None] == jnp.arange(experts_total * capacity)[None, :]
        back_pick = back_match.astype(jnp.bfloat16)
        early = back_rows.shape[0] * capacity
        grad_sent_rows = jnp.dot(
            back_pick[:, :early], back_rows.reshape(-1, model_width), preferred_element_type=jnp.float32
        ) + jnp.dot(
            back_pick[:, early:], late_rows.reshape(-1, model_width), preferred_element_type=jnp.float32
        )
        chosen_slots = lax.dynamic_slice_in_dim(
            chosen_tiles[:, 0, :], me % per * capacity, capacity, axis=1
        )
        grad_chosen = jnp.sum(jnp.where(back_match, chosen_slots.reshape(1, -1), 0.0), axis=1)
        chosen_grad = grad_chosen[:, None] * expert_pick
        grad_normed_two = grad_sent_rows + jnp.dot(
            chosen_grad, centroids, precision=lax.Precision.HIGHEST
        )
        grad_centroids = jnp.dot(chosen_grad.T, normed_two, precision=lax.Precision.HIGHEST)
        grad_hidden_norm, grad_gain_two = norm_two_back(grad_normed_two)
        grad_hidden = grad_out + grad_hidden_norm
        grad_attn = grad_hidden.astype(jnp.bfloat16)
        grad_mixed = jnp.dot(grad_attn, dense_low[3].T, preferred_element_type=jnp.float32).astype(
            jnp.bfloat16
        )
        returned = lax.all_to_all(produced_low, "expert", split_axis=0, concat_axis=0, tiled=True)
        grad_proj = attend_backward(projected, documents, totals, grad_mixed)
        grad_normed_one = jnp.einsum(
            "cte,cde->td", grad_proj, dense_low[:3], preferred_element_type=jnp.float32
        )
        grad_input_norm, grad_gain_one = norm_one_back(grad_normed_one)
        input_grad = grad_hidden + grad_input_norm
        grad_in_proj = jnp.einsum(
            "td,cte->cde", normed_low, grad_proj, preferred_element_type=jnp.float32
        )
        grad_out_proj = jnp.dot(mixed_low.T, grad_attn, preferred_element_type=jnp.float32)
        dense_grad = lax.psum_scatter(
            jnp.concatenate([grad_in_proj, grad_out_proj[None]], axis=0),
            ("dp", "expert"),
            scatter_dimension=1,
            tiled=True,
        )
        returned_rows = from_slots(returned)
        block_output = hidden_state + gate_value[:, None] * returned_rows
        vector_grad = jnp.concatenate(
            [grad_gain_one[None], grad_gain_two[None], grad_centroids], axis=0
        )
    vector_grad, squares = norm_squares(
        dense_grad, vector_grad, expert_low_grad, vector_params.shape[0], splits, owners
    )
    grad_norm = jnp.sqrt(squares)
    factor = jnp.minimum(1.0, clip_norm / (grad_norm + 1e-06))
    dense_new = adam_update(
        dense_weights, dense_grad, dense_first, dense_second, dense_average, factor, dense_rate
    )
    vector_new = adam_update(
        vector_params, vector_grad, vector_first, vector_second, vector_average, factor, vector_rate
    )
    expert_new = adam_update(
        expert_weights,
        expert_grad,
        expert_first,
        expert_second,
        expert_average,
        factor,
        expert_rate,
    )
    return (
        block_output,
        input_grad,
        dense_new[0],
        dense_new[1],
        dense_new[2],
        dense_new[3],
        vector_new[0],
        vector_new[1],
        vector_new[2],
        vector_new[3],
        expert_new[0],
        expert_new[1],
        expert_new[2],
        expert_new[3],
        grad_norm,
    )


def solution(mesh):
    placed = (
        P(("dp", "expert"), None),
        P(("dp", "expert"), None),
        P(("dp", "expert"), None),
        P(),
        P(),
        P(("dp", "expert"), None),
        P(("dp", "expert"), None),
        P(None, ("dp", "expert"), None),
        P(None, ("dp", "expert")),
        P("expert", None, None, "dp"),
        P(None, ("dp", "expert"), None),
        P(None, ("dp", "expert"), None),
        P(None, ("dp", "expert"), None),
        P(None, ("dp", "expert")),
        P(None, ("dp", "expert")),
        P(None, ("dp", "expert")),
        P("expert", None, None, "dp"),
        P("expert", None, None, "dp"),
        P("expert", None, None, "dp"),
    )
    return jax.shard_map(
        shards,
        mesh=mesh,
        in_specs=placed,
        out_specs=(
            P(("dp", "expert"), None),
            P(("dp", "expert"), None),
            P(None, ("dp", "expert"), None),
            P(None, ("dp", "expert"), None),
            P(None, ("dp", "expert"), None),
            P(None, ("dp", "expert"), None),
            P(None, ("dp", "expert")),
            P(None, ("dp", "expert")),
            P(None, ("dp", "expert")),
            P(None, ("dp", "expert")),
            P("expert", None, None, "dp"),
            P("expert", None, None, "dp"),
            P("expert", None, None, "dp"),
            P("expert", None, None, "dp"),
            P(),
        ),
        check_vma=False,
    )
```

```python
from functools import partial

import jax
import jax.numpy as jnp
from jax import lax
from jax.experimental import pallas as pl
from jax.experimental.pallas import tpu as pltpu
from jax.sharding import PartitionSpec as P

HEADS = 12
HEAD_DIM = 64
LEN = 1024
WINDOW = 512
NDOM = 8
STEP = 10


norm_eps = 1e-05
masked_score = -1e30
beta_first = 0.9
beta_second = 0.999
adam_eps = 1e-08
dense_rate = 0.1
vector_rate = 0.5
expert_rate = 0.02
weight_decay = 0.1
ema_keep = 0.9
clip_norm = 1.0


def layer_norm(values_in, gain_row):
    center = values_in - jnp.mean(values_in, axis=-1, keepdims=True)
    spread = jnp.mean(center * center, axis=-1, keepdims=True)
    return center * lax.rsqrt(spread + norm_eps) * gain_row


NT = (((1,), (1,)), ((), ()))
TN = (((0,), (0,)), ((), ()))


def fwd_kernel(QB, q_ref,k_ref,v_ref,dcol_ref,drow_ref,o_ref,lse_ref,bias_ref):
    reach = WINDOW//QB
    low_lane = lax.broadcasted_iota(jnp.int32,(QB,128),1) < HEAD_DIM
    @pl.when(pl.program_id(0)==0)
    def _():
        for i in range(LEN//QB):
            first=max(0,i-reach)*QB; W=(i+1)*QB-first
            qp=i*QB+lax.broadcasted_iota(jnp.int32,(QB,W),0)
            kp=first+lax.broadcasted_iota(jnp.int32,(QB,W),1)
            ok=(kp<=qp)&(dcol_ref[i*QB:(i+1)*QB,:]==drow_ref[:,first:first+W])
            bias_ref[i*QB:(i+1)*QB,:W]=jnp.where(ok,0.0,masked_score)
    for i in range(LEN//QB):
        rows=slice(i*QB,(i+1)*QB)
        first=max(0,i-reach)*QB; W=(i+1)*QB-first
        q=q_ref[0,rows,:]*jnp.bfloat16(HEAD_DIM**-0.5)
        zero=jnp.zeros_like(q)
        qs=jnp.concatenate([jnp.where(low_lane,q,zero),jnp.where(low_lane,zero,q)],axis=0)
        s=lax.dot_general(qs,k_ref[0,first:first+W,:],NT,preferred_element_type=jnp.float32)
        s=(s.reshape(2,QB,W)+bias_ref[rows,:W][None]).reshape(2*QB,W)
        top=jnp.max(s,axis=1,keepdims=True)
        e=jnp.exp(s-top)
        total=jnp.sum(e,axis=1,keepdims=True)
        p=(e*(1.0/total)).astype(jnp.bfloat16)
        o=jnp.dot(p,v_ref[0,first:first+W,:],preferred_element_type=jnp.float32)
        o_ref[rows,:]=jnp.where(low_lane,o[:QB],o[QB:]).astype(jnp.bfloat16)
        lse=top+jnp.log(total)
        lse_ref[0,rows,:]=jnp.where(low_lane,lse[:QB],lse[QB:])

def attend_forward(projected, documents, QB=256):
    T=projected.shape[1]; D=projected.shape[2]
    dcol=documents.reshape(T,1); drow=documents.reshape(1,T)
    def sp(c): return pl.BlockSpec((1,T,128),lambda h,c=c:(c,0,h))
    return pl.pallas_call(partial(fwd_kernel,QB),grid=(D//128,),
        in_specs=[sp(0),sp(1),sp(2),pl.BlockSpec((T,1),lambda h:(0,0)),pl.BlockSpec((1,T),lambda h:(0,0))],
        out_specs=[pl.BlockSpec((T,128),lambda h:(0,h)),pl.BlockSpec((1,T,128),lambda h:(h,0,0))],
        out_shape=[jax.ShapeDtypeStruct((T,D),jnp.bfloat16),jax.ShapeDtypeStruct((D//128,T,128),jnp.float32)],
        scratch_shapes=[pltpu.VMEM((T,min(T,WINDOW+QB)),jnp.float32)],
        compiler_params=pltpu.CompilerParams(vmem_limit_bytes=48*2**20),
    )(projected,projected,projected,dcol,drow)

QB = 256


def transposed_bias(bias_ref, dcol_ref, drow_ref, QB):
    reach = WINDOW // QB
    for i in range(LEN // QB):
        first = max(0, i - reach) * QB
        W = (i + 1) * QB - first
        kp = first + lax.broadcasted_iota(jnp.int32, (W, QB), 0)
        qp = i * QB + lax.broadcasted_iota(jnp.int32, (W, QB), 1)
        ok = (kp <= qp) & (dcol_ref[first : first + W, :] == drow_ref[:, i * QB : (i + 1) * QB])
        bias_ref[:W, i * QB : (i + 1) * QB] = jnp.where(ok, 0.0, masked_score)


def head_pair_backward(QB, q_ref, k_ref, v_ref, lse_ref, g_ref, bias_ref, dk_ref, dv_ref, put_dq):
    reach = WINDOW // QB
    low_lane = lax.broadcasted_iota(jnp.int32, (QB, 128), 1) < HEAD_DIM
    dk_ref[...] = jnp.zeros_like(dk_ref)
    dv_ref[...] = jnp.zeros_like(dv_ref)
    for i in range(LEN // QB):
        rows = slice(i * QB, (i + 1) * QB)
        first = max(0, i - reach) * QB
        W = (i + 1) * QB - first
        keys = slice(first, first + W)
        q = q_ref[0, rows, :] * jnp.bfloat16(HEAD_DIM**-0.5)
        zero = jnp.zeros_like(q)
        qs = jnp.concatenate([jnp.where(low_lane, q, zero), jnp.where(low_lane, zero, q)], axis=0)
        g = g_ref[rows, :]
        gs = jnp.concatenate([jnp.where(low_lane, g, zero), jnp.where(low_lane, zero, g)], axis=0)
        k = k_ref[0, keys, :]
        st = lax.dot_general(k, qs, NT, preferred_element_type=jnp.float32)
        bias = bias_ref[:W, rows]
        lse = jnp.transpose(lse_ref[0, rows, :])
        lse = jnp.concatenate([lse[0:1, :], lse[64:65, :]], axis=1)
        p = jnp.exp(st + jnp.concatenate([bias, bias], axis=1) - lse)
        dp = lax.dot_general(v_ref[0, keys, :], gs, NT, preferred_element_type=jnp.float32)
        inner = jnp.sum(p * dp, axis=0, keepdims=True)
        ds = (p * (dp - inner)).astype(jnp.bfloat16)
        dk_ref[keys, :] += jnp.dot(ds, qs, preferred_element_type=jnp.float32)
        dv_ref[keys, :] += jnp.dot(p.astype(jnp.bfloat16), gs, preferred_element_type=jnp.float32)
        dq = lax.dot_general(ds, k, TN, preferred_element_type=jnp.float32)
        put_dq(rows, (jnp.where(low_lane, dq[:QB], dq[QB:]) * HEAD_DIM**-0.5).astype(jnp.bfloat16))


def bwd_kernel(QB, q_ref, k_ref, v_ref, lse_ref, g_ref, dcol_ref, drow_ref, out_ref, bias_ref, dk_ref, dv_ref):
    @pl.when(pl.program_id(0) == 0)
    def _():
        transposed_bias(bias_ref, dcol_ref, drow_ref, QB)

    def put_dq(rows, value):
        out_ref[0, rows, :] = value

    head_pair_backward(QB, q_ref, k_ref, v_ref, lse_ref, g_ref, bias_ref, dk_ref, dv_ref, put_dq)
    out_ref[1, :, :] = dk_ref[...].astype(jnp.bfloat16)
    out_ref[2, :, :] = dv_ref[...].astype(jnp.bfloat16)


def attend_backward(projected, documents, lse, grad_mixed, QB=256):
    T=projected.shape[1]; D=projected.shape[2]
    dcol=documents.reshape(T,1); drow=documents.reshape(1,T)
    def sp(c): return pl.BlockSpec((1,T,128),lambda h,c=c:(c,0,h))
    return pl.pallas_call(partial(bwd_kernel,QB),grid=(D//128,),
        in_specs=[sp(0),sp(1),sp(2),pl.BlockSpec((1,T,128),lambda h:(h,0,0)),pl.BlockSpec((T,128),lambda h:(0,h)),pl.BlockSpec((T,1),lambda h:(0,0)),pl.BlockSpec((1,T),lambda h:(0,0))],
        out_specs=pl.BlockSpec((3,T,128),lambda h:(0,0,h)),
        out_shape=jax.ShapeDtypeStruct((3,T,D),jnp.bfloat16),
        scratch_shapes=[pltpu.VMEM((min(T,WINDOW+QB),T),jnp.float32),pltpu.VMEM((T,128),jnp.float32),pltpu.VMEM((T,128),jnp.float32)],
        compiler_params=pltpu.CompilerParams(vmem_limit_bytes=48*2**20),
    )(projected,projected,projected,lse,grad_mixed,dcol,drow)


MESH=pl.DeviceIdType.MESH
TILE=512

def flip(a,b,n):
    out=0
    bit=1
    while bit<n:
        out=out+bit*((a//bit+b//bit)%2)
        bit*=2
    return out

def gelu_pair(x):
    c=0.7978845608028654
    sq=x*x
    t=jnp.tanh(c*(x+0.044715*(x*sq)))
    half=0.5*(1.0+t)
    return x*half, half+x*(0.5*(1.0-t*t))*(c+(3*0.044715*c)*sq)

def moe_kernel(n,cap,square,send_ref,gate_ref,cot_ref,scale_ref,w_ref,
               back_ref,late_ref,chosen_ref,ret_ref,gw_ref,
               recv,gates,cot,w,gw,ret_s,gs_s,ch_s,g_s,racc,sacc,
               send_sem,recv_sem,gate_send,gate_recv,back_send,back_recv,ch_send,ch_recv,on_send,on_recv,w_sem,loc_sem,ret_sem,late_sem):
    per=TILE//cap
    tiles=n//per
    chunks=w_ref.shape[0]
    me=lax.axis_index("expert")
    barrier=pltpu.get_barrier_semaphore()
    def greet(o,_):
        pl.semaphore_signal(barrier,inc=1,device_id={"expert":flip(me,o,n)},device_id_type=MESH)
        return 0
    lax.fori_loop(1,n,greet,0)
    d=lax.axis_index("dp")
    sides=[flip(d,1,chunks),flip(d,2,chunks)] if square else []
    for side in sides:
        pl.semaphore_signal(barrier,inc=1,device_id={"dp":side},device_id_type=MESH)
    pl.semaphore_wait(barrier,n-1+len(sides))
    def on_copy(k):
        return pltpu.make_async_remote_copy(src_ref=w_ref.at[sides[k],k],dst_ref=w.at[sides[k],k],
            send_sem=on_send.at[k],recv_sem=on_recv.at[k],device_id={"dp":sides[1-k]},device_id_type=MESH)
    def on_in(k):
        across=flip(d,3,chunks)
        return pltpu.make_async_remote_copy(src_ref=w_ref.at[sides[k],k],dst_ref=w.at[across,k],
            send_sem=on_send.at[k],recv_sem=on_recv.at[k],device_id={"dp":sides[1-k]},device_id_type=MESH)
    for k in range(len(sides)): on_copy(k).start()

    def copies(src,dst,send,recv_,peer,there):
        return pltpu.make_async_remote_copy(src_ref=src,dst_ref=dst,send_sem=send.at[peer],recv_sem=recv_.at[there],
            device_id={"expert":peer},device_id_type=MESH)
    def row_copy(peer): return copies(send_ref.at[peer],recv.at[me],send_sem,recv_sem,peer,me)
    def gate_copy(peer): return copies(gate_ref.at[peer],gates.at[me],gate_send,gate_recv,peer,me)
    def row_in(src): return copies(send_ref.at[src],recv.at[src],send_sem,recv_sem,src,src)
    def gate_in(src): return copies(gate_ref.at[src],gates.at[src],gate_send,gate_recv,src,src)
    def back_copy(src): return copies(gs_s.at[src],back_ref.at[flip(src,me,n)],back_send,back_recv,src,me)
    def ch_copy(src): return copies(ch_s.at[src],chosen_ref.at[flip(src,me,n)],ch_send,ch_recv,src,me)
    def back_in(src): return copies(gs_s.at[src],back_ref.at[flip(src,me,n)],back_send,back_recv,src,src)
    def ch_in(src): return copies(ch_s.at[src],chosen_ref.at[flip(src,me,n)],ch_send,ch_recv,src,src)

    def push(o,_):
        gate_copy(flip(me,o,n)).start()
        row_copy(flip(me,o,n)).start()
        return 0
    last=(tiles-1)*per
    kept=n-late_ref.shape[0]
    lax.fori_loop(1,last,push,0)
    own=[pltpu.make_async_copy(send_ref.at[me],recv.at[me],loc_sem.at[0]),
         pltpu.make_async_copy(gate_ref.at[me],gates.at[me],loc_sem.at[1]),
         pltpu.make_async_copy(cot_ref,cot,loc_sem.at[2]),
        ]+[pltpu.make_async_copy(w_ref.at[c],w.at[c],w_sem.at[i]) for i,c in enumerate(([d]+sides) if square else range(chunks))]
    for c in own: c.start()
    def wipe(c,_):
        gw[c]=jnp.zeros(gw.shape[1:],jnp.float32)
        return 0
    lax.fori_loop(0,chunks,wipe,0)
    for c in own: c.wait()
    own_back=pltpu.make_async_copy(gs_s.at[me],back_ref.at[0],loc_sem.at[1])
    own_ch=pltpu.make_async_copy(ch_s.at[me],chosen_ref.at[0],loc_sem.at[0])
    def keep(o): return pltpu.make_async_copy(gs_s.at[flip(me,o,n)],late_ref.at[o-kept],late_sem.at[o-kept])

    def tile(t,_):
        @pl.when(t==1)
        def _():
            lax.fori_loop(last,n,push,0)
        block=flip(me//per,t,tiles)
        def arrive(j,_):
            src=block*per+j
            @pl.when(src!=me)
            def _():
                gate_in(src).wait_recv()
                row_in(src).wait_recv()
            return 0
        lax.fori_loop(0,per,arrive,0)
        at=pl.ds(pl.multiple_of(block*per,per),per)
        rows=pl.ds(pl.multiple_of(block*TILE,TILE),TILE)
        gate=jnp.transpose(jnp.sum(gates[at],axis=0))[:,0:1]
        scale=jnp.concatenate([jnp.broadcast_to(scale_ref[pl.ds(block*per+j,1),0:1],(cap,1)) for j in range(per)],axis=0)
        grad_out=cot[rows,:].astype(jnp.float32)*scale
        g_s[...]=(gate*grad_out).astype(jnp.bfloat16)
        racc[...]=jnp.zeros_like(racc)
        sacc[...]=jnp.zeros_like(sacc)
        def chunk(i,_):
            c=flip(d,i,chunks)
            if square:
                @pl.when((t==0)&(i==chunks-1))
                def _():
                    for k in range(2): on_in(k).wait_recv()
            x=recv[at].reshape(TILE,recv.shape[2])
            g=g_s[...]
            act,slope=gelu_pair(jnp.dot(x,w[c,0],preferred_element_type=jnp.float32))
            a=act.astype(jnp.bfloat16)
            ga=jnp.dot(g,w[c,1],preferred_element_type=jnp.float32).astype(jnp.bfloat16)
            gp=(ga.astype(jnp.float32)*slope).astype(jnp.bfloat16)
            racc[...]+=lax.dot_general(a,w[c,1],NT,preferred_element_type=jnp.float32)
            sacc[...]+=lax.dot_general(gp,w[c,0],NT,preferred_element_type=jnp.float32)
            gw[c,0]+=lax.dot_general(x,gp,TN,preferred_element_type=jnp.float32)
            gw[c,1]+=lax.dot_general(g,a,TN,preferred_element_type=jnp.float32)
            @pl.when(t==tiles-1)
            def _():
                w[c]=gw[c].astype(jnp.bfloat16)
                pltpu.make_async_copy(w.at[c],gw_ref.at[c],w_sem.at[c]).start()
            return 0
        lax.fori_loop(0,chunks,chunk,0)
        gs_s[at]=sacc[...].astype(jnp.bfloat16).reshape(per,cap,recv.shape[2])
        def give(j,_):
            src=block*per+j
            o=flip(src,me,n)
            @pl.when((src!=me)&(o<kept))
            def _():
                back_copy(src).start()
            @pl.when(src==me)
            def _():
                own_back.start()
            @pl.when(o>=kept)
            def _():
                keep(o).start()
            return 0
        lax.fori_loop(0,per,give,0)
        ret=racc[...].astype(jnp.bfloat16)
        ret_s[at]=ret.reshape(per,cap,recv.shape[2])
        pltpu.make_async_copy(ret_s.at[at],ret_ref.at[at],ret_sem.at[t]).start()
        grad_out=cot[rows,:].astype(jnp.float32)*scale
        chosen=jnp.sum(grad_out*ret.astype(jnp.float32),axis=1,keepdims=True)*gate*(1.0-gate)
        chosen=jnp.transpose(jnp.broadcast_to(chosen,(TILE,128)))[0:8,:]
        def tell(j,_):
            src=block*per+j
            ch_s[src]=chosen
            @pl.when(src!=me)
            def _():
                ch_copy(src).start()
            @pl.when(src==me)
            def _():
                own_ch.start()
            return 0
        lax.fori_loop(0,per,tell,0)
        return 0
    lax.fori_loop(0,tiles,tile,0)
    own_ch.wait()
    own_back.wait()
    def settle(o,_):
        peer=flip(me,o,n)
        gate_copy(peer).wait_send()
        row_copy(peer).wait_send()
        ch_copy(peer).wait_send()
        ch_in(peer).wait_recv()
        @pl.when(o<kept)
        def _():
            back_copy(peer).wait_send()
            back_in(peer).wait_recv()
        @pl.when(o>=kept)
        def _():
            keep(o).wait()
        return 0
    lax.fori_loop(1,n,settle,0)
    def stored(t,_):
        block=flip(me//per,t,tiles)
        at=pl.ds(pl.multiple_of(block*per,per),per)
        pltpu.make_async_copy(ret_s.at[at],ret_ref.at[at],ret_sem.at[t]).wait()
        return 0
    lax.fori_loop(0,tiles,stored,0)
    for c in range(chunks): pltpu.make_async_copy(w.at[c],gw_ref.at[c],w_sem.at[c]).wait()
    for k in range(len(sides)): on_copy(k).wait_send()

def late_kernel(n,gs_ref,out_ref,send_sem,recv_sem):
    count=gs_ref.shape[0]
    me=lax.axis_index("expert")
    barrier=pltpu.get_barrier_semaphore()
    def greet(k,_):
        pl.semaphore_signal(barrier,inc=1,device_id={"expert":flip(me,n-count+k,n)},device_id_type=MESH)
        return 0
    lax.fori_loop(0,count,greet,0)
    pl.semaphore_wait(barrier,count)
    def copy(k):
        return pltpu.make_async_remote_copy(src_ref=gs_ref.at[k],dst_ref=out_ref.at[k],send_sem=send_sem.at[k],recv_sem=recv_sem.at[k],
            device_id={"expert":flip(me,n-count+k,n)},device_id_type=MESH)
    def go(k,_):
        copy(k).start()
        return 0
    lax.fori_loop(0,count,go,0)
    def end(k,_):
        copy(k).wait()
        return 0
    lax.fori_loop(0,count,end,0)

def moe(send_rows,gate_slots,cot,scale,weights,square):
    n,cap,D=send_rows.shape
    chunks,_,_,FC=weights.shape
    per=TILE//cap
    any_=pl.BlockSpec(memory_space=pl.ANY)
    bf=jnp.bfloat16; f32=jnp.float32
    dma=pltpu.SemaphoreType.DMA
    flops=6*2*n*cap*D*chunks*FC
    back,late,chosen,ret,gw=pl.pallas_call(partial(moe_kernel,n,cap,square),
        out_shape=[jax.ShapeDtypeStruct((n-per,cap,D),bf),jax.ShapeDtypeStruct((per,cap,D),bf),jax.ShapeDtypeStruct((n,8,TILE),f32),
                   jax.ShapeDtypeStruct((n,cap,D),bf),jax.ShapeDtypeStruct(weights.shape,bf)],
        in_specs=[any_,any_,any_,pl.BlockSpec(memory_space=pltpu.VMEM),any_],
        out_specs=[any_]*5,
        scratch_shapes=[pltpu.VMEM((n,cap,D),bf),pltpu.VMEM((n,8,TILE),f32),pltpu.VMEM((n*cap,D),bf),
            pltpu.VMEM(weights.shape,bf),pltpu.VMEM(weights.shape,f32),pltpu.VMEM((n,cap,D),bf),pltpu.VMEM((n,cap,D),bf),
            pltpu.VMEM((n,8,TILE),f32),pltpu.VMEM((TILE,D),bf),pltpu.VMEM((TILE,D),f32),pltpu.VMEM((TILE,D),f32)]
            +[dma((n,))]*8+[dma((2,)),dma((2,)),dma((chunks,)),dma((3,)),dma((n//per,)),dma((per,))],
        compiler_params=pltpu.CompilerParams(vmem_limit_bytes=62*2**20,collective_id=1,has_side_effects=True),
        cost_estimate=pl.CostEstimate(flops=flops,bytes_accessed=40*2**20,transcendentals=0),
    )(send_rows,gate_slots,cot,scale,weights)
    return back,late,chosen,ret,gw

def send_late(late,n):
    per,cap,D=late.shape
    any_=pl.BlockSpec(memory_space=pl.ANY)
    bf=jnp.bfloat16
    dma=pltpu.SemaphoreType.DMA
    return pl.pallas_call(partial(late_kernel,n),
        out_shape=jax.ShapeDtypeStruct((per,cap,D),bf),in_specs=[any_],out_specs=any_,
        scratch_shapes=[dma((per,)),dma((per,))],
        compiler_params=pltpu.CompilerParams(collective_id=5,has_side_effects=True),
        cost_estimate=pl.CostEstimate(flops=0,bytes_accessed=100*2**20,transcendentals=0),
    )(late)


def near(dps,pairs):
    d=lax.axis_index("dp"); me=lax.axis_index("expert")
    core=me%2; pair=me//2
    partner={"expert":me+1-2*core}
    over=[((d+k)%dps,{"dp":(d+k)%dps}) for k in range(1,dps)]
    along=[((pair+k)%pairs,{"expert":2*((pair+k)%pairs)+core}) for k in range(1,pairs)]
    return d,pair,core,partner,over,along

def greet_all(devices):
    barrier=pltpu.get_barrier_semaphore()
    for dev in devices:
        pl.semaphore_signal(barrier,inc=1,device_id=dev,device_id_type=MESH)
    pl.semaphore_wait(barrier,len(devices))

def remote(src,dst,send,recv,dev):
    return pltpu.make_async_remote_copy(src_ref=src,dst_ref=dst,send_sem=send,recv_sem=recv,device_id=dev,device_id_type=MESH)

def upright(row):
    return jnp.transpose(row.astype(jnp.float32))[:, 0:1].astype(jnp.int32)


def head_kernel(dps, pairs, n, cap, w_ref, v_ref, x_ref, cot_ref, order_ref, counts_ref, drow_ref, ew_ref,
                w_out, vec_out, slot_out, cot_out, proj_out, normed_out, mixed_out, lse_out, hidden_out,
                gate_out, send_out, tile_out, ew_out,
                ew32, ew, both, blk, vboth, vblk, w, vall, slots, unit, normed, proj, mixed, lse, bias, sent, cots, sends,
                tiles, s1, r1, loc, zs, zr, vzs, vzr, ds_, dr, vds, vdr, ps, pr, cs, cr, ewl, xs, xr, ys, yr, out_sem, send_sem):
    r = w_ref.shape[1]
    R = 2 * r
    T, D = x_ref.shape
    d, pair, core, partner, over, along = near(dps, pairs)
    me = lax.axis_index("expert")
    bf, f32 = jnp.bfloat16, jnp.float32
    ew_load = pltpu.make_async_copy(ew_ref.at[0], ew32, ewl.at[0])
    ew_load.start()
    barrier = pltpu.get_barrier_semaphore()

    def greet(o, _):
        pl.semaphore_signal(barrier, inc=1, device_id={"expert": flip(me, o, n)}, device_id_type=MESH)
        return 0

    lax.fori_loop(1, n, greet, 0)
    for _, dev in over:
        pl.semaphore_signal(barrier, inc=1, device_id=dev, device_id_type=MESH)
    pl.semaphore_wait(barrier, n - 1 + dps - 1)

    side_x, side_y = flip(d, 1, dps), flip(d, 2, dps)
    to_x, to_y = {"dp": side_x}, {"dp": side_y}

    def x_copy(src, slot, m):
        return remote(src, ew_out.at[slot, m], xs.at[slot, m], xr.at[slot, m], to_x)

    def y_copy(src, slot, m):
        return remote(src, ew_out.at[slot, m], ys.at[slot, m], yr.at[slot, m], to_y)

    mine = pl.ds(pl.multiple_of(core * r, 8), r)
    half = pl.ds(core * 2, 2)
    rest = pl.ds(2 - core * 2, 2)

    def rows(dd, q):
        return pl.ds(pl.multiple_of((dd * pairs + q) * R, 16), R)

    c1 = [
        remote(w_ref, both.at[:, mine, :], s1.at[0], r1.at[0], partner),
        remote(v_ref, vboth.at[core], s1.at[1], r1.at[1], partner),
    ]
    for c in c1:
        c.start()
    both[:, mine, :] = w_ref[...]
    vboth[core] = v_ref[...]
    for c in c1:
        c.wait()
    blk[...] = both[...].astype(bf)
    vblk[...] = (vboth[0] + vboth[1]).astype(bf)
    w[:, rows(d, pair), :] = blk[...]
    vall[d, pair] = vblk[...]
    def along_copy(q, dev):
        return remote(blk.at[half], w.at[half, rows(d, pair), :], zs.at[q], zr.at[pair], dev)

    def over_copy(dd, q, dev):
        here = w.at[half, rows(d, q), :]
        return remote(here, here, ds_.at[dd, q], dr.at[d, q], dev)

    def hand(dd, q):
        here = w.at[half, rows(dd, q), :]
        return remote(here, here, ps.at[dd, q], pr.at[dd, q], partner)

    def v_along(q, dev):
        return remote(vblk, vall.at[d, pair], vzs.at[q], vzr.at[pair], dev)

    def v_over(dd, dev):
        return remote(vall.at[d], vall.at[d], vds.at[dd], vdr.at[d], dev)

    for q, dev in along:
        along_copy(q, dev).start()
        v_along(q, dev).start()
    for dd, dev in over:
        over_copy(dd, pair, dev).start()

    tokens_across = lax.broadcasted_iota(jnp.int32, (T, T), 1)
    position = lax.broadcasted_iota(jnp.int32, (8, T), 1)
    sorted_slot, end = position, 0
    for e in range(n):
        count = counts_ref[0, e]
        end = end + count
        sorted_slot = sorted_slot + jnp.where(position >= end, cap - count, 0)
    slot_col = upright(sorted_slot)
    order_col = upright(jnp.broadcast_to(order_ref[...], (8, T)))
    slots[...] = jnp.broadcast_to(
        jnp.sum(jnp.where(order_col == tokens_across, slot_col, 0), axis=0, keepdims=True), (8, T)
    )
    doc_col = upright(jnp.broadcast_to(drow_ref[...], (8, T)))

    def pick(p):
        here = lax.broadcasted_iota(jnp.int32, (cap, T), 0) + p * cap
        return here == slots[0:1, :]

    def cot_copy(p):
        return remote(cots.at[p], cot_out.at[me], cs.at[p], cr.at[me], {"expert": p})

    def cot_in(p):
        return remote(cots.at[p], cot_out.at[p], cs.at[p], cr.at[p], {"expert": p})

    def place(i, _):
        p = flip(me, n - 1 - i, n)
        cots[p] = jnp.dot(pick(p).astype(bf), cot_ref[...], preferred_element_type=f32).astype(bf)

        return 0

    groups = [d] + [x[0] for x in over]
    lax.fori_loop(0, n // 2, place, 0)
    for q, dev in along:
        here = w.at[half, rows(d, q), :]
        remote(here, here, zs.at[q], zr.at[q], dev).wait_recv()
        for dd, dev2 in over:
            over_copy(dd, q, dev2).start()
        hand(d, q).start()
    for q, dev in along:
        remote(vblk, vall.at[d, q], vzs.at[q], vzr.at[q], dev).wait_recv()
    for dd, dev in over:
        v_over(dd, dev).start()
    ew_load.wait()
    for m in range(2):
        ew[m] = ew32[m].astype(bf)
    own_ew = pltpu.make_async_copy(ew, ew_out.at[d], ewl.at[0])
    own_ew.start()
    for m in range(2):
        x_copy(ew.at[m], d, m).start()
        y_copy(ew.at[1 - m], d, 1 - m).start()
    lax.fori_loop(n // 2, n, place, 0)

    def give(i, _):
        cot_copy(flip(me, n - 1 - i, n)).start()
        return 0

    lax.fori_loop(0, n - 1, give, 0)
    own_cot = pltpu.make_async_copy(cots.at[me], cot_out.at[me], loc.at[0])
    own_cot.start()

    def unit_rows(b):
        at = pl.ds(b * 256, 256)
        x = x_ref[at, :].astype(f32)
        center = x - jnp.mean(x, axis=-1, keepdims=True)
        unit[at, :] = center * lax.rsqrt(jnp.mean(center * center, axis=-1, keepdims=True) + norm_eps)

    for b in range(T // 256):
        unit_rows(b)
    for i in range(LEN // QB):
        first = max(0, i - WINDOW // QB) * QB
        W = (i + 1) * QB - first
        qp = i * QB + lax.broadcasted_iota(jnp.int32, (QB, W), 0)
        kp = first + lax.broadcasted_iota(jnp.int32, (QB, W), 1)
        ok = (kp <= qp) & (doc_col[i * QB : (i + 1) * QB, :] == drow_ref[:, first : first + W])
        bias[i * QB : (i + 1) * QB, :W] = jnp.where(ok, 0.0, masked_score)
    for q in [pair] + [x[0] for x in along]:
        for dd, dev in over:
            here = w.at[half, rows(dd, q), :]
            remote(here, here, ds_.at[dd, q], dr.at[dd, q], dev).wait_recv()
            hand(dd, q).start()
    for dd, dev in over:
        remote(vall.at[dd], vall.at[dd], vds.at[dd], vdr.at[dd], dev).wait_recv()
    vec = jnp.zeros(vec_out.shape, f32)
    for dd in range(dps):
        for q in range(pairs):
            vec = vec + vall[dd, q].astype(f32)
    vec_out[...] = vec
    slot_out[...] = slots[...]
    normed[...] = (unit[...] * vec_out[0:1, :]).astype(bf)

    def from_partner(dd, q):
        there = w.at[rest, rows(dd, q), :]
        remote(there, there, ps.at[dd, q], pr.at[dd, q], partner).wait_recv()

    for dd, dev in over:
        from_partner(dd, pair)
    for q, _ in along:
        for dd in groups:
            from_partner(dd, q)

    outs = [
        pltpu.make_async_copy(w, w_out, out_sem.at[0]),
        pltpu.make_async_copy(normed, normed_out, out_sem.at[1]),
    ]
    for c in outs:
        c.start()

    def project(i, _):
        c = i // 2
        at = pl.ds(pl.multiple_of(i % 2 * (T // 2), T // 2), T // 2)
        proj[c, at, :] = jnp.dot(normed[at, :], w[c], preferred_element_type=f32).astype(bf)
        return 0

    lax.fori_loop(0, 6, project, 0)
    outs.append(pltpu.make_async_copy(proj, proj_out, out_sem.at[2]))
    outs[-1].start()
    low_lane = lax.broadcasted_iota(jnp.int32, (QB, 128), 1) < HEAD_DIM

    def attend(h, _):
        lanes = pl.ds(pl.multiple_of(h * 128, 128), 128)
        for i in range(LEN // QB):
            here = slice(i * QB, (i + 1) * QB)
            first = max(0, i - WINDOW // QB) * QB
            W = (i + 1) * QB - first
            keys = slice(first, first + W)
            q = proj[0, here, lanes] * jnp.bfloat16(HEAD_DIM**-0.5)
            zero = jnp.zeros_like(q)
            qs = jnp.concatenate([jnp.where(low_lane, q, zero), jnp.where(low_lane, zero, q)], axis=0)
            s = lax.dot_general(qs, proj[1, keys, lanes], NT, preferred_element_type=f32)
            s = (s.reshape(2, QB, W) + bias[here, :W][None]).reshape(2 * QB, W)
            top = jnp.max(s, axis=1, keepdims=True)
            e = jnp.exp(s - top)
            total = jnp.sum(e, axis=1, keepdims=True)
            p = (e * (1.0 / total)).astype(bf)
            o = jnp.dot(p, proj[2, keys, lanes], preferred_element_type=f32)
            mixed[here, lanes] = jnp.where(low_lane, o[:QB], o[QB:]).astype(bf)
            ends = top + jnp.log(total)
            lse[h, here, :] = jnp.where(low_lane, ends[:QB], ends[QB:])
        return 0

    lax.fori_loop(0, D // 128, attend, 0)
    outs += [
        pltpu.make_async_copy(mixed, mixed_out, out_sem.at[3]),
        pltpu.make_async_copy(lse, lse_out, out_sem.at[4]),
    ]
    outs[-2].start()
    outs[-1].start()
    E = vec_out.shape[0] - 2
    hidden = unit

    def finish(b, _):
        at = pl.ds(pl.multiple_of(b * 256, 256), 256)
        state = x_ref[at, :].astype(f32) + jnp.dot(mixed[at, :], w[3], preferred_element_type=f32)
        hidden[at, :] = state
        center = state - jnp.mean(state, axis=-1, keepdims=True)
        spread = jnp.mean(center * center, axis=-1, keepdims=True)
        two = center * lax.rsqrt(spread + norm_eps) * vec_out[1:2, :]
        sent[at, :] = two.astype(bf)
        which = lax.broadcasted_iota(jnp.int32, (vec_out.shape[0], 256), 0) - 2
        chosen = (which == slots[0:1, at] // cap).astype(bf)
        rows_c = lax.dot_general(chosen, vec_out[...].astype(bf), TN, preferred_element_type=f32)
        logit = jnp.sum(two * rows_c, axis=1, keepdims=True)
        gate = 1.0 / (1.0 + jnp.exp(-logit))
        gate_out[:, at] = jnp.transpose(jnp.broadcast_to(gate, (256, 128)))[0:8, :]
        return 0

    lax.fori_loop(0, T // 256, finish, 0)
    outs.append(pltpu.make_async_copy(hidden, hidden_out, out_sem.at[5]))
    outs[-1].start()
    tiles[...] = jnp.zeros(tiles.shape, f32)
    part = pl.ds(pl.multiple_of(me % (TILE // cap) * cap, 128), cap)

    def fill(p, _):
        chosen = pick(p)
        sends[p] = jnp.dot(chosen.astype(bf), sent[...], preferred_element_type=f32).astype(bf)
        tiles[p, :, part] = lax.dot_general(
            gate_out[...], chosen.astype(f32), NT, precision=lax.Precision.HIGHEST, preferred_element_type=f32
        )
        pltpu.make_async_copy(sends.at[p], send_out.at[p], send_sem).start()
        return 0

    lax.fori_loop(0, n, fill, 0)
    outs.append(pltpu.make_async_copy(tiles, tile_out, out_sem.at[6]))
    outs[-1].start()
    for q, dev in along:
        along_copy(q, dev).wait_send()
        v_along(q, dev).wait_send()
        hand(d, q).wait_send()
    for dd, dev in over:
        v_over(dd, dev).wait_send()
        for q in [pair] + [x[0] for x in along]:
            over_copy(dd, q, dev).wait_send()
            hand(dd, q).wait_send()

    def settle(o, _):
        p = flip(me, o, n)
        cot_copy(p).wait_send()
        cot_in(p).wait_recv()
        return 0

    lax.fori_loop(1, n, settle, 0)
    pltpu.make_async_copy(cots.at[me], cot_out.at[me], loc.at[0]).wait()
    own_ew.wait()
    for m in range(2):
        x_copy(ew.at[m], d, m).wait_send()
        y_copy(ew.at[m], d, m).wait_send()
        x_copy(ew.at[m], side_x, m).wait_recv()
        y_copy(ew.at[m], side_y, m).wait_recv()
    for c in outs:
        c.wait()
    pltpu.make_async_copy(sends, send_out, send_sem).wait()


def head(weights, vectors, inputs, cotangent, token_order, counts, documents, expert_weights, dps, n, cap):
    pairs = n // 2
    m, r, D = weights.shape
    T = inputs.shape[0]
    k = vectors.shape[0]
    f32, bf = jnp.float32, jnp.bfloat16
    dma = pltpu.SemaphoreType.DMA
    any_ = pl.BlockSpec(memory_space=pl.ANY)
    vm = pl.BlockSpec(memory_space=pltpu.VMEM)
    dev = lax.axis_index("dp") * n + lax.axis_index("expert")
    K = (k + 15) // 16 * 16
    placed = lax.dynamic_update_slice(jnp.zeros((K, D), f32), vectors, (0, dev * r))
    shape = jax.ShapeDtypeStruct
    grid = lambda: dma((dps, pairs))
    return pl.pallas_call(
        partial(head_kernel, dps, pairs, n, cap),
        out_shape=[
            shape((m, D, D), bf), shape((K, D), f32), shape((8, T), jnp.int32), shape((n, cap, D), bf),
            shape((3, T, D), bf), shape((T, D), bf), shape((T, D), bf), shape((D // 128, T, 128), f32),
            shape((T, D), f32), shape((8, T), f32), shape((n, cap, D), bf), shape((n, 8, TILE), f32),
            shape((dps,) + expert_weights.shape[1:], bf),
        ],
        in_specs=[vm] * 5 + [pl.BlockSpec(memory_space=pltpu.SMEM), vm, any_],
        out_specs=[any_, vm, vm, any_, any_, any_, any_, any_, any_, vm, any_, any_, any_],
        scratch_shapes=[
            pltpu.VMEM(expert_weights.shape[1:], f32), pltpu.VMEM(expert_weights.shape[1:], bf),
            pltpu.VMEM((m, 2 * r, D), f32), pltpu.VMEM((m, 2 * r, D), bf), pltpu.VMEM((2, K, D), f32),
            pltpu.VMEM((K, D), bf), pltpu.VMEM((m, D, D), bf), pltpu.VMEM((dps, pairs, K, D), bf),
            pltpu.VMEM((8, T), jnp.int32), pltpu.VMEM((T, D), f32), pltpu.VMEM((T, D), bf),
            pltpu.VMEM((3, T, D), bf), pltpu.VMEM((T, D), bf), pltpu.VMEM((D // 128, T, 128), f32),
            pltpu.VMEM((T, min(T, WINDOW + QB)), f32), pltpu.VMEM((T, D), bf), pltpu.VMEM((n, cap, D), bf),
            pltpu.VMEM((n, cap, D), bf), pltpu.VMEM((n, 8, TILE), f32),
            dma((2,)), dma((2,)), dma((1,)), dma((pairs,)), dma((pairs,)), dma((pairs,)), dma((pairs,)),
            grid(), grid(), dma((dps,)), dma((dps,)), grid(), grid(), dma((n,)), dma((n,)),
            dma((1,)), dma((dps, 2)), dma((dps, 2)), dma((dps, 2)), dma((dps, 2)), dma((7,)), dma(()),
        ],
        compiler_params=pltpu.CompilerParams(
            vmem_limit_bytes=60 * 2**20, collective_id=2, has_side_effects=True
        ),
        cost_estimate=pl.CostEstimate(flops=20 * T * D * D, bytes_accessed=200 * 2**20, transcendentals=0),
    )(weights, placed, inputs, cotangent, token_order, counts, documents, expert_weights)


def tail_kernel(dps, pairs, cap, q_ref, k_ref, v_ref, lse_ref, drow_ref, vec_ref, slot_ref, gate_ref,
                scale_ref, chosen_ref, x_ref, mixed_ref, prod_ref, w_ref, in_ref, late_ref, back_ref, cot_ref,
                hidden_ref,
                out_ref, vec_out, dx_ref, block_ref,
                bias_ref, dk_ref, dv_ref, left, right, got, own, total, in2, tb, in3, u, in4, w, gh, xin,
                ret, hid, back, cot, g_ref, chs, dcol_ref,
                ls, s1, r1, s2, r2, s3, r3, s4, r4, rs, rr, bs, br, own_sem, dx_sem, block_sem):
    h = pl.program_id(0)
    n = 2 * pairs
    count = late_ref.shape[0]
    kept = n - count
    early = kept * cap
    per = TILE // cap
    me = lax.axis_index("expert")
    d, pair, core, partner, over, along = near(dps, pairs)
    rows = out_ref.shape[1]
    R = 2 * rows
    T, D = x_ref.shape
    bf, f32 = jnp.bfloat16, jnp.float32
    B = 256
    loads = [
        pltpu.make_async_copy(back_ref, back.at[pl.ds(0, kept)], ls.at[0]),
        pltpu.make_async_copy(hidden_ref, hid, ls.at[1]),
        pltpu.make_async_copy(cot_ref, cot, ls.at[2]),
        pltpu.make_async_copy(w_ref, w, ls.at[3]),
        pltpu.make_async_copy(mixed_ref, left.at[1], ls.at[4]),
        pltpu.make_async_copy(x_ref, left.at[0], ls.at[5]),
        pltpu.make_async_copy(in_ref, xin, ls.at[6]),
    ]

    def product(m):
        return lax.dot_general(left[m // 3], right[m], TN, preferred_element_type=f32)

    def ret_copy(peer):
        return remote(prod_ref.at[peer], ret.at[me], rs.at[peer], rr.at[me], {"expert": peer})

    def ret_in(peer):
        return remote(prod_ref.at[peer], ret.at[peer], rs.at[peer], rr.at[peer], {"expert": peer})

    own_ret = pltpu.make_async_copy(prod_ref.at[me], ret.at[me], own_sem)

    def late_copy(k):
        return remote(late_ref.at[k], back.at[kept + k], bs.at[k], br.at[k], {"expert": flip(me, kept + k, n)})

    def to_partner(i):
        return remote(total.at[i], got.at[i], s1.at[i], r1.at[i], partner)

    def column(row):
        return jnp.transpose(row)[:, 0:1]

    def normal(x):
        center = x - jnp.mean(x, axis=-1, keepdims=True)
        scale = lax.rsqrt(jnp.mean(center * center, axis=-1, keepdims=True) + norm_eps)
        return center * scale, scale

    def normal_back(grad, unit, scale, gain):
        gu = grad * gain
        return scale * (
            gu - jnp.mean(gu, axis=-1, keepdims=True) - unit * jnp.mean(gu * unit, axis=-1, keepdims=True)
        )

    def offset_slots(at):
        slot = slot_ref[:, at]
        return flip(slot // cap, me, n) * cap + slot % cap

    def match(slot_rows, first, count):
        here = column(slot_rows.astype(f32))
        return here == (first + lax.broadcasted_iota(jnp.int32, (B, count), 1)).astype(f32)

    @pl.when(h == 0)
    def _():
        for c in loads:
            c.start()
        barrier = pltpu.get_barrier_semaphore()

        def greet(o, _):
            pl.semaphore_signal(barrier, inc=1, device_id={"expert": flip(me, o, n)}, device_id_type=MESH)
            return 0

        lax.fori_loop(1, n, greet, 0)
        for _, dev in over:
            pl.semaphore_signal(barrier, inc=1, device_id=dev, device_id_type=MESH)
        pl.semaphore_wait(barrier, n - 1 + dps - 1)
        for j in range(count):
            late_copy(j).start()

        def send(i, _):
            ret_copy(flip(me, 1 + i, n)).start()
            return 0

        lax.fori_loop(0, n // 2 - 1, send, 0)
        own_ret.start()
        dcol_ref[...] = upright(jnp.broadcast_to(drow_ref[...], (8, T)))
        transposed_bias(bias_ref, dcol_ref, drow_ref, QB)
        part = pl.ds(pl.multiple_of(me % per * cap, 128), cap)
        for o in range(n):
            chs[:, o * cap : (o + 1) * cap] = chosen_ref[o, :, part]
        loads[0].wait()

        def first_rows(b, _):
            at = pl.ds(pl.multiple_of(b * B, B), B)
            pick = match(offset_slots(at), 0, early).astype(bf)
            gh[at, :] = jnp.dot(pick, back[pl.ds(0, kept)].reshape(early, D), preferred_element_type=f32)
            return 0

        lax.fori_loop(0, T // B, first_rows, 0)
        vec_out[...] = jnp.zeros(vec_out.shape, f32)
        for c in loads[1:4]:
            c.wait()
        for j in range(count):
            late_copy(j).wait_recv()
        lax.fori_loop(n // 2 - 1, n - 1, send, 0)

        def second(b, _):
            at = pl.ds(pl.multiple_of(b * B, B), B)
            slot_rows = offset_slots(at)
            all_slots = match(slot_rows, 0, n * cap)
            chosen = jnp.sum(jnp.where(all_slots, chs[0:1, :], 0.0), axis=1, keepdims=True)
            pick = match(slot_rows, early, count * cap).astype(bf)
            sent = gh[at, :] + jnp.dot(
                pick, back[pl.ds(kept, count)].reshape(count * cap, D), preferred_element_type=f32
            )
            which = lax.broadcasted_iota(jnp.int32, (vec_ref.shape[0], B), 0) - 2
            expert = which == slot_ref[0:1, at] // cap
            centroid = lax.dot_general(
                expert.astype(bf), vec_ref[...].astype(bf), TN, preferred_element_type=f32
            )
            grad = sent + chosen * centroid
            unit, scale = normal(hid[at, :])
            gain = vec_ref[1:2, :]
            chosen_row = jnp.transpose(jnp.broadcast_to(chosen, (B, 128)))[0:1, :]
            vec_out[...] += jnp.dot(
                jnp.where(expert, chosen_row, 0.0), unit * gain,
                precision=lax.Precision.HIGHEST, preferred_element_type=f32,
            )
            vec_out[1:2, :] += jnp.sum(grad * unit, axis=0, keepdims=True)
            total_grad = cot[at, :].astype(f32) * scale_ref[0:1, 0:1] + normal_back(grad, unit, scale, gain)
            gh[at, :] = total_grad
            low = total_grad.astype(bf)
            right[3, at, :] = low
            g_ref[at, :] = lax.dot_general(low, w[3], NT, preferred_element_type=f32).astype(bf)
            return 0

        lax.fori_loop(0, T // B, second, 0)
        loads[4].wait()
        out = product(3)

        @pl.when(core == 0)
        def _():
            total[1] = out.astype(bf)
            to_partner(1).start()

        @pl.when(core == 1)
        def _():
            own[1] = out

    lanes = pl.ds(pl.multiple_of(h * 128, 128), 128)

    def put_dq(r, value):
        right[0, r, lanes] = value

    head_pair_backward(
        QB, q_ref, k_ref, v_ref, lse_ref, g_ref.at[:, lanes], bias_ref, dk_ref, dv_ref, put_dq
    )
    right[1, :, lanes] = dk_ref[...].astype(bf)
    right[2, :, lanes] = dv_ref[...].astype(bf)

    @pl.when(h == pl.num_programs(0) - 1)
    def _():
        loads[5].wait()

        @pl.when(core == 0)
        def _():
            total[0] = product(2).astype(bf)
            to_partner(0).start()
            own[0] = product(0)
            own[1] = product(1)

        @pl.when(core == 1)
        def _():
            total[0] = product(0).astype(bf)
            to_partner(0).start()
            total[1] = product(1).astype(bf)
            to_partner(1).start()
            own[0] = product(2)

        for i in range(2):
            to_partner(i).wait_send()
            to_partner(i).wait_recv()
            total[i] = (own[i] + got[i].astype(f32)).astype(bf)

        order = along + [(pair, None)]

        def piece(dd, q):
            return pl.ds(pl.multiple_of((dd * pairs + q) * R, 16), R)

        c2 = []
        for q, _ in order:
            for dd, dev in over:
                c = remote(total.at[:, piece(dd, q), :], in2.at[d, q], s2.at[dd, q], r2.at[d, q], dev)
                c.start()
                c2.append(c)
        loads[6].wait()

        def norm_one(b, _):
            at = pl.ds(pl.multiple_of(b * B, B), B)
            gn = sum(
                lax.dot_general(right[c, at, :], w[c], NT, preferred_element_type=f32) for c in range(3)
            )
            unit, scale = normal(xin[at, :].astype(f32))
            vec_out[0:1, :] += jnp.sum(gn * unit, axis=0, keepdims=True)
            gh[at, :] += normal_back(gn, unit, scale, vec_ref[0:1, :])
            return 0

        lax.fori_loop(0, T // B, norm_one, 0)
        dx = pltpu.make_async_copy(gh, dx_ref, dx_sem)
        dx.start()
        c3 = []
        for q, zdev in order:
            acc = total[:, piece(d, q), :].astype(f32)
            for dd, dev in over:
                remote(in2.at[dd, q], in2.at[dd, q], s2.at[dd, q], r2.at[dd, q], dev).wait_recv()
                acc = acc + in2[dd, q].astype(f32)
            if zdev is None:
                u[...] = acc
            else:
                tb[q] = acc.astype(bf)
                c = remote(tb.at[q], in3.at[pair], s3.at[q], r3.at[pair], zdev)
                c.start()
                c3.append(c)

        def settle(o, _):
            peer = flip(me, o, n)
            ret_copy(peer).wait_send()
            ret_in(peer).wait_recv()
            return 0

        lax.fori_loop(1, n, settle, 0)
        own_ret.wait()

        def add_rows(b, _):
            at = pl.ds(pl.multiple_of(b * B, B), B)
            pick = match(slot_ref[:, at], 0, n * cap).astype(bf)
            got_rows = jnp.dot(pick, ret[...].reshape(n * cap, D), preferred_element_type=f32)
            hid[at, :] += column(gate_ref[:, at]) * got_rows
            return 0

        lax.fori_loop(0, T // B, add_rows, 0)
        block = pltpu.make_async_copy(hid, block_ref, block_sem)
        block.start()
        acc = u[...]
        for q, dev in along:
            remote(in3.at[q], in3.at[q], s3.at[q], r3.at[q], dev).wait_recv()
            acc = acc + in3[q].astype(f32)
        u[...] = acc
        theirs = pl.ds(pl.multiple_of((1 - core) * rows, 8), rows)
        mine = pl.ds(pl.multiple_of(core * rows, 8), rows)
        c4 = remote(u.at[:, theirs, :], in4, s4, r4, partner)
        c4.start()
        out_ref[pl.ds(2 * core, 2)] = u[:, mine, :]
        c4.wait_recv()
        out_ref[pl.ds(2 - 2 * core, 2)] = in4[...]
        for c in c2 + c3 + [c4]:
            c.wait_send()
        for j in range(count):
            late_copy(j).wait_send()
        dx.wait()
        block.wait()


def tail(projected, lse, documents, vec, slot_rows, gate_rows, scale, chosen, normed, mixed, produced, dense_low,
         inputs, late, back, cotangent, hidden, dps, n):
    pairs = n // 2
    _, T, D = projected.shape
    rows = D // (dps * n)
    R = 2 * rows
    cap = produced.shape[1]
    count = late.shape[0]
    f32, bf = jnp.float32, jnp.bfloat16
    dma = pltpu.SemaphoreType.DMA
    any_ = pl.BlockSpec(memory_space=pl.ANY)

    def sp(c):
        return pl.BlockSpec((1, T, 128), lambda h, c=c: (c, 0, h))

    def fixed(shape):
        return pl.BlockSpec(shape, lambda h: (0,) * len(shape))

    return pl.pallas_call(
        partial(tail_kernel, dps, pairs, cap),
        grid=(D // 128,),
        out_shape=[
            jax.ShapeDtypeStruct((4, rows, D), f32),
            jax.ShapeDtypeStruct(vec.shape, f32),
            jax.ShapeDtypeStruct((T, D), f32),
            jax.ShapeDtypeStruct((T, D), f32),
        ],
        in_specs=[sp(0), sp(1), sp(2), pl.BlockSpec((1, T, 128), lambda h: (h, 0, 0)),
                  fixed((1, T)), fixed(vec.shape), fixed((8, T)), fixed((8, T)), fixed((8, 128)),
                  fixed(chosen.shape)]
        + [any_] * 9,
        out_specs=[fixed((4, rows, D)), fixed(vec.shape), any_, any_],
        scratch_shapes=[
            pltpu.VMEM((min(T, WINDOW + QB), T), f32),
            pltpu.VMEM((T, 128), f32),
            pltpu.VMEM((T, 128), f32),
            pltpu.VMEM((2, T, D), bf),
            pltpu.VMEM((4, T, D), bf),
            pltpu.VMEM((2, D, D), bf),
            pltpu.VMEM((2, D, D), f32),
            pltpu.VMEM((2, D, D), bf),
            pltpu.VMEM((dps, pairs, 2, R, D), bf),
            pltpu.VMEM((pairs, 2, R, D), bf),
            pltpu.VMEM((pairs, 2, R, D), bf),
            pltpu.VMEM((2, R, D), f32),
            pltpu.VMEM((2, rows, D), f32),
            pltpu.VMEM((4, D, D), bf),
            pltpu.VMEM((T, D), f32),
            pltpu.VMEM((T, D), bf),
            pltpu.VMEM((n, cap, D), bf),
            pltpu.VMEM((T, D), f32),
            pltpu.VMEM((n, cap, D), bf),
            pltpu.VMEM((T, D), bf),
            pltpu.VMEM((T, D), bf),
            pltpu.VMEM((8, n * cap), f32),
            pltpu.VMEM((T, 1), jnp.int32),
            dma((7,)), dma((2,)), dma((2,)), dma((dps, pairs)), dma((dps, pairs)), dma((pairs,)), dma((pairs,)),
            dma(()), dma(()), dma((n,)), dma((n,)), dma((count,)), dma((count,)), dma(()), dma(()), dma(()),
        ],
        compiler_params=pltpu.CompilerParams(
            vmem_limit_bytes=62 * 2**20, collective_id=3, has_side_effects=True
        ),
        cost_estimate=pl.CostEstimate(flops=40 * T * D * D, bytes_accessed=200 * 2**20, transcendentals=0),
    )(projected, projected, projected, lse, documents, vec, slot_rows,
      gate_rows, scale, chosen, normed, mixed, produced, dense_low, inputs, late, back, cotangent, hidden)


def norm_kernel(dps, pairs, d_ref, v_ref, e_ref, out_ref, a, b, c, s1, r1, s2, r2, s3, r3):
    d, pair, core, partner, over, along = near(dps, pairs)
    devices = [partner] + [x[1] for x in over] + [x[1] for x in along]
    barrier = pltpu.get_barrier_semaphore()
    for dev in devices:
        pl.semaphore_signal(barrier, inc=1, device_id=dev, device_id_type=MESH)

    def squares(ref):
        x = ref[...].astype(jnp.float32)
        return jnp.sum(x * x)

    part = squares(d_ref)
    for i in range(e_ref.shape[0]):
        part = part + squares(e_ref.at[i])
    pl.semaphore_wait(barrier, len(devices))
    last = lax.broadcasted_iota(jnp.int32, v_ref.shape, 0) == v_ref.shape[0] - 1
    a[core] = jnp.where(last, part, v_ref[...])
    cs = [remote(a.at[core], a.at[core], s1, r1.at[core], partner)]
    cs[0].start()
    remote(a.at[1 - core], a.at[1 - core], s1, r1.at[1 - core], partner).wait_recv()
    b[d] = a[0] + a[1]
    for dd, dev in over:
        x = remote(b.at[d], b.at[d], s2.at[dd], r2.at[d], dev)
        x.start()
        cs.append(x)
    for dd, dev in over:
        remote(b.at[dd], b.at[dd], s2.at[dd], r2.at[dd], dev).wait_recv()
    c[pair] = sum(b[k] for k in range(dps))
    for q, dev in along:
        x = remote(c.at[pair], c.at[pair], s3.at[q], r3.at[pair], dev)
        x.start()
        cs.append(x)
    for q, dev in along:
        remote(c.at[q], c.at[q], s3.at[q], r3.at[q], dev).wait_recv()
    out_ref[...] = sum(c[k] for k in range(pairs))
    for x in cs:
        x.wait_send()


def norm_squares(dense, vec, expert, k, dps, n):
    pairs = n // 2
    rows, D = vec.shape
    R = max(rows, (k // 8 + 1) * 8)
    dma = pltpu.SemaphoreType.DMA
    vm = pl.BlockSpec(memory_space=pltpu.VMEM)
    out = pl.pallas_call(
        partial(norm_kernel, dps, pairs),
        out_shape=jax.ShapeDtypeStruct((R, D), jnp.float32),
        in_specs=[vm] * 3,
        out_specs=vm,
        scratch_shapes=[
            pltpu.VMEM((2, R, D), jnp.float32),
            pltpu.VMEM((dps, R, D), jnp.float32),
            pltpu.VMEM((pairs, R, D), jnp.float32),
            dma(()), dma((2,)), dma((dps,)), dma((dps,)), dma((pairs,)), dma((pairs,)),
        ],
        compiler_params=pltpu.CompilerParams(
            vmem_limit_bytes=24 * 2**20, collective_id=4, has_side_effects=True
        ),
    )(dense, jnp.pad(vec, ((0, R - rows), (0, 0))), expert)
    total = out[:k]
    dev = lax.axis_index("dp") * n + lax.axis_index("expert")
    width = D // (dps * n)
    return lax.dynamic_slice_in_dim(total, dev * width, width, axis=1), out[R - 1, 0] + jnp.sum(total * total)


def adam_update(weight, gradient, first_moment, second_moment, average, factor, rate):
    clipped = gradient * factor
    first_new = beta_first * first_moment + (1.0 - beta_first) * clipped
    second_new = beta_second * second_moment + (1.0 - beta_second) * clipped * clipped
    first_hat = first_new / (1.0 - beta_first**STEP)
    second_hat = second_new / (1.0 - beta_second**STEP)
    updated = weight - rate * (
        first_hat / (jnp.sqrt(second_hat) + adam_eps) + weight_decay * weight
    )
    average_new = ema_keep * average + (1.0 - ema_keep) * updated
    return (updated, first_new, second_new, average_new)


def inverse_order(row_order, sorted_slot):
    at_token = row_order[:, None] == jnp.arange(row_order.shape[0])[None, :]
    return jnp.sum(jnp.where(at_token, sorted_slot[:, None], 0), axis=0)


def shards(
    inputs,
    cotangent,
    document_ids,
    domain_counts,
    domain_weight,
    token_order,
    expert_counts,
    dense_weights,
    vector_params,
    expert_weights,
    dense_first,
    dense_second,
    dense_average,
    vector_first,
    vector_second,
    vector_average,
    expert_first,
    expert_second,
    expert_average,
):
    tokens, model_width = inputs.shape
    experts_total = expert_counts.shape[1]
    capacity = 2 * tokens // experts_total
    owners = lax.axis_size("expert")
    groups = lax.axis_size(("dp", "expert"))
    sequences = tokens // LEN
    splits = lax.axis_size("dp")
    own_rows = dense_weights.shape[1]
    me = lax.axis_index("expert")
    seq_index = lax.axis_index("dp") * owners + jnp.arange(owners)
    domains = jnp.arange(NDOM)
    bounds = jnp.sum(jnp.where(domains[None, :] <= domains[:, None], domain_counts[None, :], 0), axis=1)
    domain = jnp.sum((seq_index[:, None] >= bounds[None, :]).astype(jnp.int32), axis=1)
    seq_pick = (domain[:, None] == jnp.arange(NDOM)[None, :]).astype(jnp.float32)
    seq_weight = jnp.sum(seq_pick * domain_weight[None, :], axis=1)
    seq_count = jnp.sum(seq_pick * domain_counts[None, :].astype(jnp.float32), axis=1)
    seq_scale = seq_weight * (sequences * groups) / (NDOM * seq_count)
    source_scale = jnp.broadcast_to(seq_scale[:, None], (owners, 128))
    documents = document_ids.reshape(-1)
    inputs_float = inputs.astype(jnp.float32)
    per = TILE // capacity
    fused = own_rows % 8 == 0 and capacity % 128 == 0 and splits == 4
    if fused:
        (dense_low, vec_rows, slot_rows, cot_received, projected, normed_low, mixed_low, totals,
         hidden_state, gate_rows, send_rows, gate_tiles, expert_low) = head(
            dense_weights, vector_params, inputs, cotangent, token_order, expert_counts, document_ids,
            expert_weights, splits, owners, capacity
        )
    else:
        row_counts = expert_counts[0]
        row_order = token_order[0]
        count_ends = jnp.cumsum(row_counts)
        count_starts = count_ends - row_counts
        sorted_pos = jnp.arange(tokens)
        sorted_expert = jnp.sum((sorted_pos[:, None] >= count_ends[None, :]).astype(jnp.int32), axis=1)
        sorted_pick = sorted_expert[:, None] == jnp.arange(experts_total)[None, :]
        sorted_start = jnp.sum(jnp.where(sorted_pick, count_starts[None, :], 0), axis=1)
        sorted_slot = sorted_expert * capacity + sorted_pos - sorted_start
        token_slot = inverse_order(row_order, sorted_slot)
        own_low = expert_weights[0].astype(jnp.bfloat16)
        expert_low = lax.all_gather(own_low, "dp", axis=0)
        dense_low, vector_low = (
            lax.all_gather(dense_weights.astype(jnp.bfloat16), ("dp", "expert"), axis=1, tiled=True),
            lax.all_gather(vector_params.astype(jnp.bfloat16), ("dp", "expert"), axis=1, tiled=True),
        )
        vector_low = vector_low.astype(jnp.float32)
        token_expert = token_slot // capacity
        expert_pick = (token_expert[:, None] == jnp.arange(experts_total)[None, :]).astype(jnp.float32)
        slot_match = token_slot[:, None] == jnp.arange(experts_total * capacity)[None, :]
        slot_pick = slot_match.astype(jnp.bfloat16)

        def to_slots(rows):
            placed = jnp.dot(slot_pick.T, rows, preferred_element_type=jnp.float32)
            return placed.astype(jnp.bfloat16).reshape(experts_total, capacity, model_width)

        def from_slots(rows):
            return jnp.dot(
                slot_pick, rows.reshape(-1, model_width), preferred_element_type=jnp.float32
            )

        cot_received = lax.all_to_all(
            to_slots(cotangent), "expert", split_axis=0, concat_axis=0, tiled=True
        )
        normed_one, norm_one_back = jax.vjp(layer_norm, inputs_float, vector_low[0])
        normed_low = normed_one.astype(jnp.bfloat16)
        projected = jnp.einsum(
            "td,cde->cte", normed_low, dense_low[:3], preferred_element_type=jnp.float32
        ).astype(jnp.bfloat16)
        mixed_low, totals = attend_forward(projected, documents)
        hidden_state = inputs_float + jnp.dot(
            mixed_low, dense_low[3], preferred_element_type=jnp.float32
        )
        normed_two, norm_two_back = jax.vjp(layer_norm, hidden_state, vector_low[1])
        centroids = vector_low[2:]
        logits = jnp.dot(normed_two, centroids.T, precision=lax.Precision.HIGHEST)
        gate_value = jax.nn.sigmoid(jnp.sum(logits * expert_pick, axis=1))
        send_rows = to_slots(normed_two.astype(jnp.bfloat16))
        gate_slots = jnp.sum(
            jnp.where(slot_match, gate_value[:, None], 0.0), axis=0
        ).reshape(experts_total, 1, 1, capacity)
        lane_part = (jnp.arange(per) == me % per).astype(jnp.float32)
        gate_tiles = jnp.broadcast_to(
            gate_slots * lane_part[None, None, :, None], (experts_total, 8, per, capacity)
        ).reshape(experts_total, 8, TILE)
    back_rows, late_rows, chosen_tiles, produced_low, grad_expert = moe(
        send_rows, gate_tiles, cot_received.reshape(-1, model_width), source_scale, expert_low, fused
    )
    expert_low_grad = lax.psum_scatter(grad_expert, "dp", scatter_dimension=0)
    expert_grad = expert_low_grad.astype(jnp.float32)[None]
    if fused:
        dense_grad, vector_grad, input_grad, block_output = tail(
            projected, totals, document_ids, vec_rows, slot_rows, gate_rows,
            jnp.broadcast_to(seq_scale[me], (8, 128)), chosen_tiles, normed_low, mixed_low, produced_low,
            dense_low, inputs, late_rows, back_rows, cotangent, hidden_state, splits, owners
        )
    else:
        late_rows = send_late(late_rows, owners)
        grad_out = cotangent.astype(jnp.float32) * seq_scale[me]
        back_slot = (token_slot // capacity ^ me) * capacity + token_slot % capacity
        back_match = back_slot[:, None] == jnp.arange(experts_total * capacity)[None, :]
        back_pick = back_match.astype(jnp.bfloat16)
        early = back_rows.shape[0] * capacity
        grad_sent_rows = jnp.dot(
            back_pick[:, :early], back_rows.reshape(-1, model_width), preferred_element_type=jnp.float32
        ) + jnp.dot(
            back_pick[:, early:], late_rows.reshape(-1, model_width), preferred_element_type=jnp.float32
        )
        chosen_slots = lax.dynamic_slice_in_dim(
            chosen_tiles[:, 0, :], me % per * capacity, capacity, axis=1
        )
        grad_chosen = jnp.sum(jnp.where(back_match, chosen_slots.reshape(1, -1), 0.0), axis=1)
        chosen_grad = grad_chosen[:, None] * expert_pick
        grad_normed_two = grad_sent_rows + jnp.dot(
            chosen_grad, centroids, precision=lax.Precision.HIGHEST
        )
        grad_centroids = jnp.dot(chosen_grad.T, normed_two, precision=lax.Precision.HIGHEST)
        grad_hidden_norm, grad_gain_two = norm_two_back(grad_normed_two)
        grad_hidden = grad_out + grad_hidden_norm
        grad_attn = grad_hidden.astype(jnp.bfloat16)
        grad_mixed = jnp.dot(grad_attn, dense_low[3].T, preferred_element_type=jnp.float32).astype(
            jnp.bfloat16
        )
        returned = lax.all_to_all(produced_low, "expert", split_axis=0, concat_axis=0, tiled=True)
        grad_proj = attend_backward(projected, documents, totals, grad_mixed)
        grad_normed_one = jnp.einsum(
            "cte,cde->td", grad_proj, dense_low[:3], preferred_element_type=jnp.float32
        )
        grad_input_norm, grad_gain_one = norm_one_back(grad_normed_one)
        input_grad = grad_hidden + grad_input_norm
        grad_in_proj = jnp.einsum(
            "td,cte->cde", normed_low, grad_proj, preferred_element_type=jnp.float32
        )
        grad_out_proj = jnp.dot(mixed_low.T, grad_attn, preferred_element_type=jnp.float32)
        dense_grad = lax.psum_scatter(
            jnp.concatenate([grad_in_proj, grad_out_proj[None]], axis=0),
            ("dp", "expert"),
            scatter_dimension=1,
            tiled=True,
        )
        returned_rows = from_slots(returned)
        block_output = hidden_state + gate_value[:, None] * returned_rows
        vector_grad = jnp.concatenate(
            [grad_gain_one[None], grad_gain_two[None], grad_centroids], axis=0
        )
    vector_grad, squares = norm_squares(
        dense_grad, vector_grad, expert_low_grad, vector_params.shape[0], splits, owners
    )
    grad_norm = jnp.sqrt(squares)
    factor = jnp.minimum(1.0, clip_norm / (grad_norm + 1e-06))
    dense_new = adam_update(
        dense_weights, dense_grad, dense_first, dense_second, dense_average, factor, dense_rate
    )
    vector_new = adam_update(
        vector_params, vector_grad, vector_first, vector_second, vector_average, factor, vector_rate
    )
    expert_new = adam_update(
        expert_weights,
        expert_grad,
        expert_first,
        expert_second,
        expert_average,
        factor,
        expert_rate,
    )
    return (
        block_output,
        input_grad,
        dense_new[0],
        dense_new[1],
        dense_new[2],
        dense_new[3],
        vector_new[0],
        vector_new[1],
        vector_new[2],
        vector_new[3],
        expert_new[0],
        expert_new[1],
        expert_new[2],
        expert_new[3],
        grad_norm,
    )


def solution(mesh):
    placed = (
        P(("dp", "expert"), None),
        P(("dp", "expert"), None),
        P(("dp", "expert"), None),
        P(),
        P(),
        P(("dp", "expert"), None),
        P(("dp", "expert"), None),
        P(None, ("dp", "expert"), None),
        P(None, ("dp", "expert")),
        P("expert", None, None, "dp"),
        P(None, ("dp", "expert"), None),
        P(None, ("dp", "expert"), None),
        P(None, ("dp", "expert"), None),
        P(None, ("dp", "expert")),
        P(None, ("dp", "expert")),
        P(None, ("dp", "expert")),
        P("expert", None, None, "dp"),
        P("expert", None, None, "dp"),
        P("expert", None, None, "dp"),
    )
    return jax.shard_map(
        shards,
        mesh=mesh,
        in_specs=placed,
        out_specs=(
            P(("dp", "expert"), None),
            P(("dp", "expert"), None),
            P(None, ("dp", "expert"), None),
            P(None, ("dp", "expert"), None),
            P(None, ("dp", "expert"), None),
            P(None, ("dp", "expert"), None),
            P(None, ("dp", "expert")),
            P(None, ("dp", "expert")),
            P(None, ("dp", "expert")),
            P(None, ("dp", "expert")),
            P("expert", None, None, "dp"),
            P("expert", None, None, "dp"),
            P("expert", None, None, "dp"),
            P("expert", None, None, "dp"),
            P(),
        ),
        check_vma=False,
    )
```
